32 devices in a mesh: dp: 4 (over y, core), seq: 8 (over z, x).
Axes of the slice: x: 2, y: 2, z: 4, core: 2. Of those that a mesh axis runs over, the one named last changes fastest.
Arguments:
- tokens: bfloat16 [4, 2048, 1024], P('dp', 'seq'), may hold values from -6 to 6
- w_qkv: bfloat16 [1024, 3072], P('seq'), may hold values from -0.25 to 0.25
- w_out: bfloat16 [1024, 1024], P('seq'), may hold values from -3 to 3
- w_up: bfloat16 [1024, 4096], P('seq'), may hold values from -0.1875 to 0.1875
- w_down: bfloat16 [4096, 1024], P('seq'), may hold values from -0.09375 to 0.09375
- g_attn: bfloat16 [1024], P('seq'), may hold values from 0.5 to 1.5
- g_mlp: bfloat16 [1024], P('seq'), may hold values from 0.5 to 1.5
- ssm_rate: bfloat16 [1024, 16], P('seq'), may hold values from 2.4318695e-05 to 0.049804688
- ssm_in: bfloat16 [1024, 16], P('seq'), may hold values from -0.29882812 to 0.29882812
- ssm_out: bfloat16 [1024, 16], P('seq'), may hold values from -1.5 to 1.5
- h_init: float32 [4, 1024, 16], P('dp'), may hold values from -4 to 4
- cotangent: bfloat16 [4, 2048, 1024], P('dp', 'seq'), may hold values from -6 to 6
- d_h_ends: float32 [4, 8, 1024, 16], P('dp', 'seq'), may hold values from -6 to 6
Outputs:
- result: bfloat16 [4, 2048, 1024], P('dp', 'seq')
- d_tokens: bfloat16 [4, 2048, 1024], P('dp', 'seq')
- d_w_qkv: float32 [1024, 3072], P('seq')
- d_w_out: float32 [1024, 1024], P('seq')
- d_w_up: float32 [1024, 4096], P('seq')
- d_w_down: float32 [4096, 1024], P('seq')
- d_g_attn: float32 [1024], P('seq')
- d_g_mlp: float32 [1024], P('seq')
- d_ssm_rate: float32 [1024, 16], P('seq')
- d_ssm_in: float32 [1024, 16], P('seq')
- d_ssm_out: float32 [1024, 16], P('seq')
- d_h_init: float32 [4, 1024, 16], P('dp', 'seq')
- h_ends: float32 [4, 8, 1024, 16], P('dp', 'seq')
The draws below stay inside these ranges and needn't reach their ends.
All inputs are finite; a program needn't handle non-finite values.
Results may differ from the reference program's by a relative error of at most 0.019.
Values may be sent and summed in bfloat16 or wider, within the bound.
No kernel may reach another device: no remote copies, remote signals or barrier semaphores. Data moves between devices by JAX's collectives and lax.ppermute only.
A program may use at most 256 MiB of HBM per device.

```python
import math
from functools import partial
import jax
import jax.numpy as jnp
from jax import lax

D = 1024
HEADS = 8
HD = 128
NST = 16
FF = 4096
BLK = 512
CTX = 128
TDEV = 256
LENGTH = 2048
WINDOWS = 4
N_SEQ = 8


def block_scale(stream_key, shape, cuts, low, largest):
    loudness = 1.0
    for dim, blocks in cuts:
        heights = jax.random.uniform(jax.random.fold_in(jax.random.fold_in(stream_key, 6), dim), (blocks,), jnp.float32, low / len(cuts), largest / len(cuts))
        loudness = loudness * jnp.repeat(jnp.exp(heights), shape[dim] // blocks).reshape((-1,) + (1,) * (len(shape) - 1 - dim))
    return loudness


def scatter_about(key, dims, deviation, bound, shards=(), dtype=jnp.bfloat16):
    loudness = block_scale(key, dims, shards, -0.22, 0.18) if shards else 1.0
    array = jax.random.normal(key, dims, jnp.float32) * deviation * loudness
    return jnp.minimum(jnp.maximum(array, -bound), bound).astype(dtype)


def setup_inputs(seed: int = 0) -> dict:
    keys = jax.random.split(jax.random.key(seed), 14)
    tokens = scatter_about(keys[0], (WINDOWS, LENGTH, D), 1.0, 6.0, ((0, 4), (1, 8)))
    w_qkv = scatter_about(keys[1], (D, 3 * D), (D // 2) ** -0.5, 0.25, ((0, 8),))
    w_out = scatter_about(keys[2], (D, D), (max(D // 256, 1)) ** -0.5, 3.0, ((0, 8),))
    w_up = scatter_about(keys[3], (D, FF), D ** -0.5, 0.1875, ((0, 8),))
    w_down = scatter_about(keys[4], (FF, D), FF ** -0.5, 0.09375, ((0, 8),))
    g_attn = jnp.clip(1.0 + 0.1 * jax.random.normal(keys[5], (D,), jnp.float32), 0.5, 1.5).astype(jnp.bfloat16)
    g_mlp = jnp.clip(1.0 + 0.1 * jax.random.normal(keys[6], (D,), jnp.float32), 0.5, 1.5).astype(jnp.bfloat16)
    ssm_rate = jnp.clip(jnp.exp(math.log(0.049804688) - 7.624619 * jax.random.uniform(keys[7], (D, NST), jnp.float32) ** block_scale(keys[7], (D, NST), ((0, 8),), -0.2, 0.2)), 2.4318695068359375e-05, 0.049804688).astype(jnp.bfloat16)
    ssm_in = scatter_about(keys[8], (D, NST), 0.05, 0.29882812, ((0, 8),))
    ssm_out = scatter_about(keys[9], (D, NST), NST ** -0.5, 1.5, ((0, 8),))
    h_init = scatter_about(keys[10], (WINDOWS, D, NST), 1.0, 4.0, ((0, 4),), jnp.float32)
    cotangent = scatter_about(keys[11], (WINDOWS, LENGTH, D), 1.0, 6.0, ((0, 4), (1, 8)))
    d_h_ends = scatter_about(keys[12], (WINDOWS, N_SEQ, D, NST), 1.0, 6.0, ((0, 4), (1, 8)), jnp.float32)
    return dict(tokens=tokens, w_qkv=w_qkv, w_out=w_out, w_up=w_up, w_down=w_down, g_attn=g_attn, g_mlp=g_mlp, ssm_rate=ssm_rate, ssm_in=ssm_in, ssm_out=ssm_out, h_init=h_init, cotangent=cotangent, d_h_ends=d_h_ends)


epsilon = 1e-05
highest = lax.Precision.HIGHEST
far_below = -1e+30

@jax.custom_vjp
def low(v):
    return lax.optimization_barrier(v.astype(jnp.bfloat16)).astype(jnp.float32)

@jax.custom_vjp
def low_back(v):
    return v

def low_keep(v):
    return (low(v), None)

def low_pass(kept, grad):
    return (grad,)

def back_keep(v):
    return (v, None)

def back_low(kept, grad):
    return (low(grad),)
low.defvjp(low_keep, low_pass)
low_back.defvjp(back_keep, back_low)

def end_state(inputs, decay_rate, gain_in):
    row_count = inputs.shape[1]
    lag_values = (row_count - 1 - jnp.arange(row_count)).astype(jnp.float32)
    powers = jnp.exp(-decay_rate[None] * lag_values[:, None, None])
    return jnp.einsum('wsd,sdn->wdn', inputs, powers, precision=highest) * gain_in[None]

def init_readout(state, decay_rate, gain_out):
    steps_ahead = (jnp.arange(CTX) + 1).astype(jnp.float32)
    factors = gain_out[None] * jnp.exp(-decay_rate[None] * steps_ahead[:, None, None])
    return jnp.einsum('wdn,kdn->wkd', state, factors, precision=highest)

def ssm_context(inputs, decay_rate, gain_in, gain_out, state_in):
    win_count = inputs.shape[0]
    row_count = inputs.shape[1]
    model_dim = inputs.shape[2]
    middle = row_count - CTX
    group_len = min(16, CTX)
    group_count = CTX // group_len
    mid_state = jnp.exp(-decay_rate * middle)[None] * state_in + end_state(inputs[:, :middle], decay_rate, gain_in)
    tail_rows = inputs[:, middle:].reshape(win_count, group_count, group_len, model_dim)
    offsets = jnp.arange(group_len).astype(jnp.float32)
    lag_grid = offsets[:, None] - offsets[None, :]
    kernel = jnp.exp(-decay_rate[None, None] * jnp.maximum(lag_grid, 0.0)[:, :, None, None])
    toeplitz = jnp.where((lag_grid >= 0.0)[:, :, None], lax.optimization_barrier(jnp.sum(kernel * (gain_in * gain_out)[None, None], axis=3)), 0.0)
    inner_part = jnp.einsum('wgsd,tsd->wgtd', tail_rows, toeplitz, precision=highest)
    tail_powers = jnp.exp(-decay_rate[None] * (group_len - 1.0 - offsets)[:, None, None])
    group_ends = jnp.einsum('wgsd,sdn->wgdn', tail_rows, tail_powers, precision=highest) * gain_in
    group_ids = jnp.arange(group_count).astype(jnp.float32)
    gap_grid = group_ids[:, None] - group_ids[None, :] - 1.0
    carry_mat = jnp.where((gap_grid >= 0.0)[:, :, None, None], jnp.exp(-decay_rate * group_len * jnp.maximum(gap_grid, 0.0)[:, :, None, None]), 0.0)
    start_states = jnp.exp(-decay_rate * group_len * group_ids[:, None, None])[None] * mid_state[:, None] + jnp.einsum('gjdn,wjdn->wgdn', carry_mat, group_ends, precision=highest)
    readout = gain_out * jnp.exp(-decay_rate * (offsets + 1.0)[:, None, None])
    combined = inner_part + jnp.einsum('wgdn,tdn->wgtd', start_states, readout, precision=highest)
    return combined.reshape(win_count, CTX, model_dim)

def rms_scale(values):
    return values * lax.rsqrt(lax.optimization_barrier(jnp.mean(values * values, axis=-1, keepdims=True)) + epsilon)

def block_attention(item):
    qkv_block, context_kv = item
    queries = qkv_block[:, :, :D].reshape(1, BLK, HEADS, HD)
    all_kv = jnp.concatenate([context_kv, qkv_block[:, :, D:]], axis=1)
    key_heads = all_kv[:, :, :D].reshape(1, CTX + BLK, HEADS, HD)
    value_heads = all_kv[:, :, D:].reshape(1, CTX + BLK, HEADS, HD)
    scores = low_back(jnp.einsum('wthe,wkhe->whtk', queries, key_heads, precision=highest) / math.sqrt(HD))
    keep_mask = jnp.concatenate([jnp.ones((BLK, CTX), jnp.int32) > 0, jnp.tril(jnp.ones((BLK, BLK), jnp.int32)) > 0], axis=1)
    probs = low(jax.nn.softmax(jnp.where(keep_mask, scores, far_below), axis=-1))
    return jnp.einsum('whtk,wkhe->wthe', probs, value_heads, precision=highest).reshape(1, BLK, D)

def window_forward(params, window):
    w_qkv, w_out, w_up, w_down, g_attn, g_mlp, decay_rate, state_gain, read_gain = params
    x_float = window[0][None]
    state_init = window[1][None]
    inputs = low(rms_scale(x_float) * g_attn)
    qkv = low(low_back(jnp.einsum('wtd,de->wte', inputs, w_qkv, precision=highest)))
    segments = jnp.moveaxis(inputs.reshape(1, N_SEQ, TDEV, D), 1, 0)

    def segment_step(state, segment):
        context = ssm_context(segment, decay_rate, state_gain, read_gain, state)
        new_state = jnp.exp(-decay_rate * TDEV)[None] * state + end_state(segment, decay_rate, state_gain)
        return (new_state, (context, new_state))
    last_state, outs = lax.scan(jax.checkpoint(segment_step), state_init, segments)
    contexts, ends = outs
    block_count = N_SEQ // 2
    first_context = init_readout(state_init, decay_rate, read_gain)[None]
    previous = jnp.concatenate([first_context, contexts[1::2][:-1]], axis=0)
    context_kv = low(low_back(jnp.einsum('bwcd,de->bwce', low(previous), w_qkv[:, D:], precision=highest)))
    qkv_blocks = jnp.moveaxis(qkv.reshape(1, block_count, BLK, 3 * D), 1, 0)
    attended = lax.map(jax.checkpoint(block_attention), (qkv_blocks, context_kv))
    attended = low(low_back(jnp.moveaxis(attended, 0, 1).reshape(1, LENGTH, D)))
    hidden = x_float + low_back(jnp.einsum('wtd,de->wte', attended, w_out, precision=highest))
    mlp_in = low(rms_scale(hidden) * g_mlp)
    pre_act = low_back(jnp.einsum('wtd,df->wtf', mlp_in, w_up, precision=highest))
    act_vals = low(jax.nn.gelu(pre_act, approximate=True))
    return ((hidden + jnp.einsum('wtf,fd->wtd', act_vals, w_down, precision=highest))[0], ends[:, 0])

def whole(x_float, state_init, params):
    return lax.map(jax.checkpoint(partial(window_forward, params)), (x_float, state_init))

def reference(tokens, w_qkv, w_out, w_up, w_down, g_attn, g_mlp, ssm_rate, ssm_in, ssm_out, h_init, cotangent, d_h_ends):
    params = (w_qkv.astype(jnp.float32), w_out.astype(jnp.float32), w_up.astype(jnp.float32), w_down.astype(jnp.float32), g_attn.astype(jnp.float32), g_mlp.astype(jnp.float32), ssm_rate.astype(jnp.float32), ssm_in.astype(jnp.float32), ssm_out.astype(jnp.float32))
    output, pullback = jax.vjp(whole, tokens.astype(jnp.float32), h_init.astype(jnp.float32), params)
    d_input, d_state, d_params = pullback((cotangent.astype(jnp.float32), d_h_ends.astype(jnp.float32)))
    return (output[0].astype(jnp.bfloat16), d_input.astype(jnp.bfloat16), d_params[0], d_params[1], d_params[2], d_params[3], d_params[4], d_params[5], d_params[6], d_params[7], d_params[8], d_state, output[1])
```

```python
import functools
import math

import jax
import jax.numpy as jnp
from jax import lax
from jax.experimental import pallas as pl
from jax.experimental.pallas import tpu as pltpu
from jax.sharding import PartitionSpec as P

HEADS = 8
HD = 128
CTX = 128
NST = 16
LANES = 128
GROUP = 4

epsilon = 1e-05
far_below = -1e30
bf16 = jnp.bfloat16
f32 = jnp.float32


def bits_of(axis):
    size = lax.axis_size(axis)
    return [1 << k for k in reversed(range(size.bit_length() - 1))]


def swap(a, axis, bit):
    return lax.ppermute(a, axis, [(k, k ^ bit) for k in range(lax.axis_size(axis))])


def gather_blocks(a, axis):
    blocks = {0: a}
    for bit in bits_of(axis):
        for r in list(blocks):
            blocks[r | bit] = swap(blocks[r], axis, bit)
    return [blocks[r] for r in range(lax.axis_size(axis))]


def gather_packed(a, axis):
    packed, order = a[None], [0]
    for bit in bits_of(axis):
        packed = jnp.concatenate([packed, swap(packed, axis, bit)], axis=0)
        order = order + [r | bit for r in order]
    return [packed[order.index(r)] for r in range(lax.axis_size(axis))]


def sum_to_owner(parts, axis):
    parts = dict(enumerate(parts))
    for bit in reversed(bits_of(axis)):
        for r in [r for r in parts if r & bit]:
            parts[r ^ bit] = parts[r ^ bit] + swap(parts.pop(r).astype(bf16), axis, bit).astype(f32)
    return parts[0]


def sum_to_owner_packed(parts, axis):
    parts = dict(enumerate(parts))
    for bit in reversed(bits_of(axis)):
        away = [r for r in parts if r & bit]
        got = swap(jnp.stack([parts.pop(r) for r in away]), axis, bit)
        for k, r in enumerate(away):
            parts[r ^ bit] = parts[r ^ bit] + got[k]
    return parts[0]


def trade(parts, axis):
    return [parts[0]] + [swap(parts[r], axis, r) for r in range(1, len(parts))]


def absolute(blocks, axis):
    here = lax.axis_index(axis)
    for bit in bits_of(axis):
        flip = (here & bit) != 0
        blocks = [jnp.where(flip, blocks[r ^ bit], blocks[r]) for r in range(len(blocks))]
    return blocks


def pick(a, index, axis=0):
    return lax.dynamic_index_in_dim(a, index, axis, False)


def moved(a, axis, pairs):
    return lax.ppermute(a, axis, pairs)


def whole_spec():
    return pl.BlockSpec(memory_space=pltpu.VMEM)


def ends_kernel(mid, u_ref, a_ref, mid_ref, end_ref):
    rows = u_ref.shape[0]
    a = [a_ref[n] for n in range(NST)]

    def eight(k, s):
        for t in range(8):
            u = u_ref[k * 8 + t]
            s = tuple(a[n] * s[n] + u for n in range(NST))
        return s

    zero = tuple(jnp.zeros_like(a[0]) for _ in range(NST))
    s = lax.fori_loop(0, mid // 8, eight, zero)
    for n in range(NST):
        mid_ref[n] = s[n]
    s = lax.fori_loop(mid // 8, rows // 8, eight, s)
    for n in range(NST):
        end_ref[n] = s[n]


def local_ends(u, a):
    shape = jax.ShapeDtypeStruct(a.shape, f32)
    return pl.pallas_call(
        functools.partial(ends_kernel, u.shape[0] - CTX),
        out_shape=(shape, shape),
        in_specs=[whole_spec()] * 2,
        out_specs=(whole_spec(),) * 2,
        name="ssm_ends",
    )(u, a)


def context_kernel(mid, u_ref, a_ref, gin_ref, gout_ref, h_ref, init_ref, y_ref, y0_ref):
    half = NST // 2
    for base in (0, half):
        ns = range(base, base + half)
        a = [a_ref[n] for n in ns]
        gin = [gin_ref[n] for n in ns]
        gout = [gout_ref[n] for n in ns]

        def step(k, h):
            for t in range(4):
                p = k * 4 + t
                u = u_ref[mid + p]
                h = tuple(a[n] * h[n] + gin[n] * u for n in range(half))
                y = functools.reduce(jnp.add, [gout[n] * h[n] for n in range(half)])
                y_ref[p] = y if base == 0 else y_ref[p] + y
            return h

        def start(k, h):
            for t in range(4):
                p = k * 4 + t
                h = tuple(a[n] * h[n] for n in range(half))
                y = functools.reduce(jnp.add, [gout[n] * h[n] for n in range(half)])
                y0_ref[p] = y if base == 0 else y0_ref[p] + y
            return h

        lax.fori_loop(0, CTX // 4, step, tuple(h_ref[n] for n in ns))
        lax.fori_loop(0, CTX // 4, start, tuple(init_ref[n] for n in ns))


def contexts(u, a, gin, gout, h_mid, h_init):
    shape = jax.ShapeDtypeStruct((CTX,) + u.shape[1:], f32)
    return pl.pallas_call(
        functools.partial(context_kernel, u.shape[0] - CTX),
        out_shape=(shape, shape),
        in_specs=[whole_spec()] * 6,
        out_specs=(whole_spec(),) * 2,
        name="ssm_context",
    )(u, a, gin, gout, h_mid, h_init)


def tail_kernel(dy_ref, a_ref, gout_ref, lam_ref):
    a = [a_ref[n] for n in range(NST)]
    gout = [gout_ref[n] for n in range(NST)]

    def eight(k, lam):
        for t in range(8):
            dy = dy_ref[CTX - 1 - (k * 8 + t)]
            lam = tuple(a[n] * lam[n] + gout[n] * dy for n in range(NST))
        return lam

    lam = lax.fori_loop(0, CTX // 8, eight, tuple(jnp.zeros_like(a[0]) for _ in range(NST)))
    for n in range(NST):
        lam_ref[n] = lam[n]


def tail_adjoint(dy, a, gout):
    return pl.pallas_call(
        tail_kernel,
        out_shape=jax.ShapeDtypeStruct(a.shape, f32),
        in_specs=[whole_spec()] * 3,
        out_specs=whole_spec(),
        name="ssm_tail",
    )(dy, a, gout)


def back_kernel(
    u_ref, dy_ref, dy0_ref, a_ref, gin_ref, gout_ref, h_ref, lam_ref, init_ref,
    du_ref, dgin_ref, da_ref, dgout_ref, g_ref, g0_ref, hs,
):
    first = pl.program_id(0) == 0
    rows = u_ref.shape[0]
    mid = rows - CTX
    ns = range(GROUP)
    a = [a_ref[n] for n in ns]
    gin = [gin_ref[n] for n in ns]
    gout = [gout_ref[n] for n in ns]
    zero = tuple(jnp.zeros_like(a[0]) for _ in ns)

    def ahead(k, h):
        for t in range(8):
            p = k * 8 + t
            u = u_ref[p]
            h = tuple(a[n] * h[n] + gin[n] * u for n in ns)
            for n in ns:
                hs[p + 1, n] = h[n]
        return h

    h = tuple(h_ref[n] for n in ns)
    for n in ns:
        hs[0, n] = h[n]
    lax.fori_loop(0, rows // 8, ahead, h)

    def tail(k, carry):
        lam, dgin, da, dgout = carry
        for t in range(4):
            q = CTX - 1 - (k * 4 + t)
            p = mid + q
            dy, u = dy_ref[q], u_ref[p]
            lam = tuple(lam[n] + gout[n] * dy for n in ns)
            dgout = tuple(dgout[n] + dy * hs[p + 1, n] for n in ns)
            dgin = tuple(dgin[n] + lam[n] * u for n in ns)
            da = tuple(da[n] + lam[n] * hs[p, n] for n in ns)
            du = functools.reduce(jnp.add, [gin[n] * lam[n] for n in ns])
            du_ref[p] = jnp.where(first, du, du_ref[p] + du)
            lam = tuple(a[n] * lam[n] for n in ns)
        return lam, dgin, da, dgout

    def head(k, carry):
        lam, dgin, da = carry
        for t in range(4):
            p = mid - 1 - (k * 4 + t)
            u = u_ref[p]
            dgin = tuple(dgin[n] + lam[n] * u for n in ns)
            da = tuple(da[n] + lam[n] * hs[p, n] for n in ns)
            du = functools.reduce(jnp.add, [gin[n] * lam[n] for n in ns])
            du_ref[p] = jnp.where(first, du, du_ref[p] + du)
            lam = tuple(a[n] * lam[n] for n in ns)
        return lam, dgin, da

    lam = tuple(lam_ref[n] for n in ns)
    lam, dgin, da, dgout = lax.fori_loop(0, CTX // 4, tail, (lam, zero, zero, zero))
    lam, dgin, da = lax.fori_loop(0, mid // 4, head, (lam, dgin, da))
    for n in ns:
        g_ref[n] = lam[n]
        dgin_ref[n] = dgin[n]

    def ahead_init(k, h):
        for t in range(8):
            h = tuple(a[n] * h[n] for n in ns)
            for n in ns:
                hs[k * 8 + t + 1, n] = h[n]
        return h

    h = tuple(init_ref[n] for n in ns)
    for n in ns:
        hs[0, n] = h[n]
    lax.fori_loop(0, CTX // 8, ahead_init, h)

    def back_init(k, carry):
        mu, da, dgout = carry
        for t in range(4):
            q = CTX - 1 - (k * 4 + t)
            dy = dy0_ref[q]
            mu = tuple(mu[n] + gout[n] * dy for n in ns)
            dgout = tuple(dgout[n] + dy * hs[q + 1, n] for n in ns)
            da = tuple(da[n] + mu[n] * hs[q, n] for n in ns)
            mu = tuple(a[n] * mu[n] for n in ns)
        return mu, da, dgout

    mu, da, dgout = lax.fori_loop(0, CTX // 4, back_init, (zero, da, dgout))
    for n in ns:
        g0_ref[n] = mu[n]
        da_ref[n] = da[n]
        dgout_ref[n] = dgout[n]


def ssm_back(u, dy, dy0, a, gin, gout, state_in, lam_end, h_init):
    tile = u.shape[1:]
    states = pl.BlockSpec((GROUP,) + tile, lambda g: (g, 0, 0))
    rows = pl.BlockSpec(u.shape, lambda g: (0, 0, 0))
    tail = pl.BlockSpec(dy.shape, lambda g: (0, 0, 0))
    out = jax.ShapeDtypeStruct(a.shape, f32)
    return pl.pallas_call(
        back_kernel,
        grid=(NST // GROUP,),
        out_shape=(jax.ShapeDtypeStruct(u.shape, f32),) + (out,) * 5,
        in_specs=[rows, tail, tail] + [states] * 6,
        out_specs=(rows,) + (states,) * 5,
        scratch_shapes=[pltpu.VMEM((u.shape[0] + 1, GROUP) + tile, f32)],
        compiler_params=pltpu.CompilerParams(vmem_limit_bytes=24 * 2**20),
        name="ssm_back",
    )(u, dy, dy0, a, gin, gout, state_in, lam_end, h_init)


def dot_nt(x, y):
    return lax.dot_general(x, y, (((1,), (1,)), ((), ())), preferred_element_type=f32)


def dot_nn(x, y):
    return jnp.dot(x, y, preferred_element_type=f32)


def dot_tn(x, y):
    return lax.dot_general(x, y, (((0,), (0,)), ((), ())), preferred_element_type=f32)


def softmax_parts(second, q, k_ctx, k_prev, k_own):
    rows = q.shape[0]
    scale = 1.0 / math.sqrt(HD)
    s_ctx = dot_nt(q, k_ctx) * scale
    s_prev = jnp.where(second, dot_nt(q, k_prev) * scale, far_below)
    at = lax.broadcasted_iota(jnp.int32, (rows, rows), 0)
    to = lax.broadcasted_iota(jnp.int32, (rows, rows), 1)
    s_own = jnp.where(to <= at, dot_nt(q, k_own) * scale, far_below)
    tops = [jnp.max(s, axis=-1, keepdims=True) for s in (s_ctx, s_prev, s_own)]
    top = jnp.maximum(jnp.maximum(tops[0], tops[1]), tops[2])
    es = [jnp.exp(s - top) for s in (s_ctx, s_prev, s_own)]
    sums = [jnp.sum(e, axis=-1, keepdims=True) for e in es]
    total = sums[0] + sums[1] + sums[2]
    return [e / total for e in es]


def attend_kernel(second_ref, q_ref, ko_ref, vo_ref, kp_ref, vp_ref, kc_ref, vc_ref, out_ref):
    second = second_ref[0] == 1
    probs = softmax_parts(second, q_ref[...], kc_ref[...], kp_ref[...], ko_ref[...])
    out = functools.reduce(
        jnp.add, [dot_nn(p.astype(bf16), v[...]) for p, v in zip(probs, (vc_ref, vp_ref, vo_ref))]
    )
    out_ref[...] = out.astype(bf16)


def attend_back_kernel(
    second_ref, q_ref, ko_ref, vo_ref, kp_ref, vp_ref, kc_ref, vc_ref, do_ref,
    dq_ref, dko_ref, dvo_ref, dkp_ref, dvp_ref, dkc_ref, dvc_ref,
):
    second = second_ref[0] == 1
    scale = 1.0 / math.sqrt(HD)
    q, d_out = q_ref[...], do_ref[...]
    probs = softmax_parts(second, q, kc_ref[...], kp_ref[...], ko_ref[...])
    d_probs = [dot_nt(d_out, v[...]) for v in (vc_ref, vp_ref, vo_ref)]
    delta = functools.reduce(
        jnp.add, [jnp.sum(p * d, axis=-1, keepdims=True) for p, d in zip(probs, d_probs)]
    )
    d_scores = [(p * (d - delta)).astype(bf16) for p, d in zip(probs, d_probs)]
    dq = functools.reduce(
        jnp.add, [dot_nn(d, k[...]) for d, k in zip(d_scores, (kc_ref, kp_ref, ko_ref))]
    )
    dq_ref[...] = (dq * scale).astype(dq_ref.dtype)
    for d, ref in zip(d_scores, (dkc_ref, dkp_ref, dko_ref)):
        ref[...] = (dot_tn(d, q) * scale).astype(ref.dtype)
    for p, ref in zip(probs, (dvc_ref, dvp_ref, dvo_ref)):
        ref[...] = dot_tn(p.astype(bf16), d_out).astype(ref.dtype)


def attention_specs(rows, heads):
    def at(size, part):
        return pl.BlockSpec((size, HD), lambda w, h, s: (w, part * heads + h))

    return [at(rows, 0), at(rows, 1), at(rows, 2), at(rows, 0), at(rows, 1), at(CTX, 0), at(CTX, 1)]


def attend(second, qkv, prev_kv, ctx_kv, windows):
    rows, heads = qkv.shape[0] // windows, qkv.shape[1] // (3 * HD)
    return pl.pallas_call(
        attend_kernel,
        grid_spec=pltpu.PrefetchScalarGridSpec(
            num_scalar_prefetch=1,
            grid=(windows, heads),
            in_specs=attention_specs(rows, heads),
            out_specs=pl.BlockSpec((rows, HD), lambda w, h, s: (w, h)),
        ),
        out_shape=jax.ShapeDtypeStruct((qkv.shape[0], heads * HD), bf16),
        name="attend",
    )(second, qkv, qkv, qkv, prev_kv, prev_kv, ctx_kv, ctx_kv)


def attend_back(second, qkv, prev_kv, ctx_kv, d_attended, windows):
    rows, heads = qkv.shape[0] // windows, qkv.shape[1] // (3 * HD)

    def at(size):
        return pl.BlockSpec((size, HD), lambda w, h, s: (w, h))

    def shape(size, dtype):
        return jax.ShapeDtypeStruct((windows * size, heads * HD), dtype)

    return pl.pallas_call(
        attend_back_kernel,
        grid_spec=pltpu.PrefetchScalarGridSpec(
            num_scalar_prefetch=1,
            grid=(windows, heads),
            in_specs=attention_specs(rows, heads) + [at(rows)],
            out_specs=[at(rows)] * 5 + [at(CTX)] * 2,
        ),
        out_shape=[shape(rows, bf16)]
        + [shape(rows, f32)] * 2
        + [shape(rows, bf16)] * 2
        + [shape(CTX, bf16)] * 2,
        name="attend_back",
    )(second, qkv, qkv, qkv, prev_kv, prev_kv, ctx_kv, ctx_kv, d_attended)


def gelu_tanh(values):
    return jax.nn.gelu(values, approximate=True)


def norm_back(grad_normed, normed, inv_scale, gain):
    scaled = grad_normed * gain
    return inv_scale * (scaled - normed * jnp.mean(scaled * normed, axis=-1, keepdims=True))


def on_device(
    tokens,
    w_qkv,
    w_out,
    w_up,
    w_down,
    g_attn,
    g_mlp,
    ssm_rate,
    ssm_in,
    ssm_out,
    h_init,
    cotangent,
    d_h_ends,
):
    nd, ns = lax.axis_size("dp"), lax.axis_size("seq")
    me, place = lax.axis_index("dp"), lax.axis_index("seq")
    second = place % 2
    first_block = place < 2
    rows, dim = tokens.shape[1:]
    shard = w_qkv.shape[0]
    width = HEADS * HD // nd
    cols = dim // nd
    down_rows = w_down.shape[0] // nd
    chans = shard // nd
    tile = (dim // LANES, LANES)

    x_blocks = gather_blocks(tokens[0], "dp")
    mine = [pick(p.reshape(nd, chans * NST), me) for p in (ssm_rate, ssm_in, ssm_out)]
    small = jnp.concatenate([g_attn, g_mlp] + mine).reshape(-1, LANES)
    small = jnp.stack(absolute(gather_packed(small, "seq"), "seq")).reshape(ns, -1).astype(f32)
    gain_one = small[:, :shard].reshape(dim)
    gain_two = small[:, shard : 2 * shard].reshape(dim)
    params = small[:, 2 * shard :].reshape(ns, 3, chans, NST)
    params = params.transpose(1, 3, 0, 2).reshape(3, NST, 1, ns * chans)
    params = jnp.broadcast_to(params, (3, NST, nd, ns * chans)).reshape((3, NST) + tile)
    rate, gin, gout = params[0], params[1], params[2]

    def gathered(part):
        return lax.all_gather(part, "seq", axis=0, tiled=True)

    full_qkv = gathered(pick(w_qkv.reshape(shard, 3, nd, width), me, 2).reshape(shard, 3 * width))
    full_out = gathered(pick(w_out.reshape(shard, nd, cols), me, 1))
    full_up = gathered(
        pick(w_up.reshape(shard, ns, nd, down_rows), me, 2).reshape(shard, ns * down_rows)
    )
    full_down = gathered(pick(w_down.reshape(nd, down_rows, dim), me))
    full_out = full_out.reshape(nd, width, cols)
    full_out = trade([pick(full_out, me ^ r) for r in range(nd)], "dp")
    full_out = jnp.concatenate(absolute(full_out, "dp"), axis=1)

    both = jnp.concatenate([h_init.reshape(-1, NST), d_h_ends.reshape(-1, NST)], axis=1)
    both = both.reshape(ns, nd, chans, 2 * NST)
    both = trade([pick(both, me ^ r, 1).reshape(ns * chans, 2 * NST) for r in range(nd)], "dp")
    both = jnp.stack([p.T for p in both], axis=1).reshape((2, NST) + tile)
    init, end_cot = both[0], both[1]
    g_blocks = gather_blocks(cotangent[0], "dp")

    x_all = jnp.concatenate(x_blocks, axis=0).astype(f32)
    inv_one = lax.rsqrt(jnp.mean(x_all * x_all, axis=-1, keepdims=True) + epsilon)
    normed_one = x_all * inv_one
    inputs_low = (normed_one * gain_one).astype(bf16)
    u = pick(inputs_low.reshape(nd, rows, ns, nd, chans), me, 3).astype(f32)
    u = u.transpose(1, 0, 2, 3).reshape((rows,) + tile)

    a = jnp.exp(-rate)
    s_mid, s_end = local_ends(u, a)
    decay = jnp.exp(-rate * rows)
    local_end = gin * s_end
    inclusive, exclusive, step = local_end, jnp.zeros_like(local_end), 1
    while step < ns:
        got = moved(inclusive, "seq", [(k, k + step) for k in range(ns - step)])
        exclusive = exclusive + jnp.exp(-rate * (rows * (step - 1))) * got
        inclusive = inclusive + jnp.exp(-rate * (rows * step)) * got
        step *= 2
    prefix = jnp.exp(-rate * (rows * place).astype(f32))
    state_in = prefix * init + exclusive
    state_out = decay * state_in + local_end
    ends = trade(list(state_out.reshape(NST, nd, ns * chans).transpose(1, 0, 2)), "dp")
    ends = jnp.stack(absolute(ends, "dp")).reshape(nd, NST, ns, chans)
    ends = ends.transpose(2, 0, 3, 1).reshape(1, 1, dim, NST)
    h_mid = jnp.exp(-rate * (rows - CTX)) * state_in + gin * s_mid
    y, y0 = contexts(u, a, gin, gout, h_mid, init)
    y_low = y.astype(bf16)
    to_first = moved(y_low, "seq", [(k, k + 1) for k in range(1, ns - 1, 2)])
    to_second = moved(y_low, "seq", [(k, k + 2) for k in range(1, ns - 2, 2)])
    context = jnp.where(first_block, y0.astype(bf16), jnp.where(second == 1, to_second, to_first))
    context = context.reshape(CTX, nd, ns * chans).transpose(1, 0, 2)
    from_all = gather_blocks(context, "dp")
    from_all = [jnp.stack([from_all[r][r ^ w] for w in range(nd)]) for r in range(nd)]
    context = jnp.stack(absolute(from_all, "dp")).reshape(nd, nd, CTX, ns, chans)
    context = context.transpose(1, 2, 3, 0, 4).reshape(nd * CTX, dim)

    qkv = dot_nn(inputs_low, full_qkv).astype(bf16)
    ctx_kv = dot_nn(context, full_qkv[:, width:]).astype(bf16)
    prev_kv = moved(qkv[:, width:], "seq", [(k, k + 1) for k in range(0, ns, 2)])
    second_flag = second.astype(jnp.int32).reshape(1)
    attended = attend(second_flag, qkv, prev_kv, ctx_kv, nd)

    def by_owner(partial):
        return sum_to_owner([partial[r * rows : (r + 1) * rows] for r in range(nd)], "dp")

    x_own = x_all[:rows]
    hidden = x_own + by_owner(dot_nn(attended, full_out))

    inv_two = lax.rsqrt(jnp.mean(hidden * hidden, axis=-1, keepdims=True) + epsilon)
    normed_two = hidden * inv_two
    mlp_in = (normed_two * gain_two).astype(bf16)
    mlp_in = jnp.concatenate(gather_blocks(mlp_in, "dp"), axis=0)
    pre_act = dot_nn(mlp_in, full_up)
    act, gelu_back = jax.vjp(gelu_tanh, pre_act)
    act = act.astype(bf16)
    grad_all = jnp.concatenate(g_blocks, axis=0)
    d_act = dot_nt(grad_all, full_down)
    d_pre = gelu_back(d_act)[0].astype(bf16)
    d_mlp = by_owner(dot_nt(d_pre, full_up))
    result = (hidden + by_owner(dot_nn(act, full_down))).astype(bf16)[None]
    d_down = dot_tn(act, grad_all)
    d_up = dot_tn(mlp_in, d_pre)

    def reduced(partial):
        return lax.psum_scatter(partial.astype(bf16), "seq", scatter_dimension=0, tiled=True)

    d_gain_two = jnp.sum(d_mlp * normed_two, axis=0)
    d_hidden = cotangent[0].astype(f32) + norm_back(d_mlp, normed_two, inv_two, gain_two)
    d_hidden_all = jnp.concatenate(gather_blocks(d_hidden.astype(bf16), "dp"), axis=0)

    d_attended = dot_nt(d_hidden_all, full_out).astype(bf16)
    d_out = dot_tn(attended, d_hidden_all).astype(bf16).reshape(width, nd, cols)
    d_out = trade([pick(d_out, me ^ r, 1) for r in range(nd)], "dp")
    d_out = jnp.concatenate(absolute(d_out, "dp"), axis=0)
    dq, dk_own, dv_own, dk_prev, dv_prev, dk_ctx, dv_ctx = attend_back(
        second_flag, qkv, prev_kv, ctx_kv, d_attended, nd
    )
    back_prev = moved(
        jnp.concatenate([dk_prev, dv_prev], axis=1), "seq", [(k + 1, k) for k in range(0, ns, 2)]
    ).astype(f32)
    d_kv = (jnp.concatenate([dk_own, dv_own], axis=1) + back_prev).astype(bf16)
    d_qkv = jnp.concatenate([dq, d_kv], axis=1)
    d_ctx_kv = jnp.concatenate([dk_ctx, dv_ctx], axis=1)
    d_context = dot_nt(d_ctx_kv, full_qkv[:, width:])
    d_context = d_context.reshape(nd, CTX, ns, nd, chans)
    parts = []
    for r in range(nd):
        part = pick(d_context, me ^ r, 3)
        parts.append(jnp.stack([part[r ^ w] for w in range(nd)]))
    d_context = sum_to_owner(parts, "dp").transpose(1, 0, 2, 3).reshape((CTX,) + tile)
    d_context = d_context.astype(bf16)
    dy0 = jnp.where(first_block, d_context, jnp.zeros_like(d_context)).astype(f32)
    from_first = moved(d_context, "seq", [(k + 1, k) for k in range(1, ns - 1, 2)])
    from_second = moved(d_context, "seq", [(k + 2, k) for k in range(1, ns - 2, 2)])
    dy = from_first.astype(f32) + from_second.astype(f32)

    lam_mid = tail_adjoint(dy, a, gout)
    g_local = jnp.exp(-rate * (rows - CTX + 1)) * lam_mid + decay * end_cot
    inclusive, exclusive, step = g_local, jnp.zeros_like(g_local), 1
    while step < ns:
        got = moved(inclusive, "seq", [(k + step, k) for k in range(ns - step)])
        exclusive = exclusive + jnp.exp(-rate * (rows * (step - 1))) * got
        inclusive = inclusive + jnp.exp(-rate * (rows * step)) * got
        step *= 2
    du, d_gin, d_a, d_gout, g_in, g_init = ssm_back(
        u, dy, dy0, a, gin, gout, state_in, end_cot + exclusive, init
    )
    d_init = g_init + jnp.where(place == 0, g_in, jnp.zeros_like(g_in))
    d_rate = -a * d_a

    d_wqkv = dot_tn(inputs_low, d_qkv)
    d_wqkv = d_wqkv + jnp.pad(dot_tn(context, d_ctx_kv), ((0, 0), (width, 0)))
    d_inputs = dot_nt(d_qkv, full_qkv)
    du = du.reshape(rows, nd, ns, chans).transpose(1, 0, 2, 3).reshape(nd * rows, ns, 1, chans)
    here = (jnp.arange(nd) == me).reshape(1, 1, nd, 1)
    d_inputs = d_inputs + jnp.where(here, du, 0.0).reshape(nd * rows, dim)
    d_gain_one = jnp.sum(d_inputs * normed_one, axis=0)
    d_inputs = by_owner(d_inputs)
    d_tokens = d_hidden + norm_back(d_inputs, normed_one[:rows], inv_one[:rows], gain_one)
    d_tokens = d_tokens.astype(bf16)[None]

    d_params = jnp.stack([d_rate, d_gin, d_gout]).reshape(3, NST, nd, ns, chans).sum(2)
    d_init = d_init.reshape(NST, nd, ns, chans)
    pack = jnp.concatenate(
        [
            d_params.transpose(2, 0, 1, 3).reshape(ns, -1),
            d_init.transpose(2, 1, 0, 3).reshape(ns, -1),
            d_gain_one.reshape(ns, shard),
            d_gain_two.reshape(ns, shard),
        ],
        axis=1,
    ).reshape(ns, -1, LANES)
    pack = sum_to_owner_packed([pick(pack, place ^ r) for r in range(ns)], "seq")
    packs = [p.reshape(-1) for p in gather_packed(pack, "dp")]
    one, two = 3 * NST * chans, (3 + nd) * NST * chans
    d_params = jnp.stack(absolute([p[:one] for p in packs], "dp")).reshape(nd, 3, NST, chans)
    d_params = d_params.transpose(1, 0, 3, 2).reshape(3, shard, NST)
    state_grad = [p[one:two].reshape(nd, NST, chans)[r] for r, p in enumerate(packs)]
    state_grad = jnp.stack(absolute(state_grad, "dp")).transpose(0, 2, 1).reshape(1, shard, NST)
    gains = functools.reduce(jnp.add, [p[two:] for p in packs])

    def spread(part):
        return jnp.stack(absolute(gather_blocks(part, "dp"), "dp")).astype(f32)

    d_down = spread(reduced(d_down)).reshape(nd * down_rows, dim)
    d_up = spread(reduced(d_up)).reshape(nd, shard, ns, down_rows)
    d_up = d_up.transpose(1, 2, 0, 3).reshape(shard, ns * nd * down_rows)
    d_out = spread(reduced(d_out)).transpose(1, 0, 2).reshape(shard, dim)
    d_wqkv = spread(reduced(d_wqkv)).reshape(nd, shard, 3, width)
    d_wqkv = d_wqkv.transpose(1, 2, 0, 3).reshape(shard, 3 * dim)
    return (
        result,
        d_tokens,
        d_wqkv,
        d_out,
        d_up,
        d_down,
        gains[:shard],
        gains[shard:],
        d_params[0],
        d_params[1],
        d_params[2],
        state_grad,
        ends,
    )


def solution(mesh):
    return jax.shard_map(
        on_device,
        mesh=mesh,
        in_specs=(
            P("dp", "seq", None),
            P("seq", None),
            P("seq", None),
            P("seq", None),
            P("seq", None),
            P("seq"),
            P("seq"),
            P("seq", None),
            P("seq", None),
            P("seq", None),
            P("dp", None, None),
            P("dp", "seq", None),
            P("dp", "seq", None, None),
        ),
        out_specs=(
            P("dp", "seq", None),
            P("dp", "seq", None),
            P("seq", None),
            P("seq", None),
            P("seq", None),
            P("seq", None),
            P("seq"),
            P("seq"),
            P("seq", None),
            P("seq", None),
            P("seq", None),
            P("dp", "seq", None),
            P("dp", "seq", None, None),
        ),
        check_vma=False,
    )
```

```python
import functools
import math

import jax
import jax.numpy as jnp
from jax import lax
from jax.experimental import pallas as pl
from jax.experimental.pallas import tpu as pltpu
from jax.sharding import PartitionSpec as P

HEADS = 8
HD = 128
CTX = 128
NST = 16
LANES = 128
GROUP = 4
TEAM = 4

epsilon = 1e-05
far_below = -1e30
bf16 = jnp.bfloat16
f32 = jnp.float32


def swap(a, axis, bit):
    return lax.ppermute(a, axis, [(k, k ^ bit) for k in range(lax.axis_size(axis))])


def swap_team(a, r):
    if r == 1:
        return swap(a, "dp", 1)
    if r == 2:
        return swap(a, "seq", 1)
    nd, ns = lax.axis_size("dp"), lax.axis_size("seq")
    pairs = [(d * ns + k, (d ^ 1) * ns + (k ^ 1)) for d in range(nd) for k in range(ns)]
    return lax.ppermute(a, ("dp", "seq"), pairs)


def gather_team(a):
    far = swap_team(a, 2)
    return [a, swap_team(a, 1), far, swap_team(far, 1)]


def sum_team(parts):
    here = parts[0].astype(f32) + swap_team(parts[1].astype(bf16), 1).astype(f32)
    far = parts[2].astype(f32) + swap_team(parts[3].astype(bf16), 1).astype(f32)
    return here + swap_team(far.astype(bf16), 2).astype(f32)


def trade_team(parts):
    return [parts[0]] + [swap_team(parts[r], r) for r in (1, 2, 3)]


def high_bits(axis):
    size = lax.axis_size(axis)
    return [1 << k for k in reversed(range(1, size.bit_length() - 1))]


def pick(a, index, axis=0):
    return lax.dynamic_index_in_dim(a, index, axis, False)


def ordered(blocks, index):
    bit = len(blocks) // 2
    while bit:
        flip = (index & bit) != 0
        blocks = [jnp.where(flip, blocks[r ^ bit], blocks[r]) for r in range(len(blocks))]
        bit //= 2
    return blocks


def after(x, *others):
    return lax.optimization_barrier((x, others))[0]


def whole_spec():
    return pl.BlockSpec(memory_space=pltpu.VMEM)


def scalar_spec():
    return pl.BlockSpec(memory_space=pltpu.SMEM)


def any_spec():
    return pl.BlockSpec(memory_space=pl.ANY)


FREE = pl.CostEstimate(flops=1, transcendentals=0, bytes_accessed=1)
BIG = pltpu.CompilerParams(vmem_limit_bytes=40 * 2**20)


def share_kernel(spots, copies, idx, *refs):
    ins, outs, sem = refs[:spots], refs[spots:-1], refs[-1]
    flying = []
    for n, (src, dst, rows_at, cols_at, size, to) in enumerate(copies):
        row = pl.multiple_of(rows_at(idx), 16)
        col = pl.multiple_of(cols_at(idx), LANES)
        flying.append(
            pltpu.make_async_copy(
                ins[src].at[pl.ds(row, size[0]), pl.ds(col, size[1])],
                outs[dst].at[:, pl.ds(to, size[1])],
                sem.at[n],
            )
        )
    for one in flying:
        one.start()
    for one in flying:
        one.wait()


def shares(idx, w_qkv, w_out, w_up, w_down, ny, ns):
    shard, dim = w_out.shape
    quarter = dim // TEAM
    rows, fb = shard // ny, w_down.shape[0] // TEAM
    down = fb // ny
    copies = []
    for away in (0, 1):
        def who(i, away=away):
            return i[0] ^ (2 * away)

        for part in range(3):
            copies.append((0, away, lambda i: i[1] * rows,
                           lambda i, w=who, p=part: p * dim + w(i) * quarter, (rows, quarter), part * quarter))
        copies.append((1, away, lambda i: i[1] * rows,
                       lambda i, w=who: w(i) * quarter, (rows, quarter), 3 * quarter))
        if fb % LANES == 0:
            for k in range(ns):
                copies.append((2, 2 + away, lambda i: i[1] * rows,
                               lambda i, w=who, k=k: (k * TEAM + w(i)) * fb, (rows, fb), k * fb))
        copies.append((3, 4 + away, lambda i, w=who: w(i) * fb + i[1] * down,
                       lambda i: 0, (down, dim), 0))
    sizes = [(rows, dim)] * 2 + [(rows, ns * fb)] * 2 + [(down, dim)] * 2
    out = pl.pallas_call(
        functools.partial(share_kernel, 4, copies),
        out_shape=[jax.ShapeDtypeStruct(s, bf16) for s in sizes],
        in_specs=[scalar_spec()] + [any_spec()] * 4,
        out_specs=[whole_spec()] * 6,
        scratch_shapes=[pltpu.SemaphoreType.DMA((len(copies),))],
        name="shares",
        cost_estimate=FREE,
    )(idx, w_qkv, w_out, w_up, w_down)
    out = [list(out[k : k + 2]) for k in (0, 2, 4)]
    if fb % LANES:
        mine = lax.dynamic_slice_in_dim(w_up, idx[1] * rows, rows, 0).reshape(rows, ns, TEAM, fb)
        out[1] = [pick(mine, idx[0] ^ r, 2).reshape(rows, ns * fb) for r in (0, 2)]
    return out


def place_kernel(order, cuts, idx, place, a_ref, b_ref, *outs):
    half = len(order) // 2
    rows = a_ref.shape[1]
    for k, r in enumerate(order):
        at = pl.multiple_of((place[0] ^ r) * rows, 16)
        ref = a_ref if k < half else b_ref
        if cuts:
            width = outs[0].shape[1]
            outs[0][pl.ds(at, rows), :] = ref[k % half, :, :width]
            outs[-1][pl.ds(at, rows), :] = ref[k % half, :, width:]
        else:
            outs[0][pl.ds(at, rows), :] = ref[k % half]
    for r in range(cuts):
        rows = outs[1].shape[0]
        at = pl.multiple_of((idx[0] ^ r) * rows, 16)
        outs[1 + r][...] = outs[-1][pl.ds(at, rows), :]


def gather_weight(own, away, waits):
    ny = lax.axis_size("dp") // 2
    a, order = own[None], [0]
    steps = [("seq", 1, ny)] + [("seq", bit, bit * ny) for bit in high_bits("seq")]
    steps += [("dp", bit, bit // 2) for bit in high_bits("dp")]
    came = []
    for n, (axis, bit, weight) in enumerate(steps):
        if came:
            a = jnp.concatenate([a, came[-1]], axis=0)
        out = a if came else away[None]
        if n in waits:
            out = after(out, waits[n])
        elif n - len(steps) in waits:
            out = after(out, waits[n - len(steps)])
        came.append(swap(out, axis, bit))
        order = order + [r | weight for r in order]
    return came, (a, came[-1], order)


def place_weight(idx, place, pieces, width=None):
    a, got, order = pieces
    rows, cols = len(order) * a.shape[1], a.shape[2]
    shapes = [(rows, cols)]
    scratch = []
    if width:
        shapes = [(rows, width)] + [(rows // TEAM, cols - width)] * TEAM
        scratch = [pltpu.VMEM((rows, cols - width), bf16)]
    return pl.pallas_call(
        functools.partial(place_kernel, order, TEAM if width else 0),
        out_shape=[jax.ShapeDtypeStruct(s, bf16) for s in shapes],
        in_specs=[scalar_spec()] * 2 + [whole_spec()] * 2,
        out_specs=[whole_spec()] * len(shapes),
        scratch_shapes=scratch,
        compiler_params=BIG,
        name="place_weight",
        cost_estimate=FREE,
    )(idx, place, a, got)


def columns_kernel(flips, idx, *refs):
    ins, out = refs[:-1], refs[-1]
    for r, ref in enumerate(ins):
        rows, width = ref.shape
        col = pl.multiple_of((idx[0] ^ r) * width, LANES)
        for w in range(flips):
            n = rows // flips
            v = w ^ (r & 1) if flips == 2 else w
            out[w * n : (w + 1) * n, pl.ds(col, width)] = ref[v * n : (v + 1) * n, :]


def join_columns(idx, parts, flips=1):
    rows, width = parts[0].shape
    return pl.pallas_call(
        functools.partial(columns_kernel, flips),
        out_shape=jax.ShapeDtypeStruct((rows, width * TEAM), parts[0].dtype),
        in_specs=[scalar_spec()] + [whole_spec()] * TEAM,
        out_specs=whole_spec(),
        name="join_columns",
        cost_estimate=FREE,
    )(idx, *parts)


def cut_kernel(flips, idx, x_ref, *outs):
    for r, ref in enumerate(outs):
        rows, width = ref.shape
        col = pl.multiple_of((idx[0] ^ r) * width, LANES)
        for w in range(flips):
            n = rows // flips
            v = w ^ (r & 1) if flips == 2 else w
            ref[v * n : (v + 1) * n, :] = x_ref[w * n : (w + 1) * n, pl.ds(col, width)].astype(ref.dtype)


def cut_columns(idx, x, dtypes, flips=1):
    shape = (x.shape[0], x.shape[1] // TEAM)
    return pl.pallas_call(
        functools.partial(cut_kernel, flips),
        out_shape=[jax.ShapeDtypeStruct(shape, d) for d in dtypes],
        in_specs=[scalar_spec(), whole_spec()],
        out_specs=[whole_spec()] * TEAM,
        name="cut_columns",
        cost_estimate=FREE,
    )(idx, x)


def attn_grad_kernel(idx, x_ref, dq_ref, ctx_ref, dctx_ref, *refs):
    parts, out = refs[:TEAM], refs[TEAM]
    k = pl.program_id(0)
    width = dq_ref.shape[1] // 3
    grad = dot_tn(x_ref[...], dq_ref[...])
    far = dot_tn(ctx_ref[...], dctx_ref[...])
    out[:, :width] = grad[:, :width].astype(bf16)
    out[:, width : 3 * width] = (grad[:, width:] + far).astype(bf16)
    per = parts[0].shape[0] // out.shape[0]
    member = (k // per) ^ idx[0]
    at = pl.multiple_of((k % per) * out.shape[0], 16)
    for r in range(TEAM):
        @pl.when(member == r)
        def _(r=r):
            out[:, 3 * width :] = parts[r][pl.ds(at, out.shape[0]), :]


def attn_grad(idx, inputs, d_qkv, context, d_ctx_kv, parts):
    dim, step = inputs.shape[1], LANES
    def whole(a):
        return pl.BlockSpec(a.shape, lambda k: (0, 0))

    return pl.pallas_call(
        attn_grad_kernel,
        grid=(dim // step,),
        out_shape=jax.ShapeDtypeStruct((dim, d_qkv.shape[1] + parts[0].shape[1]), bf16),
        in_specs=[
            scalar_spec(),
            pl.BlockSpec((inputs.shape[0], step), lambda k: (0, k)),
            whole(d_qkv),
            pl.BlockSpec((context.shape[0], step), lambda k: (0, k)),
            whole(d_ctx_kv),
        ]
        + [whole(p) for p in parts],
        out_specs=pl.BlockSpec((step, d_qkv.shape[1] + parts[0].shape[1]), lambda k: (k, 0)),
        compiler_params=BIG,
        name="attn_grad",
        cost_estimate=FREE,
    )(idx, inputs, d_qkv, context, d_ctx_kv, *parts)


def insert_bit(k, at, bit):
    return ((k >> at) << (at + 1)) | (bit << at) | (k & ((1 << at) - 1))


def split_kernel(before, side, at, place, x_ref, *refs):
    here = (place[0] >> side) & 1
    if before is None:
        (away_ref,) = refs
        for k in range(away_ref.shape[0]):
            away_ref[k] = x_ref[insert_bit(k, at, 1 - here)]
        return
    recv_ref, keep_ref, away_ref = refs

    def total(k):
        j = k if before is True else insert_bit(k, before[1], (place[0] >> before[0]) & 1)
        return (x_ref[j].astype(f32) + recv_ref[k].astype(f32)).astype(bf16)

    for k in range(away_ref.shape[0]):
        away_ref[k] = total(insert_bit(k, at, 1 - here))
        keep_ref[k] = total(insert_bit(k, at, here))


def reduce_weight(x, place, waits):
    ny = lax.axis_size("dp") // 2
    steps = [("dp", bit, (bit // 2).bit_length() - 1, 0) for bit in reversed(high_bits("dp"))]
    steps += [("seq", bit, (bit * ny).bit_length() - 1, 1) for bit in reversed(high_bits("seq"))]
    steps.append(("seq", 1, ny.bit_length() - 1, 0))
    recv, came = None, []
    for n, (axis, bit, side, at) in enumerate(steps):
        before = None if n == 0 else (steps[0][2:] if n == 1 else True)
        count = x.shape[0] // 2 if n == 0 else recv.shape[0] // 2
        half = jax.ShapeDtypeStruct((count,) + x.shape[1:], bf16)
        if n and n in waits:
            recv = after(recv, waits[n])
        out = pl.pallas_call(
            functools.partial(split_kernel, before, side, at),
            out_shape=[half] if n == 0 else [half, half],
            in_specs=[scalar_spec()] + [whole_spec()] * (1 if n == 0 else 2),
            out_specs=[whole_spec()] * (1 if n == 0 else 2),
            compiler_params=BIG,
            name="split_sum",
            cost_estimate=FREE,
        )(*((place, x) if n == 0 else (place, x, recv)))
        if n:
            x = out[0]
        recv = swap(out[-1], axis, bit)
        came.append(recv)
    return (x, recv), came


def final_kernel(kind, count, fb, idx, *refs):
    ins, outs = refs[:count], refs[count:]
    rows = ins[0].shape[1]
    for m, ref in enumerate(ins):
        row = pl.multiple_of((idx[1] ^ m) * rows, 16)
        for k, r in enumerate((0, 2, 1, 3)):
            member = idx[0] ^ r
            if kind == "down":
                at = pl.multiple_of(member * (rows * count) + row, 16)
                outs[0][pl.ds(at, rows), :] = ref[k].astype(f32)
            elif kind == "up":
                for n in range(ref.shape[2] // fb):
                    col = pl.multiple_of((n * TEAM + member) * fb, LANES)
                    outs[0][pl.ds(row, rows), pl.ds(col, fb)] = ref[k, :, n * fb : (n + 1) * fb].astype(f32)
            else:
                dim = outs[1].shape[1]
                quarter = dim // TEAM
                for part in range(4):
                    to = outs[0] if part < 3 else outs[1]
                    col = pl.multiple_of((part % 3) * dim * (part < 3) + member * quarter, LANES)
                    block = ref[k, :, part * quarter : (part + 1) * quarter]
                    to[pl.ds(row, rows), pl.ds(col, quarter)] = block.astype(f32)


def spread_weight(kind, own, near, idx, shapes, fb=LANES):
    pair = jnp.concatenate([own, near], axis=0)
    blocks = {0: jnp.concatenate([pair, swap(pair, "dp", 1)], axis=0)}
    for bit in high_bits("dp"):
        for m in list(blocks):
            blocks[m | (bit // 2)] = swap(blocks[m], "dp", bit)
    blocks = [blocks[m] for m in range(len(blocks))]
    return pl.pallas_call(
        functools.partial(final_kernel, kind, len(blocks), fb),
        out_shape=[jax.ShapeDtypeStruct(s, f32) for s in shapes],
        in_specs=[scalar_spec()] + [whole_spec()] * len(blocks),
        out_specs=[whole_spec()] * len(shapes),
        compiler_params=BIG,
        name="final_" + kind,
        cost_estimate=FREE,
    )(idx, *blocks)


def spread_narrow(own, near, idx, shape, fb):
    pair = jnp.concatenate([own, near], axis=0)
    blocks = {0: jnp.concatenate([pair, swap(pair, "dp", 1)], axis=0)}
    for bit in high_bits("dp"):
        for m in list(blocks):
            blocks[m | (bit // 2)] = swap(blocks[m], "dp", bit)
    rows = ordered([blocks[m] for m in range(len(blocks))], idx[1])
    rows = jnp.stack(rows, axis=1)
    teams = jnp.stack(ordered([rows[0], rows[2], rows[1], rows[3]], idx[0]))
    teams = teams.reshape(TEAM, shape[0], shape[1] // (TEAM * fb), fb).transpose(1, 2, 0, 3)
    return teams.reshape(shape).astype(f32)


def ends_kernel(mid, u_ref, a_ref, mid_ref, end_ref):
    rows = u_ref.shape[0]
    a = [a_ref[n] for n in range(NST)]

    def eight(k, s):
        for t in range(8):
            u = u_ref[k * 8 + t]
            s = tuple(a[n] * s[n] + u for n in range(NST))
        return s

    zero = tuple(jnp.zeros_like(a[0]) for _ in range(NST))
    s = lax.fori_loop(0, mid // 8, eight, zero)
    for n in range(NST):
        mid_ref[n] = s[n]
    s = lax.fori_loop(mid // 8, rows // 8, eight, s)
    for n in range(NST):
        end_ref[n] = s[n]


def local_ends(u, a):
    shape = jax.ShapeDtypeStruct(a.shape, f32)
    return pl.pallas_call(
        functools.partial(ends_kernel, u.shape[0] - CTX),
        out_shape=(shape, shape),
        in_specs=[whole_spec()] * 2,
        out_specs=(whole_spec(),) * 2,
        name="ssm_ends",
        cost_estimate=FREE,
    )(u, a)


def context_kernel(mid, u_ref, a_ref, gin_ref, gout_ref, h_ref, y_ref):
    half = NST // 2
    for base in (0, half):
        ns = range(base, base + half)
        a = [a_ref[n] for n in ns]
        gin = [gin_ref[n] for n in ns]
        gout = [gout_ref[n] for n in ns]

        def step(k, h):
            for t in range(4):
                p = k * 4 + t
                u = u_ref[mid + p]
                h = tuple(a[n] * h[n] + gin[n] * u for n in range(half))
                y = functools.reduce(jnp.add, [gout[n] * h[n] for n in range(half)])
                y_ref[p] = y if base == 0 else y_ref[p] + y
            return h

        lax.fori_loop(0, CTX // 4, step, tuple(h_ref[n] for n in ns))


def contexts(u, a, gin, gout, h_mid):
    return pl.pallas_call(
        functools.partial(context_kernel, u.shape[0] - CTX),
        out_shape=jax.ShapeDtypeStruct((CTX,) + u.shape[1:], f32),
        in_specs=[whole_spec()] * 5,
        out_specs=whole_spec(),
        name="ssm_context",
        cost_estimate=FREE,
    )(u, a, gin, gout, h_mid)


def tail_kernel(dy_ref, a_ref, gout_ref, lam_ref):
    a = [a_ref[n] for n in range(NST)]
    gout = [gout_ref[n] for n in range(NST)]

    def eight(k, lam):
        for t in range(8):
            dy = dy_ref[CTX - 1 - (k * 8 + t)]
            lam = tuple(a[n] * lam[n] + gout[n] * dy for n in range(NST))
        return lam

    lam = lax.fori_loop(0, CTX // 8, eight, tuple(jnp.zeros_like(a[0]) for _ in range(NST)))
    for n in range(NST):
        lam_ref[n] = lam[n]


def tail_adjoint(dy, a, gout):
    return pl.pallas_call(
        tail_kernel,
        out_shape=jax.ShapeDtypeStruct(a.shape, f32),
        in_specs=[whole_spec()] * 3,
        out_specs=whole_spec(),
        name="ssm_tail",
        cost_estimate=FREE,
    )(dy, a, gout)


def back_kernel(
    u_ref, dy_ref, dy0_ref, a_ref, gin_ref, gout_ref, h_ref, lam_ref, init_ref,
    du_ref, dgin_ref, da_ref, dgout_ref, g_ref, g0_ref, hs,
):
    first = pl.program_id(0) == 0
    rows = u_ref.shape[0]
    mid = rows - CTX
    ns = range(GROUP)
    a = [a_ref[n] for n in ns]
    gin = [gin_ref[n] for n in ns]
    gout = [gout_ref[n] for n in ns]
    zero = tuple(jnp.zeros_like(a[0]) for _ in ns)

    def ahead(k, h):
        for t in range(8):
            p = k * 8 + t
            u = u_ref[p]
            h = tuple(a[n] * h[n] + gin[n] * u for n in ns)
            for n in ns:
                hs[p + 1, n] = h[n]
        return h

    h = tuple(h_ref[n] for n in ns)
    for n in ns:
        hs[0, n] = h[n]
    lax.fori_loop(0, rows // 8, ahead, h)

    def tail(k, carry):
        lam, dgin, da, dgout = carry
        for t in range(4):
            q = CTX - 1 - (k * 4 + t)
            p = mid + q
            dy, u = dy_ref[q], u_ref[p]
            lam = tuple(lam[n] + gout[n] * dy for n in ns)
            dgout = tuple(dgout[n] + dy * hs[p + 1, n] for n in ns)
            dgin = tuple(dgin[n] + lam[n] * u for n in ns)
            da = tuple(da[n] + lam[n] * hs[p, n] for n in ns)
            du = functools.reduce(jnp.add, [gin[n] * lam[n] for n in ns])
            du_ref[p] = jnp.where(first, du, du_ref[p] + du)
            lam = tuple(a[n] * lam[n] for n in ns)
        return lam, dgin, da, dgout

    def head(k, carry):
        lam, dgin, da = carry
        for t in range(4):
            p = mid - 1 - (k * 4 + t)
            u = u_ref[p]
            dgin = tuple(dgin[n] + lam[n] * u for n in ns)
            da = tuple(da[n] + lam[n] * hs[p, n] for n in ns)
            du = functools.reduce(jnp.add, [gin[n] * lam[n] for n in ns])
            du_ref[p] = jnp.where(first, du, du_ref[p] + du)
            lam = tuple(a[n] * lam[n] for n in ns)
        return lam, dgin, da

    lam = tuple(lam_ref[n] for n in ns)
    lam, dgin, da, dgout = lax.fori_loop(0, CTX // 4, tail, (lam, zero, zero, zero))
    lam, dgin, da = lax.fori_loop(0, mid // 4, head, (lam, dgin, da))
    for n in ns:
        g_ref[n] = lam[n]
        dgin_ref[n] = dgin[n]

    def ahead_init(k, h):
        for t in range(8):
            h = tuple(a[n] * h[n] for n in ns)
            for n in ns:
                hs[k * 8 + t + 1, n] = h[n]
        return h

    h = tuple(init_ref[n] for n in ns)
    for n in ns:
        hs[0, n] = h[n]
    lax.fori_loop(0, CTX // 8, ahead_init, h)

    def back_init(k, carry):
        mu, da, dgout = carry
        for t in range(4):
            q = CTX - 1 - (k * 4 + t)
            dy = dy0_ref[q]
            mu = tuple(mu[n] + gout[n] * dy for n in ns)
            dgout = tuple(dgout[n] + dy * hs[q + 1, n] for n in ns)
            da = tuple(da[n] + mu[n] * hs[q, n] for n in ns)
            mu = tuple(a[n] * mu[n] for n in ns)
        return mu, da, dgout

    mu, da, dgout = lax.fori_loop(0, CTX // 4, back_init, (zero, da, dgout))
    for n in ns:
        g0_ref[n] = mu[n]
        da_ref[n] = da[n]
        dgout_ref[n] = dgout[n]


def ssm_back(u, dy, dy0, a, gin, gout, state_in, lam_end, h_init):
    tile = u.shape[1:]
    states = pl.BlockSpec((GROUP,) + tile, lambda g: (g, 0, 0))
    rows = pl.BlockSpec(u.shape, lambda g: (0, 0, 0))
    tail = pl.BlockSpec(dy.shape, lambda g: (0, 0, 0))
    out = jax.ShapeDtypeStruct(a.shape, f32)
    return pl.pallas_call(
        back_kernel,
        grid=(NST // GROUP,),
        out_shape=(jax.ShapeDtypeStruct(u.shape, f32),) + (out,) * 5,
        in_specs=[rows, tail, tail] + [states] * 6,
        out_specs=(rows,) + (states,) * 5,
        scratch_shapes=[pltpu.VMEM((u.shape[0] + 1, GROUP) + tile, f32)],
        compiler_params=pltpu.CompilerParams(vmem_limit_bytes=24 * 2**20),
        name="ssm_back",
        cost_estimate=FREE,
    )(u, dy, dy0, a, gin, gout, state_in, lam_end, h_init)


def dot_nt(x, y):
    return lax.dot_general(x, y, (((1,), (1,)), ((), ())), preferred_element_type=f32)


def dot_nn(x, y):
    return jnp.dot(x, y, preferred_element_type=f32)


def dot_tn(x, y):
    return lax.dot_general(x, y, (((0,), (0,)), ((), ())), preferred_element_type=f32)


def softmax_parts(q, keys):
    rows = q.shape[0]
    scores = [dot_nt(q, k) * (1.0 / math.sqrt(HD)) for k in keys]
    at = lax.broadcasted_iota(jnp.int32, (rows, rows), 0)
    to = lax.broadcasted_iota(jnp.int32, (rows, rows), 1)
    scores[-1] = jnp.where(to <= at, scores[-1], far_below)
    top = functools.reduce(jnp.maximum, [jnp.max(s, axis=-1, keepdims=True) for s in scores])
    es = [jnp.exp(s - top) for s in scores]
    total = functools.reduce(jnp.add, [jnp.sum(e, axis=-1, keepdims=True) for e in es])
    return [e / total for e in es]


def attend_kernel(half_ref, q0, q1, k0, k1, v0, v1, kc, vc, out_ref):
    w, h = pl.program_id(0), pl.program_id(1)
    rows = q0.shape[0]
    for half, q, keys, values in ((0, q0, (kc, k0), (vc, v0)), (1, q1, (kc, k0, k1), (vc, v0, v1))):
        probs = softmax_parts(q[...], [k[...] for k in keys])
        out = [dot_nn(p.astype(bf16), v[...]) for p, v in zip(probs, values)]
        at = pl.multiple_of(((half ^ half_ref[0]) * 2 + w) * rows, 16)
        col = pl.multiple_of(h * HD, LANES)
        out_ref[pl.ds(at, rows), pl.ds(col, HD)] = functools.reduce(jnp.add, out).astype(bf16)


def attend_back_kernel(
    half_ref, q0, q1, k0, k1, v0, v1, kc, vc, do0, do1, dqkv_ref, dctx_ref
):
    w, h = pl.program_id(0), pl.program_id(1)
    rows, heads = q0.shape[0], pl.num_programs(1)
    scale = 1.0 / math.sqrt(HD)
    dk, dv = [0.0, 0.0, 0.0], [0.0, 0.0, 0.0]

    def row_of(half):
        return pl.multiple_of(((half ^ half_ref[0]) * 2 + w) * rows, 16)

    def col_of(part):
        return pl.multiple_of((part * heads + h) * HD, LANES)

    cases = ((0, q0, do0, (kc, k0), (vc, v0)), (1, q1, do1, (kc, k0, k1), (vc, v0, v1)))
    for half, q, do, keys, values in cases:
        query, d_out = q[...], do[...]
        probs = softmax_parts(query, [k[...] for k in keys])
        d_probs = [dot_nt(d_out, v[...]) for v in values]
        sums = [jnp.sum(p * d, axis=-1, keepdims=True) for p, d in zip(probs, d_probs)]
        delta = functools.reduce(jnp.add, sums)
        d_scores = [(p * (d - delta)).astype(bf16) for p, d in zip(probs, d_probs)]
        dq = functools.reduce(jnp.add, [dot_nn(d, k[...]) for d, k in zip(d_scores, keys)])
        dqkv_ref[pl.ds(row_of(half), rows), pl.ds(col_of(0), HD)] = (dq * scale).astype(bf16)
        for n, (d, p) in enumerate(zip(d_scores, probs)):
            dk[n] = dk[n] + dot_tn(d, query)
            dv[n] = dv[n] + dot_tn(p.astype(bf16), d_out)
    ctx_row = pl.multiple_of(w * CTX, 16)
    dctx_ref[pl.ds(ctx_row, CTX), pl.ds(col_of(0), HD)] = (dk[0] * scale).astype(bf16)
    dctx_ref[pl.ds(ctx_row, CTX), pl.ds(col_of(1), HD)] = dv[0].astype(bf16)
    for half in (0, 1):
        dqkv_ref[pl.ds(row_of(half), rows), pl.ds(col_of(1), HD)] = (dk[1 + half] * scale).astype(bf16)
        dqkv_ref[pl.ds(row_of(half), rows), pl.ds(col_of(2), HD)] = dv[1 + half].astype(bf16)


def attention_specs(rows, heads):
    def at(half, part):
        return pl.BlockSpec((rows, HD), lambda w, h, s: ((half ^ s[0]) * 2 + w, part * heads + h))

    def ctx(part):
        return pl.BlockSpec((CTX, HD), lambda w, h, s: (w, part * heads + h))

    return [at(half, part) for part in range(3) for half in (0, 1)] + [ctx(0), ctx(1)]


def whole_block(shape):
    return pl.BlockSpec(shape, lambda w, h, s: (0, 0))


def attend(half, qkv, ctx_kv):
    rows, heads = qkv.shape[0] // TEAM, qkv.shape[1] // (3 * HD)
    out = (qkv.shape[0], heads * HD)
    return pl.pallas_call(
        attend_kernel,
        grid_spec=pltpu.PrefetchScalarGridSpec(
            num_scalar_prefetch=1,
            grid=(2, heads),
            in_specs=attention_specs(rows, heads),
            out_specs=whole_block(out),
        ),
        out_shape=jax.ShapeDtypeStruct(out, bf16),
        compiler_params=BIG,
        name="attend",
        cost_estimate=FREE,
    )(half, *[qkv] * 6, ctx_kv, ctx_kv)


def attend_back(half, qkv, ctx_kv, d_attended):
    rows, heads = qkv.shape[0] // TEAM, qkv.shape[1] // (3 * HD)

    def at(side):
        return pl.BlockSpec((rows, HD), lambda w, h, s: ((side ^ s[0]) * 2 + w, h))

    return pl.pallas_call(
        attend_back_kernel,
        grid_spec=pltpu.PrefetchScalarGridSpec(
            num_scalar_prefetch=1,
            grid=(2, heads),
            in_specs=attention_specs(rows, heads) + [at(0), at(1)],
            out_specs=[whole_block(qkv.shape), whole_block(ctx_kv.shape)],
        ),
        out_shape=[jax.ShapeDtypeStruct(qkv.shape, bf16), jax.ShapeDtypeStruct(ctx_kv.shape, bf16)],
        compiler_params=BIG,
        name="attend_back",
        cost_estimate=FREE,
    )(half, *[qkv] * 6, ctx_kv, ctx_kv, d_attended, d_attended)


def gelu_tanh(values):
    return jax.nn.gelu(values, approximate=True)


def norm_back(grad_normed, normed, inv_scale, gain):
    scaled = grad_normed * gain
    return inv_scale * (scaled - normed * jnp.mean(scaled * normed, axis=-1, keepdims=True))


def on_device(
    tokens,
    w_qkv,
    w_out,
    w_up,
    w_down,
    g_attn,
    g_mlp,
    ssm_rate,
    ssm_in,
    ssm_out,
    h_init,
    cotangent,
    d_h_ends,
):
    nd, ns = lax.axis_size("dp"), lax.axis_size("seq")
    ny = nd // 2
    dp, seq = lax.axis_index("dp"), lax.axis_index("seq")
    late = seq % 2 == 1
    block = seq // 2
    me = (seq % 2) * 2 + dp % 2
    idx = jnp.stack([me, dp // 2]).astype(jnp.int32)
    place = (seq * ny + dp // 2).astype(jnp.int32).reshape(1)
    half = (seq % 2).astype(jnp.int32).reshape(1)
    rows, dim = tokens.shape[1:]
    shard = w_qkv.shape[0]
    width = HEADS * HD // TEAM
    cols = dim // TEAM
    fb = w_down.shape[0] // TEAM
    tile = (dim // LANES, LANES)
    half_tile = (dim // LANES // 2, LANES)

    small = [p.T for p in (ssm_rate, ssm_in, ssm_out)] + [g_attn[None], g_mlp[None]]
    small = jnp.concatenate(small, axis=0)[None]
    for bit in [1] + high_bits("seq")[::-1]:
        got = swap(small, "seq", bit)
        upper = (seq & bit) != 0
        small = jnp.concatenate([jnp.where(upper, got, small), jnp.where(upper, small, got)], axis=0)
    small = small.astype(f32)
    gain_one = small[:, 3 * NST].reshape(dim)
    gain_two = small[:, 3 * NST + 1].reshape(dim)
    params = small[:, : 3 * NST].transpose(1, 0, 2).reshape(3 * NST, dim)
    params = lax.dynamic_slice_in_dim(params, me * cols, cols, 1)
    params = jnp.broadcast_to(params[:, None], (3 * NST, TEAM, cols)).reshape((3, NST) + tile)
    rate, gin, gout = params[0], params[1], params[2]
    half_rate = rate[:, : tile[0] // 2]
    share_attn, share_up, share_down = shares(idx, w_qkv, w_out, w_up, w_down, ny, ns)
    x_blocks = gather_team(after(tokens[0], share_attn[1]))
    came_attn, attn_pieces = gather_weight(*share_attn, {})
    full_qkv, *full_out = place_weight(idx, place, attn_pieces, 3 * width)
    full_out = join_columns(idx, trade_team(full_out))
    waits = {0: came_attn[1], 1: came_attn[-2], -1: came_attn[-1]}
    came_up, up_pieces = gather_weight(*share_up, waits)
    (full_up,) = place_weight(idx, place, up_pieces)
    waits = {0: came_attn[1], 1: came_up[-2], -1: came_up[-1]}
    came_down, down_pieces = gather_weight(*share_down, waits)
    (full_down,) = place_weight(idx, place, down_pieces)

    def channels_of(a, r):
        return lax.dynamic_slice_in_dim(a, (me ^ r) * cols, cols, 0).T

    init = h_init[0]
    init = [channels_of(init, 0), swap_team(channels_of(init, 1), 1)]
    init = jnp.stack(init, axis=1).reshape((NST,) + half_tile)
    end_cot = trade_team([channels_of(d_h_ends[0, 0], r) for r in range(TEAM)])
    end_cot = [jnp.stack(end_cot[k : k + 2], axis=1).reshape((NST,) + half_tile) for k in (0, 2)]
    end_cot = ordered(end_cot, seq % 2)
    g_blocks = gather_team(after(cotangent[0], came_attn[-2]))

    def by_half(a, axis=1):
        n = a.shape[axis] // 2
        own, other = lax.slice_in_dim(a, 0, n, axis=axis), lax.slice_in_dim(a, n, 2 * n, axis=axis)
        return ordered([own, other], seq % 2)

    def by_owner(first, second):
        return jnp.concatenate(ordered([first, second], seq % 2), axis=1)

    x_all = jnp.concatenate(x_blocks, axis=0).astype(f32)
    inv_one = lax.rsqrt(jnp.mean(x_all * x_all, axis=-1, keepdims=True) + epsilon)
    normed_one = x_all * inv_one
    inputs_low = (normed_one * gain_one).astype(bf16)
    u = after(inputs_low, came_attn[1])
    u = lax.dynamic_slice_in_dim(u, me * cols, cols, 1).astype(f32)
    u = u.reshape(TEAM, rows, cols // LANES, LANES).transpose(1, 0, 2, 3).reshape((rows,) + tile)

    a = jnp.exp(-rate)
    s_mid, s_end = local_ends(u, a)
    decay = jnp.exp(-half_rate * rows)
    first_end, second_end = by_half(gin * s_end)
    span = 2 * rows

    def chain(inclusive, back):
        exclusive, step = jnp.zeros_like(inclusive), 1
        while step < ns // 2:
            pairs = [(k, k + 2 * step) for k in range(ns - 2 * step)]
            got = lax.ppermute(inclusive, "seq", [(t, f) for f, t in pairs] if back else pairs)
            exclusive = exclusive + jnp.exp(-half_rate * (span * (step - 1))) * got
            inclusive = inclusive + jnp.exp(-half_rate * (span * step)) * got
            step *= 2
        return exclusive

    entering = chain(decay * first_end + second_end, False)
    state_zero = jnp.exp(-half_rate * (span * block).astype(f32)) * init + entering
    state_one = decay * state_zero + first_end
    state_two = decay * state_one + second_end
    state_in = by_owner(state_zero, state_one)
    ends = by_owner(state_one, state_two).reshape(NST, TEAM, cols)
    ends = ordered(trade_team([ends[:, r] for r in range(TEAM)]), me)
    ends = jnp.concatenate(ends, axis=1).T[None, None]
    on_second = by_owner(jnp.zeros_like(init), jnp.ones_like(init))
    h_mid = jnp.exp(-rate * (rows - CTX)) * state_in + gin * s_mid
    h_mid = jnp.where(on_second > 0, h_mid, jnp.concatenate([init, init], axis=1))
    y = contexts(u, a, gin * on_second, gout, after(h_mid, came_attn[-2]))
    y_first, y_second = by_half(y.astype(bf16))
    passed = lax.ppermute(y_second, "seq", [(k, k + 2) for k in range(ns - 2)])
    context = jnp.where(block == 0, y_first, passed)
    context = context.reshape(CTX, 2, cols).transpose(1, 0, 2).reshape(2 * CTX, cols)
    context = join_columns(idx, gather_team(context), 2)

    qkv = dot_nn(inputs_low, full_qkv).astype(bf16)
    ctx_kv = dot_nn(context, full_qkv[:, width:]).astype(bf16)
    attended = attend(half, qkv, ctx_kv)

    def own_sum(partial):
        return sum_team([partial[r * rows : (r + 1) * rows] for r in range(TEAM)])

    hidden = x_all[:rows] + own_sum(dot_nn(attended, full_out))

    inv_two = lax.rsqrt(jnp.mean(hidden * hidden, axis=-1, keepdims=True) + epsilon)
    normed_two = hidden * inv_two
    mlp_in = (normed_two * gain_two).astype(bf16)
    mlp_in = jnp.concatenate(gather_team(mlp_in), axis=0)
    pre_act = dot_nn(mlp_in, full_up)
    act, gelu_back = jax.vjp(gelu_tanh, pre_act)
    act = act.astype(bf16)
    grad_all = jnp.concatenate(g_blocks, axis=0)
    d_act = dot_nt(grad_all, full_down)
    d_pre = gelu_back(d_act)[0].astype(bf16)
    d_mlp_part = dot_nt(d_pre, full_up)
    d_mlp = own_sum(d_mlp_part)
    act_late, d_pre_late = after((act, d_pre), d_mlp_part)
    d_down = dot_tn(act_late, grad_all).astype(bf16)
    d_up = dot_tn(mlp_in, d_pre_late).astype(bf16)
    result = own_sum(dot_nn(after(act_late, d_mlp), full_down))
    result = (hidden + result).astype(bf16)[None]

    d_gain_two = jnp.sum(d_mlp * normed_two, axis=0)
    d_hidden = cotangent[0].astype(f32) + norm_back(d_mlp, normed_two, inv_two, gain_two)
    d_hidden_all = jnp.concatenate(gather_team(d_hidden.astype(bf16)), axis=0)

    d_attended = dot_nt(d_hidden_all, full_out).astype(bf16)
    d_out = dot_tn(attended, d_hidden_all).astype(bf16)
    d_out = trade_team(cut_columns(idx, d_out, [bf16] * TEAM))
    d_qkv, d_ctx_kv = attend_back(half, qkv, ctx_kv, d_attended)
    d_context = dot_nt(d_ctx_kv, full_qkv[:, width:])
    d_context = cut_columns(idx, d_context, [f32, bf16, f32, bf16], 2)
    d_context = sum_team(d_context).astype(bf16).reshape(2, CTX, cols)
    d_context = d_context.transpose(1, 0, 2).reshape((CTX,) + half_tile)
    d_attn = attn_grad(idx, inputs_low, d_qkv, context, d_ctx_kv, d_out)
    dy0 = jnp.where(block == 0, d_context, jnp.zeros_like(d_context)).astype(f32)
    dy = lax.ppermute(d_context, "seq", [(k + 2, k) for k in range(ns - 2)]).astype(f32)

    lam_mid = tail_adjoint(dy, a[:, : tile[0] // 2], gout[:, : tile[0] // 2])
    g_second = jnp.exp(-half_rate * (rows - CTX + 1)) * lam_mid + decay * end_cot[1]
    leaving = chain(decay * (end_cot[0] + g_second), True)
    lam_end = by_owner(end_cot[0] + g_second + decay * leaving, end_cot[1] + leaving)
    none = jnp.zeros_like(dy)
    du, d_gin, d_a, d_gout, g_in, g_init = ssm_back(
        u,
        by_owner(none, dy),
        jnp.concatenate([dy0, none], axis=1),
        a,
        gin,
        gout,
        state_in,
        lam_end,
        jnp.concatenate([init, init], axis=1),
    )
    g_first = by_half(g_in)[0]
    d_init = g_init[:, : tile[0] // 2] + jnp.where(block == 0, g_first, jnp.zeros_like(g_first))
    d_rate = -a * d_a

    d_inputs = dot_nt(d_qkv, full_qkv)
    du = du.reshape(rows, TEAM, cols // LANES, LANES).transpose(1, 0, 2, 3).reshape(-1, cols)
    at_own = lax.dynamic_slice_in_dim(d_inputs, me * cols, cols, 1) + du
    d_inputs = lax.dynamic_update_slice_in_dim(d_inputs, at_own, me * cols, 1)
    d_gain_one = jnp.sum(d_inputs * normed_one, axis=0)
    d_inputs = own_sum(d_inputs)
    d_tokens = d_hidden + norm_back(d_inputs, normed_one[:rows], inv_one[:rows], gain_one)
    d_tokens = d_tokens.astype(bf16)[None]

    d_params = jnp.stack([d_rate, d_gin, d_gout]).reshape(3 * NST, TEAM, cols).sum(1)
    d_gains = jnp.concatenate([d_gain_one, d_gain_two])
    pack = [d_params.reshape(-1, LANES), d_gains.reshape(-1, LANES), d_init.reshape(-1, LANES)]
    pack = jnp.concatenate(pack, axis=0)
    for bit in high_bits("seq"):
        pack = pack + swap(pack, "seq", bit)
    one, two = 3 * NST * cols // LANES, 3 * NST * cols // LANES + 2 * dim // LANES
    shared = pack[:two]
    for bit in high_bits("dp"):
        shared = shared + swap(shared, "dp", bit)
    packs = jnp.stack(gather_team(jnp.concatenate([shared, pack[two:]], axis=0)))
    gains = packs[:, one:two].sum(0).reshape(2, ns, shard)
    gains = pick(gains, seq, 1)
    member = me ^ (seq * shard // cols)
    inner = seq * shard % cols
    chosen = pick(packs, member)
    d_params = chosen[:one].reshape(3 * NST, cols)
    d_params = lax.dynamic_slice_in_dim(d_params, inner, shard, 1).reshape(3, NST, shard)
    d_params = d_params.transpose(0, 2, 1)
    state_grad = chosen[two:].reshape(NST, 2, cols)
    state_grad = pick(state_grad, member % 2, 1)
    state_grad = lax.dynamic_slice_in_dim(state_grad, inner, shard, 1).T[None]

    def reduced(partial, waits):
        return reduce_weight(partial.reshape(ns * ny, -1, partial.shape[1]), place, waits)

    d_down, came_down = reduced(d_down, {1: d_qkv, 2: d_attn, 3: lam_mid})
    d_up, came_up = reduced(d_up, {1: d_attn, 2: lam_mid, 3: du})
    d_attn, came_attn = reduced(d_attn, {1: leaving, 2: du})
    d_down = spread_weight("down", *d_down, idx, [w_down.shape])[0]
    if fb % LANES:
        d_up = spread_narrow(*d_up, idx, w_up.shape, fb)
    else:
        d_up = spread_weight("up", *d_up, idx, [w_up.shape], fb)[0]
    d_wqkv, d_out = spread_weight("attn", *d_attn, idx, [w_qkv.shape, w_out.shape])
    return (
        result,
        d_tokens,
        d_wqkv,
        d_out,
        d_up,
        d_down,
        gains[0],
        gains[1],
        d_params[0],
        d_params[1],
        d_params[2],
        state_grad,
        ends,
    )


def solution(mesh):
    return jax.shard_map(
        on_device,
        mesh=mesh,
        in_specs=(
            P("dp", "seq", None),
            P("seq", None),
            P("seq", None),
            P("seq", None),
            P("seq", None),
            P("seq"),
            P("seq"),
            P("seq", None),
            P("seq", None),
            P("seq", None),
            P("dp", None, None),
            P("dp", "seq", None),
            P("dp", "seq", None, None),
        ),
        out_specs=(
            P("dp", "seq", None),
            P("dp", "seq", None),
            P("seq", None),
            P("seq", None),
            P("seq", None),
            P("seq", None),
            P("seq"),
            P("seq"),
            P("seq", None),
            P("seq", None),
            P("seq", None),
            P("dp", "seq", None),
            P("dp", "seq", None, None),
        ),
        check_vma=False,
    )
```

```python
import functools
import math

import jax
import jax.numpy as jnp
from jax import lax
from jax.experimental import pallas as pl
from jax.experimental.pallas import tpu as pltpu
from jax.sharding import PartitionSpec as P

HEADS = 8
HD = 128
CTX = 128
NST = 16
LANES = 128
GROUP = 4
TEAM = 4

epsilon = 1e-05
far_below = -1e30
bf16 = jnp.bfloat16
f32 = jnp.float32


def swap(a, axis, bit):
    return lax.ppermute(a, axis, [(k, k ^ bit) for k in range(lax.axis_size(axis))])


def swap_team(a, r):
    if r == 1:
        return swap(a, "dp", 1)
    if r == 2:
        return swap(a, "seq", 1)
    nd, ns = lax.axis_size("dp"), lax.axis_size("seq")
    pairs = [(d * ns + k, (d ^ 1) * ns + (k ^ 1)) for d in range(nd) for k in range(ns)]
    return lax.ppermute(a, ("dp", "seq"), pairs)


def gather_team(a):
    far = swap_team(a, 2)
    return [a, swap_team(a, 1), far, swap_team(far, 1)]


def far_kernel(mine, came, out):
    out[...] = (mine[...] + came[...].astype(f32)).astype(bf16)


def sum_team(parts, middle=None, end=None):
    one, three = swap_team(parts[1], 1), swap_team(parts[3], 1)
    if middle is not None:
        three = after(three, middle)
    shape = jax.ShapeDtypeStruct(three.shape, bf16)
    near = call(far_kernel, "far_sum", shape, (parts[2], three), 0)
    far = swap_team(near, 2)
    if end is not None:
        one, far = after((one, far), end)
    return parts[0], one, far, near


def trade_team(parts):
    return [parts[0]] + [swap_team(parts[r], r) for r in (1, 2, 3)]


def high_bits(axis):
    size = lax.axis_size(axis)
    return [1 << k for k in reversed(range(1, size.bit_length() - 1))]


def pick(a, index, axis=0):
    return lax.dynamic_index_in_dim(a, index, axis, False)


def ordered(blocks, index):
    bit = len(blocks) // 2
    while bit:
        flip = (index & bit) != 0
        blocks = [jnp.where(flip, blocks[r ^ bit], blocks[r]) for r in range(len(blocks))]
        bit //= 2
    return blocks


def after(x, *others):
    return lax.optimization_barrier((x, others))[0]


def whole_spec():
    return pl.BlockSpec(memory_space=pltpu.VMEM)


def scalar_spec():
    return pl.BlockSpec(memory_space=pltpu.SMEM)


def any_spec():
    return pl.BlockSpec(memory_space=pl.ANY)


BIG = pltpu.CompilerParams(vmem_limit_bytes=32 * 2**20)
MIDDLE = pltpu.CompilerParams(vmem_limit_bytes=24 * 2**20)
SMALL = pltpu.CompilerParams(vmem_limit_bytes=20 * 2**20)


def block_of(shape):
    return pl.BlockSpec(shape, lambda *k: (0,) * len(shape), pipeline_mode=pl.Buffered(1))


def call(kernel, name, out_shape, args, scalars=1, **more):
    specs = [scalar_spec()] * scalars + [block_of(a.shape) for a in args[scalars:]]
    return pl.pallas_call(
        kernel,
        grid=(1,),
        out_shape=out_shape,
        in_specs=specs,
        out_specs=jax.tree.map(lambda o: block_of(o.shape), out_shape),
        compiler_params=MIDDLE,
        name=name,
        **more,
    )(*args)


def share_kernel(spots, copies, idx, *refs):
    ins, outs, sem = refs[:spots], refs[spots:-1], refs[-1]
    flying = []
    for n, (src, dst, rows_at, cols_at, size, to) in enumerate(copies):
        row = pl.multiple_of(rows_at(idx), 16)
        col = pl.multiple_of(cols_at(idx), LANES)
        flying.append(
            pltpu.make_async_copy(
                ins[src].at[pl.ds(row, size[0]), pl.ds(col, size[1])],
                outs[dst].at[:, pl.ds(to, size[1])],
                sem.at[n],
            )
        )
    for one in flying:
        one.start()
    for one in flying:
        one.wait()


def shares(idx, w_qkv, w_out, w_up, w_down, ny, ns):
    shard, dim = w_out.shape
    quarter = dim // TEAM
    rows, fb = shard // ny, w_down.shape[0] // TEAM
    copies = []
    for away in (0, 1):
        def who(i, away=away):
            return i[0] ^ (2 * away)

        for part in range(3):
            copies.append((0, away, lambda i: i[1] * rows,
                           lambda i, w=who, p=part: p * dim + w(i) * quarter, (rows, quarter), part * quarter))
        copies.append((1, away, lambda i: i[1] * rows,
                       lambda i, w=who: w(i) * quarter, (rows, quarter), 3 * quarter))
        if fb % LANES == 0:
            for k in range(ns):
                copies.append((2, 2 + away, lambda i: i[1] * rows,
                               lambda i, w=who, k=k: (k * TEAM + w(i)) * fb, (rows, fb), k * fb))
        for h in (0, 1):
            copies.append((3, 4 + 2 * h + away, lambda i, w=who, h=h: w(i) * fb + h * (fb // 2),
                           lambda i: 0, (fb // 2, dim), 0))
    sizes = [(rows, dim)] * 2 + [(rows, ns * fb)] * 2 + [(fb // 2, dim)] * 4
    out = pl.pallas_call(
        functools.partial(share_kernel, 4, copies),
        out_shape=[jax.ShapeDtypeStruct(s, bf16) for s in sizes],
        in_specs=[scalar_spec()] + [any_spec()] * 4,
        out_specs=[whole_spec()] * 8,
        scratch_shapes=[pltpu.SemaphoreType.DMA((len(copies),))],
        name="shares",
    )(idx, w_qkv, w_out, w_up, w_down)
    out = [list(out[k : k + 2]) for k in (0, 2, 4, 6)]
    if fb % LANES:
        mine = lax.dynamic_slice_in_dim(w_up, idx[1] * rows, rows, 0).reshape(rows, ns, TEAM, fb)
        out[1] = [pick(mine, idx[0] ^ r, 2).reshape(rows, ns * fb) for r in (0, 2)]
    return out


def place_kernel(maps, cuts, idx, places, *refs):
    ins, outs = refs[: len(maps)], refs[len(maps) :]
    for ref, (which, order, step, offset) in zip(ins, maps):
        rows = ref.shape[1]
        for k, r in enumerate(order):
            at = pl.multiple_of(((places[which] ^ r) * step + offset) * rows, 16)
            if cuts:
                width = outs[0].shape[1]
                outs[0][pl.ds(at, rows), :] = ref[k, :, :width]
                outs[-1][pl.ds(at, rows), :] = ref[k, :, width:]
            else:
                outs[0][pl.ds(at, rows), :] = ref[k]
    for r in range(cuts):
        rows = outs[1].shape[0]
        at = pl.multiple_of((idx[0] ^ r) * rows, 16)
        outs[1 + r][...] = outs[-1][pl.ds(at, rows), :]


def append_kernel(a_ref, b_ref, out):
    count = a_ref.shape[0]
    out[:count] = a_ref[...]
    out[count:] = b_ref[...]


def append(a, b):
    shape = jax.ShapeDtypeStruct((a.shape[0] + b.shape[0],) + a.shape[1:], bf16)
    return call(append_kernel, "append", shape, (a, b), 0)


class Gathering:
    def __init__(self, own, away, parted):
        ny = lax.axis_size("dp") // 2 if parted else 1
        self.seq_steps = [(1, ny)] + [(bit, bit * ny) for bit in high_bits("seq")]
        self.a, self.away, self.order, self.n = own[None], away[None], [0], 0

    def step(self, wait=None):
        bit, weight = self.seq_steps[self.n]
        if self.n:
            self.a = append(self.a, self.came)
            self.order = self.order + [r | self.seq_steps[self.n - 1][1] for r in self.order]
        sent = self.a if self.n else self.away
        self.came = swap(sent if wait is None else after(sent, wait), "seq", bit)
        self.n += 1
        if self.n == len(self.seq_steps):
            last = [r | weight for r in self.order]
            self.pieces = [(self.a, self.order), (self.came, last)]
        return self.came

    def rest(self, wait=None):
        while self.n < len(self.seq_steps) - 1:
            self.step(wait)
            wait = None
        return self.came

    def across(self, k, wait=None):
        new = [self.pieces[k]]
        for bit in high_bits("dp"):
            for a, order in list(new):
                a = a if wait is None else after(a, wait)
                new.append((swap(a, "dp", bit), [r | (bit // 2) for r in order]))
        self.pieces += new[1:]
        return new[1][0]


def place_weight(idx, places, groups, width=None):
    arrays = [a for pieces, *_ in groups for a, _ in pieces]
    maps = [(which, order, step, at) for pieces, which, step, at in groups for _, order in pieces]
    rows, cols = sum(a.shape[0] * a.shape[1] for a in arrays), arrays[0].shape[2]
    shapes = [(rows, cols)]
    scratch = []
    if width:
        shapes = [(rows, width)] + [(rows // TEAM, cols - width)] * TEAM
        scratch = [pltpu.VMEM((rows, cols - width), bf16)]
    return call(
        functools.partial(place_kernel, maps, TEAM if width else 0),
        "place_weight",
        [jax.ShapeDtypeStruct(s, bf16) for s in shapes],
        (idx, places, *arrays),
        2,
        scratch_shapes=scratch,
    )


def attn_grad_kernel(idx, x_ref, dq_ref, ctx_ref, dctx_ref, *refs):
    parts, out = refs[:TEAM], refs[TEAM]
    k = pl.program_id(0)
    width = dq_ref.shape[1] // 3
    grad = dot_tn(x_ref[...], dq_ref[...])
    far = dot_tn(ctx_ref[...], dctx_ref[...])
    out[:, :width] = grad[:, :width].astype(bf16)
    out[:, width : 3 * width] = (grad[:, width:] + far).astype(bf16)
    per = parts[0].shape[0] // out.shape[0]
    member = (k // per) ^ idx[0]
    at = pl.multiple_of((k % per) * out.shape[0], 16)
    for r in range(TEAM):
        @pl.when(member == r)
        def _(r=r):
            out[:, 3 * width :] = parts[r][pl.ds(at, out.shape[0]), :]


def attn_grad(idx, inputs, d_qkv, context, d_ctx_kv, parts):
    dim, step = inputs.shape[1], LANES
    return pl.pallas_call(
        attn_grad_kernel,
        grid=(dim // step,),
        out_shape=jax.ShapeDtypeStruct((dim, d_qkv.shape[1] + parts[0].shape[1]), bf16),
        in_specs=[
            scalar_spec(),
            pl.BlockSpec((inputs.shape[0], step), lambda k: (0, k)),
            block_of(d_qkv.shape),
            pl.BlockSpec((context.shape[0], step), lambda k: (0, k)),
            block_of(d_ctx_kv.shape),
        ]
        + [block_of(p.shape) for p in parts],
        out_specs=pl.BlockSpec((step, d_qkv.shape[1] + parts[0].shape[1]), lambda k: (k, 0)),
        compiler_params=SMALL,
        name="attn_grad",
    )(idx, inputs, d_qkv, context, d_ctx_kv, *parts)


def insert_bit(k, at, bit):
    return ((k >> at) << (at + 1)) | (bit << at) | (k & ((1 << at) - 1))


def split_kernel(before, side, at, place, x_ref, *refs):
    here = (place[0] >> side) & 1
    if before is None:
        (away_ref,) = refs
        for k in range(away_ref.shape[0]):
            away_ref[k] = x_ref[insert_bit(k, at, 1 - here)]
        return
    recv_ref, keep_ref, away_ref = refs

    def total(k):
        j = k if before is True else insert_bit(k, before[1], (place[0] >> before[0]) & 1)
        return (x_ref[j].astype(f32) + recv_ref[k].astype(f32)).astype(bf16)

    for k in range(away_ref.shape[0]):
        away_ref[k] = total(insert_bit(k, at, 1 - here))
        keep_ref[k] = total(insert_bit(k, at, here))


class Reduction:
    def __init__(self, x, place):
        ny = lax.axis_size("dp") // 2
        ns = lax.axis_size("seq")
        y_bits = ny.bit_length() - 1
        steps = [("dp", bit, (bit // 2).bit_length() - 1, 0) for bit in reversed(high_bits("dp"))]
        steps += [("seq", b, (b * ny).bit_length() - 1, 1) for b in reversed(high_bits("seq"))]
        self.steps = steps + [("seq", 1, y_bits, 0)]
        self.place, self.n, self.came = place, 0, None
        self.kept = x.reshape(ns * ny, -1, x.shape[1])

    def step(self, wait=None):
        n, x, recv = self.n, self.kept, self.came
        axis, bit, side, at = self.steps[n]
        if n == 0 and wait is not None:
            x = after(x, wait)
        elif wait is not None:
            recv = after(recv, wait)
        before = None if n == 0 else (self.steps[0][2:] if n == 1 else True)
        count = x.shape[0] // 2 if n == 0 else recv.shape[0] // 2
        half = jax.ShapeDtypeStruct((count,) + x.shape[1:], bf16)
        out = call(
            functools.partial(split_kernel, before, side, at),
            "split_sum",
            [half] if n == 0 else [half, half],
            (self.place, x) if n == 0 else (self.place, x, recv),
        )
        if n:
            self.kept = out[0]
        self.sent = out[-1]
        self.came = swap(self.sent, axis, bit)
        self.n += 1
        return self.sent

    def last(self, wait=None):
        while self.n < len(self.steps):
            self.step(wait)
            wait = None
        return self.kept, self.came


def halves_kernel(place, x_ref, out_ref, in_ref):
    y, z = place[0] & 1, (place[0] >> 2) & 1
    for k in range(out_ref.shape[0]):
        low = ((k >> 1) << 3) | ((k & 1) << 1) | (1 - y)
        out_ref[k] = x_ref[low | ((1 - z) << 2)]
        in_ref[k] = x_ref[low | (z << 2)]


def leave_kernel(place, x_ref, came_ref, out_ref):
    y, z = place[0] & 1, (place[0] >> 2) & 1
    for k in range(out_ref.shape[0]):
        mine = x_ref[((k >> 1) << 3) | ((1 - z) << 2) | ((k & 1) << 1) | y]
        out_ref[k] = (mine.astype(f32) + came_ref[k].astype(f32)).astype(bf16)


def stay_kernel(place, x_ref, came_ref, near_ref, keep_ref, out_ref):
    y, z, far = place[0] & 1, (place[0] >> 2) & 1, (place[0] >> 3) & 1

    def total(k):
        mine = x_ref[((k >> 1) << 3) | (z << 2) | ((k & 1) << 1) | y]
        return (mine.astype(f32) + came_ref[k].astype(f32) + near_ref[k].astype(f32)).astype(bf16)

    for k in (0, 1):
        keep_ref[k] = total((far << 1) | k)
        out_ref[k] = total(((1 - far) << 1) | k)


class HalvedReduction(Reduction):
    def step(self, wait=None):
        n = self.n
        if n > 2:
            self.steps = [None, None, None, ("seq", 1, 1, 0)]
            return super().step(wait)
        x = self.kept
        four = jax.ShapeDtypeStruct((x.shape[0] // 4,) + x.shape[1:], bf16)
        two = jax.ShapeDtypeStruct((2,) + x.shape[1:], bf16)
        if n == 0:
            x = x if wait is None else after(x, wait)
            out, stay = call(halves_kernel, "halves", (four, four), (self.place, x))
            self.sent = out
            self.out, self.stay = swap(out, "dp", 2), swap(stay, "dp", 2)
        elif n == 1:
            came = self.out if wait is None else after(self.out, wait)
            self.sent = call(leave_kernel, "leave_sum", four, (self.place, x, came))
            self.near = swap(self.sent, "seq", 2)
        else:
            came = self.near if wait is None else after(self.near, wait)
            args = (self.place, x, self.stay, came)
            self.kept, self.sent = call(stay_kernel, "stay_sum", (two, two), args)
            self.came = swap(self.sent, "seq", 4)
        self.n += 1
        return self.sent


def final_kernel(kind, fb, idx, mine_ref, other_ref, *outs):
    count, rows, width = mine_ref.shape
    for k in range(count):
        row = pl.multiple_of((idx[1] ^ (k // 2)) * rows, 16)
        for core, ref in enumerate((mine_ref, other_ref)):
            member = idx[0] ^ (2 * (k % 2) + core)
            if kind == "down":
                at = pl.multiple_of(member * (rows * count // 2) + row, 16)
                outs[0][pl.ds(at, rows), :] = ref[k].astype(f32)
            elif kind == "up":
                for n in range(width // fb):
                    col = pl.multiple_of((n * TEAM + member) * fb, LANES)
                    block = ref[k, :, n * fb : (n + 1) * fb]
                    outs[0][pl.ds(row, rows), pl.ds(col, fb)] = block.astype(f32)
            else:
                dim = outs[1].shape[1]
                quarter = dim // TEAM
                for part in range(4):
                    to = outs[0] if part < 3 else outs[1]
                    col = pl.multiple_of((part % 3) * dim * (part < 3) + member * quarter, LANES)
                    block = ref[k, :, part * quarter : (part + 1) * quarter]
                    to[pl.ds(row, rows), pl.ds(col, quarter)] = block.astype(f32)


def spread(own, near):
    blocks = {0: append(own, near)}
    for bit in high_bits("dp"):
        for m in list(blocks):
            blocks[m | (bit // 2)] = swap(blocks[m], "dp", bit)
    blocks = [blocks[m] for m in range(len(blocks))]
    while len(blocks) > 1:
        blocks = [append(a, b) for a, b in zip(blocks[0::2], blocks[1::2])]
    return blocks[0], swap(blocks[0], "dp", 1)


def spread_weight(kind, pair, idx, shapes, fb=LANES):
    return call(
        functools.partial(final_kernel, kind, fb),
        "final_" + kind,
        [jax.ShapeDtypeStruct(s, f32) for s in shapes],
        (idx, *spread(*pair)),
    )


def spread_narrow(pair, idx, shape, fb):
    mine, other = spread(*pair)
    teams = [mine[0::2], other[0::2], mine[1::2], other[1::2]]
    teams = jnp.stack(ordered(teams, idx[0]))
    rows = jnp.stack(ordered([teams[:, m] for m in range(teams.shape[1])], idx[1]), axis=1)
    rows = rows.reshape(TEAM, shape[0], shape[1] // (TEAM * fb), fb).transpose(1, 2, 0, 3)
    return rows.reshape(shape).astype(f32)


def ends_kernel(mid, u_ref, a_ref, mid_ref, end_ref):
    rows = u_ref.shape[0]
    a = [a_ref[n] for n in range(NST)]

    def eight(k, s):
        for t in range(8):
            u = u_ref[k * 8 + t]
            s = tuple(a[n] * s[n] + u for n in range(NST))
        return s

    zero = tuple(jnp.zeros_like(a[0]) for _ in range(NST))
    s = lax.fori_loop(0, mid // 8, eight, zero)
    for n in range(NST):
        mid_ref[n] = s[n]
    s = lax.fori_loop(mid // 8, rows // 8, eight, s)
    for n in range(NST):
        end_ref[n] = s[n]


def local_ends(u, a):
    shape = jax.ShapeDtypeStruct(a.shape, f32)
    kernel = functools.partial(ends_kernel, u.shape[0] - CTX)
    return call(kernel, "ssm_ends", (shape, shape), (u, a), 0)


def context_kernel(mid, late, u_ref, a_ref, gin_ref, gout_ref, h_ref, first_ref, second_ref, y_ref):
    half = NST // 2
    for base in (0, half):
        ns = range(base, base + half)
        a = [a_ref[n] for n in ns]
        gin = [gin_ref[n] for n in ns]
        gout = [gout_ref[n] for n in ns]

        def step(k, h):
            for t in range(4):
                p = k * 4 + t
                u = u_ref[mid + p]
                h = tuple(a[n] * h[n] + gin[n] * u for n in range(half))
                y = functools.reduce(jnp.add, [gout[n] * h[n] for n in range(half)])
                y_ref[p] = y if base == 0 else y_ref[p] + y
            return h

        lax.fori_loop(0, CTX // 4, step, tuple(h_ref[n] for n in ns))
    per = y_ref.shape[1] // TEAM
    for w in range(2):
        for c in range(per):
            own, other = y_ref[:, w * per + c, :], y_ref[:, (2 + w) * per + c, :]
            at = (slice(w * CTX, (w + 1) * CTX), slice(c * LANES, (c + 1) * LANES))
            first_ref[at] = jnp.where(late[0] == 1, other, own).astype(bf16)
            second_ref[at] = jnp.where(late[0] == 1, own, other).astype(bf16)


def contexts(half, u, a, gin, gout, h_mid):
    shape = jax.ShapeDtypeStruct((2 * CTX, u.shape[1] * LANES // TEAM), bf16)
    return call(
        functools.partial(context_kernel, u.shape[0] - CTX),
        "ssm_context",
        (shape, shape),
        (half, u, a, gin, gout, h_mid),
        scratch_shapes=[pltpu.VMEM((CTX,) + u.shape[1:], f32)],
    )


def tail_kernel(dy_ref, a_ref, gout_ref, lam_ref):
    half = dy_ref.shape[1]
    a = [a_ref[n, :half] for n in range(NST)]
    gout = [gout_ref[n, :half] for n in range(NST)]

    def eight(k, lam):
        for t in range(8):
            dy = dy_ref[CTX - 1 - (k * 8 + t)]
            lam = tuple(a[n] * lam[n] + gout[n] * dy for n in range(NST))
        return lam

    lam = lax.fori_loop(0, CTX // 8, eight, tuple(jnp.zeros_like(a[0]) for _ in range(NST)))
    for n in range(NST):
        lam_ref[n] = lam[n]


def tail_adjoint(dy, a, gout):
    shape = jax.ShapeDtypeStruct((NST,) + dy.shape[1:], f32)
    return call(tail_kernel, "ssm_tail", shape, (dy, a, gout), 0)


def first_context_kernel(dy0_ref, a_ref, gout_ref, init_ref, da_ref, dgout_ref, g0_ref, hs):
    ns = range(GROUP)
    a = [a_ref[n] for n in ns]
    gout = [gout_ref[n] for n in ns]
    zero = tuple(jnp.zeros_like(a[0]) for _ in ns)

    def ahead(k, h):
        for t in range(8):
            h = tuple(a[n] * h[n] for n in ns)
            for n in ns:
                hs[k * 8 + t + 1, n] = h[n]
        return h

    h = tuple(init_ref[n] for n in ns)
    for n in ns:
        hs[0, n] = h[n]
    lax.fori_loop(0, CTX // 8, ahead, h)

    def back(k, carry):
        mu, da, dgout = carry
        for t in range(4):
            q = CTX - 1 - (k * 4 + t)
            dy = dy0_ref[q]
            mu = tuple(mu[n] + gout[n] * dy for n in ns)
            dgout = tuple(dgout[n] + dy * hs[q + 1, n] for n in ns)
            da = tuple(da[n] + mu[n] * hs[q, n] for n in ns)
            mu = tuple(a[n] * mu[n] for n in ns)
        return mu, da, dgout

    mu, da, dgout = lax.fori_loop(0, CTX // 4, back, (zero, zero, zero))
    for n in ns:
        g0_ref[n] = mu[n]
        da_ref[n] = da[n]
        dgout_ref[n] = dgout[n]


def first_context_back(dy0, a, gout, h_init):
    tile = dy0.shape[1:]
    states = pl.BlockSpec((GROUP,) + tile, lambda g: (g, 0, 0))
    return pl.pallas_call(
        first_context_kernel,
        grid=(NST // GROUP,),
        out_shape=(jax.ShapeDtypeStruct(a.shape, f32),) * 3,
        in_specs=[pl.BlockSpec(dy0.shape, lambda g: (0, 0, 0))] + [states] * 3,
        out_specs=(states,) * 3,
        scratch_shapes=[pltpu.VMEM((CTX + 1, GROUP) + tile, f32)],
        name="first_context",
    )(dy0, a, gout, h_init)


def back_kernel(
    u_ref, dy_ref, a_ref, gin_ref, gout_ref, h_ref, lam_ref, da0_ref, dgout0_ref,
    du_ref, dgin_ref, da_ref, dgout_ref, g_ref, hs,
):
    first = pl.program_id(0) == 0
    rows = u_ref.shape[0]
    mid = rows - CTX
    ns = range(GROUP)
    a = [a_ref[n] for n in ns]
    gin = [gin_ref[n] for n in ns]
    gout = [gout_ref[n] for n in ns]
    zero = tuple(jnp.zeros_like(a[0]) for _ in ns)

    def ahead(k, h):
        for t in range(8):
            p = k * 8 + t
            u = u_ref[p]
            h = tuple(a[n] * h[n] + gin[n] * u for n in ns)
            for n in ns:
                hs[p + 1, n] = h[n]
        return h

    h = tuple(h_ref[n] for n in ns)
    for n in ns:
        hs[0, n] = h[n]
    lax.fori_loop(0, rows // 8, ahead, h)

    def tail(k, carry):
        lam, dgin, da, dgout = carry
        for t in range(4):
            q = CTX - 1 - (k * 4 + t)
            p = mid + q
            dy, u = dy_ref[q], u_ref[p]
            lam = tuple(lam[n] + gout[n] * dy for n in ns)
            dgout = tuple(dgout[n] + dy * hs[p + 1, n] for n in ns)
            dgin = tuple(dgin[n] + lam[n] * u for n in ns)
            da = tuple(da[n] + lam[n] * hs[p, n] for n in ns)
            du = functools.reduce(jnp.add, [gin[n] * lam[n] for n in ns])
            du_ref[p] = jnp.where(first, du, du_ref[p] + du)
            lam = tuple(a[n] * lam[n] for n in ns)
        return lam, dgin, da, dgout

    def head(k, carry):
        lam, dgin, da = carry
        for t in range(4):
            p = mid - 1 - (k * 4 + t)
            u = u_ref[p]
            dgin = tuple(dgin[n] + lam[n] * u for n in ns)
            da = tuple(da[n] + lam[n] * hs[p, n] for n in ns)
            du = functools.reduce(jnp.add, [gin[n] * lam[n] for n in ns])
            du_ref[p] = jnp.where(first, du, du_ref[p] + du)
            lam = tuple(a[n] * lam[n] for n in ns)
        return lam, dgin, da

    lam = tuple(lam_ref[n] for n in ns)
    da0, dgout0 = tuple(da0_ref[n] for n in ns), tuple(dgout0_ref[n] for n in ns)
    lam, dgin, da, dgout = lax.fori_loop(0, CTX // 4, tail, (lam, zero, da0, dgout0))
    lam, dgin, da = lax.fori_loop(0, mid // 4, head, (lam, dgin, da))
    for n in ns:
        g_ref[n] = lam[n]
        dgin_ref[n] = dgin[n]
        da_ref[n] = da[n]
        dgout_ref[n] = dgout[n]


def ssm_back(u, dy, a, gin, gout, state_in, lam_end, da0, dgout0):
    tile = u.shape[1:]
    states = pl.BlockSpec((GROUP,) + tile, lambda g: (g, 0, 0))
    rows = pl.BlockSpec(u.shape, lambda g: (0, 0, 0))
    tail = pl.BlockSpec(dy.shape, lambda g: (0, 0, 0))
    out = jax.ShapeDtypeStruct(a.shape, f32)
    return pl.pallas_call(
        back_kernel,
        grid=(NST // GROUP,),
        out_shape=(jax.ShapeDtypeStruct(u.shape, f32),) + (out,) * 4,
        in_specs=[rows, tail] + [states] * 7,
        out_specs=(rows,) + (states,) * 4,
        scratch_shapes=[pltpu.VMEM((u.shape[0] + 1, GROUP) + tile, f32)],
        compiler_params=SMALL,
        name="ssm_back",
    )(u, dy, a, gin, gout, state_in, lam_end, da0, dgout0)


def dot_nt(x, y):
    return lax.dot_general(x, y, (((1,), (1,)), ((), ())), preferred_element_type=f32)


def dot_nn(x, y):
    return jnp.dot(x, y, preferred_element_type=f32)


def dot_tn(x, y):
    return lax.dot_general(x, y, (((0,), (0,)), ((), ())), preferred_element_type=f32)


def softmax_parts(q, keys):
    rows = q.shape[0]
    scores = [dot_nt(q, k) * (1.0 / math.sqrt(HD)) for k in keys]
    at = lax.broadcasted_iota(jnp.int32, (rows, rows), 0)
    to = lax.broadcasted_iota(jnp.int32, (rows, rows), 1)
    scores[-1] = jnp.where(to <= at, scores[-1], far_below)
    top = functools.reduce(jnp.maximum, [jnp.max(s, axis=-1, keepdims=True) for s in scores])
    es = [jnp.exp(s - top) for s in scores]
    total = functools.reduce(jnp.add, [jnp.sum(e, axis=-1, keepdims=True) for e in es])
    return [e / total for e in es]


def attend_kernel(half_ref, q0, q1, k0, k1, v0, v1, kc, vc, out_ref):
    w, h = pl.program_id(0), pl.program_id(1)
    rows = q0.shape[0]
    for half, q, keys, values in ((0, q0, (kc, k0), (vc, v0)), (1, q1, (kc, k0, k1), (vc, v0, v1))):
        probs = softmax_parts(q[...], [k[...] for k in keys])
        out = [dot_nn(p.astype(bf16), v[...]) for p, v in zip(probs, values)]
        at = pl.multiple_of(((half ^ half_ref[0]) * 2 + w) * rows, 16)
        col = pl.multiple_of(h * HD, LANES)
        out_ref[pl.ds(at, rows), pl.ds(col, HD)] = functools.reduce(jnp.add, out).astype(bf16)


def attend_back_kernel(
    half_ref, q0, q1, k0, k1, v0, v1, kc, vc, do0, do1, dqkv_ref, dctx_ref
):
    w, h = pl.program_id(0), pl.program_id(1)
    rows, heads = q0.shape[0], pl.num_programs(1)
    scale = 1.0 / math.sqrt(HD)
    dk, dv = [0.0, 0.0, 0.0], [0.0, 0.0, 0.0]

    def row_of(half):
        return pl.multiple_of(((half ^ half_ref[0]) * 2 + w) * rows, 16)

    def col_of(part):
        return pl.multiple_of((part * heads + h) * HD, LANES)

    cases = ((0, q0, do0, (kc, k0), (vc, v0)), (1, q1, do1, (kc, k0, k1), (vc, v0, v1)))
    for half, q, do, keys, values in cases:
        query, d_out = q[...], do[...]
        probs = softmax_parts(query, [k[...] for k in keys])
        d_probs = [dot_nt(d_out, v[...]) for v in values]
        sums = [jnp.sum(p * d, axis=-1, keepdims=True) for p, d in zip(probs, d_probs)]
        delta = functools.reduce(jnp.add, sums)
        d_scores = [(p * (d - delta)).astype(bf16) for p, d in zip(probs, d_probs)]
        dq = functools.reduce(jnp.add, [dot_nn(d, k[...]) for d, k in zip(d_scores, keys)])
        dqkv_ref[pl.ds(row_of(half), rows), pl.ds(col_of(0), HD)] = (dq * scale).astype(bf16)
        for n, (d, p) in enumerate(zip(d_scores, probs)):
            dk[n] = dk[n] + dot_tn(d, query)
            dv[n] = dv[n] + dot_tn(p.astype(bf16), d_out)
    ctx_row = pl.multiple_of(w * CTX, 16)
    dctx_ref[pl.ds(ctx_row, CTX), pl.ds(col_of(0), HD)] = (dk[0] * scale).astype(bf16)
    dctx_ref[pl.ds(ctx_row, CTX), pl.ds(col_of(1), HD)] = dv[0].astype(bf16)
    for half in (0, 1):
        dqkv_ref[pl.ds(row_of(half), rows), pl.ds(col_of(1), HD)] = (dk[1 + half] * scale).astype(bf16)
        dqkv_ref[pl.ds(row_of(half), rows), pl.ds(col_of(2), HD)] = dv[1 + half].astype(bf16)


def attention_specs(rows, heads):
    def at(half, part):
        return pl.BlockSpec((rows, HD), lambda w, h, s: ((half ^ s[0]) * 2 + w, part * heads + h))

    def ctx(part):
        return pl.BlockSpec((CTX, HD), lambda w, h, s: (w, part * heads + h))

    return [at(half, part) for part in range(3) for half in (0, 1)] + [ctx(0), ctx(1)]


def whole_block(shape):
    return pl.BlockSpec(shape, lambda w, h, s: (0, 0))


def attend(half, qkv, ctx_kv):
    rows, heads = qkv.shape[0] // TEAM, qkv.shape[1] // (3 * HD)
    out = (qkv.shape[0], heads * HD)
    return pl.pallas_call(
        attend_kernel,
        grid_spec=pltpu.PrefetchScalarGridSpec(
            num_scalar_prefetch=1,
            grid=(2, heads),
            in_specs=attention_specs(rows, heads),
            out_specs=whole_block(out),
        ),
        out_shape=jax.ShapeDtypeStruct(out, bf16),
        compiler_params=SMALL,
        name="attend",
    )(half, *[qkv] * 6, ctx_kv, ctx_kv)


def attend_back(half, qkv, ctx_kv, d_attended):
    rows, heads = qkv.shape[0] // TEAM, qkv.shape[1] // (3 * HD)

    def at(side):
        return pl.BlockSpec((rows, HD), lambda w, h, s: ((side ^ s[0]) * 2 + w, h))

    return pl.pallas_call(
        attend_back_kernel,
        grid_spec=pltpu.PrefetchScalarGridSpec(
            num_scalar_prefetch=1,
            grid=(2, heads),
            in_specs=attention_specs(rows, heads) + [at(0), at(1)],
            out_specs=[whole_block(qkv.shape), whole_block(ctx_kv.shape)],
        ),
        out_shape=[jax.ShapeDtypeStruct(qkv.shape, bf16), jax.ShapeDtypeStruct(ctx_kv.shape, bf16)],
        compiler_params=SMALL,
        name="attend_back",
    )(half, *[qkv] * 6, ctx_kv, ctx_kv, d_attended, d_attended)


def pack_kernel(rate, gin, gout, g_one, g_two, out):
    for k, ref in enumerate((rate, gin, gout)):
        out[0, k * NST : (k + 1) * NST, :] = ref[...].astype(f32).T.astype(bf16)
    out[0, 3 * NST : 3 * NST + 1, :] = g_one[...]
    out[0, 3 * NST + 1 : 3 * NST + 2, :] = g_two[...]


def norm_kernel(idx, gain, x0, x1, x2, x3, low_ref, inv_ref, u_ref):
    rows, dim = x0.shape
    cols = dim // TEAM
    for r, ref in enumerate((x0, x1, x2, x3)):
        x = ref[...].astype(f32)
        inv = lax.rsqrt(jnp.mean(x * x, axis=-1, keepdims=True) + epsilon)
        inv_ref[r * rows : (r + 1) * rows, :] = inv
        low_ref[r * rows : (r + 1) * rows, :] = (x * inv * gain[...]).astype(bf16)
        for c in range(cols // LANES):
            at = pl.multiple_of(idx[0] * cols + c * LANES, LANES)
            u = low_ref[r * rows : (r + 1) * rows, pl.ds(at, LANES)].astype(f32)
            u_ref[:, r * (cols // LANES) + c, :] = u


def first_norm(idx, gain, blocks):
    rows, dim = blocks[0].shape
    shapes = (
        jax.ShapeDtypeStruct((TEAM * rows, dim), bf16),
        jax.ShapeDtypeStruct((TEAM * rows, 1), f32),
        jax.ShapeDtypeStruct((rows, dim // LANES, LANES), f32),
    )
    return call(norm_kernel, "first_norm", shapes, (idx, gain[None], *blocks))


def part_types(rows, dim):
    return tuple(jax.ShapeDtypeStruct((rows, dim), (f32, bf16)[r % 2]) for r in range(TEAM))


def dot_kernel(x_ref, w_ref, *parts):
    rows = parts[0].shape[0]
    for r in (3, 1, 2, 0):
        part = dot_nn(x_ref[r * rows : (r + 1) * rows, :], w_ref[...])
        parts[r][...] = part.astype(parts[r].dtype)


def dot_parts(name, x, w):
    return call(dot_kernel, name, part_types(x.shape[0] // TEAM, w.shape[1]), (x, w), 0)


def out_kernel(idx, x_ref, w0, w1, w2, w3, *parts):
    rows, cols = parts[0].shape[0], w0.shape[1]
    for r in (3, 1, 2, 0):
        for q, w in enumerate((w0, w1, w2, w3)):
            at = pl.multiple_of((idx[0] ^ q) * cols, LANES)
            part = dot_nn(x_ref[r * rows : (r + 1) * rows, :], w[...])
            parts[r][:, pl.ds(at, cols)] = part.astype(parts[r].dtype)


def context_kv_kernel(idx, w_ref, c0, c1, c2, c3, kv_ref, context_ref):
    cols = c0.shape[1]
    width = w_ref.shape[1] // 3
    for r, part in enumerate((c0, c1, c2, c3)):
        at = pl.multiple_of((idx[0] ^ r) * cols, LANES)
        for w in (0, 1):
            v = w ^ (r & 1)
            context_ref[w * CTX : (w + 1) * CTX, pl.ds(at, cols)] = part[v * CTX : (v + 1) * CTX, :]
    kv_ref[...] = dot_nn(context_ref[...], w_ref[:, width:]).astype(bf16)


def mlp_kernel(m0, m1, m2, m3, g0, g1, g2, g3, up, down, act_ref, dpre_ref, *parts_and_sum):
    parts, total = parts_and_sum[:-1], parts_and_sum[-1]
    k = pl.program_id(0)
    rows = m0.shape[0]
    c = math.sqrt(2.0 / math.pi)
    for r, (m, g) in enumerate(((m0, g0), (m1, g1), (m2, g2), (m3, g3))):
        at = slice(r * rows, (r + 1) * rows)
        x = dot_nn(m[...], up[...])
        t = jnp.tanh(c * (x + 0.044715 * (x * x * x)))
        cdf = 0.5 * (1.0 + t)
        act_ref[at, :] = (x * cdf).astype(bf16)
        slope = cdf + (0.5 * c) * x * (1.0 - t * t) * (1.0 + (3 * 0.044715) * (x * x))
        d_pre = (dot_nt(g[...], down[...]) * slope).astype(bf16)
        dpre_ref[at, :] = d_pre
        new = dot_nt(d_pre, up[...])
        total[at, :] = jnp.where(k == 0, new, total[at, :] + new)

    @pl.when(k == pl.num_programs(0) - 1)
    def _():
        for r, part in enumerate(parts):
            part[...] = total[r * rows : (r + 1) * rows, :].astype(part.dtype)


def feed_forward(mlp_blocks, grad_blocks, up, down):
    rows, dim = mlp_blocks[0].shape
    units = up.shape[1]
    step = 256

    unit_out = jax.ShapeDtypeStruct((TEAM * rows, units), bf16)
    return pl.pallas_call(
        mlp_kernel,
        grid=(units // step,),
        out_shape=(unit_out, unit_out) + part_types(rows, dim),
        in_specs=[block_of((rows, dim))] * 8
        + [pl.BlockSpec((dim, step), lambda k: (0, k)), pl.BlockSpec((step, dim), lambda k: (k, 0))],
        out_specs=(pl.BlockSpec((TEAM * rows, step), lambda k: (0, k)),) * 2
        + (block_of((rows, dim)),) * TEAM,
        scratch_shapes=[pltpu.VMEM((TEAM * rows, dim), f32)],
        compiler_params=MIDDLE,
        name="feed_forward",
    )(*mlp_blocks, *grad_blocks, up, down)


def mlp_grad_kernel(x_ref, y0, y1, y2, y3, out):
    rows = y0.shape[0]
    grads = [dot_tn(x_ref[r * rows : (r + 1) * rows, :], y[...]) for r, y in enumerate((y0, y1, y2, y3))]
    out[...] = functools.reduce(jnp.add, grads).astype(bf16)


def down_grad(act, grad_blocks):
    rows, dim = grad_blocks[0].shape
    step = 256
    return pl.pallas_call(
        mlp_grad_kernel,
        grid=(act.shape[1] // step,),
        out_shape=jax.ShapeDtypeStruct((act.shape[1], dim), bf16),
        in_specs=[pl.BlockSpec((act.shape[0], step), lambda k: (0, k))]
        + [block_of((rows, dim))] * TEAM,
        out_specs=pl.BlockSpec((step, dim), lambda k: (k, 0)),
        compiler_params=SMALL,
        name="down_grad",
    )(act, *grad_blocks)


def up_grad_kernel(x0, x1, x2, x3, y_ref, out):
    rows = x0.shape[0]
    grads = [dot_tn(x[...], y_ref[r * rows : (r + 1) * rows, :]) for r, x in enumerate((x0, x1, x2, x3))]
    out[...] = functools.reduce(jnp.add, grads).astype(bf16)


def up_grad(mlp_blocks, d_pre):
    rows, dim = mlp_blocks[0].shape
    step = 256
    return pl.pallas_call(
        up_grad_kernel,
        grid=(dim // step,),
        out_shape=jax.ShapeDtypeStruct((dim, d_pre.shape[1]), bf16),
        in_specs=[pl.BlockSpec((rows, step), lambda k: (0, k))] * TEAM
        + [block_of(d_pre.shape)],
        out_specs=pl.BlockSpec((step, d_pre.shape[1]), lambda k: (k, 0)),
        compiler_params=SMALL,
        name="up_grad",
    )(*mlp_blocks, d_pre)


def attended_grad_kernel(idx, w0, w1, w2, w3, h0, h1, h2, h3, out):
    rows, cols = h0.shape[0], w0.shape[1]
    for r, h in enumerate((h0, h1, h2, h3)):
        grad = 0.0
        for q, w in enumerate((w0, w1, w2, w3)):
            at = pl.multiple_of((idx[0] ^ q) * cols, LANES)
            grad = grad + dot_nt(h[:, pl.ds(at, cols)], w[...])
        out[r * rows : (r + 1) * rows, :] = grad.astype(bf16)


def out_grad_kernel(idx, att_ref, h0, h1, h2, h3, *parts):
    rows, cols = h0.shape[0], parts[0].shape[1]
    for q, part in enumerate(parts):
        at = pl.multiple_of((idx[0] ^ q) * cols, LANES)
        grads = [
            dot_tn(att_ref[r * rows : (r + 1) * rows, :], h[:, pl.ds(at, cols)])
            for r, h in enumerate((h0, h1, h2, h3))
        ]
        part[...] = functools.reduce(jnp.add, grads).astype(bf16)


def context_grad_kernel(idx, d_ref, w_ref, *parts):
    cols = parts[0].shape[1]
    width = w_ref.shape[1] // 3
    for r, part in enumerate(parts):
        at = pl.multiple_of((idx[0] ^ r) * cols, 16)
        for w in (0, 1):
            v = w ^ (r & 1)
            grad = dot_nt(d_ref[w * CTX : (w + 1) * CTX, :], w_ref[pl.ds(at, cols), width:])
            part[v * CTX : (v + 1) * CTX, :] = grad.astype(part.dtype)


def inputs_grad_kernel(idx, dq_ref, w_ref, du_ref, inv_ref, x0, x1, x2, x3, *outs):
    parts, gain_ref, work = outs[:TEAM], outs[TEAM], outs[TEAM + 1]
    rows, dim = x0.shape
    cols = dim // TEAM
    gain = 0.0
    for r, x in enumerate((x0, x1, x2, x3)):
        at = slice(r * rows, (r + 1) * rows)
        work[...] = dot_nt(dq_ref[at, :], w_ref[...])
        for c in range(cols // LANES):
            col = pl.ds(pl.multiple_of(idx[0] * cols + c * LANES, LANES), LANES)
            work[:, col] = work[:, col] + du_ref[:, r * (cols // LANES) + c, :]
        grad = work[...]
        parts[r][...] = grad.astype(parts[r].dtype)
        gain = gain + jnp.sum(grad * (x[...].astype(f32) * inv_ref[at, :]), axis=0, keepdims=True)
    gain_ref[...] = gain


def cut_states_kernel(idx, init_ref, ends_ref, i0, i1, e0, e1, e2, e3):
    cols = i0.shape[1]
    for r, out in enumerate((e0, e1, e2, e3)):
        at = pl.multiple_of((idx[0] ^ r) * cols, 16)
        out[...] = ends_ref[pl.ds(at, cols), :].T
        if r < 2:
            (i0, i1)[r][...] = init_ref[pl.ds(at, cols), :].T


def join_states_kernel(late, i0, i1, e0, e1, e2, e3, init_ref, twice_ref, first_ref, second_ref):
    per = init_ref.shape[1] // 2
    for w in range(2):
        for c in range(per):
            at = slice(c * LANES, (c + 1) * LANES)
            init = (i0, i1)[w][:, at]
            init_ref[:, w * per + c, :] = init
            twice_ref[:, w * per + c, :] = init
            twice_ref[:, (2 + w) * per + c, :] = init
            own, other = (e0, e1)[w][:, at], (e2, e3)[w][:, at]
            first_ref[:, w * per + c, :] = jnp.where(late[0] == 1, other, own)
            second_ref[:, w * per + c, :] = jnp.where(late[0] == 1, own, other)


def cut_ends_kernel(late, first_ref, second_ref, e0, e1, e2, e3):
    per = first_ref.shape[1] // 2
    for w in range(2):
        for c in range(per):
            at = slice(c * LANES, (c + 1) * LANES)
            one, two = first_ref[:, w * per + c, :], second_ref[:, w * per + c, :]
            (e0, e1)[w][:, at] = jnp.where(late[0] == 1, two, one)
            (e2, e3)[w][:, at] = jnp.where(late[0] == 1, one, two)


def join_ends_kernel(idx, e0, e1, e2, e3, out):
    cols = e0.shape[1]
    for r, part in enumerate((e0, e1, e2, e3)):
        at = pl.multiple_of((idx[0] ^ r) * cols, 16)
        out[pl.ds(at, cols), :] = part[...].T


def small_kernel(spots, p0, p1, p2, p3, gains_ref, rate_ref, in_ref, out_ref, init_ref):
    packs = [p[...] for p in (p0, p1, p2, p3)]
    tiles = packs[0].shape[0] - 3 * NST * 2 - NST * 4
    one, two = 3 * NST * 2, 3 * NST * 2 + tiles
    gains = functools.reduce(jnp.add, [p[one:two] for p in packs])
    row = lax.broadcasted_iota(jnp.int32, gains.shape, 0)
    for k in (0, 1):
        mine = row == k * (tiles // 2) + spots[1]
        gains_ref[k : k + 1, :] = jnp.sum(jnp.where(mine, gains, 0.0), axis=0, keepdims=True)
    chosen = packs[0]
    for r in (1, 2, 3):
        chosen = jnp.where(spots[0] == r, packs[r], chosen)
    side = spots[1] % 2 == 1
    params = chosen[:one].reshape(3 * NST, 2, LANES)
    params = jnp.where(side, params[:, 1], params[:, 0])
    for k, ref in enumerate((rate_ref, in_ref, out_ref)):
        ref[...] = params[k * NST : (k + 1) * NST].T
    init = chosen[two:].reshape(NST, 4, LANES)
    window = [jnp.where(side, init[:, 2 * w + 1], init[:, 2 * w]) for w in (0, 1)]
    init_ref[...] = jnp.where(spots[0] % 2 == 1, window[1], window[0]).T


def added(p0, one, far):
    return p0[...] + one[...].astype(f32) + far[...].astype(f32)


def second_norm_kernel(tok, p0, one, far, gain, hidden_ref, inv_ref, low_ref):
    hidden = tok[...].astype(f32) + added(p0, one, far)
    inv = lax.rsqrt(jnp.mean(hidden * hidden, axis=-1, keepdims=True) + epsilon)
    hidden_ref[...] = hidden
    inv_ref[...] = inv
    low_ref[...] = (hidden * inv * gain[...]).astype(bf16)


def result_kernel(hidden, p0, one, far, out):
    out[...] = (hidden[...] + added(p0, one, far)).astype(bf16)


def norm_back(grad, normed, inv, gain):
    scaled = grad * gain
    return inv * (scaled - normed * jnp.mean(scaled * normed, axis=-1, keepdims=True))


def hidden_grad_kernel(cot, hidden, inv, gain, p0, one, far, out_ref, low_ref, gain_ref):
    grad = added(p0, one, far)
    normed = hidden[...] * inv[...]
    gain_ref[...] = jnp.sum(grad * normed, axis=0, keepdims=True)
    out = cot[...].astype(f32) + norm_back(grad, normed, inv[...], gain[...])
    out_ref[...] = out
    low_ref[...] = out.astype(bf16)


def tokens_grad_kernel(d_hidden, tok, inv, gain, p0, one, far, out):
    grad = added(p0, one, far)
    normed = tok[...].astype(f32) * inv[...]
    out[...] = (d_hidden[...] + norm_back(grad, normed, inv[...], gain[...])).astype(bf16)


def context_sum_kernel(p0, one, far, out):
    out[...] = added(p0, one, far).astype(bf16)


def context_rows_kernel(flags, came, own, dy_ref, dy_full, dy0_full):
    per = dy_ref.shape[1] // 2
    zero = jnp.zeros((CTX, LANES), f32)
    for w in range(2):
        for c in range(per):
            at = (slice(w * CTX, (w + 1) * CTX), slice(c * LANES, (c + 1) * LANES))
            dy = came[at].astype(f32)
            dy_ref[:, w * per + c, :] = dy
            dy_full[:, w * per + c, :] = jnp.where(flags[0] == 1, dy, zero)
            dy_full[:, (2 + w) * per + c, :] = jnp.where(flags[0] == 1, zero, dy)
            dy0_full[:, w * per + c, :] = jnp.where(flags[1] == 0, own[at].astype(f32), zero)
            dy0_full[:, (2 + w) * per + c, :] = zero


def on_device(
    tokens,
    w_qkv,
    w_out,
    w_up,
    w_down,
    g_attn,
    g_mlp,
    ssm_rate,
    ssm_in,
    ssm_out,
    h_init,
    cotangent,
    d_h_ends,
):
    nd, ns = lax.axis_size("dp"), lax.axis_size("seq")
    ny = nd // 2
    dp, seq = lax.axis_index("dp"), lax.axis_index("seq")
    late = seq % 2 == 1
    block = seq // 2
    me = (seq % 2) * 2 + dp % 2
    idx = jnp.stack([me, dp // 2]).astype(jnp.int32)
    place = (seq * ny + dp // 2).astype(jnp.int32).reshape(1)
    half = (seq % 2).astype(jnp.int32).reshape(1)
    rows, dim = tokens.shape[1:]
    shard = w_qkv.shape[0]
    width = HEADS * HD // TEAM
    cols = dim // TEAM
    fb = w_down.shape[0] // TEAM
    tile = (dim // LANES, LANES)
    half_tile = (dim // LANES // 2, LANES)

    def like(shape, dtype):
        return jax.ShapeDtypeStruct(shape, dtype)


    share_attn, share_up, *share_down = shares(idx, w_qkv, w_out, w_up, w_down, ny, ns)
    attn, up = Gathering(*share_attn, True), Gathering(*share_up, True)
    down = [Gathering(*share, False) for share in share_down]
    attn_pair = attn.step()
    x_blocks = gather_team(after(tokens[0], attn_pair))
    up.step(attn_pair)
    attn_first = attn.rest()
    for part in down:
        part.step(attn_first)
    attn_second = attn.step()
    attn_third = attn.across(0)
    attn_last = attn.across(1)
    up_first = up.rest(attn_second)
    small = call(
        pack_kernel,
        "pack_small",
        jax.ShapeDtypeStruct((1, 3 * NST + 2, shard), bf16),
        (ssm_rate, ssm_in, ssm_out, g_attn[None], after(g_mlp[None], share_attn[1])),
        0,
    )
    for bit in [1] + high_bits("seq")[::-1]:
        got = swap(small, "seq", bit)
        upper = (seq & bit) != 0
        small = jnp.concatenate([jnp.where(upper, got, small), jnp.where(upper, small, got)], axis=0)
    small = small.astype(f32)
    gain_one = small[:, 3 * NST].reshape(dim)
    gain_two = small[:, 3 * NST + 1].reshape(dim)
    params = small[:, : 3 * NST].transpose(1, 0, 2).reshape(3 * NST, dim)
    params = lax.dynamic_slice_in_dim(params, me * cols, cols, 1)
    params = jnp.broadcast_to(params[:, None], (3 * NST, TEAM, cols)).reshape((3, NST) + tile)
    rate, gin, gout = params[0], params[1], params[2]
    half_rate = rate[:, : tile[0] // 2]

    by_channel = like((NST, cols), f32)
    init, near_init, *end_cot = call(
        cut_states_kernel,
        "cut_states",
        (by_channel,) * 6,
        (idx, h_init[0], after(d_h_ends[0, 0], share_attn[1])),
    )
    init, init_twice, end_first, end_second = call(
        join_states_kernel,
        "join_states",
        tuple(like((NST,) + t, f32) for t in (half_tile, tile, half_tile, half_tile)),
        (half, init, swap_team(near_init, 1), *trade_team(end_cot)),
    )
    end_cot = [end_first, end_second]
    g_blocks = gather_team(after(cotangent[0], attn_first))

    def by_half(a, axis=1):
        n = a.shape[axis] // 2
        own, other = lax.slice_in_dim(a, 0, n, axis=axis), lax.slice_in_dim(a, n, 2 * n, axis=axis)
        return ordered([own, other], seq % 2)

    def by_owner(first, second):
        return jnp.concatenate(ordered([first, second], seq % 2), axis=1)

    inputs_low, inv_one, u = first_norm(idx, after(gain_one, attn_first), x_blocks)

    a = jnp.exp(-rate)
    s_mid, s_end = local_ends(u, a)
    decay = jnp.exp(-half_rate * rows)
    first_end, second_end = by_half(gin * s_end)
    span = 2 * rows

    def chain(inclusive, back, meanwhile):
        exclusive, step = jnp.zeros_like(inclusive), 1
        while step < ns // 2:
            pairs = [(k, k + 2 * step) for k in range(ns - 2 * step)]
            got = lax.ppermute(inclusive, "seq", [(t, f) for f, t in pairs] if back else pairs)
            got = after(got, meanwhile)
            exclusive = exclusive + jnp.exp(-half_rate * (span * (step - 1))) * got
            inclusive = inclusive + jnp.exp(-half_rate * (span * step)) * got
            step *= 2
        return exclusive

    entering = chain(decay * first_end + second_end, False, up_first)
    state_zero = jnp.exp(-half_rate * (span * block).astype(f32)) * init + entering
    state_one = decay * state_zero + first_end
    state_two = decay * state_one + second_end
    state_in = by_owner(state_zero, state_one)
    ends = call(cut_ends_kernel, "cut_ends", (by_channel,) * TEAM, (half, state_one, state_two))
    ends = call(join_ends_kernel, "join_ends", like((dim, NST), f32), (idx, *trade_team(ends)))
    on_second = by_owner(jnp.zeros_like(init), jnp.ones_like(init))
    h_mid = jnp.exp(-rate * (rows - CTX)) * state_in + gin * s_mid
    h_mid = jnp.where(on_second > 0, h_mid, init_twice)
    h_mid = after(h_mid, (attn_second, attn_third))
    y_first, y_second = contexts(half, u, a, gin * on_second, gout, h_mid)
    passed = lax.ppermute(y_second, "seq", [(k, k + 2) for k in range(ns - 2)])
    up_second = up.step(entering)
    up_third = up.across(0, attn_last)
    context = jnp.where(block == 0, y_first, after(passed, up_second))
    down_first = down[0].rest(passed)
    down_second = down[1].rest(up_third)
    context = gather_team(context)

    places = jnp.stack([place[0], seq]).astype(jnp.int32)
    full_qkv, *full_out = place_weight(idx, places, [(attn.pieces, 0, 1, 0)], 3 * width)
    full_qkv = after(full_qkv, (down_first, up_third))
    full_out = trade_team(full_out)
    qkv = dot_nn(inputs_low, full_qkv).astype(bf16)
    ctx_kv, context = call(
        context_kv_kernel,
        "context_kv",
        (like((2 * CTX, 2 * width), bf16), like((2 * CTX, dim), bf16)),
        (idx, full_qkv, *context),
    )
    attended = attend(half, qkv, ctx_kv)

    down_third = down[0].step(down_second)
    up_last = up.across(1, up_third)
    attended = after(attended, (g_blocks[2], down_second))
    attended_parts = call(out_kernel, "out_dot", part_types(rows, dim), (idx, attended, *full_out))
    attended_parts = sum_team(attended_parts, None, (ends, down_third, up_last))
    down[1].step(down_third)
    (full_up,) = place_weight(idx, places, [(up.pieces, 0, 1, 0)])
    down = [(part.pieces, 1, 2, h) for h, part in enumerate(down)]
    (full_down,) = place_weight(idx, places, down)

    hidden, inv_two, mlp_in = call(
        second_norm_kernel,
        "second_norm",
        (like((rows, dim), f32), like((rows, 1), f32), like((rows, dim), bf16)),
        (tokens[0], *attended_parts[:3], gain_two[None]),
        0,
    )
    mlp_in = gather_team(mlp_in)
    act, d_pre, *d_mlp = feed_forward(mlp_in, g_blocks, full_up, full_down)
    d_down = down_grad(act, g_blocks)
    reduction = HalvedReduction if (nd, ns) == (4, 8) else Reduction
    sum_down = reduction(d_down, place)
    sum_down.step()
    d_up = up_grad(mlp_in, after(d_pre, sum_down.sent))
    sum_up = reduction(d_up, place)
    sum_up.step()
    result = dot_parts("down_dot", after(act, sum_up.sent), full_down)
    d_mlp = sum_team(d_mlp, d_down, result)
    sum_down.step(d_mlp[3])
    d_hidden, d_hidden_low, d_gain_two = call(
        hidden_grad_kernel,
        "hidden_grad",
        (like((rows, dim), f32), like((rows, dim), bf16), like((1, dim), f32)),
        (after(cotangent[0], sum_down.sent), hidden, inv_two, gain_two[None], *d_mlp[:3]),
        0,
    )
    hidden_blocks = gather_team(d_hidden_low)
    sum_down.step(d_hidden)

    d_attended = call(
        attended_grad_kernel,
        "attended_grad",
        jax.ShapeDtypeStruct(attended.shape, bf16),
        (idx, after(full_out[0], sum_down.sent), *full_out[1:], *hidden_blocks),
    )
    d_out = call(
        out_grad_kernel,
        "out_grad",
        (jax.ShapeDtypeStruct((width, cols), bf16),) * TEAM,
        (idx, after(attended, d_attended), *hidden_blocks),
    )
    d_qkv, d_ctx_kv = attend_back(half, qkv, ctx_kv, after(d_attended, d_out))
    d_out = trade_team(d_out)
    sum_up.step(d_ctx_kv)
    d_context = call(
        context_grad_kernel,
        "context_grad",
        part_types(2 * CTX, cols),
        (idx, after(d_ctx_kv, sum_up.sent), full_qkv),
    )
    d_attn = attn_grad(idx, inputs_low, after(d_qkv, d_context), context, d_ctx_kv, d_out)
    sum_attn = reduction(d_attn, place)
    sum_attn.step()
    d_context = sum_team(d_context, None, sum_attn.sent)
    d_context = call(context_sum_kernel, "context_sum", like((2 * CTX, cols), bf16), d_context[:3], 0)
    came = lax.ppermute(d_context, "seq", [(k + 2, k) for k in range(ns - 2)])
    flags = jnp.stack([seq % 2, block]).astype(jnp.int32)
    dy, dy_full, dy0_full = call(
        context_rows_kernel,
        "context_rows",
        (like((CTX,) + half_tile, f32), like((CTX,) + tile, f32), like((CTX,) + tile, f32)),
        (flags, came, d_context),
    )

    lam_mid = tail_adjoint(dy, a, gout)
    g_second = jnp.exp(-half_rate * (rows - CTX + 1)) * lam_mid + decay * end_cot[1]
    d_a, d_gout, g_init = first_context_back(after(dy0_full, lam_mid), a, gout, init_twice)
    leaving = chain(decay * (end_cot[0] + g_second), True, g_init)
    sum_up.step(leaving)
    sum_attn.step(sum_up.sent)
    sum_down.step(sum_attn.sent)
    lam_end = by_owner(end_cot[0] + g_second + decay * leaving, end_cot[1] + leaving)
    du, d_gin, d_a, d_gout, g_in = ssm_back(
        u, dy_full, a, gin, gout, state_in, after(lam_end, sum_down.sent), d_a, d_gout
    )
    g_first = by_half(g_in)[0]
    d_init = g_init[:, : tile[0] // 2] + jnp.where(block == 0, g_first, jnp.zeros_like(g_first))
    d_rate = -a * d_a

    *d_inputs, d_gain_one = call(
        inputs_grad_kernel,
        "inputs_grad",
        part_types(rows, dim) + (jax.ShapeDtypeStruct((1, dim), f32),),
        (idx, d_qkv, full_qkv, du, inv_one, *x_blocks),
        scratch_shapes=[pltpu.VMEM((rows, dim), f32)],
    )
    d_down = spread_weight("down", sum_down.last(), idx, [w_down.shape])[0]
    sum_up.step(d_gain_one)
    sum_attn.step(sum_up.sent)
    result = sum_team(result, d_context, du)
    result = call(result_kernel, "result_sum", like((rows, dim), bf16), (hidden, *result[:3]), 0)
    *d_inputs, d_inputs_far = sum_team(d_inputs, None, d_down)
    d_tokens = call(
        tokens_grad_kernel,
        "tokens_grad",
        like((rows, dim), bf16),
        (d_hidden, tokens[0], inv_one[:rows], gain_one[None], *d_inputs),
        0,
    )

    d_params = after(jnp.stack([d_rate, d_gin, d_gout]), d_gain_one)
    d_params = d_params.reshape(3 * NST, TEAM, cols).sum(1)
    d_gains = jnp.concatenate([d_gain_one[0], d_gain_two[0]])
    pack = [d_params.reshape(-1, LANES), d_gains.reshape(-1, LANES), d_init.reshape(-1, LANES)]
    pack = after(jnp.concatenate(pack, axis=0), (sum_attn.sent, d_inputs_far))
    for n, bit in enumerate(high_bits("seq")):
        if n == 1:
            pack = after(pack, sum_attn.step())
        pack = pack + swap(pack, "seq", bit)
    one, two = 3 * NST * cols // LANES, 3 * NST * cols // LANES + 2 * dim // LANES
    shared = pack[:two]
    for bit in high_bits("dp"):
        shared = shared + swap(shared, "dp", bit)
    packs = gather_team(jnp.concatenate([shared, pack[two:]], axis=0))
    if shard == LANES:
        spots = jnp.stack([me ^ (seq * shard // cols), seq]).astype(jnp.int32)
        gains, *d_params, state_grad = call(
            small_kernel,
            "small_grads",
            (like((2, shard), f32),) + (like((shard, NST), f32),) * 4,
            (spots, *packs),
        )
        state_grad = state_grad[None]
    else:
        packs = jnp.stack(packs)
        gains = packs[:, one:two].sum(0).reshape(2, ns, shard)
        gains = pick(gains, seq, 1)
        member = me ^ (seq * shard // cols)
        inner = seq * shard % cols
        chosen = pick(packs, member)
        d_params = chosen[:one].reshape(3 * NST, cols)
        d_params = lax.dynamic_slice_in_dim(d_params, inner, shard, 1).reshape(3, NST, shard)
        d_params = d_params.transpose(0, 2, 1)
        state_grad = chosen[two:].reshape(NST, 2, cols)
        state_grad = pick(state_grad, member % 2, 1)
        state_grad = lax.dynamic_slice_in_dim(state_grad, inner, shard, 1).T[None]

    if fb % LANES:
        d_up = spread_narrow(sum_up.last(), idx, w_up.shape, fb)
    else:
        d_up = spread_weight("up", sum_up.last(), idx, [w_up.shape], fb)[0]
    d_wqkv, d_out = spread_weight("attn", sum_attn.last(), idx, [w_qkv.shape, w_out.shape])
    return (
        result[None],
        d_tokens[None],
        d_wqkv,
        d_out,
        d_up,
        d_down,
        gains[0],
        gains[1],
        d_params[0],
        d_params[1],
        d_params[2],
        state_grad,
        ends[None, None],
    )


def solution(mesh):
    return jax.shard_map(
        on_device,
        mesh=mesh,
        in_specs=(
            P("dp", "seq", None),
            P("seq", None),
            P("seq", None),
            P("seq", None),
            P("seq", None),
            P("seq"),
            P("seq"),
            P("seq", None),
            P("seq", None),
            P("seq", None),
            P("dp", None, None),
            P("dp", "seq", None),
            P("dp", "seq", None, None),
        ),
        out_specs=(
            P("dp", "seq", None),
            P("dp", "seq", None),
            P("seq", None),
            P("seq", None),
            P("seq", None),
            P("seq", None),
            P("seq"),
            P("seq"),
            P("seq", None),
            P("seq", None),
            P("seq", None),
            P("dp", "seq", None),
            P("dp", "seq", None, None),
        ),
        check_vma=False,
    )
```

```python
import functools
import math

import jax
import jax.numpy as jnp
from jax import lax
from jax.experimental import pallas as pl
from jax.experimental.pallas import tpu as pltpu
from jax.sharding import PartitionSpec as P

HEADS = 8
HD = 128
CTX = 128
NST = 16
LANES = 128
GROUP = 4
TEAM = 4

epsilon = 1e-05
far_below = -1e30
bf16 = jnp.bfloat16
f32 = jnp.float32


def swap(a, axis, bit):
    return lax.ppermute(a, axis, [(k, k ^ bit) for k in range(lax.axis_size(axis))])


def swap_team(a, r):
    if r == 1:
        return swap(a, "dp", 1)
    if r == 2:
        return swap(a, "seq", 1)
    nd, ns = lax.axis_size("dp"), lax.axis_size("seq")
    pairs = [(d * ns + k, (d ^ 1) * ns + (k ^ 1)) for d in range(nd) for k in range(ns)]
    return lax.ppermute(a, ("dp", "seq"), pairs)


def gather_team(a):
    far = swap_team(a, 2)
    return [a, swap_team(a, 1), far, swap_team(far, 1)]


def far_kernel(mine, came, out):
    out[...] = (mine[...] + came[...].astype(f32)).astype(bf16)


def sum_team(parts, middle=None, end=None):
    one, three = swap_team(parts[1], 1), swap_team(parts[3], 1)
    if middle is not None:
        three = after(three, middle)
    shape = jax.ShapeDtypeStruct(three.shape, bf16)
    near = call(far_kernel, "far_sum", shape, (parts[2], three), 0)
    far = swap_team(near, 2)
    if end is not None:
        one, far = after((one, far), end)
    return parts[0], one, far, near


def trade_team(parts):
    return [parts[0]] + [swap_team(parts[r], r) for r in (1, 2, 3)]


def high_bits(axis):
    size = lax.axis_size(axis)
    return [1 << k for k in reversed(range(1, size.bit_length() - 1))]


def pick(a, index, axis=0):
    return lax.dynamic_index_in_dim(a, index, axis, False)


def ordered(blocks, index):
    bit = len(blocks) // 2
    while bit:
        flip = (index & bit) != 0
        blocks = [jnp.where(flip, blocks[r ^ bit], blocks[r]) for r in range(len(blocks))]
        bit //= 2
    return blocks


def after(x, *others):
    return lax.optimization_barrier((x, others))[0]


def whole_spec():
    return pl.BlockSpec(memory_space=pltpu.VMEM)


def scalar_spec():
    return pl.BlockSpec(memory_space=pltpu.SMEM)


def any_spec():
    return pl.BlockSpec(memory_space=pl.ANY)


BIG = pltpu.CompilerParams(vmem_limit_bytes=32 * 2**20)
MIDDLE = pltpu.CompilerParams(vmem_limit_bytes=24 * 2**20)
SMALL = pltpu.CompilerParams(vmem_limit_bytes=20 * 2**20)


def block_of(shape):
    return pl.BlockSpec(shape, lambda *k: (0,) * len(shape), pipeline_mode=pl.Buffered(1))


def call(kernel, name, out_shape, args, scalars=1, **more):
    specs = [scalar_spec()] * scalars + [block_of(a.shape) for a in args[scalars:]]
    return pl.pallas_call(
        kernel,
        grid=(1,),
        out_shape=out_shape,
        in_specs=specs,
        out_specs=jax.tree.map(lambda o: block_of(o.shape), out_shape),
        compiler_params=MIDDLE,
        name=name,
        **more,
    )(*args)


def share_kernel(spots, copies, idx, *refs):
    ins, outs, sem = refs[:spots], refs[spots:-1], refs[-1]
    flying = []
    for n, (src, dst, rows_at, cols_at, size, to) in enumerate(copies):
        row = pl.multiple_of(rows_at(idx), 16)
        col = pl.multiple_of(cols_at(idx), LANES)
        flying.append(
            pltpu.make_async_copy(
                ins[src].at[pl.ds(row, size[0]), pl.ds(col, size[1])],
                outs[dst].at[:, pl.ds(to, size[1])],
                sem.at[n],
            )
        )
    for one in flying:
        one.start()
    for one in flying:
        one.wait()


def shares(idx, w_qkv, w_out, w_up, w_down, ny, ns):
    shard, dim = w_out.shape
    quarter = dim // TEAM
    rows, fb = shard // ny, w_down.shape[0] // TEAM
    copies = []
    for away in (0, 1):
        def who(i, away=away):
            return i[0] ^ (2 * away)

        for part in range(3):
            copies.append((0, away, lambda i: i[1] * rows,
                           lambda i, w=who, p=part: p * dim + w(i) * quarter, (rows, quarter), part * quarter))
        copies.append((1, away, lambda i: i[1] * rows,
                       lambda i, w=who: w(i) * quarter, (rows, quarter), 3 * quarter))
        if fb % LANES == 0:
            for k in range(ns):
                copies.append((2, 2 + away, lambda i: i[1] * rows,
                               lambda i, w=who, k=k: (k * TEAM + w(i)) * fb, (rows, fb), k * fb))
        for h in (0, 1):
            copies.append((3, 4 + 2 * h + away, lambda i, w=who, h=h: w(i) * fb + h * (fb // 2),
                           lambda i: 0, (fb // 2, dim), 0))
    sizes = [(rows, dim)] * 2 + [(rows, ns * fb)] * 2 + [(fb // 2, dim)] * 4
    out = pl.pallas_call(
        functools.partial(share_kernel, 4, copies),
        out_shape=[jax.ShapeDtypeStruct(s, bf16) for s in sizes],
        in_specs=[scalar_spec()] + [any_spec()] * 4,
        out_specs=[whole_spec()] * 8,
        scratch_shapes=[pltpu.SemaphoreType.DMA((len(copies),))],
        name="shares",
    )(idx, w_qkv, w_out, w_up, w_down)
    out = [list(out[k : k + 2]) for k in (0, 2, 4, 6)]
    if fb % LANES:
        mine = lax.dynamic_slice_in_dim(w_up, idx[1] * rows, rows, 0).reshape(rows, ns, TEAM, fb)
        out[1] = [pick(mine, idx[0] ^ r, 2).reshape(rows, ns * fb) for r in (0, 2)]
    return out


def place_kernel(maps, cuts, idx, places, *refs):
    ins, outs = refs[: len(maps)], refs[len(maps) :]
    for ref, (which, order, step, offset) in zip(ins, maps):
        rows = ref.shape[1]
        for k, r in enumerate(order):
            at = pl.multiple_of(((places[which] ^ r) * step + offset) * rows, 16)
            if cuts:
                width = outs[0].shape[1]
                outs[0][pl.ds(at, rows), :] = ref[k, :, :width]
                outs[-1][pl.ds(at, rows), :] = ref[k, :, width:]
            else:
                outs[0][pl.ds(at, rows), :] = ref[k]
    for r in range(cuts):
        rows = outs[1].shape[0]
        at = pl.multiple_of((idx[0] ^ r) * rows, 16)
        outs[1 + r][...] = outs[-1][pl.ds(at, rows), :]


def append_kernel(a_ref, b_ref, out):
    count = a_ref.shape[0]
    out[:count] = a_ref[...]
    out[count:] = b_ref[...]


def append(a, b):
    shape = jax.ShapeDtypeStruct((a.shape[0] + b.shape[0],) + a.shape[1:], bf16)
    return call(append_kernel, "append", shape, (a, b), 0)


class Gathering:
    def __init__(self, own, away, parted):
        ny = lax.axis_size("dp") // 2 if parted else 1
        self.seq_steps = [(1, ny)] + [(bit, bit * ny) for bit in high_bits("seq")]
        self.a, self.away, self.order, self.n = own[None], away[None], [0], 0

    def step(self, wait=None):
        bit, weight = self.seq_steps[self.n]
        if self.n:
            self.a = append(self.a, self.came)
            self.order = self.order + [r | self.seq_steps[self.n - 1][1] for r in self.order]
        sent = self.a if self.n else self.away
        self.came = swap(sent if wait is None else after(sent, wait), "seq", bit)
        self.n += 1
        if self.n == len(self.seq_steps):
            last = [r | weight for r in self.order]
            self.pieces = [(self.a, self.order), (self.came, last)]
        return self.came

    def rest(self, wait=None):
        while self.n < len(self.seq_steps) - 1:
            self.step(wait)
            wait = None
        return self.came

    def across(self, k, wait=None):
        new = [self.pieces[k]]
        for bit in high_bits("dp"):
            for a, order in list(new):
                a = a if wait is None else after(a, wait)
                new.append((swap(a, "dp", bit), [r | (bit // 2) for r in order]))
        self.pieces += new[1:]
        return new[1][0]


def place_weight(idx, places, groups, width=None):
    arrays = [a for pieces, *_ in groups for a, _ in pieces]
    maps = [(which, order, step, at) for pieces, which, step, at in groups for _, order in pieces]
    rows, cols = sum(a.shape[0] * a.shape[1] for a in arrays), arrays[0].shape[2]
    shapes = [(rows, cols)]
    scratch = []
    if width:
        shapes = [(rows, width)] + [(rows // TEAM, cols - width)] * TEAM
        scratch = [pltpu.VMEM((rows, cols - width), bf16)]
    return call(
        functools.partial(place_kernel, maps, TEAM if width else 0),
        "place_weight",
        [jax.ShapeDtypeStruct(s, bf16) for s in shapes],
        (idx, places, *arrays),
        2,
        scratch_shapes=scratch,
    )


def attn_grad_kernel(idx, x_ref, dq_ref, ctx_ref, dctx_ref, *refs):
    parts, out = refs[:TEAM], refs[TEAM]
    k = pl.program_id(0)
    width = dq_ref.shape[1] // 3
    grad = dot_tn(x_ref[...], dq_ref[...])
    far = dot_tn(ctx_ref[...], dctx_ref[...])
    out[:, :width] = grad[:, :width].astype(bf16)
    out[:, width : 3 * width] = (grad[:, width:] + far).astype(bf16)
    per = parts[0].shape[0] // out.shape[0]
    member = (k // per) ^ idx[0]
    at = pl.multiple_of((k % per) * out.shape[0], 16)
    for r in range(TEAM):
        @pl.when(member == r)
        def _(r=r):
            out[:, 3 * width :] = parts[r][pl.ds(at, out.shape[0]), :]


def attn_grad(idx, inputs, d_qkv, context, d_ctx_kv, parts):
    dim, step = inputs.shape[1], LANES
    return pl.pallas_call(
        attn_grad_kernel,
        grid=(dim // step,),
        out_shape=jax.ShapeDtypeStruct((dim, d_qkv.shape[1] + parts[0].shape[1]), bf16),
        in_specs=[
            scalar_spec(),
            pl.BlockSpec((inputs.shape[0], step), lambda k: (0, k)),
            block_of(d_qkv.shape),
            pl.BlockSpec((context.shape[0], step), lambda k: (0, k)),
            block_of(d_ctx_kv.shape),
        ]
        + [block_of(p.shape) for p in parts],
        out_specs=pl.BlockSpec((step, d_qkv.shape[1] + parts[0].shape[1]), lambda k: (k, 0)),
        compiler_params=SMALL,
        name="attn_grad",
    )(idx, inputs, d_qkv, context, d_ctx_kv, *parts)


def insert_bit(k, at, bit):
    return ((k >> at) << (at + 1)) | (bit << at) | (k & ((1 << at) - 1))


def split_kernel(before, side, at, place, x_ref, *refs):
    here = (place[0] >> side) & 1
    if before is None:
        (away_ref,) = refs
        for k in range(away_ref.shape[0]):
            away_ref[k] = x_ref[insert_bit(k, at, 1 - here)]
        return
    recv_ref, keep_ref, away_ref = refs

    def total(k):
        j = k if before is True else insert_bit(k, before[1], (place[0] >> before[0]) & 1)
        return (x_ref[j].astype(f32) + recv_ref[k].astype(f32)).astype(bf16)

    for k in range(away_ref.shape[0]):
        away_ref[k] = total(insert_bit(k, at, 1 - here))
        keep_ref[k] = total(insert_bit(k, at, here))


class Reduction:
    def __init__(self, x, place):
        ny = lax.axis_size("dp") // 2
        ns = lax.axis_size("seq")
        y_bits = ny.bit_length() - 1
        steps = [("dp", bit, (bit // 2).bit_length() - 1, 0) for bit in reversed(high_bits("dp"))]
        steps += [("seq", b, (b * ny).bit_length() - 1, 1) for b in reversed(high_bits("seq"))]
        self.steps = steps + [("seq", 1, y_bits, 0)]
        self.place, self.n, self.came = place, 0, None
        self.kept = x.reshape(ns * ny, -1, x.shape[1])

    def step(self, wait=None):
        n, x, recv = self.n, self.kept, self.came
        axis, bit, side, at = self.steps[n]
        if n == 0 and wait is not None:
            x = after(x, wait)
        elif wait is not None:
            recv = after(recv, wait)
        before = None if n == 0 else (self.steps[0][2:] if n == 1 else True)
        count = x.shape[0] // 2 if n == 0 else recv.shape[0] // 2
        half = jax.ShapeDtypeStruct((count,) + x.shape[1:], bf16)
        out = call(
            functools.partial(split_kernel, before, side, at),
            "split_sum",
            [half] if n == 0 else [half, half],
            (self.place, x) if n == 0 else (self.place, x, recv),
        )
        if n:
            self.kept = out[0]
        self.sent = out[-1]
        self.came = swap(self.sent, axis, bit)
        self.n += 1
        return self.sent

    def last(self, wait=None):
        while self.n < len(self.steps):
            self.step(wait)
            wait = None
        return self.kept, self.came


def halves_kernel(place, x_ref, out_ref, in_ref):
    y, z = place[0] & 1, (place[0] >> 2) & 1
    for k in range(out_ref.shape[0]):
        low = ((k >> 1) << 3) | ((k & 1) << 1) | (1 - y)
        out_ref[k] = x_ref[low | ((1 - z) << 2)]
        in_ref[k] = x_ref[low | (z << 2)]


def leave_kernel(place, x_ref, came_ref, out_ref):
    y, z = place[0] & 1, (place[0] >> 2) & 1
    for k in range(out_ref.shape[0]):
        mine = x_ref[((k >> 1) << 3) | ((1 - z) << 2) | ((k & 1) << 1) | y]
        out_ref[k] = (mine.astype(f32) + came_ref[k].astype(f32)).astype(bf16)


def stay_kernel(place, x_ref, came_ref, near_ref, keep_ref, out_ref):
    y, z, far = place[0] & 1, (place[0] >> 2) & 1, (place[0] >> 3) & 1

    def total(k):
        mine = x_ref[((k >> 1) << 3) | (z << 2) | ((k & 1) << 1) | y]
        return (mine.astype(f32) + came_ref[k].astype(f32) + near_ref[k].astype(f32)).astype(bf16)

    for k in (0, 1):
        keep_ref[k] = total((far << 1) | k)
        out_ref[k] = total(((1 - far) << 1) | k)


class HalvedReduction(Reduction):
    def step(self, wait=None):
        n = self.n
        if n > 2:
            self.steps = [None, None, None, ("seq", 1, 1, 0)]
            return super().step(wait)
        x = self.kept
        four = jax.ShapeDtypeStruct((x.shape[0] // 4,) + x.shape[1:], bf16)
        two = jax.ShapeDtypeStruct((2,) + x.shape[1:], bf16)
        if n == 0:
            x = x if wait is None else after(x, wait)
            out, stay = call(halves_kernel, "halves", (four, four), (self.place, x))
            self.sent = out
            self.out, self.stay = swap(out, "dp", 2), swap(stay, "dp", 2)
        elif n == 1:
            came = self.out if wait is None else after(self.out, wait)
            self.sent = call(leave_kernel, "leave_sum", four, (self.place, x, came))
            self.near = swap(self.sent, "seq", 2)
        else:
            came = self.near if wait is None else after(self.near, wait)
            args = (self.place, x, self.stay, came)
            self.kept, self.sent = call(stay_kernel, "stay_sum", (two, two), args)
            self.came = swap(self.sent, "seq", 4)
        self.n += 1
        return self.sent


def final_kernel(kind, fb, idx, mine_ref, other_ref, *outs):
    count, rows, width = mine_ref.shape
    for k in range(count):
        row = pl.multiple_of((idx[1] ^ (k // 2)) * rows, 16)
        for core, ref in enumerate((mine_ref, other_ref)):
            member = idx[0] ^ (2 * (k % 2) + core)
            if kind == "down":
                at = pl.multiple_of(member * (rows * count // 2) + row, 16)
                outs[0][pl.ds(at, rows), :] = ref[k].astype(f32)
            elif kind == "up":
                for n in range(width // fb):
                    col = pl.multiple_of((n * TEAM + member) * fb, LANES)
                    block = ref[k, :, n * fb : (n + 1) * fb]
                    outs[0][pl.ds(row, rows), pl.ds(col, fb)] = block.astype(f32)
            else:
                dim = outs[1].shape[1]
                quarter = dim // TEAM
                for part in range(4):
                    to = outs[0] if part < 3 else outs[1]
                    col = pl.multiple_of((part % 3) * dim * (part < 3) + member * quarter, LANES)
                    block = ref[k, :, part * quarter : (part + 1) * quarter]
                    to[pl.ds(row, rows), pl.ds(col, quarter)] = block.astype(f32)


def spread(own, near):
    blocks = {0: append(own, near)}
    for bit in high_bits("dp"):
        for m in list(blocks):
            blocks[m | (bit // 2)] = swap(blocks[m], "dp", bit)
    blocks = [blocks[m] for m in range(len(blocks))]
    while len(blocks) > 1:
        blocks = [append(a, b) for a, b in zip(blocks[0::2], blocks[1::2])]
    return blocks[0], swap(blocks[0], "dp", 1)


def spread_weight(kind, pair, idx, shapes, fb=LANES):
    return call(
        functools.partial(final_kernel, kind, fb),
        "final_" + kind,
        [jax.ShapeDtypeStruct(s, f32) for s in shapes],
        (idx, *spread(*pair)),
    )


def spread_narrow(pair, idx, shape, fb):
    mine, other = spread(*pair)
    teams = [mine[0::2], other[0::2], mine[1::2], other[1::2]]
    teams = jnp.stack(ordered(teams, idx[0]))
    rows = jnp.stack(ordered([teams[:, m] for m in range(teams.shape[1])], idx[1]), axis=1)
    rows = rows.reshape(TEAM, shape[0], shape[1] // (TEAM * fb), fb).transpose(1, 2, 0, 3)
    return rows.reshape(shape).astype(f32)


def ends_kernel(mid, u_ref, a_ref, mid_ref, end_ref):
    rows = u_ref.shape[0]
    a = [a_ref[n] for n in range(NST)]

    def eight(k, s):
        for t in range(8):
            u = u_ref[k * 8 + t]
            s = tuple(a[n] * s[n] + u for n in range(NST))
        return s

    zero = tuple(jnp.zeros_like(a[0]) for _ in range(NST))
    s = lax.fori_loop(0, mid // 8, eight, zero)
    for n in range(NST):
        mid_ref[n] = s[n]
    s = lax.fori_loop(mid // 8, rows // 8, eight, s)
    for n in range(NST):
        end_ref[n] = s[n]


def local_ends(u, a):
    shape = jax.ShapeDtypeStruct(a.shape, f32)
    kernel = functools.partial(ends_kernel, u.shape[0] - CTX)
    return call(kernel, "ssm_ends", (shape, shape), (u, a), 0)


def context_kernel(mid, late, u_ref, a_ref, gin_ref, gout_ref, h_ref, first_ref, second_ref, y_ref):
    half = NST // 2
    for base in (0, half):
        ns = range(base, base + half)
        a = [a_ref[n] for n in ns]
        gin = [gin_ref[n] for n in ns]
        gout = [gout_ref[n] for n in ns]

        def step(k, h):
            for t in range(4):
                p = k * 4 + t
                u = u_ref[mid + p]
                h = tuple(a[n] * h[n] + gin[n] * u for n in range(half))
                y = functools.reduce(jnp.add, [gout[n] * h[n] for n in range(half)])
                y_ref[p] = y if base == 0 else y_ref[p] + y
            return h

        lax.fori_loop(0, CTX // 4, step, tuple(h_ref[n] for n in ns))
    per = y_ref.shape[1] // TEAM
    for w in range(2):
        for c in range(per):
            own, other = y_ref[:, w * per + c, :], y_ref[:, (2 + w) * per + c, :]
            at = (slice(w * CTX, (w + 1) * CTX), slice(c * LANES, (c + 1) * LANES))
            first_ref[at] = jnp.where(late[0] == 1, other, own).astype(bf16)
            second_ref[at] = jnp.where(late[0] == 1, own, other).astype(bf16)


def contexts(half, u, a, gin, gout, h_mid):
    shape = jax.ShapeDtypeStruct((2 * CTX, u.shape[1] * LANES // TEAM), bf16)
    return call(
        functools.partial(context_kernel, u.shape[0] - CTX),
        "ssm_context",
        (shape, shape),
        (half, u, a, gin, gout, h_mid),
        scratch_shapes=[pltpu.VMEM((CTX,) + u.shape[1:], f32)],
    )


def tail_kernel(dy_ref, a_ref, gout_ref, lam_ref):
    half = dy_ref.shape[1]
    a = [a_ref[n, :half] for n in range(NST)]
    gout = [gout_ref[n, :half] for n in range(NST)]

    def eight(k, lam):
        for t in range(8):
            dy = dy_ref[CTX - 1 - (k * 8 + t)]
            lam = tuple(a[n] * lam[n] + gout[n] * dy for n in range(NST))
        return lam

    lam = lax.fori_loop(0, CTX // 8, eight, tuple(jnp.zeros_like(a[0]) for _ in range(NST)))
    for n in range(NST):
        lam_ref[n] = lam[n]


def tail_adjoint(dy, a, gout):
    shape = jax.ShapeDtypeStruct((NST,) + dy.shape[1:], f32)
    return call(tail_kernel, "ssm_tail", shape, (dy, a, gout), 0)


def first_context_kernel(dy0_ref, a_ref, gout_ref, init_ref, da_ref, dgout_ref, g0_ref, hs):
    ns = range(GROUP)
    a = [a_ref[n] for n in ns]
    gout = [gout_ref[n] for n in ns]
    zero = tuple(jnp.zeros_like(a[0]) for _ in ns)

    def ahead(k, h):
        for t in range(8):
            h = tuple(a[n] * h[n] for n in ns)
            for n in ns:
                hs[k * 8 + t + 1, n] = h[n]
        return h

    h = tuple(init_ref[n] for n in ns)
    for n in ns:
        hs[0, n] = h[n]
    lax.fori_loop(0, CTX // 8, ahead, h)

    def back(k, carry):
        mu, da, dgout = carry
        for t in range(4):
            q = CTX - 1 - (k * 4 + t)
            dy = dy0_ref[q]
            mu = tuple(mu[n] + gout[n] * dy for n in ns)
            dgout = tuple(dgout[n] + dy * hs[q + 1, n] for n in ns)
            da = tuple(da[n] + mu[n] * hs[q, n] for n in ns)
            mu = tuple(a[n] * mu[n] for n in ns)
        return mu, da, dgout

    mu, da, dgout = lax.fori_loop(0, CTX // 4, back, (zero, zero, zero))
    for n in ns:
        g0_ref[n] = mu[n]
        da_ref[n] = da[n]
        dgout_ref[n] = dgout[n]


def first_context_back(dy0, a, gout, h_init):
    tile = dy0.shape[1:]
    states = pl.BlockSpec((GROUP,) + tile, lambda g: (g, 0, 0))
    return pl.pallas_call(
        first_context_kernel,
        grid=(NST // GROUP,),
        out_shape=(jax.ShapeDtypeStruct(a.shape, f32),) * 3,
        in_specs=[pl.BlockSpec(dy0.shape, lambda g: (0, 0, 0))] + [states] * 3,
        out_specs=(states,) * 3,
        scratch_shapes=[pltpu.VMEM((CTX + 1, GROUP) + tile, f32)],
        name="first_context",
    )(dy0, a, gout, h_init)


def back_kernel(
    u_ref, dy_ref, a_ref, gin_ref, gout_ref, h_ref, lam_ref, da0_ref, dgout0_ref,
    du_ref, dgin_ref, da_ref, dgout_ref, g_ref, hs,
):
    first = pl.program_id(0) == 0
    rows = u_ref.shape[0]
    mid = rows - CTX
    ns = range(GROUP)
    a = [a_ref[n] for n in ns]
    gin = [gin_ref[n] for n in ns]
    gout = [gout_ref[n] for n in ns]
    zero = tuple(jnp.zeros_like(a[0]) for _ in ns)

    def ahead(k, h):
        for t in range(8):
            p = k * 8 + t
            u = u_ref[p]
            h = tuple(a[n] * h[n] + gin[n] * u for n in ns)
            for n in ns:
                hs[p + 1, n] = h[n]
        return h

    h = tuple(h_ref[n] for n in ns)
    for n in ns:
        hs[0, n] = h[n]
    lax.fori_loop(0, rows // 8, ahead, h)

    def tail(k, carry):
        lam, dgin, da, dgout = carry
        for t in range(4):
            q = CTX - 1 - (k * 4 + t)
            p = mid + q
            dy, u = dy_ref[q], u_ref[p]
            lam = tuple(lam[n] + gout[n] * dy for n in ns)
            dgout = tuple(dgout[n] + dy * hs[p + 1, n] for n in ns)
            dgin = tuple(dgin[n] + lam[n] * u for n in ns)
            da = tuple(da[n] + lam[n] * hs[p, n] for n in ns)
            du = functools.reduce(jnp.add, [gin[n] * lam[n] for n in ns])
            du_ref[p] = jnp.where(first, du, du_ref[p] + du)
            lam = tuple(a[n] * lam[n] for n in ns)
        return lam, dgin, da, dgout

    def head(k, carry):
        lam, dgin, da = carry
        for t in range(4):
            p = mid - 1 - (k * 4 + t)
            u = u_ref[p]
            dgin = tuple(dgin[n] + lam[n] * u for n in ns)
            da = tuple(da[n] + lam[n] * hs[p, n] for n in ns)
            du = functools.reduce(jnp.add, [gin[n] * lam[n] for n in ns])
            du_ref[p] = jnp.where(first, du, du_ref[p] + du)
            lam = tuple(a[n] * lam[n] for n in ns)
        return lam, dgin, da

    lam = tuple(lam_ref[n] for n in ns)
    da0, dgout0 = tuple(da0_ref[n] for n in ns), tuple(dgout0_ref[n] for n in ns)
    lam, dgin, da, dgout = lax.fori_loop(0, CTX // 4, tail, (lam, zero, da0, dgout0))
    lam, dgin, da = lax.fori_loop(0, mid // 4, head, (lam, dgin, da))
    for n in ns:
        g_ref[n] = lam[n]
        dgin_ref[n] = dgin[n]
        da_ref[n] = da[n]
        dgout_ref[n] = dgout[n]


def ssm_back(u, dy, a, gin, gout, state_in, lam_end, da0, dgout0):
    tile = u.shape[1:]
    states = pl.BlockSpec((GROUP,) + tile, lambda g: (g, 0, 0))
    rows = pl.BlockSpec(u.shape, lambda g: (0, 0, 0))
    tail = pl.BlockSpec(dy.shape, lambda g: (0, 0, 0))
    out = jax.ShapeDtypeStruct(a.shape, f32)
    return pl.pallas_call(
        back_kernel,
        grid=(NST // GROUP,),
        out_shape=(jax.ShapeDtypeStruct(u.shape, f32),) + (out,) * 4,
        in_specs=[rows, tail] + [states] * 7,
        out_specs=(rows,) + (states,) * 4,
        scratch_shapes=[pltpu.VMEM((u.shape[0] + 1, GROUP) + tile, f32)],
        compiler_params=SMALL,
        name="ssm_back",
    )(u, dy, a, gin, gout, state_in, lam_end, da0, dgout0)


def dot_nt(x, y):
    return lax.dot_general(x, y, (((1,), (1,)), ((), ())), preferred_element_type=f32)


def dot_nn(x, y):
    return jnp.dot(x, y, preferred_element_type=f32)


def dot_tn(x, y):
    return lax.dot_general(x, y, (((0,), (0,)), ((), ())), preferred_element_type=f32)


def softmax_parts(q, keys):
    rows = q.shape[0]
    scores = [dot_nt(q, k) * (1.0 / math.sqrt(HD)) for k in keys]
    at = lax.broadcasted_iota(jnp.int32, (rows, rows), 0)
    to = lax.broadcasted_iota(jnp.int32, (rows, rows), 1)
    scores[-1] = jnp.where(to <= at, scores[-1], far_below)
    top = functools.reduce(jnp.maximum, [jnp.max(s, axis=-1, keepdims=True) for s in scores])
    es = [jnp.exp(s - top) for s in scores]
    total = functools.reduce(jnp.add, [jnp.sum(e, axis=-1, keepdims=True) for e in es])
    return [e / total for e in es]


def attend_kernel(half_ref, q0, q1, k0, k1, v0, v1, kc, vc, out_ref):
    w, h = pl.program_id(0), pl.program_id(1)
    rows = q0.shape[0]
    for half, q, keys, values in ((0, q0, (kc, k0), (vc, v0)), (1, q1, (kc, k0, k1), (vc, v0, v1))):
        probs = softmax_parts(q[...], [k[...] for k in keys])
        out = [dot_nn(p.astype(bf16), v[...]) for p, v in zip(probs, values)]
        at = pl.multiple_of(((half ^ half_ref[0]) * 2 + w) * rows, 16)
        col = pl.multiple_of(h * HD, LANES)
        out_ref[pl.ds(at, rows), pl.ds(col, HD)] = functools.reduce(jnp.add, out).astype(bf16)


def attend_back_kernel(
    half_ref, q0, q1, k0, k1, v0, v1, kc, vc, do0, do1, dqkv_ref, dctx_ref
):
    w, h = pl.program_id(0), pl.program_id(1)
    rows, heads = q0.shape[0], pl.num_programs(1)
    scale = 1.0 / math.sqrt(HD)
    dk, dv = [0.0, 0.0, 0.0], [0.0, 0.0, 0.0]

    def row_of(half):
        return pl.multiple_of(((half ^ half_ref[0]) * 2 + w) * rows, 16)

    def col_of(part):
        return pl.multiple_of((part * heads + h) * HD, LANES)

    cases = ((0, q0, do0, (kc, k0), (vc, v0)), (1, q1, do1, (kc, k0, k1), (vc, v0, v1)))
    for half, q, do, keys, values in cases:
        query, d_out = q[...], do[...]
        probs = softmax_parts(query, [k[...] for k in keys])
        d_probs = [dot_nt(d_out, v[...]) for v in values]
        sums = [jnp.sum(p * d, axis=-1, keepdims=True) for p, d in zip(probs, d_probs)]
        delta = functools.reduce(jnp.add, sums)
        d_scores = [(p * (d - delta)).astype(bf16) for p, d in zip(probs, d_probs)]
        dq = functools.reduce(jnp.add, [dot_nn(d, k[...]) for d, k in zip(d_scores, keys)])
        dqkv_ref[pl.ds(row_of(half), rows), pl.ds(col_of(0), HD)] = (dq * scale).astype(bf16)
        for n, (d, p) in enumerate(zip(d_scores, probs)):
            dk[n] = dk[n] + dot_tn(d, query)
            dv[n] = dv[n] + dot_tn(p.astype(bf16), d_out)
    ctx_row = pl.multiple_of(w * CTX, 16)
    dctx_ref[pl.ds(ctx_row, CTX), pl.ds(col_of(0), HD)] = (dk[0] * scale).astype(bf16)
    dctx_ref[pl.ds(ctx_row, CTX), pl.ds(col_of(1), HD)] = dv[0].astype(bf16)
    for half in (0, 1):
        dqkv_ref[pl.ds(row_of(half), rows), pl.ds(col_of(1), HD)] = (dk[1 + half] * scale).astype(bf16)
        dqkv_ref[pl.ds(row_of(half), rows), pl.ds(col_of(2), HD)] = dv[1 + half].astype(bf16)


def attention_specs(rows, heads):
    def at(half, part):
        return pl.BlockSpec((rows, HD), lambda w, h, s: ((half ^ s[0]) * 2 + w, part * heads + h))

    def ctx(part):
        return pl.BlockSpec((CTX, HD), lambda w, h, s: (w, part * heads + h))

    return [at(half, part) for part in range(3) for half in (0, 1)] + [ctx(0), ctx(1)]


def whole_block(shape):
    return pl.BlockSpec(shape, lambda w, h, s: (0, 0))


def attend(half, qkv, ctx_kv):
    rows, heads = qkv.shape[0] // TEAM, qkv.shape[1] // (3 * HD)
    out = (qkv.shape[0], heads * HD)
    return pl.pallas_call(
        attend_kernel,
        grid_spec=pltpu.PrefetchScalarGridSpec(
            num_scalar_prefetch=1,
            grid=(2, heads),
            in_specs=attention_specs(rows, heads),
            out_specs=whole_block(out),
        ),
        out_shape=jax.ShapeDtypeStruct(out, bf16),
        compiler_params=SMALL,
        name="attend",
    )(half, *[qkv] * 6, ctx_kv, ctx_kv)


def attend_back(half, qkv, ctx_kv, d_attended):
    rows, heads = qkv.shape[0] // TEAM, qkv.shape[1] // (3 * HD)

    def at(side):
        return pl.BlockSpec((rows, HD), lambda w, h, s: ((side ^ s[0]) * 2 + w, h))

    return pl.pallas_call(
        attend_back_kernel,
        grid_spec=pltpu.PrefetchScalarGridSpec(
            num_scalar_prefetch=1,
            grid=(2, heads),
            in_specs=attention_specs(rows, heads) + [at(0), at(1)],
            out_specs=[whole_block(qkv.shape), whole_block(ctx_kv.shape)],
        ),
        out_shape=[jax.ShapeDtypeStruct(qkv.shape, bf16), jax.ShapeDtypeStruct(ctx_kv.shape, bf16)],
        compiler_params=SMALL,
        name="attend_back",
    )(half, *[qkv] * 6, ctx_kv, ctx_kv, d_attended, d_attended)


def pack_kernel(rate, gin, gout, g_one, g_two, out):
    for k, ref in enumerate((rate, gin, gout)):
        out[0, k * NST : (k + 1) * NST, :] = ref[...]
    out[0, 3 * NST : 3 * NST + 1, :] = g_one[...]
    out[0, 3 * NST + 1 : 3 * NST + 2, :] = g_two[...]


def norm_kernel(idx, gain, x0, x1, x2, x3, low_ref, inv_ref, u_ref):
    rows, dim = x0.shape
    cols = dim // TEAM
    for r, ref in enumerate((x0, x1, x2, x3)):
        x = ref[...].astype(f32)
        inv = lax.rsqrt(jnp.mean(x * x, axis=-1, keepdims=True) + epsilon)
        inv_ref[r * rows : (r + 1) * rows, :] = inv
        low_ref[r * rows : (r + 1) * rows, :] = (x * inv * gain[...]).astype(bf16)
        for c in range(cols // LANES):
            at = pl.multiple_of(idx[0] * cols + c * LANES, LANES)
            u = low_ref[r * rows : (r + 1) * rows, pl.ds(at, LANES)].astype(f32)
            u_ref[:, r * (cols // LANES) + c, :] = u


def first_norm(idx, gain, blocks):
    rows, dim = blocks[0].shape
    shapes = (
        jax.ShapeDtypeStruct((TEAM * rows, dim), bf16),
        jax.ShapeDtypeStruct((TEAM * rows, 1), f32),
        jax.ShapeDtypeStruct((rows, dim // LANES, LANES), f32),
    )
    return call(norm_kernel, "first_norm", shapes, (idx, gain[None], *blocks))


def part_types(rows, dim):
    return tuple(jax.ShapeDtypeStruct((rows, dim), (f32, bf16)[r % 2]) for r in range(TEAM))


def dot_kernel(x_ref, w_ref, *parts):
    rows = parts[0].shape[0]
    for r in (3, 1, 2, 0):
        part = dot_nn(x_ref[r * rows : (r + 1) * rows, :], w_ref[...])
        parts[r][...] = part.astype(parts[r].dtype)


def dot_parts(name, x, w):
    return call(dot_kernel, name, part_types(x.shape[0] // TEAM, w.shape[1]), (x, w), 0)


def out_kernel(idx, x_ref, w0, w1, w2, w3, *parts):
    rows, cols = parts[0].shape[0], w0.shape[1]
    for r in (3, 1, 2, 0):
        for q, w in enumerate((w0, w1, w2, w3)):
            at = pl.multiple_of((idx[0] ^ q) * cols, LANES)
            part = dot_nn(x_ref[r * rows : (r + 1) * rows, :], w[...])
            parts[r][:, pl.ds(at, cols)] = part.astype(parts[r].dtype)


def context_kv_kernel(idx, w_ref, c0, c1, c2, c3, kv_ref, context_ref):
    cols = c0.shape[1]
    width = w_ref.shape[1] // 3
    for r, part in enumerate((c0, c1, c2, c3)):
        at = pl.multiple_of((idx[0] ^ r) * cols, LANES)
        for w in (0, 1):
            v = w ^ (r & 1)
            context_ref[w * CTX : (w + 1) * CTX, pl.ds(at, cols)] = part[v * CTX : (v + 1) * CTX, :]
    kv_ref[...] = dot_nn(context_ref[...], w_ref[:, width:]).astype(bf16)


def mlp_kernel(m0, m1, m2, m3, g0, g1, g2, g3, up, down, act_ref, dpre_ref, *parts_and_sum):
    parts, total = parts_and_sum[:-1], parts_and_sum[-1]
    k = pl.program_id(0)
    rows = m0.shape[0]
    c = math.sqrt(2.0 / math.pi)
    for r, (m, g) in enumerate(((m0, g0), (m1, g1), (m2, g2), (m3, g3))):
        at = slice(r * rows, (r + 1) * rows)
        x = dot_nn(m[...], up[...])
        t = jnp.tanh(c * (x + 0.044715 * (x * x * x)))
        cdf = 0.5 * (1.0 + t)
        act_ref[at, :] = (x * cdf).astype(bf16)
        slope = cdf + (0.5 * c) * x * (1.0 - t * t) * (1.0 + (3 * 0.044715) * (x * x))
        d_pre = (dot_nt(g[...], down[...]) * slope).astype(bf16)
        dpre_ref[at, :] = d_pre
        new = dot_nt(d_pre, up[...])
        total[at, :] = jnp.where(k == 0, new, total[at, :] + new)

    @pl.when(k == pl.num_programs(0) - 1)
    def _():
        for r, part in enumerate(parts):
            part[...] = total[r * rows : (r + 1) * rows, :].astype(part.dtype)


def feed_forward(mlp_blocks, grad_blocks, up, down):
    rows, dim = mlp_blocks[0].shape
    units = up.shape[1]
    step = 256

    unit_out = jax.ShapeDtypeStruct((TEAM * rows, units), bf16)
    return pl.pallas_call(
        mlp_kernel,
        grid=(units // step,),
        out_shape=(unit_out, unit_out) + part_types(rows, dim),
        in_specs=[block_of((rows, dim))] * 8
        + [pl.BlockSpec((dim, step), lambda k: (0, k)), pl.BlockSpec((step, dim), lambda k: (k, 0))],
        out_specs=(pl.BlockSpec((TEAM * rows, step), lambda k: (0, k)),) * 2
        + (block_of((rows, dim)),) * TEAM,
        scratch_shapes=[pltpu.VMEM((TEAM * rows, dim), f32)],
        compiler_params=MIDDLE,
        name="feed_forward",
    )(*mlp_blocks, *grad_blocks, up, down)


def mlp_grad_kernel(x_ref, y0, y1, y2, y3, out):
    rows = y0.shape[0]
    grads = [dot_tn(x_ref[r * rows : (r + 1) * rows, :], y[...]) for r, y in enumerate((y0, y1, y2, y3))]
    out[...] = functools.reduce(jnp.add, grads).astype(bf16)


def down_grad(act, grad_blocks):
    rows, dim = grad_blocks[0].shape
    step = 256
    return pl.pallas_call(
        mlp_grad_kernel,
        grid=(act.shape[1] // step,),
        out_shape=jax.ShapeDtypeStruct((act.shape[1], dim), bf16),
        in_specs=[pl.BlockSpec((act.shape[0], step), lambda k: (0, k))]
        + [block_of((rows, dim))] * TEAM,
        out_specs=pl.BlockSpec((step, dim), lambda k: (k, 0)),
        compiler_params=SMALL,
        name="down_grad",
    )(act, *grad_blocks)


def up_grad_kernel(x0, x1, x2, x3, y_ref, out):
    rows = x0.shape[0]
    grads = [dot_tn(x[...], y_ref[r * rows : (r + 1) * rows, :]) for r, x in enumerate((x0, x1, x2, x3))]
    out[...] = functools.reduce(jnp.add, grads).astype(bf16)


def up_grad(mlp_blocks, d_pre):
    rows, dim = mlp_blocks[0].shape
    step = 256
    return pl.pallas_call(
        up_grad_kernel,
        grid=(dim // step,),
        out_shape=jax.ShapeDtypeStruct((dim, d_pre.shape[1]), bf16),
        in_specs=[pl.BlockSpec((rows, step), lambda k: (0, k))] * TEAM
        + [block_of(d_pre.shape)],
        out_specs=pl.BlockSpec((step, d_pre.shape[1]), lambda k: (k, 0)),
        compiler_params=SMALL,
        name="up_grad",
    )(*mlp_blocks, d_pre)


def attended_grad_kernel(idx, w0, w1, w2, w3, h0, h1, h2, h3, out):
    rows, cols = h0.shape[0], w0.shape[1]
    for r, h in enumerate((h0, h1, h2, h3)):
        grad = 0.0
        for q, w in enumerate((w0, w1, w2, w3)):
            at = pl.multiple_of((idx[0] ^ q) * cols, LANES)
            grad = grad + dot_nt(h[:, pl.ds(at, cols)], w[...])
        out[r * rows : (r + 1) * rows, :] = grad.astype(bf16)


def out_grad_kernel(idx, att_ref, h0, h1, h2, h3, *parts):
    rows, cols = h0.shape[0], parts[0].shape[1]
    for q, part in enumerate(parts):
        at = pl.multiple_of((idx[0] ^ q) * cols, LANES)
        grads = [
            dot_tn(att_ref[r * rows : (r + 1) * rows, :], h[:, pl.ds(at, cols)])
            for r, h in enumerate((h0, h1, h2, h3))
        ]
        part[...] = functools.reduce(jnp.add, grads).astype(bf16)


def context_grad_kernel(idx, d_ref, w_ref, *parts):
    cols = parts[0].shape[1]
    width = w_ref.shape[1] // 3
    for r, part in enumerate(parts):
        at = pl.multiple_of((idx[0] ^ r) * cols, 16)
        for w in (0, 1):
            v = w ^ (r & 1)
            grad = dot_nt(d_ref[w * CTX : (w + 1) * CTX, :], w_ref[pl.ds(at, cols), width:])
            part[v * CTX : (v + 1) * CTX, :] = grad.astype(part.dtype)


def inputs_grad_kernel(idx, dq_ref, w_ref, du_ref, inv_ref, x0, x1, x2, x3, *outs):
    parts, gain_ref, work = outs[:TEAM], outs[TEAM], outs[TEAM + 1]
    rows, dim = x0.shape
    cols = dim // TEAM
    gain = 0.0
    for r, x in enumerate((x0, x1, x2, x3)):
        at = slice(r * rows, (r + 1) * rows)
        work[...] = dot_nt(dq_ref[at, :], w_ref[...])
        for c in range(cols // LANES):
            col = pl.ds(pl.multiple_of(idx[0] * cols + c * LANES, LANES), LANES)
            work[:, col] = work[:, col] + du_ref[:, r * (cols // LANES) + c, :]
        grad = work[...]
        parts[r][...] = grad.astype(parts[r].dtype)
        gain = gain + jnp.sum(grad * (x[...].astype(f32) * inv_ref[at, :]), axis=0, keepdims=True)
    gain_ref[...] = gain


def cut_states_kernel(idx, init_ref, ends_ref, i0, i1, e0, e1, e2, e3):
    cols = i0.shape[1]
    for r, out in enumerate((e0, e1, e2, e3)):
        at = pl.multiple_of((idx[0] ^ r) * cols, LANES)
        out[...] = ends_ref[:, pl.ds(at, cols)]
        if r < 2:
            (i0, i1)[r][...] = init_ref[:, pl.ds(at, cols)]


def join_states_kernel(late, i0, i1, e0, e1, e2, e3, init_ref, twice_ref, first_ref, second_ref):
    per = init_ref.shape[1] // 2
    for w in range(2):
        for c in range(per):
            at = slice(c * LANES, (c + 1) * LANES)
            init = (i0, i1)[w][:, at]
            init_ref[:, w * per + c, :] = init
            twice_ref[:, w * per + c, :] = init
            twice_ref[:, (2 + w) * per + c, :] = init
            own, other = (e0, e1)[w][:, at], (e2, e3)[w][:, at]
            first_ref[:, w * per + c, :] = jnp.where(late[0] == 1, other, own)
            second_ref[:, w * per + c, :] = jnp.where(late[0] == 1, own, other)


def cut_ends_kernel(late, first_ref, second_ref, e0, e1, e2, e3):
    per = first_ref.shape[1] // 2
    for w in range(2):
        for c in range(per):
            at = slice(c * LANES, (c + 1) * LANES)
            one, two = first_ref[:, w * per + c, :], second_ref[:, w * per + c, :]
            (e0, e1)[w][:, at] = jnp.where(late[0] == 1, two, one)
            (e2, e3)[w][:, at] = jnp.where(late[0] == 1, one, two)


def join_ends_kernel(idx, e0, e1, e2, e3, out):
    cols = e0.shape[1]
    for r, part in enumerate((e0, e1, e2, e3)):
        at = pl.multiple_of((idx[0] ^ r) * cols, LANES)
        out[:, pl.ds(at, cols)] = part[...]


def small_kernel(spots, p0, p1, p2, p3, gains_ref, rate_ref, in_ref, out_ref, init_ref):
    packs = [p[...] for p in (p0, p1, p2, p3)]
    tiles = packs[0].shape[0] - 3 * NST * 2 - NST * 4
    one, two = 3 * NST * 2, 3 * NST * 2 + tiles
    gains = functools.reduce(jnp.add, [p[one:two] for p in packs])
    row = lax.broadcasted_iota(jnp.int32, gains.shape, 0)
    for k in (0, 1):
        mine = row == k * (tiles // 2) + spots[1]
        gains_ref[k : k + 1, :] = jnp.sum(jnp.where(mine, gains, 0.0), axis=0, keepdims=True)
    chosen = packs[0]
    for r in (1, 2, 3):
        chosen = jnp.where(spots[0] == r, packs[r], chosen)
    side = spots[1] % 2 == 1
    params = chosen[:one].reshape(3 * NST, 2, LANES)
    params = jnp.where(side, params[:, 1], params[:, 0])
    for k, ref in enumerate((rate_ref, in_ref, out_ref)):
        ref[...] = params[k * NST : (k + 1) * NST]
    init = chosen[two:].reshape(NST, 4, LANES)
    window = [jnp.where(side, init[:, 2 * w + 1], init[:, 2 * w]) for w in (0, 1)]
    init_ref[...] = jnp.where(spots[0] % 2 == 1, window[1], window[0])


def added(p0, one, far):
    return p0[...] + one[...].astype(f32) + far[...].astype(f32)


def second_norm_kernel(tok, p0, one, far, gain, hidden_ref, inv_ref, low_ref):
    hidden = tok[...].astype(f32) + added(p0, one, far)
    inv = lax.rsqrt(jnp.mean(hidden * hidden, axis=-1, keepdims=True) + epsilon)
    hidden_ref[...] = hidden
    inv_ref[...] = inv
    low_ref[...] = (hidden * inv * gain[...]).astype(bf16)


def result_kernel(hidden, p0, one, far, out):
    out[...] = (hidden[...] + added(p0, one, far)).astype(bf16)


def norm_back(grad, normed, inv, gain):
    scaled = grad * gain
    return inv * (scaled - normed * jnp.mean(scaled * normed, axis=-1, keepdims=True))


def hidden_grad_kernel(cot, hidden, inv, gain, p0, one, far, out_ref, low_ref, gain_ref):
    grad = added(p0, one, far)
    normed = hidden[...] * inv[...]
    gain_ref[...] = jnp.sum(grad * normed, axis=0, keepdims=True)
    out = cot[...].astype(f32) + norm_back(grad, normed, inv[...], gain[...])
    out_ref[...] = out
    low_ref[...] = out.astype(bf16)


def tokens_grad_kernel(d_hidden, tok, inv, gain, p0, one, far, out):
    grad = added(p0, one, far)
    normed = tok[...].astype(f32) * inv[...]
    out[...] = (d_hidden[...] + norm_back(grad, normed, inv[...], gain[...])).astype(bf16)


def context_sum_kernel(p0, one, far, out):
    out[...] = added(p0, one, far).astype(bf16)


def context_rows_kernel(flags, came, own, dy_ref, dy_full, dy0_full):
    per = dy_ref.shape[1] // 2
    zero = jnp.zeros((CTX, LANES), f32)
    for w in range(2):
        for c in range(per):
            at = (slice(w * CTX, (w + 1) * CTX), slice(c * LANES, (c + 1) * LANES))
            dy = came[at].astype(f32)
            dy_ref[:, w * per + c, :] = dy
            dy_full[:, w * per + c, :] = jnp.where(flags[0] == 1, dy, zero)
            dy_full[:, (2 + w) * per + c, :] = jnp.where(flags[0] == 1, zero, dy)
            dy0_full[:, w * per + c, :] = jnp.where(flags[1] == 0, own[at].astype(f32), zero)
            dy0_full[:, (2 + w) * per + c, :] = zero


def on_device(
    tokens,
    w_qkv,
    w_out,
    w_up,
    w_down,
    g_attn,
    g_mlp,
    ssm_rate,
    ssm_in,
    ssm_out,
    h_init,
    cotangent,
    d_h_ends,
):
    nd, ns = lax.axis_size("dp"), lax.axis_size("seq")
    ny = nd // 2
    dp, seq = lax.axis_index("dp"), lax.axis_index("seq")
    late = seq % 2 == 1
    block = seq // 2
    me = (seq % 2) * 2 + dp % 2
    idx = jnp.stack([me, dp // 2]).astype(jnp.int32)
    place = (seq * ny + dp // 2).astype(jnp.int32).reshape(1)
    half = (seq % 2).astype(jnp.int32).reshape(1)
    rows, dim = tokens.shape[1:]
    shard = w_qkv.shape[0]
    width = HEADS * HD // TEAM
    cols = dim // TEAM
    fb = w_down.shape[0] // TEAM
    tile = (dim // LANES, LANES)
    half_tile = (dim // LANES // 2, LANES)

    def like(shape, dtype):
        return jax.ShapeDtypeStruct(shape, dtype)


    share_attn, share_up, *share_down = shares(idx, w_qkv, w_out, w_up, w_down, ny, ns)
    attn, up = Gathering(*share_attn, True), Gathering(*share_up, True)
    down = [Gathering(*share, False) for share in share_down]
    attn_pair = attn.step()
    x_blocks = gather_team(after(tokens[0], attn_pair))
    up.step(attn_pair)
    attn_first = attn.rest()
    for part in down:
        part.step(attn_first)
    attn_second = attn.step()
    attn_third = attn.across(0)
    attn_last = attn.across(1)
    small = call(
        pack_kernel,
        "pack_small",
        jax.ShapeDtypeStruct((1, 3 * NST + 2, shard), bf16),
        after((ssm_rate.T, ssm_in.T, ssm_out.T, g_attn[None], g_mlp[None]), share_attn[1]),
        0,
    )
    for bit in [1] + high_bits("seq")[::-1]:
        got = swap(small, "seq", bit)
        upper = (seq & bit) != 0
        small = jnp.concatenate([jnp.where(upper, got, small), jnp.where(upper, small, got)], axis=0)
    small = small.astype(f32)
    gain_one = small[:, 3 * NST].reshape(dim)
    gain_two = small[:, 3 * NST + 1].reshape(dim)
    params = small[:, : 3 * NST].transpose(1, 0, 2).reshape(3 * NST, dim)
    params = lax.dynamic_slice_in_dim(params, me * cols, cols, 1)
    params = jnp.broadcast_to(params[:, None], (3 * NST, TEAM, cols)).reshape((3, NST) + tile)
    rate, gin, gout = params[0], params[1], params[2]
    half_rate = rate[:, : tile[0] // 2]

    by_channel = like((NST, cols), f32)
    init, near_init, *end_cot = call(
        cut_states_kernel,
        "cut_states",
        (by_channel,) * 6,
        (idx, h_init[0].T, after(d_h_ends[0, 0].T, share_attn[1])),
    )
    init, init_twice, end_first, end_second = call(
        join_states_kernel,
        "join_states",
        tuple(like((NST,) + t, f32) for t in (half_tile, tile, half_tile, half_tile)),
        (half, init, swap_team(near_init, 1), *trade_team(end_cot)),
    )
    end_cot = [end_first, end_second]
    g_blocks = gather_team(after(cotangent[0], attn_first))

    def by_half(a, axis=1):
        n = a.shape[axis] // 2
        own, other = lax.slice_in_dim(a, 0, n, axis=axis), lax.slice_in_dim(a, n, 2 * n, axis=axis)
        return ordered([own, other], seq % 2)

    def by_owner(first, second):
        return jnp.concatenate(ordered([first, second], seq % 2), axis=1)

    inputs_low, inv_one, u = first_norm(idx, after(gain_one, attn_first), x_blocks)

    a = jnp.exp(-rate)
    s_mid, s_end = local_ends(u, a)
    up_first = up.rest((attn_second, s_end))
    decay = jnp.exp(-half_rate * rows)
    first_end, second_end = by_half(gin * s_end)
    span = 2 * rows

    def chain(inclusive, back, wait):
        exclusive, step = jnp.zeros_like(inclusive), 1
        while step < ns // 2:
            pairs = [(k, k + 2 * step) for k in range(ns - 2 * step)]
            got = lax.ppermute(inclusive, "seq", [(t, f) for f, t in pairs] if back else pairs)
            if step == 1:
                got = after(got, wait)
            exclusive = exclusive + jnp.exp(-half_rate * (span * (step - 1))) * got
            inclusive = inclusive + jnp.exp(-half_rate * (span * step)) * got
            step *= 2
        return exclusive

    entering = chain(after(decay * first_end + second_end, attn_third), False, up_first)
    state_zero = jnp.exp(-half_rate * (span * block).astype(f32)) * init + entering
    state_one = decay * state_zero + first_end
    state_two = decay * state_one + second_end
    state_in = by_owner(state_zero, state_one)
    ends = call(cut_ends_kernel, "cut_ends", (by_channel,) * TEAM, (half, state_one, state_two))
    ends = call(join_ends_kernel, "join_ends", like((NST, dim), f32), (idx, *trade_team(ends)))
    on_second = by_owner(jnp.zeros_like(init), jnp.ones_like(init))
    h_mid = jnp.exp(-rate * (rows - CTX)) * state_in + gin * s_mid
    h_mid = jnp.where(on_second > 0, h_mid, init_twice)
    h_mid = after(h_mid, (attn_second, attn_last))
    y_first, y_second = contexts(half, u, a, gin * on_second, gout, h_mid)
    passed = lax.ppermute(y_second, "seq", [(k, k + 2) for k in range(ns - 2)])
    up_second = up.step(entering)
    up_third = up.across(0)
    context = jnp.where(block == 0, y_first, after(passed, up_second))
    down_first = down[0].rest(passed)
    down_second = down[1].rest(up_third)
    context = gather_team(context)

    places = jnp.stack([place[0], seq]).astype(jnp.int32)
    full_qkv, *full_out = place_weight(idx, places, [(attn.pieces, 0, 1, 0)], 3 * width)
    full_qkv = after(full_qkv, (down_first, up_third))
    full_out = trade_team(full_out)
    qkv = dot_nn(inputs_low, full_qkv).astype(bf16)
    ctx_kv, context = call(
        context_kv_kernel,
        "context_kv",
        (like((2 * CTX, 2 * width), bf16), like((2 * CTX, dim), bf16)),
        (idx, full_qkv, *context),
    )
    attended = attend(half, qkv, ctx_kv)

    down_third = down[0].step(down_second)
    up_last = up.across(1, up_third)
    attended = after(attended, (g_blocks[2], down_second))
    attended_parts = call(out_kernel, "out_dot", part_types(rows, dim), (idx, attended, *full_out))
    attended_parts = sum_team(attended_parts, None, (ends, down_third, up_last))
    down[1].step(down_third)
    (full_up,) = place_weight(idx, places, [(up.pieces, 0, 1, 0)])
    down = [(part.pieces, 1, 2, h) for h, part in enumerate(down)]
    (full_down,) = place_weight(idx, places, down)

    hidden, inv_two, mlp_in = call(
        second_norm_kernel,
        "second_norm",
        (like((rows, dim), f32), like((rows, 1), f32), like((rows, dim), bf16)),
        (tokens[0], *attended_parts[:3], gain_two[None]),
        0,
    )
    mlp_in = gather_team(mlp_in)
    act, d_pre, *d_mlp = feed_forward(mlp_in, g_blocks, full_up, full_down)
    d_down = down_grad(act, g_blocks)
    reduction = HalvedReduction if (nd, ns) == (4, 8) else Reduction
    sum_down = reduction(d_down, place)
    sum_down.step()
    d_up = up_grad(mlp_in, after(d_pre, sum_down.sent))
    sum_up = reduction(d_up, place)
    sum_up.step()
    result = dot_parts("down_dot", after(act, sum_up.sent), full_down)
    d_mlp = sum_team(d_mlp, d_down, result)
    sum_down.step(d_mlp[3])
    d_hidden, d_hidden_low, d_gain_two = call(
        hidden_grad_kernel,
        "hidden_grad",
        (like((rows, dim), f32), like((rows, dim), bf16), like((1, dim), f32)),
        (after(cotangent[0], sum_down.sent), hidden, inv_two, gain_two[None], *d_mlp[:3]),
        0,
    )
    hidden_blocks = gather_team(d_hidden_low)
    sum_down.step(d_hidden)

    d_attended = call(
        attended_grad_kernel,
        "attended_grad",
        jax.ShapeDtypeStruct(attended.shape, bf16),
        (idx, after(full_out[0], sum_down.sent), *full_out[1:], *hidden_blocks),
    )
    d_out = call(
        out_grad_kernel,
        "out_grad",
        (jax.ShapeDtypeStruct((width, cols), bf16),) * TEAM,
        (idx, after(attended, d_attended), *hidden_blocks),
    )
    d_qkv, d_ctx_kv = attend_back(half, qkv, ctx_kv, after(d_attended, d_out))
    d_out = trade_team(d_out)
    sum_up.step(d_ctx_kv)
    d_context = call(
        context_grad_kernel,
        "context_grad",
        part_types(2 * CTX, cols),
        (idx, after(d_ctx_kv, sum_up.sent), full_qkv),
    )
    d_attn = attn_grad(idx, inputs_low, after(d_qkv, d_context), context, d_ctx_kv, d_out)
    sum_attn = reduction(d_attn, place)
    sum_attn.step()
    d_context = sum_team(d_context, None, sum_attn.sent)
    d_context = call(context_sum_kernel, "context_sum", like((2 * CTX, cols), bf16), d_context[:3], 0)
    came = lax.ppermute(d_context, "seq", [(k + 2, k) for k in range(ns - 2)])
    flags = jnp.stack([seq % 2, block]).astype(jnp.int32)
    dy, dy_full, dy0_full = call(
        context_rows_kernel,
        "context_rows",
        (like((CTX,) + half_tile, f32), like((CTX,) + tile, f32), like((CTX,) + tile, f32)),
        (flags, came, d_context),
    )

    lam_mid = tail_adjoint(dy, a, gout)
    g_second = jnp.exp(-half_rate * (rows - CTX + 1)) * lam_mid + decay * end_cot[1]
    d_a, d_gout, g_init = first_context_back(after(dy0_full, lam_mid), a, gout, init_twice)
    leaving = chain(decay * (end_cot[0] + g_second), True, (g_init, sum_attn.out if reduction is HalvedReduction else g_init))
    sum_up.step(leaving)
    sum_attn.step(sum_up.sent)
    sum_down.step(sum_attn.sent)
    result = sum_team(result, d_context)
    result = call(result_kernel, "result_sum", like((rows, dim), bf16), (hidden, *result[:3]), 0)
    lam_end = by_owner(end_cot[0] + g_second + decay * leaving, end_cot[1] + leaving)
    du, d_gin, d_a, d_gout, g_in = ssm_back(
        u, dy_full, a, gin, gout, state_in, after(lam_end, sum_down.sent), d_a, d_gout
    )
    g_first = by_half(g_in)[0]
    d_init = g_init[:, : tile[0] // 2] + jnp.where(block == 0, g_first, jnp.zeros_like(g_first))
    d_rate = -a * d_a

    *d_inputs, d_gain_one = call(
        inputs_grad_kernel,
        "inputs_grad",
        part_types(rows, dim) + (jax.ShapeDtypeStruct((1, dim), f32),),
        (idx, d_qkv, full_qkv, after(du, result), inv_one, *x_blocks),
        scratch_shapes=[pltpu.VMEM((rows, dim), f32)],
    )
    *d_inputs, d_inputs_far = sum_team(d_inputs)
    sum_up.step(d_inputs_far)
    sum_attn.step(sum_up.sent)
    d_down = spread_weight("down", sum_down.last(), idx, [w_down.shape])[0]
    d_tokens = call(
        tokens_grad_kernel,
        "tokens_grad",
        like((rows, dim), bf16),
        (d_hidden, tokens[0], inv_one[:rows], gain_one[None], *d_inputs),
        0,
    )

    d_params = after(jnp.stack([d_rate, d_gin, d_gout]), d_gain_one)
    d_params = d_params.reshape(3 * NST, TEAM, cols).sum(1)
    d_gains = jnp.concatenate([d_gain_one[0], d_gain_two[0]])
    pack = [d_params.reshape(-1, LANES), d_gains.reshape(-1, LANES), d_init.reshape(-1, LANES)]
    pack = after(jnp.concatenate(pack, axis=0), d_inputs_far)
    for n, bit in enumerate(high_bits("seq")):
        if n == 1:
            pack = after(pack, sum_attn.step())
        pack = pack + swap(pack, "seq", bit)
    one, two = 3 * NST * cols // LANES, 3 * NST * cols // LANES + 2 * dim // LANES
    shared = pack[:two]
    shared = after(shared, d_down)
    for bit in high_bits("dp"):
        shared = shared + swap(shared, "dp", bit)
    packs = gather_team(jnp.concatenate([shared, pack[two:]], axis=0))
    if shard == LANES:
        spots = jnp.stack([me ^ (seq * shard // cols), seq]).astype(jnp.int32)
        gains, *d_params, state_grad = call(
            small_kernel,
            "small_grads",
            (like((2, shard), f32),) + (like((NST, shard), f32),) * 4,
            (spots, *packs),
        )
        d_params, state_grad = [p.T for p in d_params], state_grad.T[None]
    else:
        packs = jnp.stack(packs)
        gains = packs[:, one:two].sum(0).reshape(2, ns, shard)
        gains = pick(gains, seq, 1)
        member = me ^ (seq * shard // cols)
        inner = seq * shard % cols
        chosen = pick(packs, member)
        d_params = chosen[:one].reshape(3 * NST, cols)
        d_params = lax.dynamic_slice_in_dim(d_params, inner, shard, 1).reshape(3, NST, shard)
        d_params = d_params.transpose(0, 2, 1)
        state_grad = chosen[two:].reshape(NST, 2, cols)
        state_grad = pick(state_grad, member % 2, 1)
        state_grad = lax.dynamic_slice_in_dim(state_grad, inner, shard, 1).T[None]

    if fb % LANES:
        d_up = spread_narrow(sum_up.last(), idx, w_up.shape, fb)
    else:
        d_up = spread_weight("up", sum_up.last(), idx, [w_up.shape], fb)[0]
    d_wqkv, d_out = spread_weight("attn", sum_attn.last(), idx, [w_qkv.shape, w_out.shape])
    return (
        result[None],
        d_tokens[None],
        d_wqkv,
        d_out,
        d_up,
        d_down,
        gains[0],
        gains[1],
        d_params[0],
        d_params[1],
        d_params[2],
        state_grad,
        ends.T[None, None],
    )


def solution(mesh):
    return jax.shard_map(
        on_device,
        mesh=mesh,
        in_specs=(
            P("dp", "seq", None),
            P("seq", None),
            P("seq", None),
            P("seq", None),
            P("seq", None),
            P("seq"),
            P("seq"),
            P("seq", None),
            P("seq", None),
            P("seq", None),
            P("dp", None, None),
            P("dp", "seq", None),
            P("dp", "seq", None, None),
        ),
        out_specs=(
            P("dp", "seq", None),
            P("dp", "seq", None),
            P("seq", None),
            P("seq", None),
            P("seq", None),
            P("seq", None),
            P("seq"),
            P("seq"),
            P("seq", None),
            P("seq", None),
            P("seq", None),
            P("dp", "seq", None),
            P("dp", "seq", None, None),
        ),
        check_vma=False,
    )
```

```python
import functools
import math

import jax
import jax.numpy as jnp
from jax import lax
from jax.experimental import pallas as pl
from jax.experimental.pallas import tpu as pltpu
from jax.sharding import PartitionSpec as P

HEADS = 8
HD = 128
CTX = 128
NST = 16
LANES = 128
GROUP = 4
TEAM = 4

epsilon = 1e-05
far_below = -1e30
bf16 = jnp.bfloat16
f32 = jnp.float32


def swap(a, axis, bit):
    return lax.ppermute(a, axis, [(k, k ^ bit) for k in range(lax.axis_size(axis))])


def swap_team(a, r):
    if r == 1:
        return swap(a, "dp", 1)
    if r == 2:
        return swap(a, "seq", 1)
    nd, ns = lax.axis_size("dp"), lax.axis_size("seq")
    pairs = [(d * ns + k, (d ^ 1) * ns + (k ^ 1)) for d in range(nd) for k in range(ns)]
    return lax.ppermute(a, ("dp", "seq"), pairs)


def gather_team(a):
    far = swap_team(a, 2)
    return [a, swap_team(a, 1), far, swap_team(far, 1)]


def far_kernel(mine, came, out):
    out[...] = (mine[...] + came[...].astype(f32)).astype(bf16)


def sum_team(parts, middle=None, end=None):
    one, three = swap_team(parts[1], 1), swap_team(parts[3], 1)
    if middle is not None:
        three = after(three, middle)
    shape = jax.ShapeDtypeStruct(three.shape, bf16)
    near = call(far_kernel, "far_sum", shape, (parts[2], three), 0)
    far = swap_team(near, 2)
    if end is not None:
        one, far = after((one, far), end)
    return parts[0], one, far, near


def trade_team(parts):
    return [parts[0]] + [swap_team(parts[r], r) for r in (1, 2, 3)]


def high_bits(axis):
    size = lax.axis_size(axis)
    return [1 << k for k in reversed(range(1, size.bit_length() - 1))]


def pick(a, index, axis=0):
    return lax.dynamic_index_in_dim(a, index, axis, False)


def ordered(blocks, index):
    bit = len(blocks) // 2
    while bit:
        flip = (index & bit) != 0
        blocks = [jnp.where(flip, blocks[r ^ bit], blocks[r]) for r in range(len(blocks))]
        bit //= 2
    return blocks


def after(x, *others):
    return lax.optimization_barrier((x, others))[0]


def whole_spec():
    return pl.BlockSpec(memory_space=pltpu.VMEM)


def scalar_spec():
    return pl.BlockSpec(memory_space=pltpu.SMEM)


def any_spec():
    return pl.BlockSpec(memory_space=pl.ANY)


BIG = pltpu.CompilerParams(vmem_limit_bytes=32 * 2**20)
MIDDLE = pltpu.CompilerParams(vmem_limit_bytes=24 * 2**20)
SMALL = pltpu.CompilerParams(vmem_limit_bytes=20 * 2**20)


def block_of(shape):
    return pl.BlockSpec(shape, lambda *k: (0,) * len(shape), pipeline_mode=pl.Buffered(1))


def call(kernel, name, out_shape, args, scalars=1, **more):
    specs = [scalar_spec()] * scalars + [block_of(a.shape) for a in args[scalars:]]
    return pl.pallas_call(
        kernel,
        grid=(1,),
        out_shape=out_shape,
        in_specs=specs,
        out_specs=jax.tree.map(lambda o: block_of(o.shape), out_shape),
        compiler_params=MIDDLE,
        name=name,
        **more,
    )(*args)


def share_kernel(spots, copies, idx, *refs):
    ins, outs, sem = refs[:spots], refs[spots:-1], refs[-1]
    flying = []
    for n, (src, dst, rows_at, cols_at, size, to) in enumerate(copies):
        row = pl.multiple_of(rows_at(idx), 16)
        col = pl.multiple_of(cols_at(idx), LANES)
        flying.append(
            pltpu.make_async_copy(
                ins[src].at[pl.ds(row, size[0]), pl.ds(col, size[1])],
                outs[dst].at[:, pl.ds(to, size[1])],
                sem.at[n],
            )
        )
    for one in flying:
        one.start()
    for one in flying:
        one.wait()


def shares(idx, w_qkv, w_out, w_up, w_down, ny, ns):
    shard, dim = w_out.shape
    quarter = dim // TEAM
    rows, fb = shard // ny, w_down.shape[0] // TEAM
    low = fb // ny
    copies = []
    for away in (0, 1):
        def who(i, away=away):
            return i[0] ^ (2 * away)

        for part in range(3):
            copies.append((0, away, lambda i: i[1] * rows,
                           lambda i, w=who, p=part: p * dim + w(i) * quarter, (rows, quarter), part * quarter))
        copies.append((1, away, lambda i: i[1] * rows,
                       lambda i, w=who: w(i) * quarter, (rows, quarter), 3 * quarter))
        if fb % LANES == 0:
            for k in range(ns):
                copies.append((2, 2 + away, lambda i: i[1] * rows,
                               lambda i, w=who, k=k: (k * TEAM + w(i)) * fb, (rows, fb), k * fb))
        copies.append((3, 4 + away, lambda i, w=who: w(i) * fb + i[1] * low, lambda i: 0, (low, dim), 0))
    sizes = [(rows, dim)] * 2 + [(rows, ns * fb)] * 2 + [(low, dim)] * 2
    out = pl.pallas_call(
        functools.partial(share_kernel, 4, copies),
        out_shape=[jax.ShapeDtypeStruct(s, bf16) for s in sizes],
        in_specs=[scalar_spec()] + [any_spec()] * 4,
        out_specs=[whole_spec()] * 6,
        scratch_shapes=[pltpu.SemaphoreType.DMA((len(copies),))],
        name="shares",
    )(idx, w_qkv, w_out, w_up, w_down)
    out = [list(out[k : k + 2]) for k in (0, 2, 4)]
    if fb % LANES:
        mine = lax.dynamic_slice_in_dim(w_up, idx[1] * rows, rows, 0).reshape(rows, ns, TEAM, fb)
        out[1] = [pick(mine, idx[0] ^ r, 2).reshape(rows, ns * fb) for r in (0, 2)]
    return out


def place_kernel(maps, cuts, idx, places, *refs):
    ins, outs = refs[: len(maps)], refs[len(maps) :]
    for ref, (which, order, step, offset) in zip(ins, maps):
        rows = ref.shape[1]
        for k, r in enumerate(order):
            at = pl.multiple_of(((places[which] ^ r) * step + offset) * rows, 16)
            if cuts:
                width = outs[0].shape[1]
                outs[0][pl.ds(at, rows), :] = ref[k, :, :width]
                outs[-1][pl.ds(at, rows), :] = ref[k, :, width:]
            else:
                outs[0][pl.ds(at, rows), :] = ref[k]
    for r in range(cuts):
        rows = outs[1].shape[0]
        at = pl.multiple_of((idx[0] ^ r) * rows, 16)
        outs[1 + r][...] = outs[-1][pl.ds(at, rows), :]


def append_kernel(a_ref, b_ref, out):
    count = a_ref.shape[0]
    out[:count] = a_ref[...]
    out[count:] = b_ref[...]


def append(a, b):
    shape = jax.ShapeDtypeStruct((a.shape[0] + b.shape[0],) + a.shape[1:], bf16)
    return call(append_kernel, "append", shape, (a, b), 0)


class Gathering:
    def __init__(self, own, away, parted):
        ny = lax.axis_size("dp") // 2 if parted else 1
        self.seq_steps = [(1, ny)] + [(bit, bit * ny) for bit in high_bits("seq")]
        self.a, self.away, self.order, self.n = own[None], away[None], [0], 0

    def step(self, wait=None):
        bit, weight = self.seq_steps[self.n]
        if self.n:
            self.a = append(self.a, self.came)
            self.order = self.order + [r | self.seq_steps[self.n - 1][1] for r in self.order]
        sent = self.a if self.n else self.away
        self.came = swap(sent if wait is None else after(sent, wait), "seq", bit)
        self.n += 1
        if self.n == len(self.seq_steps):
            last = [r | weight for r in self.order]
            self.pieces = [(self.a, self.order), (self.came, last)]
        return self.came

    def rest(self, wait=None):
        while self.n < len(self.seq_steps) - 1:
            self.step(wait)
            wait = None
        return self.came

    def across(self, k, wait=None):
        new = [self.pieces[k]]
        for bit in high_bits("dp"):
            for a, order in list(new):
                a = a if wait is None else after(a, wait)
                new.append((swap(a, "dp", bit), [r | (bit // 2) for r in order]))
        self.pieces += new[1:]
        return new[1][0]


def place_weight(idx, places, groups, width=None):
    arrays = [a for pieces, *_ in groups for a, _ in pieces]
    maps = [(which, order, step, at) for pieces, which, step, at in groups for _, order in pieces]
    rows, cols = sum(a.shape[0] * a.shape[1] for a in arrays), arrays[0].shape[2]
    shapes = [(rows, cols)]
    scratch = []
    if width:
        shapes = [(rows, width)] + [(rows // TEAM, cols - width)] * TEAM
        scratch = [pltpu.VMEM((rows, cols - width), bf16)]
    return call(
        functools.partial(place_kernel, maps, TEAM if width else 0),
        "place_weight",
        [jax.ShapeDtypeStruct(s, bf16) for s in shapes],
        (idx, places, *arrays),
        2,
        scratch_shapes=scratch,
    )


def attn_grad_kernel(idx, x_ref, dq_ref, ctx_ref, dctx_ref, *refs):
    parts, out = refs[:TEAM], refs[TEAM]
    k = pl.program_id(0)
    width = dq_ref.shape[1] // 3
    grad = dot_tn(x_ref[...], dq_ref[...])
    far = dot_tn(ctx_ref[...], dctx_ref[...])
    out[:, :width] = grad[:, :width].astype(bf16)
    out[:, width : 3 * width] = (grad[:, width:] + far).astype(bf16)
    per = parts[0].shape[0] // out.shape[0]
    member = (k // per) ^ idx[0]
    at = pl.multiple_of((k % per) * out.shape[0], 16)
    for r in range(TEAM):
        @pl.when(member == r)
        def _(r=r):
            out[:, 3 * width :] = parts[r][pl.ds(at, out.shape[0]), :]


def attn_grad(idx, inputs, d_qkv, context, d_ctx_kv, parts):
    dim, step = inputs.shape[1], LANES
    return pl.pallas_call(
        attn_grad_kernel,
        grid=(dim // step,),
        out_shape=jax.ShapeDtypeStruct((dim, d_qkv.shape[1] + parts[0].shape[1]), bf16),
        in_specs=[
            scalar_spec(),
            pl.BlockSpec((inputs.shape[0], step), lambda k: (0, k)),
            block_of(d_qkv.shape),
            pl.BlockSpec((context.shape[0], step), lambda k: (0, k)),
            block_of(d_ctx_kv.shape),
        ]
        + [block_of(p.shape) for p in parts],
        out_specs=pl.BlockSpec((step, d_qkv.shape[1] + parts[0].shape[1]), lambda k: (k, 0)),
        compiler_params=SMALL,
        name="attn_grad",
    )(idx, inputs, d_qkv, context, d_ctx_kv, *parts)


def insert_bit(k, at, bit):
    return ((k >> at) << (at + 1)) | (bit << at) | (k & ((1 << at) - 1))


def split_kernel(before, side, at, place, x_ref, *refs):
    here = (place[0] >> side) & 1
    if before is None:
        (away_ref,) = refs
        for k in range(away_ref.shape[0]):
            away_ref[k] = x_ref[insert_bit(k, at, 1 - here)]
        return
    recv_ref, keep_ref, away_ref = refs

    def total(k):
        j = k if before is True else insert_bit(k, before[1], (place[0] >> before[0]) & 1)
        return (x_ref[j].astype(f32) + recv_ref[k].astype(f32)).astype(bf16)

    for k in range(away_ref.shape[0]):
        away_ref[k] = total(insert_bit(k, at, 1 - here))
        keep_ref[k] = total(insert_bit(k, at, here))


class Reduction:
    def __init__(self, x, place):
        ny = lax.axis_size("dp") // 2
        ns = lax.axis_size("seq")
        y_bits = ny.bit_length() - 1
        steps = [("dp", bit, (bit // 2).bit_length() - 1, 0) for bit in reversed(high_bits("dp"))]
        steps += [("seq", b, (b * ny).bit_length() - 1, 1) for b in reversed(high_bits("seq"))]
        self.steps = steps + [("seq", 1, y_bits, 0)]
        self.place, self.n, self.came = place, 0, None
        self.kept = x.reshape(ns * ny, -1, x.shape[1])

    def step(self, wait=None):
        n, x, recv = self.n, self.kept, self.came
        axis, bit, side, at = self.steps[n]
        if n == 0 and wait is not None:
            x = after(x, wait)
        elif wait is not None:
            recv = after(recv, wait)
        before = None if n == 0 else (self.steps[0][2:] if n == 1 else True)
        count = x.shape[0] // 2 if n == 0 else recv.shape[0] // 2
        half = jax.ShapeDtypeStruct((count,) + x.shape[1:], bf16)
        out = call(
            functools.partial(split_kernel, before, side, at),
            "split_sum",
            [half] if n == 0 else [half, half],
            (self.place, x) if n == 0 else (self.place, x, recv),
        )
        if n:
            self.kept = out[0]
        self.sent = out[-1]
        self.came = swap(self.sent, axis, bit)
        self.n += 1
        return self.sent

    def last(self, wait=None):
        while self.n < len(self.steps):
            self.step(wait)
            wait = None
        return self.kept, self.came


def halves_kernel(place, x_ref, out_ref, in_ref):
    y, z = place[0] & 1, (place[0] >> 2) & 1
    for k in range(out_ref.shape[0]):
        low = ((k >> 1) << 3) | ((k & 1) << 1) | (1 - y)
        out_ref[k] = x_ref[low | ((1 - z) << 2)]
        in_ref[k] = x_ref[low | (z << 2)]


def leave_kernel(place, x_ref, came_ref, out_ref):
    y, z = place[0] & 1, (place[0] >> 2) & 1
    for k in range(out_ref.shape[0]):
        mine = x_ref[((k >> 1) << 3) | ((1 - z) << 2) | ((k & 1) << 1) | y]
        out_ref[k] = (mine.astype(f32) + came_ref[k].astype(f32)).astype(bf16)


def stay_kernel(place, x_ref, came_ref, near_ref, keep_ref, out_ref):
    y, z, far = place[0] & 1, (place[0] >> 2) & 1, (place[0] >> 3) & 1

    def total(k):
        mine = x_ref[((k >> 1) << 3) | (z << 2) | ((k & 1) << 1) | y]
        return (mine.astype(f32) + came_ref[k].astype(f32) + near_ref[k].astype(f32)).astype(bf16)

    for k in (0, 1):
        keep_ref[k] = total((far << 1) | k)
        out_ref[k] = total(((1 - far) << 1) | k)


class HalvedReduction(Reduction):
    def step(self, wait=None):
        n = self.n
        if n > 2:
            self.steps = [None, None, None, ("seq", 1, 1, 0)]
            return super().step(wait)
        x = self.kept
        four = jax.ShapeDtypeStruct((x.shape[0] // 4,) + x.shape[1:], bf16)
        two = jax.ShapeDtypeStruct((2,) + x.shape[1:], bf16)
        if n == 0:
            x = x if wait is None else after(x, wait)
            out, stay = call(halves_kernel, "halves", (four, four), (self.place, x))
            self.sent = out
            self.out, self.stay = swap(out, "dp", 2), swap(stay, "dp", 2)
        elif n == 1:
            came = self.out if wait is None else after(self.out, wait)
            self.sent = call(leave_kernel, "leave_sum", four, (self.place, x, came))
            self.near = swap(self.sent, "seq", 2)
        else:
            came = self.near if wait is None else after(self.near, wait)
            args = (self.place, x, self.stay, came)
            self.kept, self.sent = call(stay_kernel, "stay_sum", (two, two), args)
            self.came = swap(self.sent, "seq", 4)
        self.n += 1
        return self.sent


def final_kernel(kind, fb, idx, mine_ref, other_ref, *outs):
    count, rows, width = mine_ref.shape
    for k in range(count):
        row = pl.multiple_of((idx[1] ^ (k // 2)) * rows, 16)
        for core, ref in enumerate((mine_ref, other_ref)):
            member = idx[0] ^ (2 * (k % 2) + core)
            if kind == "down":
                at = pl.multiple_of(member * (rows * count // 2) + row, 16)
                outs[0][pl.ds(at, rows), :] = ref[k].astype(f32)
            elif kind == "up":
                for n in range(width // fb):
                    col = pl.multiple_of((n * TEAM + member) * fb, LANES)
                    block = ref[k, :, n * fb : (n + 1) * fb]
                    outs[0][pl.ds(row, rows), pl.ds(col, fb)] = block.astype(f32)
            else:
                dim = outs[1].shape[1]
                quarter = dim // TEAM
                for part in range(4):
                    to = outs[0] if part < 3 else outs[1]
                    col = pl.multiple_of((part % 3) * dim * (part < 3) + member * quarter, LANES)
                    block = ref[k, :, part * quarter : (part + 1) * quarter]
                    to[pl.ds(row, rows), pl.ds(col, quarter)] = block.astype(f32)


def spread(own, near):
    blocks = {0: append(own, near)}
    for bit in high_bits("dp"):
        for m in list(blocks):
            blocks[m | (bit // 2)] = swap(blocks[m], "dp", bit)
    blocks = [blocks[m] for m in range(len(blocks))]
    while len(blocks) > 1:
        blocks = [append(a, b) for a, b in zip(blocks[0::2], blocks[1::2])]
    return blocks[0], swap(blocks[0], "dp", 1)


def spread_weight(kind, pair, idx, shapes, fb=LANES):
    return call(
        functools.partial(final_kernel, kind, fb),
        "final_" + kind,
        [jax.ShapeDtypeStruct(s, f32) for s in shapes],
        (idx, *spread(*pair)),
    )


def spread_narrow(pair, idx, shape, fb):
    mine, other = spread(*pair)
    teams = [mine[0::2], other[0::2], mine[1::2], other[1::2]]
    teams = jnp.stack(ordered(teams, idx[0]))
    rows = jnp.stack(ordered([teams[:, m] for m in range(teams.shape[1])], idx[1]), axis=1)
    rows = rows.reshape(TEAM, shape[0], shape[1] // (TEAM * fb), fb).transpose(1, 2, 0, 3)
    return rows.reshape(shape).astype(f32)


def ends_kernel(mid, u_ref, a_ref, mid_ref, end_ref):
    rows = u_ref.shape[0]
    a = [a_ref[n] for n in range(NST)]

    def eight(k, s):
        for t in range(8):
            u = u_ref[k * 8 + t]
            s = tuple(a[n] * s[n] + u for n in range(NST))
        return s

    zero = tuple(jnp.zeros_like(a[0]) for _ in range(NST))
    s = lax.fori_loop(0, mid // 8, eight, zero)
    for n in range(NST):
        mid_ref[n] = s[n]
    s = lax.fori_loop(mid // 8, rows // 8, eight, s)
    for n in range(NST):
        end_ref[n] = s[n]


def local_ends(u, a):
    shape = jax.ShapeDtypeStruct(a.shape, f32)
    kernel = functools.partial(ends_kernel, u.shape[0] - CTX)
    return call(kernel, "ssm_ends", (shape, shape), (u, a), 0)


def context_kernel(mid, late, u_ref, a_ref, gin_ref, gout_ref, h_ref, first_ref, second_ref, y_ref):
    half = NST // 2
    for base in (0, half):
        ns = range(base, base + half)
        a = [a_ref[n] for n in ns]
        gin = [gin_ref[n] for n in ns]
        gout = [gout_ref[n] for n in ns]

        def step(k, h):
            for t in range(4):
                p = k * 4 + t
                u = u_ref[mid + p]
                h = tuple(a[n] * h[n] + gin[n] * u for n in range(half))
                y = functools.reduce(jnp.add, [gout[n] * h[n] for n in range(half)])
                y_ref[p] = y if base == 0 else y_ref[p] + y
            return h

        lax.fori_loop(0, CTX // 4, step, tuple(h_ref[n] for n in ns))
    per = y_ref.shape[1] // TEAM
    for w in range(2):
        for c in range(per):
            own, other = y_ref[:, w * per + c, :], y_ref[:, (2 + w) * per + c, :]
            at = (slice(w * CTX, (w + 1) * CTX), slice(c * LANES, (c + 1) * LANES))
            first_ref[at] = jnp.where(late[0] == 1, other, own).astype(bf16)
            second_ref[at] = jnp.where(late[0] == 1, own, other).astype(bf16)


def contexts(half, u, a, gin, gout, h_mid):
    shape = jax.ShapeDtypeStruct((2 * CTX, u.shape[1] * LANES // TEAM), bf16)
    return call(
        functools.partial(context_kernel, u.shape[0] - CTX),
        "ssm_context",
        (shape, shape),
        (half, u, a, gin, gout, h_mid),
        scratch_shapes=[pltpu.VMEM((CTX,) + u.shape[1:], f32)],
    )


def tail_kernel(dy_ref, a_ref, gout_ref, lam_ref):
    half = dy_ref.shape[1]
    a = [a_ref[n, :half] for n in range(NST)]
    gout = [gout_ref[n, :half] for n in range(NST)]

    def eight(k, lam):
        for t in range(8):
            dy = dy_ref[CTX - 1 - (k * 8 + t)]
            lam = tuple(a[n] * lam[n] + gout[n] * dy for n in range(NST))
        return lam

    lam = lax.fori_loop(0, CTX // 8, eight, tuple(jnp.zeros_like(a[0]) for _ in range(NST)))
    for n in range(NST):
        lam_ref[n] = lam[n]


def tail_adjoint(dy, a, gout):
    shape = jax.ShapeDtypeStruct((NST,) + dy.shape[1:], f32)
    return call(tail_kernel, "ssm_tail", shape, (dy, a, gout), 0)


def first_context_kernel(dy0_ref, a_ref, gout_ref, init_ref, da_ref, dgout_ref, g0_ref, hs):
    ns = range(GROUP)
    a = [a_ref[n] for n in ns]
    gout = [gout_ref[n] for n in ns]
    zero = tuple(jnp.zeros_like(a[0]) for _ in ns)

    def ahead(k, h):
        for t in range(8):
            h = tuple(a[n] * h[n] for n in ns)
            for n in ns:
                hs[k * 8 + t + 1, n] = h[n]
        return h

    h = tuple(init_ref[n] for n in ns)
    for n in ns:
        hs[0, n] = h[n]
    lax.fori_loop(0, CTX // 8, ahead, h)

    def back(k, carry):
        mu, da, dgout = carry
        for t in range(4):
            q = CTX - 1 - (k * 4 + t)
            dy = dy0_ref[q]
            mu = tuple(mu[n] + gout[n] * dy for n in ns)
            dgout = tuple(dgout[n] + dy * hs[q + 1, n] for n in ns)
            da = tuple(da[n] + mu[n] * hs[q, n] for n in ns)
            mu = tuple(a[n] * mu[n] for n in ns)
        return mu, da, dgout

    mu, da, dgout = lax.fori_loop(0, CTX // 4, back, (zero, zero, zero))
    for n in ns:
        g0_ref[n] = mu[n]
        da_ref[n] = da[n]
        dgout_ref[n] = dgout[n]


def first_context_back(dy0, a, gout, h_init):
    tile = dy0.shape[1:]
    states = pl.BlockSpec((GROUP,) + tile, lambda g: (g, 0, 0))
    return pl.pallas_call(
        first_context_kernel,
        grid=(NST // GROUP,),
        out_shape=(jax.ShapeDtypeStruct(a.shape, f32),) * 3,
        in_specs=[pl.BlockSpec(dy0.shape, lambda g: (0, 0, 0))] + [states] * 3,
        out_specs=(states,) * 3,
        scratch_shapes=[pltpu.VMEM((CTX + 1, GROUP) + tile, f32)],
        name="first_context",
    )(dy0, a, gout, h_init)


def back_kernel(
    u_ref, dy_ref, a_ref, gin_ref, gout_ref, h_ref, lam_ref, da0_ref, dgout0_ref,
    du_ref, dgin_ref, da_ref, dgout_ref, g_ref, hs,
):
    first = pl.program_id(0) == 0
    rows = u_ref.shape[0]
    mid = rows - CTX
    ns = range(GROUP)
    a = [a_ref[n] for n in ns]
    gin = [gin_ref[n] for n in ns]
    gout = [gout_ref[n] for n in ns]
    zero = tuple(jnp.zeros_like(a[0]) for _ in ns)

    def ahead(k, h):
        for t in range(8):
            p = k * 8 + t
            u = u_ref[p]
            h = tuple(a[n] * h[n] + gin[n] * u for n in ns)
            for n in ns:
                hs[p + 1, n] = h[n]
        return h

    h = tuple(h_ref[n] for n in ns)
    for n in ns:
        hs[0, n] = h[n]
    lax.fori_loop(0, rows // 8, ahead, h)

    def tail(k, carry):
        lam, dgin, da, dgout = carry
        for t in range(4):
            q = CTX - 1 - (k * 4 + t)
            p = mid + q
            dy, u = dy_ref[q], u_ref[p]
            lam = tuple(lam[n] + gout[n] * dy for n in ns)
            dgout = tuple(dgout[n] + dy * hs[p + 1, n] for n in ns)
            dgin = tuple(dgin[n] + lam[n] * u for n in ns)
            da = tuple(da[n] + lam[n] * hs[p, n] for n in ns)
            du = functools.reduce(jnp.add, [gin[n] * lam[n] for n in ns])
            du_ref[p] = jnp.where(first, du, du_ref[p] + du)
            lam = tuple(a[n] * lam[n] for n in ns)
        return lam, dgin, da, dgout

    def head(k, carry):
        lam, dgin, da = carry
        for t in range(4):
            p = mid - 1 - (k * 4 + t)
            u = u_ref[p]
            dgin = tuple(dgin[n] + lam[n] * u for n in ns)
            da = tuple(da[n] + lam[n] * hs[p, n] for n in ns)
            du = functools.reduce(jnp.add, [gin[n] * lam[n] for n in ns])
            du_ref[p] = jnp.where(first, du, du_ref[p] + du)
            lam = tuple(a[n] * lam[n] for n in ns)
        return lam, dgin, da

    lam = tuple(lam_ref[n] for n in ns)
    da0, dgout0 = tuple(da0_ref[n] for n in ns), tuple(dgout0_ref[n] for n in ns)
    lam, dgin, da, dgout = lax.fori_loop(0, CTX // 4, tail, (lam, zero, da0, dgout0))
    lam, dgin, da = lax.fori_loop(0, mid // 4, head, (lam, dgin, da))
    for n in ns:
        g_ref[n] = lam[n]
        dgin_ref[n] = dgin[n]
        da_ref[n] = da[n]
        dgout_ref[n] = dgout[n]


def ssm_back(u, dy, a, gin, gout, state_in, lam_end, da0, dgout0):
    tile = u.shape[1:]
    states = pl.BlockSpec((GROUP,) + tile, lambda g: (g, 0, 0))
    rows = pl.BlockSpec(u.shape, lambda g: (0, 0, 0))
    tail = pl.BlockSpec(dy.shape, lambda g: (0, 0, 0))
    out = jax.ShapeDtypeStruct(a.shape, f32)
    return pl.pallas_call(
        back_kernel,
        grid=(NST // GROUP,),
        out_shape=(jax.ShapeDtypeStruct(u.shape, f32),) + (out,) * 4,
        in_specs=[rows, tail] + [states] * 7,
        out_specs=(rows,) + (states,) * 4,
        scratch_shapes=[pltpu.VMEM((u.shape[0] + 1, GROUP) + tile, f32)],
        compiler_params=SMALL,
        name="ssm_back",
    )(u, dy, a, gin, gout, state_in, lam_end, da0, dgout0)


def dot_nt(x, y):
    return lax.dot_general(x, y, (((1,), (1,)), ((), ())), preferred_element_type=f32)


def dot_nn(x, y):
    return jnp.dot(x, y, preferred_element_type=f32)


def dot_tn(x, y):
    return lax.dot_general(x, y, (((0,), (0,)), ((), ())), preferred_element_type=f32)


def softmax_parts(q, keys):
    rows = q.shape[0]
    scores = [dot_nt(q, k) * (1.0 / math.sqrt(HD)) for k in keys]
    at = lax.broadcasted_iota(jnp.int32, (rows, rows), 0)
    to = lax.broadcasted_iota(jnp.int32, (rows, rows), 1)
    scores[-1] = jnp.where(to <= at, scores[-1], far_below)
    top = functools.reduce(jnp.maximum, [jnp.max(s, axis=-1, keepdims=True) for s in scores])
    es = [jnp.exp(s - top) for s in scores]
    total = functools.reduce(jnp.add, [jnp.sum(e, axis=-1, keepdims=True) for e in es])
    return [e / total for e in es]


def attend_kernel(half_ref, q0, q1, k0, k1, v0, v1, kc, vc, out_ref):
    w, h = pl.program_id(0), pl.program_id(1)
    rows = q0.shape[0]
    for half, q, keys, values in ((0, q0, (kc, k0), (vc, v0)), (1, q1, (kc, k0, k1), (vc, v0, v1))):
        probs = softmax_parts(q[...], [k[...] for k in keys])
        out = [dot_nn(p.astype(bf16), v[...]) for p, v in zip(probs, values)]
        at = pl.multiple_of(((half ^ half_ref[0]) * 2 + w) * rows, 16)
        col = pl.multiple_of(h * HD, LANES)
        out_ref[pl.ds(at, rows), pl.ds(col, HD)] = functools.reduce(jnp.add, out).astype(bf16)


def attend_back_kernel(
    half_ref, q0, q1, k0, k1, v0, v1, kc, vc, do0, do1, dqkv_ref, dctx_ref
):
    w, h = pl.program_id(0), pl.program_id(1)
    rows, heads = q0.shape[0], pl.num_programs(1)
    scale = 1.0 / math.sqrt(HD)
    dk, dv = [0.0, 0.0, 0.0], [0.0, 0.0, 0.0]

    def row_of(half):
        return pl.multiple_of(((half ^ half_ref[0]) * 2 + w) * rows, 16)

    def col_of(part):
        return pl.multiple_of((part * heads + h) * HD, LANES)

    cases = ((0, q0, do0, (kc, k0), (vc, v0)), (1, q1, do1, (kc, k0, k1), (vc, v0, v1)))
    for half, q, do, keys, values in cases:
        query, d_out = q[...], do[...]
        probs = softmax_parts(query, [k[...] for k in keys])
        d_probs = [dot_nt(d_out, v[...]) for v in values]
        sums = [jnp.sum(p * d, axis=-1, keepdims=True) for p, d in zip(probs, d_probs)]
        delta = functools.reduce(jnp.add, sums)
        d_scores = [(p * (d - delta)).astype(bf16) for p, d in zip(probs, d_probs)]
        dq = functools.reduce(jnp.add, [dot_nn(d, k[...]) for d, k in zip(d_scores, keys)])
        dqkv_ref[pl.ds(row_of(half), rows), pl.ds(col_of(0), HD)] = (dq * scale).astype(bf16)
        for n, (d, p) in enumerate(zip(d_scores, probs)):
            dk[n] = dk[n] + dot_tn(d, query)
            dv[n] = dv[n] + dot_tn(p.astype(bf16), d_out)
    ctx_row = pl.multiple_of(w * CTX, 16)
    dctx_ref[pl.ds(ctx_row, CTX), pl.ds(col_of(0), HD)] = (dk[0] * scale).astype(bf16)
    dctx_ref[pl.ds(ctx_row, CTX), pl.ds(col_of(1), HD)] = dv[0].astype(bf16)
    for half in (0, 1):
        dqkv_ref[pl.ds(row_of(half), rows), pl.ds(col_of(1), HD)] = (dk[1 + half] * scale).astype(bf16)
        dqkv_ref[pl.ds(row_of(half), rows), pl.ds(col_of(2), HD)] = dv[1 + half].astype(bf16)


def attention_specs(rows, heads):
    def at(half, part):
        return pl.BlockSpec((rows, HD), lambda w, h, s: ((half ^ s[0]) * 2 + w, part * heads + h))

    def ctx(part):
        return pl.BlockSpec((CTX, HD), lambda w, h, s: (w, part * heads + h))

    return [at(half, part) for part in range(3) for half in (0, 1)] + [ctx(0), ctx(1)]


def whole_block(shape):
    return pl.BlockSpec(shape, lambda w, h, s: (0, 0))


def attend(half, qkv, ctx_kv):
    rows, heads = qkv.shape[0] // TEAM, qkv.shape[1] // (3 * HD)
    out = (qkv.shape[0], heads * HD)
    return pl.pallas_call(
        attend_kernel,
        grid_spec=pltpu.PrefetchScalarGridSpec(
            num_scalar_prefetch=1,
            grid=(2, heads),
            in_specs=attention_specs(rows, heads),
            out_specs=whole_block(out),
        ),
        out_shape=jax.ShapeDtypeStruct(out, bf16),
        compiler_params=SMALL,
        name="attend",
    )(half, *[qkv] * 6, ctx_kv, ctx_kv)


def attend_back(half, qkv, ctx_kv, d_attended):
    rows, heads = qkv.shape[0] // TEAM, qkv.shape[1] // (3 * HD)

    def at(side):
        return pl.BlockSpec((rows, HD), lambda w, h, s: ((side ^ s[0]) * 2 + w, h))

    return pl.pallas_call(
        attend_back_kernel,
        grid_spec=pltpu.PrefetchScalarGridSpec(
            num_scalar_prefetch=1,
            grid=(2, heads),
            in_specs=attention_specs(rows, heads) + [at(0), at(1)],
            out_specs=[whole_block(qkv.shape), whole_block(ctx_kv.shape)],
        ),
        out_shape=[jax.ShapeDtypeStruct(qkv.shape, bf16), jax.ShapeDtypeStruct(ctx_kv.shape, bf16)],
        compiler_params=SMALL,
        name="attend_back",
    )(half, *[qkv] * 6, ctx_kv, ctx_kv, d_attended, d_attended)


def pack_kernel(rate, gin, gout, g_one, g_two, out):
    for k, ref in enumerate((rate, gin, gout)):
        out[0, k * NST : (k + 1) * NST, :] = ref[...]
    out[0, 3 * NST : 3 * NST + 1, :] = g_one[...]
    out[0, 3 * NST + 1 : 3 * NST + 2, :] = g_two[...]


def norm_kernel(idx, gain, x0, x1, x2, x3, low_ref, inv_ref, u_ref):
    rows, dim = x0.shape
    cols = dim // TEAM
    for r, ref in enumerate((x0, x1, x2, x3)):
        x = ref[...].astype(f32)
        inv = lax.rsqrt(jnp.mean(x * x, axis=-1, keepdims=True) + epsilon)
        inv_ref[r * rows : (r + 1) * rows, :] = inv
        low_ref[r * rows : (r + 1) * rows, :] = (x * inv * gain[...]).astype(bf16)
        for c in range(cols // LANES):
            at = pl.multiple_of(idx[0] * cols + c * LANES, LANES)
            u = low_ref[r * rows : (r + 1) * rows, pl.ds(at, LANES)].astype(f32)
            u_ref[:, r * (cols // LANES) + c, :] = u


def first_norm(idx, gain, blocks):
    rows, dim = blocks[0].shape
    shapes = (
        jax.ShapeDtypeStruct((TEAM * rows, dim), bf16),
        jax.ShapeDtypeStruct((TEAM * rows, 1), f32),
        jax.ShapeDtypeStruct((rows, dim // LANES, LANES), f32),
    )
    return call(norm_kernel, "first_norm", shapes, (idx, gain[None], *blocks))


def part_types(rows, dim):
    return tuple(jax.ShapeDtypeStruct((rows, dim), (f32, bf16)[r % 2]) for r in range(TEAM))


def dot_kernel(x_ref, w_ref, *parts):
    rows = parts[0].shape[0]
    for r in (3, 1, 2, 0):
        part = dot_nn(x_ref[r * rows : (r + 1) * rows, :], w_ref[...])
        parts[r][...] = part.astype(parts[r].dtype)


def dot_parts(name, x, w):
    return call(dot_kernel, name, part_types(x.shape[0] // TEAM, w.shape[1]), (x, w), 0)


def out_kernel(idx, x_ref, w0, w1, w2, w3, *parts):
    rows, cols = parts[0].shape[0], w0.shape[1]
    for r in (3, 1, 2, 0):
        for q, w in enumerate((w0, w1, w2, w3)):
            at = pl.multiple_of((idx[0] ^ q) * cols, LANES)
            part = dot_nn(x_ref[r * rows : (r + 1) * rows, :], w[...])
            parts[r][:, pl.ds(at, cols)] = part.astype(parts[r].dtype)


def context_kv_kernel(idx, w_ref, c0, c1, c2, c3, kv_ref, context_ref):
    cols = c0.shape[1]
    width = w_ref.shape[1] // 3
    for r, part in enumerate((c0, c1, c2, c3)):
        at = pl.multiple_of((idx[0] ^ r) * cols, LANES)
        for w in (0, 1):
            v = w ^ (r & 1)
            context_ref[w * CTX : (w + 1) * CTX, pl.ds(at, cols)] = part[v * CTX : (v + 1) * CTX, :]
    kv_ref[...] = dot_nn(context_ref[...], w_ref[:, width:]).astype(bf16)


def mlp_kernel(m0, m1, m2, m3, g0, g1, g2, g3, up, down, act_ref, dpre_ref, *parts_and_sum):
    parts, total = parts_and_sum[:-1], parts_and_sum[-1]
    k = pl.program_id(0)
    rows = m0.shape[0]
    c = math.sqrt(2.0 / math.pi)
    for r, (m, g) in enumerate(((m0, g0), (m1, g1), (m2, g2), (m3, g3))):
        at = slice(r * rows, (r + 1) * rows)
        x = dot_nn(m[...], up[...])
        t = jnp.tanh(c * (x + 0.044715 * (x * x * x)))
        cdf = 0.5 * (1.0 + t)
        act_ref[at, :] = (x * cdf).astype(bf16)
        slope = cdf + (0.5 * c) * x * (1.0 - t * t) * (1.0 + (3 * 0.044715) * (x * x))
        d_pre = (dot_nt(g[...], down[...]) * slope).astype(bf16)
        dpre_ref[at, :] = d_pre
        new = dot_nt(d_pre, up[...])
        total[at, :] = jnp.where(k == 0, new, total[at, :] + new)

    @pl.when(k == pl.num_programs(0) - 1)
    def _():
        for r, part in enumerate(parts):
            part[...] = total[r * rows : (r + 1) * rows, :].astype(part.dtype)


def feed_forward(mlp_blocks, grad_blocks, up, down):
    rows, dim = mlp_blocks[0].shape
    units = up.shape[1]
    step = 256

    unit_out = jax.ShapeDtypeStruct((TEAM * rows, units), bf16)
    return pl.pallas_call(
        mlp_kernel,
        grid=(units // step,),
        out_shape=(unit_out, unit_out) + part_types(rows, dim),
        in_specs=[block_of((rows, dim))] * 8
        + [pl.BlockSpec((dim, step), lambda k: (0, k)), pl.BlockSpec((step, dim), lambda k: (k, 0))],
        out_specs=(pl.BlockSpec((TEAM * rows, step), lambda k: (0, k)),) * 2
        + (block_of((rows, dim)),) * TEAM,
        scratch_shapes=[pltpu.VMEM((TEAM * rows, dim), f32)],
        compiler_params=MIDDLE,
        name="feed_forward",
    )(*mlp_blocks, *grad_blocks, up, down)


def mlp_grad_kernel(x_ref, y0, y1, y2, y3, out):
    rows = y0.shape[0]
    grads = [dot_tn(x_ref[r * rows : (r + 1) * rows, :], y[...]) for r, y in enumerate((y0, y1, y2, y3))]
    out[...] = functools.reduce(jnp.add, grads).astype(bf16)


def down_grad(act, grad_blocks):
    rows, dim = grad_blocks[0].shape
    step = 256
    return pl.pallas_call(
        mlp_grad_kernel,
        grid=(act.shape[1] // step,),
        out_shape=jax.ShapeDtypeStruct((act.shape[1], dim), bf16),
        in_specs=[pl.BlockSpec((act.shape[0], step), lambda k: (0, k))]
        + [block_of((rows, dim))] * TEAM,
        out_specs=pl.BlockSpec((step, dim), lambda k: (k, 0)),
        compiler_params=SMALL,
        name="down_grad",
    )(act, *grad_blocks)


def up_grad_kernel(x0, x1, x2, x3, y_ref, out):
    rows = x0.shape[0]
    grads = [dot_tn(x[...], y_ref[r * rows : (r + 1) * rows, :]) for r, x in enumerate((x0, x1, x2, x3))]
    out[...] = functools.reduce(jnp.add, grads).astype(bf16)


def up_grad(mlp_blocks, d_pre):
    rows, dim = mlp_blocks[0].shape
    step = 256
    return pl.pallas_call(
        up_grad_kernel,
        grid=(dim // step,),
        out_shape=jax.ShapeDtypeStruct((dim, d_pre.shape[1]), bf16),
        in_specs=[pl.BlockSpec((rows, step), lambda k: (0, k))] * TEAM
        + [block_of(d_pre.shape)],
        out_specs=pl.BlockSpec((step, d_pre.shape[1]), lambda k: (k, 0)),
        compiler_params=SMALL,
        name="up_grad",
    )(*mlp_blocks, d_pre)


def attended_grad_kernel(idx, w0, w1, w2, w3, h0, h1, h2, h3, out):
    rows, cols = h0.shape[0], w0.shape[1]
    for r, h in enumerate((h0, h1, h2, h3)):
        grad = 0.0
        for q, w in enumerate((w0, w1, w2, w3)):
            at = pl.multiple_of((idx[0] ^ q) * cols, LANES)
            grad = grad + dot_nt(h[:, pl.ds(at, cols)], w[...])
        out[r * rows : (r + 1) * rows, :] = grad.astype(bf16)


def out_grad_kernel(idx, att_ref, h0, h1, h2, h3, *parts):
    rows, cols = h0.shape[0], parts[0].shape[1]
    for q, part in enumerate(parts):
        at = pl.multiple_of((idx[0] ^ q) * cols, LANES)
        grads = [
            dot_tn(att_ref[r * rows : (r + 1) * rows, :], h[:, pl.ds(at, cols)])
            for r, h in enumerate((h0, h1, h2, h3))
        ]
        part[...] = functools.reduce(jnp.add, grads).astype(bf16)


def context_grad_kernel(idx, d_ref, w_ref, *parts):
    cols = parts[0].shape[1]
    width = w_ref.shape[1] // 3
    for r, part in enumerate(parts):
        at = pl.multiple_of((idx[0] ^ r) * cols, 16)
        for w in (0, 1):
            v = w ^ (r & 1)
            grad = dot_nt(d_ref[w * CTX : (w + 1) * CTX, :], w_ref[pl.ds(at, cols), width:])
            part[v * CTX : (v + 1) * CTX, :] = grad.astype(part.dtype)


def inputs_grad_kernel(idx, dq_ref, w_ref, du_ref, inv_ref, x0, x1, x2, x3, *outs):
    parts, gain_ref, work = outs[:TEAM], outs[TEAM], outs[TEAM + 1]
    rows, dim = x0.shape
    cols = dim // TEAM
    gain = 0.0
    for r, x in enumerate((x0, x1, x2, x3)):
        at = slice(r * rows, (r + 1) * rows)
        work[...] = dot_nt(dq_ref[at, :], w_ref[...])
        for c in range(cols // LANES):
            col = pl.ds(pl.multiple_of(idx[0] * cols + c * LANES, LANES), LANES)
            work[:, col] = work[:, col] + du_ref[:, r * (cols // LANES) + c, :]
        grad = work[...]
        parts[r][...] = grad.astype(parts[r].dtype)
        gain = gain + jnp.sum(grad * (x[...].astype(f32) * inv_ref[at, :]), axis=0, keepdims=True)
    gain_ref[...] = gain


def cut_states_kernel(idx, init_ref, ends_ref, i0, i1, e0, e1, e2, e3):
    cols = i0.shape[1]
    for r, out in enumerate((e0, e1, e2, e3)):
        at = pl.multiple_of((idx[0] ^ r) * cols, LANES)
        out[...] = ends_ref[:, pl.ds(at, cols)]
        if r < 2:
            (i0, i1)[r][...] = init_ref[:, pl.ds(at, cols)]


def join_states_kernel(late, i0, i1, e0, e1, e2, e3, init_ref, twice_ref, first_ref, second_ref):
    per = init_ref.shape[1] // 2
    for w in range(2):
        for c in range(per):
            at = slice(c * LANES, (c + 1) * LANES)
            init = (i0, i1)[w][:, at]
            init_ref[:, w * per + c, :] = init
            twice_ref[:, w * per + c, :] = init
            twice_ref[:, (2 + w) * per + c, :] = init
            own, other = (e0, e1)[w][:, at], (e2, e3)[w][:, at]
            first_ref[:, w * per + c, :] = jnp.where(late[0] == 1, other, own)
            second_ref[:, w * per + c, :] = jnp.where(late[0] == 1, own, other)


def cut_ends_kernel(late, first_ref, second_ref, e0, e1, e2, e3):
    per = first_ref.shape[1] // 2
    for w in range(2):
        for c in range(per):
            at = slice(c * LANES, (c + 1) * LANES)
            one, two = first_ref[:, w * per + c, :], second_ref[:, w * per + c, :]
            (e0, e1)[w][:, at] = jnp.where(late[0] == 1, two, one)
            (e2, e3)[w][:, at] = jnp.where(late[0] == 1, one, two)


def join_ends_kernel(idx, e0, e1, e2, e3, out):
    cols = e0.shape[1]
    for r, part in enumerate((e0, e1, e2, e3)):
        at = pl.multiple_of((idx[0] ^ r) * cols, LANES)
        out[:, pl.ds(at, cols)] = part[...]


def small_kernel(spots, p0, p1, p2, p3, gains_ref, rate_ref, in_ref, out_ref, init_ref):
    packs = [p[...] for p in (p0, p1, p2, p3)]
    tiles = packs[0].shape[0] - 3 * NST * 2 - NST * 4
    one, two = 3 * NST * 2, 3 * NST * 2 + tiles
    gains = functools.reduce(jnp.add, [p[one:two] for p in packs])
    row = lax.broadcasted_iota(jnp.int32, gains.shape, 0)
    for k in (0, 1):
        mine = row == k * (tiles // 2) + spots[1]
        gains_ref[k : k + 1, :] = jnp.sum(jnp.where(mine, gains, 0.0), axis=0, keepdims=True)
    chosen = packs[0]
    for r in (1, 2, 3):
        chosen = jnp.where(spots[0] == r, packs[r], chosen)
    side = spots[1] % 2 == 1
    params = chosen[:one].reshape(3 * NST, 2, LANES)
    params = jnp.where(side, params[:, 1], params[:, 0])
    for k, ref in enumerate((rate_ref, in_ref, out_ref)):
        ref[...] = params[k * NST : (k + 1) * NST]
    init = chosen[two:].reshape(NST, 4, LANES)
    window = [jnp.where(side, init[:, 2 * w + 1], init[:, 2 * w]) for w in (0, 1)]
    init_ref[...] = jnp.where(spots[0] % 2 == 1, window[1], window[0])


def added(p0, one, far):
    return p0[...] + one[...].astype(f32) + far[...].astype(f32)


def second_norm_kernel(tok, p0, one, far, gain, hidden_ref, inv_ref, low_ref):
    hidden = tok[...].astype(f32) + added(p0, one, far)
    inv = lax.rsqrt(jnp.mean(hidden * hidden, axis=-1, keepdims=True) + epsilon)
    hidden_ref[...] = hidden
    inv_ref[...] = inv
    low_ref[...] = (hidden * inv * gain[...]).astype(bf16)


def result_kernel(hidden, p0, one, far, out):
    out[...] = (hidden[...] + added(p0, one, far)).astype(bf16)


def norm_back(grad, normed, inv, gain):
    scaled = grad * gain
    return inv * (scaled - normed * jnp.mean(scaled * normed, axis=-1, keepdims=True))


def hidden_grad_kernel(cot, hidden, inv, gain, p0, one, far, out_ref, low_ref, gain_ref):
    grad = added(p0, one, far)
    normed = hidden[...] * inv[...]
    gain_ref[...] = jnp.sum(grad * normed, axis=0, keepdims=True)
    out = cot[...].astype(f32) + norm_back(grad, normed, inv[...], gain[...])
    out_ref[...] = out
    low_ref[...] = out.astype(bf16)


def tokens_grad_kernel(d_hidden, tok, inv, gain, p0, one, far, out):
    grad = added(p0, one, far)
    normed = tok[...].astype(f32) * inv[...]
    out[...] = (d_hidden[...] + norm_back(grad, normed, inv[...], gain[...])).astype(bf16)


def context_sum_kernel(p0, one, far, out):
    out[...] = added(p0, one, far).astype(bf16)


def context_rows_kernel(flags, came, own, dy_ref, dy_full, dy0_full):
    per = dy_ref.shape[1] // 2
    zero = jnp.zeros((CTX, LANES), f32)
    for w in range(2):
        for c in range(per):
            at = (slice(w * CTX, (w + 1) * CTX), slice(c * LANES, (c + 1) * LANES))
            dy = came[at].astype(f32)
            dy_ref[:, w * per + c, :] = dy
            dy_full[:, w * per + c, :] = jnp.where(flags[0] == 1, dy, zero)
            dy_full[:, (2 + w) * per + c, :] = jnp.where(flags[0] == 1, zero, dy)
            dy0_full[:, w * per + c, :] = jnp.where(flags[1] == 0, own[at].astype(f32), zero)
            dy0_full[:, (2 + w) * per + c, :] = zero


def on_device(
    tokens,
    w_qkv,
    w_out,
    w_up,
    w_down,
    g_attn,
    g_mlp,
    ssm_rate,
    ssm_in,
    ssm_out,
    h_init,
    cotangent,
    d_h_ends,
):
    nd, ns = lax.axis_size("dp"), lax.axis_size("seq")
    ny = nd // 2
    dp, seq = lax.axis_index("dp"), lax.axis_index("seq")
    late = seq % 2 == 1
    block = seq // 2
    me = (seq % 2) * 2 + dp % 2
    idx = jnp.stack([me, dp // 2]).astype(jnp.int32)
    place = (seq * ny + dp // 2).astype(jnp.int32).reshape(1)
    half = (seq % 2).astype(jnp.int32).reshape(1)
    rows, dim = tokens.shape[1:]
    shard = w_qkv.shape[0]
    width = HEADS * HD // TEAM
    cols = dim // TEAM
    fb = w_down.shape[0] // TEAM
    tile = (dim // LANES, LANES)
    half_tile = (dim // LANES // 2, LANES)

    def like(shape, dtype):
        return jax.ShapeDtypeStruct(shape, dtype)


    share_attn, share_up, share_down = shares(idx, w_qkv, w_out, w_up, w_down, ny, ns)
    attn, up = Gathering(*share_attn, True), Gathering(*share_up, True)
    down = Gathering(*share_down, True)
    attn_pair = attn.step()
    x_blocks = gather_team(after(tokens[0], attn_pair))
    up_pair = up.step(attn_pair)
    attn_first = attn.rest()
    attn_own = attn.a
    down_pair = down.step(attn_first)
    attn_second = attn.step(up_pair)
    attn_third = attn.across(0)
    small = call(
        pack_kernel,
        "pack_small",
        jax.ShapeDtypeStruct((1, 3 * NST + 2, shard), bf16),
        after((ssm_rate.T, ssm_in.T, ssm_out.T, g_attn[None], g_mlp[None]), share_attn[1]),
        0,
    )
    for bit in [1] + high_bits("seq")[::-1]:
        got = swap(after(small, attn_own) if bit > 2 else small, "seq", bit)
        upper = (seq & bit) != 0
        small = jnp.concatenate([jnp.where(upper, got, small), jnp.where(upper, small, got)], axis=0)
    small = small.astype(f32)
    gain_one = small[:, 3 * NST].reshape(dim)
    gain_two = small[:, 3 * NST + 1].reshape(dim)
    params = small[:, : 3 * NST].transpose(1, 0, 2).reshape(3 * NST, dim)
    params = lax.dynamic_slice_in_dim(params, me * cols, cols, 1)
    params = jnp.broadcast_to(params[:, None], (3 * NST, TEAM, cols)).reshape((3, NST) + tile)
    rate, gin, gout = params[0], params[1], params[2]
    half_rate = rate[:, : tile[0] // 2]

    by_channel = like((NST, cols), f32)
    init, near_init, *end_cot = call(
        cut_states_kernel,
        "cut_states",
        (by_channel,) * 6,
        (idx, h_init[0].T, after(d_h_ends[0, 0].T, share_attn[1])),
    )
    init, init_twice, end_first, end_second = call(
        join_states_kernel,
        "join_states",
        tuple(like((NST,) + t, f32) for t in (half_tile, tile, half_tile, half_tile)),
        (half, init, swap_team(near_init, 1), *trade_team(end_cot)),
    )
    end_cot = [end_first, end_second]
    g_blocks = gather_team(after(cotangent[0], attn_first))

    def by_half(a, axis=1):
        n = a.shape[axis] // 2
        own, other = lax.slice_in_dim(a, 0, n, axis=axis), lax.slice_in_dim(a, n, 2 * n, axis=axis)
        return ordered([own, other], seq % 2)

    def by_owner(first, second):
        return jnp.concatenate(ordered([first, second], seq % 2), axis=1)

    inputs_low, inv_one, u = first_norm(idx, after(gain_one, attn_first), x_blocks)

    a = jnp.exp(-rate)
    s_mid, s_end = local_ends(u, a)
    attn_last = attn.across(1, s_end)
    up_first = up.rest((attn_second, s_end))
    decay = jnp.exp(-half_rate * rows)
    first_end, second_end = by_half(gin * s_end)
    span = 2 * rows

    def chain(inclusive, back, wait):
        exclusive, step = jnp.zeros_like(inclusive), 1
        while step < ns // 2:
            pairs = [(k, k + 2 * step) for k in range(ns - 2 * step)]
            got = lax.ppermute(inclusive, "seq", [(t, f) for f, t in pairs] if back else pairs)
            if step == 1:
                got = after(got, wait)
            exclusive = exclusive + jnp.exp(-half_rate * (span * (step - 1))) * got
            inclusive = inclusive + jnp.exp(-half_rate * (span * step)) * got
            step *= 2
        return exclusive

    entering = chain(after(decay * first_end + second_end, attn_third), False, (up_first, attn_last))
    state_zero = jnp.exp(-half_rate * (span * block).astype(f32)) * init + entering
    state_one = decay * state_zero + first_end
    state_two = decay * state_one + second_end
    state_in = by_owner(state_zero, state_one)
    ends = call(cut_ends_kernel, "cut_ends", (by_channel,) * TEAM, (half, state_one, state_two))
    ends = call(join_ends_kernel, "join_ends", like((NST, dim), f32), (idx, *trade_team(ends)))
    on_second = by_owner(jnp.zeros_like(init), jnp.ones_like(init))
    h_mid = jnp.exp(-rate * (rows - CTX)) * state_in + gin * s_mid
    h_mid = jnp.where(on_second > 0, h_mid, init_twice)
    y_first, y_second = contexts(half, u, a, gin * on_second, gout, h_mid)
    passed = lax.ppermute(y_second, "seq", [(k, k + 2) for k in range(ns - 2)])
    up_second = up.step(entering)
    up_third = up.across(0)
    places = jnp.stack([place[0], seq]).astype(jnp.int32)
    full_qkv, *full_out = place_weight(idx, places, [(attn.pieces, 0, 1, 0)], 3 * width)
    full_out = trade_team(full_out)
    context = jnp.where(block == 0, y_first, after(passed, (up_second, full_qkv, down_pair)))
    down_first = down.rest(passed)

    full_qkv = after(full_qkv, up_third)
    qkv = dot_nn(inputs_low, full_qkv).astype(bf16)
    context = after(gather_team(context), qkv)
    ctx_kv, context = call(
        context_kv_kernel,
        "context_kv",
        (like((2 * CTX, 2 * width), bf16), like((2 * CTX, dim), bf16)),
        (idx, full_qkv, *context),
    )
    attended = attend(half, qkv, ctx_kv)

    up_last = up.across(1, up_third)
    attended = after(attended, (g_blocks[2], down_first, up_last))
    down_second = down.step()
    down_third = down.across(0, up_last)
    attended_parts = call(out_kernel, "out_dot", part_types(rows, dim), (idx, attended, *full_out))
    attended_parts = sum_team(attended_parts, None, (down_second, down_third))
    down.across(1, down_third)
    (full_up,) = place_weight(idx, places, [(up.pieces, 0, 1, 0)])
    (full_down,) = place_weight(idx, places, [(down.pieces, 0, 1, 0)])

    hidden, inv_two, mlp_in = call(
        second_norm_kernel,
        "second_norm",
        (like((rows, dim), f32), like((rows, 1), f32), like((rows, dim), bf16)),
        (tokens[0], *attended_parts[:3], gain_two[None]),
        0,
    )
    mlp_in = gather_team(mlp_in)
    mlp_in = after(mlp_in, full_up)
    act, d_pre, *d_mlp = feed_forward(mlp_in, g_blocks, full_up, full_down)
    d_down = down_grad(act, g_blocks)
    reduction = HalvedReduction if (nd, ns) == (4, 8) else Reduction
    sum_down = reduction(d_down, place)
    sum_down.step()
    d_up = up_grad(mlp_in, after(d_pre, sum_down.sent))
    sum_up = reduction(d_up, place)
    sum_up.step()
    result = dot_parts("down_dot", after(act, sum_up.sent), full_down)
    d_mlp = sum_team(d_mlp, d_down, result)
    sum_down.step(d_mlp[3])
    d_hidden, d_hidden_low, d_gain_two = call(
        hidden_grad_kernel,
        "hidden_grad",
        (like((rows, dim), f32), like((rows, dim), bf16), like((1, dim), f32)),
        (after(cotangent[0], sum_down.sent), hidden, inv_two, gain_two[None], *d_mlp[:3]),
        0,
    )
    hidden_blocks = gather_team(d_hidden_low)
    sum_down.step(d_hidden)

    d_attended = call(
        attended_grad_kernel,
        "attended_grad",
        jax.ShapeDtypeStruct(attended.shape, bf16),
        (idx, after(full_out[0], sum_down.sent), *full_out[1:], *hidden_blocks),
    )
    d_out = call(
        out_grad_kernel,
        "out_grad",
        (jax.ShapeDtypeStruct((width, cols), bf16),) * TEAM,
        (idx, after(attended, d_attended), *hidden_blocks),
    )
    d_qkv, d_ctx_kv = attend_back(half, qkv, ctx_kv, after(d_attended, d_out))
    d_out = trade_team(d_out)
    sum_up.step(d_ctx_kv)
    sum_down.step(sum_up.sent)
    d_context = call(
        context_grad_kernel,
        "context_grad",
        part_types(2 * CTX, cols),
        (idx, after(d_ctx_kv, (sum_up.sent, sum_down.sent, d_out)), full_qkv),
    )
    d_attn = attn_grad(idx, inputs_low, after(d_qkv, d_context), context, d_ctx_kv, d_out)
    sum_attn = reduction(d_attn, place)
    sum_attn.step()
    d_context = sum_team(d_context, None, d_attn)
    d_context = call(context_sum_kernel, "context_sum", like((2 * CTX, cols), bf16), d_context[:3], 0)
    came = lax.ppermute(d_context, "seq", [(k + 2, k) for k in range(ns - 2)])
    flags = jnp.stack([seq % 2, block]).astype(jnp.int32)
    dy, dy_full, dy0_full = call(
        context_rows_kernel,
        "context_rows",
        (like((CTX,) + half_tile, f32), like((CTX,) + tile, f32), like((CTX,) + tile, f32)),
        (flags, after(came, (ends, sum_attn.sent)), d_context),
    )

    lam_mid = tail_adjoint(dy, a, gout)
    g_second = jnp.exp(-half_rate * (rows - CTX + 1)) * lam_mid + decay * end_cot[1]
    d_a, d_gout, g_init = first_context_back(after(dy0_full, lam_mid), a, gout, init_twice)
    d_down_pair = sum_down.last()
    leaving = chain(decay * (end_cot[0] + g_second), True, (g_init, d_down_pair[1], sum_attn.out if reduction is HalvedReduction else g_init))
    sum_up.step(leaving)
    sum_attn.step(sum_up.sent)
    result = sum_team(result, d_context)
    result = call(result_kernel, "result_sum", like((rows, dim), bf16), (hidden, *result[:3]), 0)
    lam_end = by_owner(end_cot[0] + g_second + decay * leaving, end_cot[1] + leaving)
    du, d_gin, d_a, d_gout, g_in = ssm_back(
        u, dy_full, a, gin, gout, state_in, after(lam_end, sum_attn.sent), d_a, d_gout
    )
    g_first = by_half(g_in)[0]
    d_init = g_init[:, : tile[0] // 2] + jnp.where(block == 0, g_first, jnp.zeros_like(g_first))
    d_rate = -a * d_a

    sum_up.step(du)
    *d_inputs, d_gain_one = call(
        inputs_grad_kernel,
        "inputs_grad",
        part_types(rows, dim) + (jax.ShapeDtypeStruct((1, dim), f32),),
        (idx, d_qkv, full_qkv, after(du, (result, sum_up.sent)), inv_one, *x_blocks),
        scratch_shapes=[pltpu.VMEM((rows, dim), f32)],
    )
    sum_attn.step(d_gain_one)
    d_inputs = after(d_inputs, sum_attn.sent)
    *d_inputs, d_inputs_far = sum_team(d_inputs)
    d_up_pair = after(sum_up.last(), d_inputs_far)
    d_down = spread_weight("down", d_down_pair, idx, [w_down.shape])[0]
    if fb % LANES:
        d_up = spread_narrow(d_up_pair, idx, w_up.shape, fb)
    else:
        d_up = spread_weight("up", d_up_pair, idx, [w_up.shape], fb)[0]
    d_tokens = call(
        tokens_grad_kernel,
        "tokens_grad",
        like((rows, dim), bf16),
        (d_hidden, tokens[0], inv_one[:rows], gain_one[None], *d_inputs),
        0,
    )

    d_params = after(jnp.stack([d_rate, d_gin, d_gout]), d_gain_one)
    d_params = d_params.reshape(3 * NST, TEAM, cols).sum(1)
    d_gains = jnp.concatenate([d_gain_one[0], d_gain_two[0]])
    pack = [d_params.reshape(-1, LANES), d_gains.reshape(-1, LANES), d_init.reshape(-1, LANES)]
    pack = after(jnp.concatenate(pack, axis=0), d_inputs_far)
    for n, bit in enumerate(high_bits("seq")):
        if n == 0:
            pack = after(pack, (sum_attn.step(), d_tokens))
        if n == 1:
            pack = after(pack, d_down)
        pack = pack + swap(pack, "seq", bit)
    one, two = 3 * NST * cols // LANES, 3 * NST * cols // LANES + 2 * dim // LANES
    shared = pack[:two]
    shared = after(shared, d_up)
    for bit in high_bits("dp"):
        shared = shared + swap(shared, "dp", bit)
    packs = gather_team(jnp.concatenate([shared, pack[two:]], axis=0))
    if shard == LANES:
        spots = jnp.stack([me ^ (seq * shard // cols), seq]).astype(jnp.int32)
        gains, *d_params, state_grad = call(
            small_kernel,
            "small_grads",
            (like((2, shard), f32),) + (like((NST, shard), f32),) * 4,
            (spots, *packs),
        )
        d_params, state_grad = [p.T for p in d_params], state_grad.T[None]
    else:
        packs = jnp.stack(packs)
        gains = packs[:, one:two].sum(0).reshape(2, ns, shard)
        gains = pick(gains, seq, 1)
        member = me ^ (seq * shard // cols)
        inner = seq * shard % cols
        chosen = pick(packs, member)
        d_params = chosen[:one].reshape(3 * NST, cols)
        d_params = lax.dynamic_slice_in_dim(d_params, inner, shard, 1).reshape(3, NST, shard)
        d_params = d_params.transpose(0, 2, 1)
        state_grad = chosen[two:].reshape(NST, 2, cols)
        state_grad = pick(state_grad, member % 2, 1)
        state_grad = lax.dynamic_slice_in_dim(state_grad, inner, shard, 1).T[None]

    d_wqkv, d_out = spread_weight("attn", sum_attn.last(), idx, [w_qkv.shape, w_out.shape])
    return (
        result[None],
        d_tokens[None],
        d_wqkv,
        d_out,
        d_up,
        d_down,
        gains[0],
        gains[1],
        d_params[0],
        d_params[1],
        d_params[2],
        state_grad,
        ends.T[None, None],
    )


def solution(mesh):
    return jax.shard_map(
        on_device,
        mesh=mesh,
        in_specs=(
            P("dp", "seq", None),
            P("seq", None),
            P("seq", None),
            P("seq", None),
            P("seq", None),
            P("seq"),
            P("seq"),
            P("seq", None),
            P("seq", None),
            P("seq", None),
            P("dp", None, None),
            P("dp", "seq", None),
            P("dp", "seq", None, None),
        ),
        out_specs=(
            P("dp", "seq", None),
            P("dp", "seq", None),
            P("seq", None),
            P("seq", None),
            P("seq", None),
            P("seq", None),
            P("seq"),
            P("seq"),
            P("seq", None),
            P("seq", None),
            P("seq", None),
            P("dp", "seq", None),
            P("dp", "seq", None, None),
        ),
        check_vma=False,
    )
```

```python
import functools
import math

import jax
import jax.numpy as jnp
from jax import lax
from jax.experimental import pallas as pl
from jax.experimental.pallas import tpu as pltpu
from jax.sharding import PartitionSpec as P

HEADS = 8
HD = 128
CTX = 128
NST = 16
LANES = 128
GROUP = 4
TEAM = 4

epsilon = 1e-05
far_below = -1e30
bf16 = jnp.bfloat16
f32 = jnp.float32


def swap(a, axis, bit):
    return lax.ppermute(a, axis, [(k, k ^ bit) for k in range(lax.axis_size(axis))])


def swap_team(a, r):
    if r == 1:
        return swap(a, "dp", 1)
    if r == 2:
        return swap(a, "seq", 1)
    nd, ns = lax.axis_size("dp"), lax.axis_size("seq")
    pairs = [(d * ns + k, (d ^ 1) * ns + (k ^ 1)) for d in range(nd) for k in range(ns)]
    return lax.ppermute(a, ("dp", "seq"), pairs)


def gather_team(a):
    far = swap_team(a, 2)
    return [a, swap_team(a, 1), far, swap_team(far, 1)]


def far_kernel(mine, came, out):
    out[...] = (mine[...] + came[...].astype(f32)).astype(bf16)


def sum_team(parts, middle=None, end=None):
    one, three = swap_team(parts[1], 1), swap_team(parts[3], 1)
    if middle is not None:
        three = after(three, middle)
    shape = jax.ShapeDtypeStruct(three.shape, bf16)
    near = call(far_kernel, "far_sum", shape, (parts[2], three), 0)
    far = swap_team(near, 2)
    if end is not None:
        one, far = after((one, far), end)
    return parts[0], one, far, near


def trade_team(parts):
    return [parts[0]] + [swap_team(parts[r], r) for r in (1, 2, 3)]


def high_bits(axis):
    size = lax.axis_size(axis)
    return [1 << k for k in reversed(range(1, size.bit_length() - 1))]


def pick(a, index, axis=0):
    return lax.dynamic_index_in_dim(a, index, axis, False)


def ordered(blocks, index):
    bit = len(blocks) // 2
    while bit:
        flip = (index & bit) != 0
        blocks = [jnp.where(flip, blocks[r ^ bit], blocks[r]) for r in range(len(blocks))]
        bit //= 2
    return blocks


def after(x, *others):
    return lax.optimization_barrier((x, others))[0]


def whole_spec():
    return pl.BlockSpec(memory_space=pltpu.VMEM)


def scalar_spec():
    return pl.BlockSpec(memory_space=pltpu.SMEM)


def any_spec():
    return pl.BlockSpec(memory_space=pl.ANY)


BIG = pltpu.CompilerParams(vmem_limit_bytes=32 * 2**20)
MIDDLE = pltpu.CompilerParams(vmem_limit_bytes=24 * 2**20)
SMALL = pltpu.CompilerParams(vmem_limit_bytes=20 * 2**20)


def block_of(shape):
    return pl.BlockSpec(shape, lambda *k: (0,) * len(shape), pipeline_mode=pl.Buffered(1))


def call(kernel, name, out_shape, args, scalars=1, **more):
    specs = [scalar_spec()] * scalars + [block_of(a.shape) for a in args[scalars:]]
    return pl.pallas_call(
        kernel,
        grid=(1,),
        out_shape=out_shape,
        in_specs=specs,
        out_specs=jax.tree.map(lambda o: block_of(o.shape), out_shape),
        compiler_params=MIDDLE,
        name=name,
        **more,
    )(*args)


def share_kernel(spots, copies, idx, *refs):
    ins, outs, sem = refs[:spots], refs[spots:-1], refs[-1]
    flying = []
    for n, (src, dst, rows_at, cols_at, size, to) in enumerate(copies):
        row = pl.multiple_of(rows_at(idx), 16)
        col = pl.multiple_of(cols_at(idx), LANES)
        flying.append(
            pltpu.make_async_copy(
                ins[src].at[pl.ds(row, size[0]), pl.ds(col, size[1])],
                outs[dst].at[:, pl.ds(to, size[1])],
                sem.at[n],
            )
        )
    for one in flying:
        one.start()
    for one in flying:
        one.wait()


def shares(idx, w_qkv, w_out, w_up, w_down, ny, ns):
    shard, dim = w_out.shape
    quarter = dim // TEAM
    rows, fb = shard // ny, w_down.shape[0] // TEAM
    low = fb // ny
    copies = []
    for away in (0, 1):
        def who(i, away=away):
            return i[0] ^ (2 * away)

        for part in range(3):
            copies.append((0, away, lambda i: i[1] * rows,
                           lambda i, w=who, p=part: p * dim + w(i) * quarter, (rows, quarter), part * quarter))
        copies.append((1, away, lambda i: i[1] * rows,
                       lambda i, w=who: w(i) * quarter, (rows, quarter), 3 * quarter))
        if fb % LANES == 0:
            for k in range(ns):
                copies.append((2, 2 + away, lambda i: i[1] * rows,
                               lambda i, w=who, k=k: (k * TEAM + w(i)) * fb, (rows, fb), k * fb))
        copies.append((3, 4 + away, lambda i, w=who: w(i) * fb + i[1] * low, lambda i: 0, (low, dim), 0))
    sizes = [(rows, dim)] * 2 + [(rows, ns * fb)] * 2 + [(low, dim)] * 2
    out = pl.pallas_call(
        functools.partial(share_kernel, 4, copies),
        out_shape=[jax.ShapeDtypeStruct(s, bf16) for s in sizes],
        in_specs=[scalar_spec()] + [any_spec()] * 4,
        out_specs=[whole_spec()] * 6,
        scratch_shapes=[pltpu.SemaphoreType.DMA((len(copies),))],
        name="shares",
    )(idx, w_qkv, w_out, w_up, w_down)
    out = [list(out[k : k + 2]) for k in (0, 2, 4)]
    if fb % LANES:
        mine = lax.dynamic_slice_in_dim(w_up, idx[1] * rows, rows, 0).reshape(rows, ns, TEAM, fb)
        out[1] = [pick(mine, idx[0] ^ r, 2).reshape(rows, ns * fb) for r in (0, 2)]
    return out


def place_kernel(maps, cuts, idx, places, *refs):
    ins, outs = refs[: len(maps)], refs[len(maps) :]
    for ref, (which, order, step, offset) in zip(ins, maps):
        rows = ref.shape[1]
        for k, r in enumerate(order):
            at = pl.multiple_of(((places[which] ^ r) * step + offset) * rows, 16)
            if cuts:
                width = outs[0].shape[1]
                outs[0][pl.ds(at, rows), :] = ref[k, :, :width]
                outs[-1][pl.ds(at, rows), :] = ref[k, :, width:]
            else:
                outs[0][pl.ds(at, rows), :] = ref[k]
    for r in range(cuts):
        rows = outs[1].shape[0]
        at = pl.multiple_of((idx[0] ^ r) * rows, 16)
        outs[1 + r][...] = outs[-1][pl.ds(at, rows), :]


def append_kernel(a_ref, b_ref, out):
    count = a_ref.shape[0]
    out[:count] = a_ref[...]
    out[count:] = b_ref[...]


def append(a, b):
    shape = jax.ShapeDtypeStruct((a.shape[0] + b.shape[0],) + a.shape[1:], bf16)
    return call(append_kernel, "append", shape, (a, b), 0)


class Gathering:
    def __init__(self, own, away, parted):
        ny = lax.axis_size("dp") // 2 if parted else 1
        self.seq_steps = [(1, ny)] + [(bit, bit * ny) for bit in high_bits("seq")]
        self.a, self.away, self.order, self.n = own[None], away[None], [0], 0

    def step(self, wait=None):
        bit, weight = self.seq_steps[self.n]
        if self.n:
            self.a = append(self.a, self.came)
            self.order = self.order + [r | self.seq_steps[self.n - 1][1] for r in self.order]
        sent = self.a if self.n else self.away
        self.came = swap(sent if wait is None else after(sent, wait), "seq", bit)
        self.n += 1
        if self.n == len(self.seq_steps):
            last = [r | weight for r in self.order]
            self.pieces = [(self.a, self.order), (self.came, last)]
        return self.came

    def rest(self, wait=None):
        while self.n < len(self.seq_steps) - 1:
            self.step(wait)
            wait = None
        return self.came

    def across(self, k, wait=None):
        new = [self.pieces[k]]
        for bit in high_bits("dp"):
            for a, order in list(new):
                a = a if wait is None else after(a, wait)
                new.append((swap(a, "dp", bit), [r | (bit // 2) for r in order]))
        self.pieces += new[1:]
        return new[1][0]


def place_weight(idx, places, groups, width=None):
    arrays = [a for pieces, *_ in groups for a, _ in pieces]
    maps = [(which, order, step, at) for pieces, which, step, at in groups for _, order in pieces]
    rows, cols = sum(a.shape[0] * a.shape[1] for a in arrays), arrays[0].shape[2]
    shapes = [(rows, cols)]
    scratch = []
    if width:
        shapes = [(rows, width)] + [(rows // TEAM, cols - width)] * TEAM
        scratch = [pltpu.VMEM((rows, cols - width), bf16)]
    return call(
        functools.partial(place_kernel, maps, TEAM if width else 0),
        "place_weight",
        [jax.ShapeDtypeStruct(s, bf16) for s in shapes],
        (idx, places, *arrays),
        2,
        scratch_shapes=scratch,
    )


def attn_grad_kernel(idx, x_ref, dq_ref, ctx_ref, dctx_ref, *refs):
    parts, out = refs[:TEAM], refs[TEAM]
    k = pl.program_id(0)
    width = dq_ref.shape[1] // 3
    grad = dot_tn(x_ref[...], dq_ref[...])
    far = dot_tn(ctx_ref[...], dctx_ref[...])
    out[:, :width] = grad[:, :width].astype(bf16)
    out[:, width : 3 * width] = (grad[:, width:] + far).astype(bf16)
    per = parts[0].shape[0] // out.shape[0]
    member = (k // per) ^ idx[0]
    at = pl.multiple_of((k % per) * out.shape[0], 16)
    for r in range(TEAM):
        @pl.when(member == r)
        def _(r=r):
            out[:, 3 * width :] = parts[r][pl.ds(at, out.shape[0]), :]


def attn_grad(idx, inputs, d_qkv, context, d_ctx_kv, parts):
    dim, step = inputs.shape[1], LANES
    return pl.pallas_call(
        attn_grad_kernel,
        grid=(dim // step,),
        out_shape=jax.ShapeDtypeStruct((dim, d_qkv.shape[1] + parts[0].shape[1]), bf16),
        in_specs=[
            scalar_spec(),
            pl.BlockSpec((inputs.shape[0], step), lambda k: (0, k)),
            block_of(d_qkv.shape),
            pl.BlockSpec((context.shape[0], step), lambda k: (0, k)),
            block_of(d_ctx_kv.shape),
        ]
        + [block_of(p.shape) for p in parts],
        out_specs=pl.BlockSpec((step, d_qkv.shape[1] + parts[0].shape[1]), lambda k: (k, 0)),
        compiler_params=SMALL,
        name="attn_grad",
    )(idx, inputs, d_qkv, context, d_ctx_kv, *parts)


def insert_bit(k, at, bit):
    return ((k >> at) << (at + 1)) | (bit << at) | (k & ((1 << at) - 1))


def split_kernel(before, side, at, place, x_ref, *refs):
    here = (place[0] >> side) & 1
    if before is None:
        (away_ref,) = refs
        for k in range(away_ref.shape[0]):
            away_ref[k] = x_ref[insert_bit(k, at, 1 - here)]
        return
    recv_ref, keep_ref, away_ref = refs

    def total(k):
        j = k if before is True else insert_bit(k, before[1], (place[0] >> before[0]) & 1)
        return (x_ref[j].astype(f32) + recv_ref[k].astype(f32)).astype(bf16)

    for k in range(away_ref.shape[0]):
        away_ref[k] = total(insert_bit(k, at, 1 - here))
        keep_ref[k] = total(insert_bit(k, at, here))


class Reduction:
    def __init__(self, x, place):
        ny = lax.axis_size("dp") // 2
        ns = lax.axis_size("seq")
        y_bits = ny.bit_length() - 1
        steps = [("dp", bit, (bit // 2).bit_length() - 1, 0) for bit in reversed(high_bits("dp"))]
        steps += [("seq", b, (b * ny).bit_length() - 1, 1) for b in reversed(high_bits("seq"))]
        self.steps = steps + [("seq", 1, y_bits, 0)]
        self.place, self.n, self.came = place, 0, None
        self.kept = x.reshape(ns * ny, -1, x.shape[1])

    def step(self, wait=None):
        n, x, recv = self.n, self.kept, self.came
        axis, bit, side, at = self.steps[n]
        if n == 0 and wait is not None:
            x = after(x, wait)
        elif wait is not None:
            recv = after(recv, wait)
        before = None if n == 0 else (self.steps[0][2:] if n == 1 else True)
        count = x.shape[0] // 2 if n == 0 else recv.shape[0] // 2
        half = jax.ShapeDtypeStruct((count,) + x.shape[1:], bf16)
        out = call(
            functools.partial(split_kernel, before, side, at),
            "split_sum",
            [half] if n == 0 else [half, half],
            (self.place, x) if n == 0 else (self.place, x, recv),
        )
        if n:
            self.kept = out[0]
        self.sent = out[-1]
        self.came = swap(self.sent, axis, bit)
        self.n += 1
        return self.sent

    def last(self, wait=None):
        while self.n < len(self.steps):
            self.step(wait)
            wait = None
        return self.kept, self.came


def halves_kernel(place, x_ref, out_ref, in_ref):
    y, z = place[0] & 1, (place[0] >> 2) & 1
    for k in range(out_ref.shape[0]):
        low = ((k >> 1) << 3) | ((k & 1) << 1) | (1 - y)
        out_ref[k] = x_ref[low | ((1 - z) << 2)]
        in_ref[k] = x_ref[low | (z << 2)]


def leave_kernel(place, x_ref, came_ref, out_ref):
    y, z = place[0] & 1, (place[0] >> 2) & 1
    for k in range(out_ref.shape[0]):
        mine = x_ref[((k >> 1) << 3) | ((1 - z) << 2) | ((k & 1) << 1) | y]
        out_ref[k] = (mine.astype(f32) + came_ref[k].astype(f32)).astype(bf16)


def stay_kernel(place, x_ref, came_ref, near_ref, keep_ref, out_ref):
    y, z, far = place[0] & 1, (place[0] >> 2) & 1, (place[0] >> 3) & 1

    def total(k):
        mine = x_ref[((k >> 1) << 3) | (z << 2) | ((k & 1) << 1) | y]
        return (mine.astype(f32) + came_ref[k].astype(f32) + near_ref[k].astype(f32)).astype(bf16)

    for k in (0, 1):
        keep_ref[k] = total((far << 1) | k)
        out_ref[k] = total(((1 - far) << 1) | k)


class HalvedReduction(Reduction):
    def step(self, wait=None):
        n = self.n
        if n > 2:
            self.steps = [None, None, None, ("seq", 1, 1, 0)]
            return super().step(wait)
        x = self.kept
        four = jax.ShapeDtypeStruct((x.shape[0] // 4,) + x.shape[1:], bf16)
        two = jax.ShapeDtypeStruct((2,) + x.shape[1:], bf16)
        if n == 0:
            x = x if wait is None else after(x, wait)
            out, stay = call(halves_kernel, "halves", (four, four), (self.place, x))
            self.sent = out
            self.out, self.stay = swap(out, "dp", 2), swap(stay, "dp", 2)
        elif n == 1:
            came = self.out if wait is None else after(self.out, wait)
            self.sent = call(leave_kernel, "leave_sum", four, (self.place, x, came))
            self.near = swap(self.sent, "seq", 2)
        else:
            came = self.near if wait is None else after(self.near, wait)
            args = (self.place, x, self.stay, came)
            self.kept, self.sent = call(stay_kernel, "stay_sum", (two, two), args)
            self.came = swap(self.sent, "seq", 4)
        self.n += 1
        return self.sent


def final_kernel(kind, fb, idx, mine_ref, other_ref, *outs):
    count, rows, width = mine_ref.shape
    for k in range(count):
        row = pl.multiple_of((idx[1] ^ (k // 2)) * rows, 16)
        for core, ref in enumerate((mine_ref, other_ref)):
            member = idx[0] ^ (2 * (k % 2) + core)
            if kind == "down":
                at = pl.multiple_of(member * (rows * count // 2) + row, 16)
                outs[0][pl.ds(at, rows), :] = ref[k].astype(f32)
            elif kind == "up":
                for n in range(width // fb):
                    col = pl.multiple_of((n * TEAM + member) * fb, LANES)
                    block = ref[k, :, n * fb : (n + 1) * fb]
                    outs[0][pl.ds(row, rows), pl.ds(col, fb)] = block.astype(f32)
            else:
                dim = outs[1].shape[1]
                quarter = dim // TEAM
                for part in range(4):
                    to = outs[0] if part < 3 else outs[1]
                    col = pl.multiple_of((part % 3) * dim * (part < 3) + member * quarter, LANES)
                    block = ref[k, :, part * quarter : (part + 1) * quarter]
                    to[pl.ds(row, rows), pl.ds(col, quarter)] = block.astype(f32)


def spread_places(pair):
    blocks = {0: append(*pair)}
    for bit in high_bits("dp"):
        for m in list(blocks):
            blocks[m | (bit // 2)] = swap(blocks[m], "dp", bit)
    return [blocks[m] for m in range(len(blocks))]


def spread_cores(blocks):
    while len(blocks) > 1:
        blocks = [append(a, b) for a, b in zip(blocks[0::2], blocks[1::2])]
    return blocks[0], swap(blocks[0], "dp", 1)


def spread_weight(kind, blocks, idx, shapes, fb=LANES):
    return call(
        functools.partial(final_kernel, kind, fb),
        "final_" + kind,
        [jax.ShapeDtypeStruct(s, f32) for s in shapes],
        (idx, *spread_cores(blocks)),
    )


def spread_narrow(blocks, idx, shape, fb):
    mine, other = spread_cores(blocks)
    teams = [mine[0::2], other[0::2], mine[1::2], other[1::2]]
    teams = jnp.stack(ordered(teams, idx[0]))
    rows = jnp.stack(ordered([teams[:, m] for m in range(teams.shape[1])], idx[1]), axis=1)
    rows = rows.reshape(TEAM, shape[0], shape[1] // (TEAM * fb), fb).transpose(1, 2, 0, 3)
    return rows.reshape(shape).astype(f32)


def ends_kernel(mid, u_ref, a_ref, mid_ref, end_ref):
    rows = u_ref.shape[0]
    a = [a_ref[n] for n in range(NST)]

    def eight(k, s):
        for t in range(8):
            u = u_ref[k * 8 + t]
            s = tuple(a[n] * s[n] + u for n in range(NST))
        return s

    zero = tuple(jnp.zeros_like(a[0]) for _ in range(NST))
    s = lax.fori_loop(0, mid // 8, eight, zero)
    for n in range(NST):
        mid_ref[n] = s[n]
    s = lax.fori_loop(mid // 8, rows // 8, eight, s)
    for n in range(NST):
        end_ref[n] = s[n]


def local_ends(u, a):
    shape = jax.ShapeDtypeStruct(a.shape, f32)
    kernel = functools.partial(ends_kernel, u.shape[0] - CTX)
    return call(kernel, "ssm_ends", (shape, shape), (u, a), 0)


def context_kernel(mid, late, u_ref, a_ref, gin_ref, gout_ref, h_ref, first_ref, second_ref, y_ref):
    half = NST // 2
    for base in (0, half):
        ns = range(base, base + half)
        a = [a_ref[n] for n in ns]
        gin = [gin_ref[n] for n in ns]
        gout = [gout_ref[n] for n in ns]

        def step(k, h):
            for t in range(4):
                p = k * 4 + t
                u = u_ref[mid + p]
                h = tuple(a[n] * h[n] + gin[n] * u for n in range(half))
                y = functools.reduce(jnp.add, [gout[n] * h[n] for n in range(half)])
                y_ref[p] = y if base == 0 else y_ref[p] + y
            return h

        lax.fori_loop(0, CTX // 4, step, tuple(h_ref[n] for n in ns))
    per = y_ref.shape[1] // TEAM
    for w in range(2):
        for c in range(per):
            own, other = y_ref[:, w * per + c, :], y_ref[:, (2 + w) * per + c, :]
            at = (slice(w * CTX, (w + 1) * CTX), slice(c * LANES, (c + 1) * LANES))
            first_ref[at] = jnp.where(late[0] == 1, other, own).astype(bf16)
            second_ref[at] = jnp.where(late[0] == 1, own, other).astype(bf16)


def contexts(half, u, a, gin, gout, h_mid):
    shape = jax.ShapeDtypeStruct((2 * CTX, u.shape[1] * LANES // TEAM), bf16)
    return call(
        functools.partial(context_kernel, u.shape[0] - CTX),
        "ssm_context",
        (shape, shape),
        (half, u, a, gin, gout, h_mid),
        scratch_shapes=[pltpu.VMEM((CTX,) + u.shape[1:], f32)],
    )


def tail_kernel(dy_ref, a_ref, gout_ref, lam_ref):
    half = dy_ref.shape[1]
    a = [a_ref[n, :half] for n in range(NST)]
    gout = [gout_ref[n, :half] for n in range(NST)]

    def eight(k, lam):
        for t in range(8):
            dy = dy_ref[CTX - 1 - (k * 8 + t)]
            lam = tuple(a[n] * lam[n] + gout[n] * dy for n in range(NST))
        return lam

    lam = lax.fori_loop(0, CTX // 8, eight, tuple(jnp.zeros_like(a[0]) for _ in range(NST)))
    for n in range(NST):
        lam_ref[n] = lam[n]


def tail_adjoint(dy, a, gout):
    shape = jax.ShapeDtypeStruct((NST,) + dy.shape[1:], f32)
    return call(tail_kernel, "ssm_tail", shape, (dy, a, gout), 0)


def first_context_kernel(dy0_ref, a_ref, gout_ref, init_ref, da_ref, dgout_ref, g0_ref, hs):
    half = a_ref.shape[1] // 2
    ns = range(a_ref.shape[0] // 2)

    def paired(ref):
        return [jnp.concatenate([ref[2 * n, :half], ref[2 * n + 1, :half]], axis=0) for n in ns]

    a, gout, init = paired(a_ref), paired(gout_ref), paired(init_ref)
    zero = tuple(jnp.zeros_like(a[0]) for _ in ns)

    def ahead(k, h):
        for t in range(8):
            h = tuple(a[n] * h[n] for n in ns)
            for n in ns:
                hs[k * 8 + t + 1, n] = h[n]
        return h

    h = tuple(init)
    for n in ns:
        hs[0, n] = h[n]
    lax.fori_loop(0, CTX // 8, ahead, h)

    def back(k, carry):
        mu, da, dgout = carry
        for t in range(4):
            q = CTX - 1 - (k * 4 + t)
            dy = dy0_ref[q]
            mu = tuple(mu[n] + gout[n] * dy for n in ns)
            dgout = tuple(dgout[n] + dy * hs[q + 1, n] for n in ns)
            da = tuple(da[n] + mu[n] * hs[q, n] for n in ns)
            mu = tuple(a[n] * mu[n] for n in ns)
        return mu, da, dgout

    results = lax.fori_loop(0, CTX // 4, back, (zero, zero, zero))
    rest = jnp.zeros_like(a[0][:half])
    for ref, values in zip((g0_ref, da_ref, dgout_ref), results):
        for n in ns:
            ref[2 * n] = jnp.concatenate([values[n][:half], rest], axis=0)
            ref[2 * n + 1] = jnp.concatenate([values[n][half:], rest], axis=0)


def first_context_back(dy0, a, gout, h_init):
    tile = dy0.shape[1:]
    states = pl.BlockSpec((2 * GROUP,) + tile, lambda g: (g, 0, 0))
    return pl.pallas_call(
        first_context_kernel,
        grid=(NST // (2 * GROUP),),
        out_shape=(jax.ShapeDtypeStruct(a.shape, f32),) * 3,
        in_specs=[pl.BlockSpec(dy0.shape, lambda g: (0, 0, 0))] + [states] * 3,
        out_specs=(states,) * 3,
        scratch_shapes=[pltpu.VMEM((CTX + 1, GROUP) + tile, f32)],
        name="first_context",
    )(dy0, a, gout, h_init)


def back_kernel(
    u_ref, dy_ref, a_ref, gin_ref, gout_ref, h_ref, lam_ref, da0_ref, dgout0_ref,
    du_ref, dgin_ref, da_ref, dgout_ref, g_ref, hs,
):
    first = pl.program_id(0) == 0
    rows = u_ref.shape[0]
    mid = rows - CTX
    ns = range(GROUP)
    a = [a_ref[n] for n in ns]
    gin = [gin_ref[n] for n in ns]
    gout = [gout_ref[n] for n in ns]
    zero = tuple(jnp.zeros_like(a[0]) for _ in ns)

    def ahead(k, h):
        for t in range(8):
            p = k * 8 + t
            u = u_ref[p]
            h = tuple(a[n] * h[n] + gin[n] * u for n in ns)
            for n in ns:
                hs[p + 1, n] = h[n]
        return h

    h = tuple(h_ref[n] for n in ns)
    for n in ns:
        hs[0, n] = h[n]
    lax.fori_loop(0, rows // 8, ahead, h)

    def tail(k, carry):
        lam, dgin, da, dgout = carry
        for t in range(4):
            q = CTX - 1 - (k * 4 + t)
            p = mid + q
            dy, u = dy_ref[q], u_ref[p]
            lam = tuple(lam[n] + gout[n] * dy for n in ns)
            dgout = tuple(dgout[n] + dy * hs[p + 1, n] for n in ns)
            dgin = tuple(dgin[n] + lam[n] * u for n in ns)
            da = tuple(da[n] + lam[n] * hs[p, n] for n in ns)
            du = functools.reduce(jnp.add, [gin[n] * lam[n] for n in ns])
            du_ref[p] = jnp.where(first, du, du_ref[p] + du)
            lam = tuple(a[n] * lam[n] for n in ns)
        return lam, dgin, da, dgout

    def head(k, carry):
        lam, dgin, da = carry
        for t in range(4):
            p = mid - 1 - (k * 4 + t)
            u = u_ref[p]
            dgin = tuple(dgin[n] + lam[n] * u for n in ns)
            da = tuple(da[n] + lam[n] * hs[p, n] for n in ns)
            du = functools.reduce(jnp.add, [gin[n] * lam[n] for n in ns])
            du_ref[p] = jnp.where(first, du, du_ref[p] + du)
            lam = tuple(a[n] * lam[n] for n in ns)
        return lam, dgin, da

    lam = tuple(lam_ref[n] for n in ns)
    da0, dgout0 = tuple(da0_ref[n] for n in ns), tuple(dgout0_ref[n] for n in ns)
    lam, dgin, da, dgout = lax.fori_loop(0, CTX // 4, tail, (lam, zero, da0, dgout0))
    lam, dgin, da = lax.fori_loop(0, mid // 4, head, (lam, dgin, da))
    for n in ns:
        g_ref[n] = lam[n]
        dgin_ref[n] = dgin[n]
        da_ref[n] = da[n]
        dgout_ref[n] = dgout[n]


def ssm_back(u, dy, a, gin, gout, state_in, lam_end, da0, dgout0):
    tile = u.shape[1:]
    states = pl.BlockSpec((GROUP,) + tile, lambda g: (g, 0, 0))
    rows = pl.BlockSpec(u.shape, lambda g: (0, 0, 0))
    tail = pl.BlockSpec(dy.shape, lambda g: (0, 0, 0))
    out = jax.ShapeDtypeStruct(a.shape, f32)
    return pl.pallas_call(
        back_kernel,
        grid=(NST // GROUP,),
        out_shape=(jax.ShapeDtypeStruct(u.shape, f32),) + (out,) * 4,
        in_specs=[rows, tail] + [states] * 7,
        out_specs=(rows,) + (states,) * 4,
        scratch_shapes=[pltpu.VMEM((u.shape[0] + 1, GROUP) + tile, f32)],
        compiler_params=SMALL,
        name="ssm_back",
    )(u, dy, a, gin, gout, state_in, lam_end, da0, dgout0)


def dot_nt(x, y):
    return lax.dot_general(x, y, (((1,), (1,)), ((), ())), preferred_element_type=f32)


def dot_nn(x, y):
    return jnp.dot(x, y, preferred_element_type=f32)


def dot_tn(x, y):
    return lax.dot_general(x, y, (((0,), (0,)), ((), ())), preferred_element_type=f32)


def softmax_parts(q, keys):
    rows = q.shape[0]
    scores = [dot_nt(q, k) * (1.0 / math.sqrt(HD)) for k in keys]
    at = lax.broadcasted_iota(jnp.int32, (rows, rows), 0)
    to = lax.broadcasted_iota(jnp.int32, (rows, rows), 1)
    scores[-1] = jnp.where(to <= at, scores[-1], far_below)
    top = functools.reduce(jnp.maximum, [jnp.max(s, axis=-1, keepdims=True) for s in scores])
    es = [jnp.exp(s - top) for s in scores]
    total = functools.reduce(jnp.add, [jnp.sum(e, axis=-1, keepdims=True) for e in es])
    return [e / total for e in es]


def attend_kernel(half_ref, q0, q1, k0, k1, v0, v1, kc, vc, out_ref):
    w, h = pl.program_id(0), pl.program_id(1)
    rows = q0.shape[0]
    for half, q, keys, values in ((0, q0, (kc, k0), (vc, v0)), (1, q1, (kc, k0, k1), (vc, v0, v1))):
        probs = softmax_parts(q[...], [k[...] for k in keys])
        out = [dot_nn(p.astype(bf16), v[...]) for p, v in zip(probs, values)]
        at = pl.multiple_of(((half ^ half_ref[0]) * 2 + w) * rows, 16)
        col = pl.multiple_of(h * HD, LANES)
        out_ref[pl.ds(at, rows), pl.ds(col, HD)] = functools.reduce(jnp.add, out).astype(bf16)


def attend_back_kernel(
    half_ref, q0, q1, k0, k1, v0, v1, kc, vc, do0, do1, dqkv_ref, dctx_ref
):
    w, h = pl.program_id(0), pl.program_id(1)
    rows, heads = q0.shape[0], pl.num_programs(1)
    scale = 1.0 / math.sqrt(HD)
    dk, dv = [0.0, 0.0, 0.0], [0.0, 0.0, 0.0]

    def row_of(half):
        return pl.multiple_of(((half ^ half_ref[0]) * 2 + w) * rows, 16)

    def col_of(part):
        return pl.multiple_of((part * heads + h) * HD, LANES)

    cases = ((0, q0, do0, (kc, k0), (vc, v0)), (1, q1, do1, (kc, k0, k1), (vc, v0, v1)))
    for half, q, do, keys, values in cases:
        query, d_out = q[...], do[...]
        probs = softmax_parts(query, [k[...] for k in keys])
        d_probs = [dot_nt(d_out, v[...]) for v in values]
        sums = [jnp.sum(p * d, axis=-1, keepdims=True) for p, d in zip(probs, d_probs)]
        delta = functools.reduce(jnp.add, sums)
        d_scores = [(p * (d - delta)).astype(bf16) for p, d in zip(probs, d_probs)]
        dq = functools.reduce(jnp.add, [dot_nn(d, k[...]) for d, k in zip(d_scores, keys)])
        dqkv_ref[pl.ds(row_of(half), rows), pl.ds(col_of(0), HD)] = (dq * scale).astype(bf16)
        for n, (d, p) in enumerate(zip(d_scores, probs)):
            dk[n] = dk[n] + dot_tn(d, query)
            dv[n] = dv[n] + dot_tn(p.astype(bf16), d_out)
    ctx_row = pl.multiple_of(w * CTX, 16)
    dctx_ref[pl.ds(ctx_row, CTX), pl.ds(col_of(0), HD)] = (dk[0] * scale).astype(bf16)
    dctx_ref[pl.ds(ctx_row, CTX), pl.ds(col_of(1), HD)] = dv[0].astype(bf16)
    for half in (0, 1):
        dqkv_ref[pl.ds(row_of(half), rows), pl.ds(col_of(1), HD)] = (dk[1 + half] * scale).astype(bf16)
        dqkv_ref[pl.ds(row_of(half), rows), pl.ds(col_of(2), HD)] = dv[1 + half].astype(bf16)


def attention_specs(rows, heads):
    def at(half, part):
        return pl.BlockSpec((rows, HD), lambda w, h, s: ((half ^ s[0]) * 2 + w, part * heads + h))

    def ctx(part):
        return pl.BlockSpec((CTX, HD), lambda w, h, s: (w, part * heads + h))

    return [at(half, part) for part in range(3) for half in (0, 1)] + [ctx(0), ctx(1)]


def whole_block(shape):
    return pl.BlockSpec(shape, lambda w, h, s: (0, 0))


def attend(half, qkv, ctx_kv):
    rows, heads = qkv.shape[0] // TEAM, qkv.shape[1] // (3 * HD)
    out = (qkv.shape[0], heads * HD)
    return pl.pallas_call(
        attend_kernel,
        grid_spec=pltpu.PrefetchScalarGridSpec(
            num_scalar_prefetch=1,
            grid=(2, heads),
            in_specs=attention_specs(rows, heads),
            out_specs=whole_block(out),
        ),
        out_shape=jax.ShapeDtypeStruct(out, bf16),
        compiler_params=SMALL,
        name="attend",
    )(half, *[qkv] * 6, ctx_kv, ctx_kv)


def attend_back(half, qkv, ctx_kv, d_attended):
    rows, heads = qkv.shape[0] // TEAM, qkv.shape[1] // (3 * HD)

    def at(side):
        return pl.BlockSpec((rows, HD), lambda w, h, s: ((side ^ s[0]) * 2 + w, h))

    return pl.pallas_call(
        attend_back_kernel,
        grid_spec=pltpu.PrefetchScalarGridSpec(
            num_scalar_prefetch=1,
            grid=(2, heads),
            in_specs=attention_specs(rows, heads) + [at(0), at(1)],
            out_specs=[whole_block(qkv.shape), whole_block(ctx_kv.shape)],
        ),
        out_shape=[jax.ShapeDtypeStruct(qkv.shape, bf16), jax.ShapeDtypeStruct(ctx_kv.shape, bf16)],
        compiler_params=SMALL,
        name="attend_back",
    )(half, *[qkv] * 6, ctx_kv, ctx_kv, d_attended, d_attended)


def pack_kernel(rate, gin, gout, g_one, g_two, out):
    for k, ref in enumerate((rate, gin, gout)):
        out[0, k * NST : (k + 1) * NST, :] = ref[...]
    out[0, 3 * NST : 3 * NST + 1, :] = g_one[...]
    out[0, 3 * NST + 1 : 3 * NST + 2, :] = g_two[...]


def norm_kernel(idx, gain, x0, x1, x2, x3, low_ref, inv_ref, u_ref):
    rows, dim = x0.shape
    cols = dim // TEAM
    for r, ref in enumerate((x0, x1, x2, x3)):
        x = ref[...].astype(f32)
        inv = lax.rsqrt(jnp.mean(x * x, axis=-1, keepdims=True) + epsilon)
        inv_ref[r * rows : (r + 1) * rows, :] = inv
        low_ref[r * rows : (r + 1) * rows, :] = (x * inv * gain[...]).astype(bf16)
        for c in range(cols // LANES):
            at = pl.multiple_of(idx[0] * cols + c * LANES, LANES)
            u = low_ref[r * rows : (r + 1) * rows, pl.ds(at, LANES)].astype(f32)
            u_ref[:, r * (cols // LANES) + c, :] = u


def first_norm(idx, gain, blocks):
    rows, dim = blocks[0].shape
    shapes = (
        jax.ShapeDtypeStruct((TEAM * rows, dim), bf16),
        jax.ShapeDtypeStruct((TEAM * rows, 1), f32),
        jax.ShapeDtypeStruct((rows, dim // LANES, LANES), f32),
    )
    return call(norm_kernel, "first_norm", shapes, (idx, gain[None], *blocks))


def part_types(rows, dim):
    return tuple(jax.ShapeDtypeStruct((rows, dim), (f32, bf16)[r % 2]) for r in range(TEAM))


def dot_kernel(x_ref, w_ref, *parts):
    rows = parts[0].shape[0]
    for r in (3, 1, 2, 0):
        part = dot_nn(x_ref[r * rows : (r + 1) * rows, :], w_ref[...])
        parts[r][...] = part.astype(parts[r].dtype)


def dot_parts(name, x, w):
    return call(dot_kernel, name, part_types(x.shape[0] // TEAM, w.shape[1]), (x, w), 0)


def out_kernel(idx, x_ref, w0, w1, w2, w3, *parts):
    rows, cols = parts[0].shape[0], w0.shape[1]
    for r in (3, 1, 2, 0):
        for q, w in enumerate((w0, w1, w2, w3)):
            at = pl.multiple_of((idx[0] ^ q) * cols, LANES)
            part = dot_nn(x_ref[r * rows : (r + 1) * rows, :], w[...])
            parts[r][:, pl.ds(at, cols)] = part.astype(parts[r].dtype)


def context_kv_kernel(idx, w_ref, c0, c1, c2, c3, kv_ref, context_ref):
    cols = c0.shape[1]
    width = w_ref.shape[1] // 3
    for r, part in enumerate((c0, c1, c2, c3)):
        at = pl.multiple_of((idx[0] ^ r) * cols, LANES)
        for w in (0, 1):
            v = w ^ (r & 1)
            context_ref[w * CTX : (w + 1) * CTX, pl.ds(at, cols)] = part[v * CTX : (v + 1) * CTX, :]
    kv_ref[...] = dot_nn(context_ref[...], w_ref[:, width:]).astype(bf16)


def mlp_kernel(m0, m1, m2, m3, g0, g1, g2, g3, up, down, act_ref, dpre_ref, *parts_and_sum):
    parts, total = parts_and_sum[:-1], parts_and_sum[-1]
    k = pl.program_id(0)
    rows = m0.shape[0]
    c = math.sqrt(2.0 / math.pi)
    for r, (m, g) in enumerate(((m0, g0), (m1, g1), (m2, g2), (m3, g3))):
        at = slice(r * rows, (r + 1) * rows)
        x = dot_nn(m[...], up[...])
        t = jnp.tanh(c * (x + 0.044715 * (x * x * x)))
        cdf = 0.5 * (1.0 + t)
        act_ref[at, :] = (x * cdf).astype(bf16)
        slope = cdf + (0.5 * c) * x * (1.0 - t * t) * (1.0 + (3 * 0.044715) * (x * x))
        d_pre = (dot_nt(g[...], down[...]) * slope).astype(bf16)
        dpre_ref[at, :] = d_pre
        new = dot_nt(d_pre, up[...])
        total[at, :] = jnp.where(k == 0, new, total[at, :] + new)

    @pl.when(k == pl.num_programs(0) - 1)
    def _():
        for r, part in enumerate(parts):
            part[...] = total[r * rows : (r + 1) * rows, :].astype(part.dtype)


def feed_forward(mlp_blocks, grad_blocks, up, down):
    rows, dim = mlp_blocks[0].shape
    units = up.shape[1]
    step = 256

    unit_out = jax.ShapeDtypeStruct((TEAM * rows, units), bf16)
    return pl.pallas_call(
        mlp_kernel,
        grid=(units // step,),
        out_shape=(unit_out, unit_out) + part_types(rows, dim),
        in_specs=[block_of((rows, dim))] * 8
        + [pl.BlockSpec((dim, step), lambda k: (0, k)), pl.BlockSpec((step, dim), lambda k: (k, 0))],
        out_specs=(pl.BlockSpec((TEAM * rows, step), lambda k: (0, k)),) * 2
        + (block_of((rows, dim)),) * TEAM,
        scratch_shapes=[pltpu.VMEM((TEAM * rows, dim), f32)],
        compiler_params=MIDDLE,
        name="feed_forward",
    )(*mlp_blocks, *grad_blocks, up, down)


def mlp_grad_kernel(x_ref, y0, y1, y2, y3, out):
    rows = y0.shape[0]
    grads = [dot_tn(x_ref[r * rows : (r + 1) * rows, :], y[...]) for r, y in enumerate((y0, y1, y2, y3))]
    out[...] = functools.reduce(jnp.add, grads).astype(bf16)


def down_grad(act, grad_blocks):
    rows, dim = grad_blocks[0].shape
    step = 256
    return pl.pallas_call(
        mlp_grad_kernel,
        grid=(act.shape[1] // step,),
        out_shape=jax.ShapeDtypeStruct((act.shape[1], dim), bf16),
        in_specs=[pl.BlockSpec((act.shape[0], step), lambda k: (0, k))]
        + [block_of((rows, dim))] * TEAM,
        out_specs=pl.BlockSpec((step, dim), lambda k: (k, 0)),
        compiler_params=SMALL,
        name="down_grad",
    )(act, *grad_blocks)


def up_grad_kernel(x0, x1, x2, x3, y_ref, out):
    rows = x0.shape[0]
    grads = [dot_tn(x[...], y_ref[r * rows : (r + 1) * rows, :]) for r, x in enumerate((x0, x1, x2, x3))]
    out[...] = functools.reduce(jnp.add, grads).astype(bf16)


def up_grad(mlp_blocks, d_pre):
    rows, dim = mlp_blocks[0].shape
    step = 256
    return pl.pallas_call(
        up_grad_kernel,
        grid=(dim // step,),
        out_shape=jax.ShapeDtypeStruct((dim, d_pre.shape[1]), bf16),
        in_specs=[pl.BlockSpec((rows, step), lambda k: (0, k))] * TEAM
        + [block_of(d_pre.shape)],
        out_specs=pl.BlockSpec((step, d_pre.shape[1]), lambda k: (k, 0)),
        compiler_params=SMALL,
        name="up_grad",
    )(*mlp_blocks, d_pre)


def attended_grad_kernel(idx, w0, w1, w2, w3, h0, h1, h2, h3, out):
    rows, cols = h0.shape[0], w0.shape[1]
    for r, h in enumerate((h0, h1, h2, h3)):
        grad = 0.0
        for q, w in enumerate((w0, w1, w2, w3)):
            at = pl.multiple_of((idx[0] ^ q) * cols, LANES)
            grad = grad + dot_nt(h[:, pl.ds(at, cols)], w[...])
        out[r * rows : (r + 1) * rows, :] = grad.astype(bf16)


def out_grad_kernel(idx, att_ref, h0, h1, h2, h3, *parts):
    rows, cols = h0.shape[0], parts[0].shape[1]
    for q, part in enumerate(parts):
        at = pl.multiple_of((idx[0] ^ q) * cols, LANES)
        grads = [
            dot_tn(att_ref[r * rows : (r + 1) * rows, :], h[:, pl.ds(at, cols)])
            for r, h in enumerate((h0, h1, h2, h3))
        ]
        part[...] = functools.reduce(jnp.add, grads).astype(bf16)


def context_grad_kernel(idx, d_ref, w_ref, *parts):
    cols = parts[0].shape[1]
    width = w_ref.shape[1] // 3
    for r, part in enumerate(parts):
        at = pl.multiple_of((idx[0] ^ r) * cols, 16)
        for w in (0, 1):
            v = w ^ (r & 1)
            grad = dot_nt(d_ref[w * CTX : (w + 1) * CTX, :], w_ref[pl.ds(at, cols), width:])
            part[v * CTX : (v + 1) * CTX, :] = grad.astype(part.dtype)


def inputs_grad_kernel(idx, dq_ref, w_ref, du_ref, inv_ref, x0, x1, x2, x3, *outs):
    parts, gain_ref, work = outs[:TEAM], outs[TEAM], outs[TEAM + 1]
    rows, dim = x0.shape
    cols = dim // TEAM
    gain = 0.0
    for r, x in enumerate((x0, x1, x2, x3)):
        at = slice(r * rows, (r + 1) * rows)
        work[...] = dot_nt(dq_ref[at, :], w_ref[...])
        for c in range(cols // LANES):
            col = pl.ds(pl.multiple_of(idx[0] * cols + c * LANES, LANES), LANES)
            work[:, col] = work[:, col] + du_ref[:, r * (cols // LANES) + c, :]
        grad = work[...]
        parts[r][...] = grad.astype(parts[r].dtype)
        gain = gain + jnp.sum(grad * (x[...].astype(f32) * inv_ref[at, :]), axis=0, keepdims=True)
    gain_ref[...] = gain


def cut_states_kernel(idx, init_ref, ends_ref, i0, i1, e0, e1, e2, e3):
    cols = i0.shape[1]
    for r, out in enumerate((e0, e1, e2, e3)):
        at = pl.multiple_of((idx[0] ^ r) * cols, LANES)
        out[...] = ends_ref[:, pl.ds(at, cols)]
        if r < 2:
            (i0, i1)[r][...] = init_ref[:, pl.ds(at, cols)]


def join_states_kernel(late, i0, i1, e0, e1, e2, e3, init_ref, twice_ref, first_ref, second_ref):
    per = init_ref.shape[1] // 2
    for w in range(2):
        for c in range(per):
            at = slice(c * LANES, (c + 1) * LANES)
            init = (i0, i1)[w][:, at]
            init_ref[:, w * per + c, :] = init
            twice_ref[:, w * per + c, :] = init
            twice_ref[:, (2 + w) * per + c, :] = init
            own, other = (e0, e1)[w][:, at], (e2, e3)[w][:, at]
            first_ref[:, w * per + c, :] = jnp.where(late[0] == 1, other, own)
            second_ref[:, w * per + c, :] = jnp.where(late[0] == 1, own, other)


def cut_ends_kernel(late, first_ref, second_ref, e0, e1, e2, e3):
    per = first_ref.shape[1] // 2
    for w in range(2):
        for c in range(per):
            at = slice(c * LANES, (c + 1) * LANES)
            one, two = first_ref[:, w * per + c, :], second_ref[:, w * per + c, :]
            (e0, e1)[w][:, at] = jnp.where(late[0] == 1, two, one)
            (e2, e3)[w][:, at] = jnp.where(late[0] == 1, one, two)


def join_ends_kernel(idx, e0, e1, e2, e3, out):
    cols = e0.shape[1]
    for r, part in enumerate((e0, e1, e2, e3)):
        at = pl.multiple_of((idx[0] ^ r) * cols, LANES)
        out[:, pl.ds(at, cols)] = part[...]


def small_pack_kernel(flags, a, d_a, d_in, d_out, g_in, g_init, one, two, out):
    per = d_a.shape[1] // TEAM
    row = 0
    for k, ref in enumerate((d_a, d_in, d_out)):
        for c in range(per):
            total = 0.0
            for r in range(TEAM):
                part = ref[:, r * per + c, :]
                total = total + (-a[:, r * per + c, :] * part if k == 0 else part)
            out[row : row + NST, :] = total
            row += NST
    for ref in (one, two):
        for c in range(ref.shape[1] // LANES):
            out[row : row + 1, :] = ref[:, c * LANES : (c + 1) * LANES]
            row += 1
    for s in range(2 * per):
        first = jnp.where(flags[0] == 1, g_in[:, 2 * per + s, :], g_in[:, s, :])
        out[row : row + NST, :] = g_init[:, s, :] + jnp.where(flags[1] == 0, first, 0.0)
        row += NST


def small_kernel(spots, p0, p1, p2, p3, gains_ref, rate_ref, in_ref, out_ref, init_ref):
    packs = [p[...] for p in (p0, p1, p2, p3)]
    tiles = packs[0].shape[0] - 3 * NST * 2 - NST * 4
    one, two = 3 * NST * 2, 3 * NST * 2 + tiles
    gains = functools.reduce(jnp.add, [p[one:two] for p in packs])
    row = lax.broadcasted_iota(jnp.int32, gains.shape, 0)
    for k in (0, 1):
        mine = row == k * (tiles // 2) + spots[1]
        gains_ref[k : k + 1, :] = jnp.sum(jnp.where(mine, gains, 0.0), axis=0, keepdims=True)
    chosen = packs[0]
    for r in (1, 2, 3):
        chosen = jnp.where(spots[0] == r, packs[r], chosen)
    side = spots[1] % 2 == 1

    def of_side(at):
        return jnp.where(side, chosen[at + NST : at + 2 * NST], chosen[at : at + NST])

    for k, ref in enumerate((rate_ref, in_ref, out_ref)):
        ref[...] = of_side(2 * NST * k)
    window = [of_side(two + 2 * NST * w) for w in (0, 1)]
    init_ref[...] = jnp.where(spots[0] % 2 == 1, window[1], window[0])


def added(p0, one, far):
    return p0[...] + one[...].astype(f32) + far[...].astype(f32)


def second_norm_kernel(tok, p0, one, far, gain, hidden_ref, inv_ref, low_ref):
    hidden = tok[...].astype(f32) + added(p0, one, far)
    inv = lax.rsqrt(jnp.mean(hidden * hidden, axis=-1, keepdims=True) + epsilon)
    hidden_ref[...] = hidden
    inv_ref[...] = inv
    low_ref[...] = (hidden * inv * gain[...]).astype(bf16)


def result_kernel(hidden, p0, one, far, out):
    out[...] = (hidden[...] + added(p0, one, far)).astype(bf16)


def norm_back(grad, normed, inv, gain):
    scaled = grad * gain
    return inv * (scaled - normed * jnp.mean(scaled * normed, axis=-1, keepdims=True))


def hidden_grad_kernel(cot, hidden, inv, gain, p0, one, far, out_ref, low_ref, gain_ref):
    grad = added(p0, one, far)
    normed = hidden[...] * inv[...]
    gain_ref[...] = jnp.sum(grad * normed, axis=0, keepdims=True)
    out = cot[...].astype(f32) + norm_back(grad, normed, inv[...], gain[...])
    out_ref[...] = out
    low_ref[...] = out.astype(bf16)


def tokens_grad_kernel(d_hidden, tok, inv, gain, p0, one, far, out):
    grad = added(p0, one, far)
    normed = tok[...].astype(f32) * inv[...]
    out[...] = (d_hidden[...] + norm_back(grad, normed, inv[...], gain[...])).astype(bf16)


def context_sum_kernel(p0, one, far, out):
    out[...] = added(p0, one, far).astype(bf16)


def first_rows_kernel(flags, own, dy0_full):
    per = dy0_full.shape[1] // TEAM
    zero = jnp.zeros((CTX, LANES), f32)
    for w in range(2):
        for c in range(per):
            at = (slice(w * CTX, (w + 1) * CTX), slice(c * LANES, (c + 1) * LANES))
            dy0 = jnp.where(flags[1] == 0, own[at].astype(f32), zero)
            dy0_full[:, w * per + c, :] = dy0
            dy0_full[:, (2 + w) * per + c, :] = dy0


def context_rows_kernel(flags, came, dy_ref, dy_full):
    per = dy_ref.shape[1] // 2
    zero = jnp.zeros((CTX, LANES), f32)
    for w in range(2):
        for c in range(per):
            at = (slice(w * CTX, (w + 1) * CTX), slice(c * LANES, (c + 1) * LANES))
            dy = came[at].astype(f32)
            dy_ref[:, w * per + c, :] = dy
            dy_full[:, w * per + c, :] = jnp.where(flags[0] == 1, dy, zero)
            dy_full[:, (2 + w) * per + c, :] = jnp.where(flags[0] == 1, zero, dy)


def on_device(
    tokens,
    w_qkv,
    w_out,
    w_up,
    w_down,
    g_attn,
    g_mlp,
    ssm_rate,
    ssm_in,
    ssm_out,
    h_init,
    cotangent,
    d_h_ends,
):
    nd, ns = lax.axis_size("dp"), lax.axis_size("seq")
    ny = nd // 2
    dp, seq = lax.axis_index("dp"), lax.axis_index("seq")
    late = seq % 2 == 1
    block = seq // 2
    me = (seq % 2) * 2 + dp % 2
    idx = jnp.stack([me, dp // 2]).astype(jnp.int32)
    place = (seq * ny + dp // 2).astype(jnp.int32).reshape(1)
    half = (seq % 2).astype(jnp.int32).reshape(1)
    rows, dim = tokens.shape[1:]
    shard = w_qkv.shape[0]
    width = HEADS * HD // TEAM
    cols = dim // TEAM
    fb = w_down.shape[0] // TEAM
    tile = (dim // LANES, LANES)
    half_tile = (dim // LANES // 2, LANES)

    def like(shape, dtype):
        return jax.ShapeDtypeStruct(shape, dtype)


    share_attn, share_up, share_down = shares(idx, w_qkv, w_out, w_up, w_down, ny, ns)
    attn, up = Gathering(*share_attn, True), Gathering(*share_up, True)
    down = Gathering(*share_down, True)
    attn_pair = attn.step()
    x_blocks = gather_team(after(tokens[0], attn_pair))
    up_pair = up.step(attn_pair)
    attn_first = attn.rest()
    attn_own = attn.a
    down_pair = down.step(attn_first)
    attn_second = attn.step(up_pair)
    attn_third = attn.across(0)
    small = call(
        pack_kernel,
        "pack_small",
        jax.ShapeDtypeStruct((1, 3 * NST + 2, shard), bf16),
        after((ssm_rate.T, ssm_in.T, ssm_out.T, g_attn[None], g_mlp[None]), share_attn[1]),
        0,
    )
    for bit in [1] + high_bits("seq")[::-1]:
        got = swap(after(small, attn_own) if bit > 2 else small, "seq", bit)
        upper = (seq & bit) != 0
        small = jnp.concatenate([jnp.where(upper, got, small), jnp.where(upper, small, got)], axis=0)
    small = small.astype(f32)
    gain_one = small[:, 3 * NST].reshape(dim)
    gain_two = small[:, 3 * NST + 1].reshape(dim)
    params = small[:, : 3 * NST].transpose(1, 0, 2).reshape(3 * NST, dim)
    params = lax.dynamic_slice_in_dim(params, me * cols, cols, 1)
    params = jnp.broadcast_to(params[:, None], (3 * NST, TEAM, cols)).reshape((3, NST) + tile)
    rate, gin, gout = params[0], params[1], params[2]
    half_rate = rate[:, : tile[0] // 2]

    by_channel = like((NST, cols), f32)
    init, near_init, *end_cot = call(
        cut_states_kernel,
        "cut_states",
        (by_channel,) * 6,
        (idx, h_init[0].T, after(d_h_ends[0, 0].T, share_attn[1])),
    )
    init, init_twice, end_first, end_second = call(
        join_states_kernel,
        "join_states",
        tuple(like((NST,) + t, f32) for t in (half_tile, tile, half_tile, half_tile)),
        (half, init, swap_team(near_init, 1), *trade_team(end_cot)),
    )
    end_cot = [end_first, end_second]

    def by_half(a, axis=1):
        n = a.shape[axis] // 2
        own, other = lax.slice_in_dim(a, 0, n, axis=axis), lax.slice_in_dim(a, n, 2 * n, axis=axis)
        return ordered([own, other], seq % 2)

    def by_owner(first, second):
        return jnp.concatenate(ordered([first, second], seq % 2), axis=1)

    inputs_low, inv_one, u = first_norm(idx, after(gain_one, attn_first), x_blocks)

    a = jnp.exp(-rate)
    s_mid, s_end = local_ends(u, a)
    attn_last = attn.across(1, s_end)
    up_first = up.rest((attn_second, s_end))
    decay = jnp.exp(-half_rate * rows)
    first_end, second_end = by_half(gin * s_end)
    span = 2 * rows

    def chain(inclusive, back, wait):
        exclusive, step = jnp.zeros_like(inclusive), 1
        while step < ns // 2:
            pairs = [(k, k + 2 * step) for k in range(ns - 2 * step)]
            got = lax.ppermute(inclusive, "seq", [(t, f) for f, t in pairs] if back else pairs)
            if step == 1:
                got = after(got, wait)
            exclusive = exclusive + jnp.exp(-half_rate * (span * (step - 1))) * got
            inclusive = inclusive + jnp.exp(-half_rate * (span * step)) * got
            step *= 2
        return exclusive

    entering = chain(after(decay * first_end + second_end, attn_third), False, (up_first, attn_last))
    state_zero = jnp.exp(-half_rate * (span * block).astype(f32)) * init + entering
    state_one = decay * state_zero + first_end
    state_two = decay * state_one + second_end
    state_in = by_owner(state_zero, state_one)
    ends = call(cut_ends_kernel, "cut_ends", (by_channel,) * TEAM, (half, state_one, state_two))
    ends = call(join_ends_kernel, "join_ends", like((NST, dim), f32), (idx, *trade_team(ends)))
    on_second = by_owner(jnp.zeros_like(init), jnp.ones_like(init))
    h_mid = jnp.exp(-rate * (rows - CTX)) * state_in + gin * s_mid
    h_mid = jnp.where(on_second > 0, h_mid, init_twice)
    y_first, y_second = contexts(half, u, a, gin * on_second, gout, h_mid)
    passed = lax.ppermute(y_second, "seq", [(k, k + 2) for k in range(ns - 2)])
    up_second = up.step(entering)
    up_third = up.across(0)
    places = jnp.stack([place[0], seq]).astype(jnp.int32)
    full_qkv, *full_out = place_weight(idx, places, [(attn.pieces, 0, 1, 0)], 3 * width)
    full_out = trade_team(full_out)
    context = jnp.where(block == 0, y_first, after(passed, (up_second, full_qkv, down_pair)))
    down_first = down.rest(passed)

    full_qkv = after(full_qkv, up_third)
    qkv = dot_nn(inputs_low, full_qkv).astype(bf16)
    context = gather_team(context)
    g_blocks = gather_team(after(cotangent[0], context[2]))
    context = after(context, qkv)
    ctx_kv, context = call(
        context_kv_kernel,
        "context_kv",
        (like((2 * CTX, 2 * width), bf16), like((2 * CTX, dim), bf16)),
        (idx, full_qkv, *context),
    )
    attended = attend(half, qkv, ctx_kv)

    up_last = up.across(1, up_third)
    down.came = after(down.came, ctx_kv)
    attended = after(attended, (g_blocks[2], down.came, up_last))
    down_second = down.step()
    down_third = down.across(0, up_last)
    attended_parts = call(out_kernel, "out_dot", part_types(rows, dim), (idx, attended, *full_out))
    attended_parts = sum_team(attended_parts, None, (down_second, down_third))
    down.across(1, down_third)
    (full_up,) = place_weight(idx, places, [(up.pieces, 0, 1, 0)])
    (full_down,) = place_weight(idx, places, [(down.pieces, 0, 1, 0)])

    hidden, inv_two, mlp_in = call(
        second_norm_kernel,
        "second_norm",
        (like((rows, dim), f32), like((rows, 1), f32), like((rows, dim), bf16)),
        (tokens[0], *attended_parts[:3], gain_two[None]),
        0,
    )
    mlp_in = gather_team(mlp_in)
    mlp_in = after(mlp_in, full_up)
    act, d_pre, *d_mlp = feed_forward(mlp_in, g_blocks, full_up, full_down)
    d_down = down_grad(act, g_blocks)
    reduction = HalvedReduction if (nd, ns) == (4, 8) else Reduction
    sum_down = reduction(d_down, place)
    sum_down.step()
    d_up = up_grad(mlp_in, after(d_pre, sum_down.sent))
    sum_up = reduction(d_up, place)
    sum_up.step()
    result = dot_parts("down_dot", after(act, sum_up.sent), full_down)
    d_mlp = sum_team(d_mlp, d_down, result)
    sum_down.step(d_mlp[3])
    d_hidden, d_hidden_low, d_gain_two = call(
        hidden_grad_kernel,
        "hidden_grad",
        (like((rows, dim), f32), like((rows, dim), bf16), like((1, dim), f32)),
        (after(cotangent[0], sum_down.sent), hidden, inv_two, gain_two[None], *d_mlp[:3]),
        0,
    )
    hidden_blocks = gather_team(d_hidden_low)
    sum_down.step(d_hidden)

    d_attended = call(
        attended_grad_kernel,
        "attended_grad",
        jax.ShapeDtypeStruct(attended.shape, bf16),
        (idx, after(full_out[0], sum_down.sent), *full_out[1:], *hidden_blocks),
    )
    d_out = call(
        out_grad_kernel,
        "out_grad",
        (jax.ShapeDtypeStruct((width, cols), bf16),) * TEAM,
        (idx, after(attended, d_attended), *hidden_blocks),
    )
    d_qkv, d_ctx_kv = attend_back(half, qkv, ctx_kv, after(d_attended, d_out))
    d_out = trade_team(d_out)
    sum_up.step(d_ctx_kv)
    sum_down.step(sum_up.sent)
    d_context = call(
        context_grad_kernel,
        "context_grad",
        part_types(2 * CTX, cols),
        (idx, after(d_ctx_kv, (sum_up.sent, sum_down.sent, d_out)), full_qkv),
    )
    d_attn = attn_grad(idx, inputs_low, after(d_qkv, d_context), context, d_ctx_kv, d_out)
    sum_attn = reduction(d_attn, place)
    d_context = sum_team(d_context, None, d_attn)
    d_context = call(context_sum_kernel, "context_sum", like((2 * CTX, cols), bf16), d_context[:3], 0)
    came = lax.ppermute(d_context, "seq", [(k + 2, k) for k in range(ns - 2)])
    sum_attn.step(d_context)
    flags = jnp.stack([seq % 2, block]).astype(jnp.int32)
    dy0_full = call(first_rows_kernel, "first_rows", like((CTX,) + tile, f32), (flags, d_context))
    dy, dy_full = call(
        context_rows_kernel,
        "context_rows",
        (like((CTX,) + half_tile, f32), like((CTX,) + tile, f32)),
        (flags, after(came, (ends, dy0_full, sum_attn.sent))),
    )

    lam_mid = tail_adjoint(dy, a, gout)
    g_second = jnp.exp(-half_rate * (rows - CTX + 1)) * lam_mid + decay * end_cot[1]
    d_down_pair = sum_down.last()
    d_a, d_gout, g_init = first_context_back(after(dy0_full, lam_mid), a, gout, init_twice)
    leaving = chain(decay * (end_cot[0] + g_second), True, (g_init, d_down_pair[1], sum_attn.out if reduction is HalvedReduction else g_init))
    down_blocks = spread_places(d_down_pair)
    sum_up.step(leaving)
    sum_attn.step(sum_up.sent)
    result = sum_team(result, d_context)
    result = call(result_kernel, "result_sum", like((rows, dim), bf16), (hidden, *result[:3]), 0)
    lam_end = by_owner(end_cot[0] + g_second + decay * leaving, end_cot[1] + leaving)
    du, d_gin, d_a, d_gout, g_in = ssm_back(
        u, dy_full, a, gin, gout, state_in, after(lam_end, sum_attn.sent), d_a, d_gout
    )

    sum_up.step(du)
    *d_inputs, d_gain_one = call(
        inputs_grad_kernel,
        "inputs_grad",
        part_types(rows, dim) + (jax.ShapeDtypeStruct((1, dim), f32),),
        (idx, d_qkv, full_qkv, after(du, (result, sum_up.sent, down_blocks)), inv_one, *x_blocks),
        scratch_shapes=[pltpu.VMEM((rows, dim), f32)],
    )
    sum_attn.step(d_gain_one)
    d_inputs = after(d_inputs, sum_attn.sent)
    small_rows = (3 * NST * cols + 2 * dim + 2 * NST * cols) // LANES
    pack = call(
        small_pack_kernel,
        "small_pack",
        like((small_rows, LANES), f32),
        (flags, a, d_a, d_gin, d_gout, g_in, g_init, d_gain_one, d_gain_two),
    )
    small, first, *others = pack, *high_bits("seq")
    pack = pack + swap(pack, "seq", first)
    *d_inputs, d_inputs_far = sum_team(d_inputs, small)
    d_tokens = call(
        tokens_grad_kernel,
        "tokens_grad",
        like((rows, dim), bf16),
        (d_hidden, tokens[0], inv_one[:rows], gain_one[None], *d_inputs),
        0,
    )

    up_blocks = spread_places(after(sum_up.last(), d_tokens))
    d_down = spread_weight("down", down_blocks, idx, [w_down.shape])[0]
    if fb % LANES:
        d_up = spread_narrow(up_blocks, idx, w_up.shape, fb)
    else:
        d_up = spread_weight("up", up_blocks, idx, [w_up.shape], fb)[0]
    sum_attn.step((pack, d_tokens))
    for bit in others:
        pack = pack + swap(pack, "seq", bit)
    one, two = 3 * NST * cols // LANES, 3 * NST * cols // LANES + 2 * dim // LANES
    shared = pack[:two]
    for bit in high_bits("dp"):
        shared = shared + swap(shared, "dp", bit)
    packs = gather_team(after(jnp.concatenate([shared, pack[two:]], axis=0), (d_down, d_up)))
    if shard == LANES:
        spots = jnp.stack([me ^ (seq * shard // cols), seq]).astype(jnp.int32)
        gains, *d_params, state_grad = call(
            small_kernel,
            "small_grads",
            (like((2, shard), f32),) + (like((NST, shard), f32),) * 4,
            (spots, *packs),
        )
        d_params, state_grad = [p.T for p in d_params], state_grad.T[None]
    else:
        packs = jnp.stack(packs)
        gains = packs[:, one:two].sum(0).reshape(2, ns, shard)
        gains = pick(gains, seq, 1)
        member = me ^ (seq * shard // cols)
        inner = seq * shard % cols
        chosen = pick(packs, member)
        d_params = chosen[:one].reshape(3, cols // LANES, NST, LANES).transpose(0, 2, 1, 3)
        d_params = d_params.reshape(3 * NST, cols)
        d_params = lax.dynamic_slice_in_dim(d_params, inner, shard, 1).reshape(3, NST, shard)
        d_params = d_params.transpose(0, 2, 1)
        state_grad = chosen[two:].reshape(2, cols // LANES, NST, LANES).transpose(2, 0, 1, 3)
        state_grad = state_grad.reshape(NST, 2, cols)
        state_grad = pick(state_grad, member % 2, 1)
        state_grad = lax.dynamic_slice_in_dim(state_grad, inner, shard, 1).T[None]

    d_wqkv, d_out = spread_weight("attn", spread_places(after(sum_attn.last(), pack)), idx, [w_qkv.shape, w_out.shape])
    return (
        result[None],
        d_tokens[None],
        d_wqkv,
        d_out,
        d_up,
        d_down,
        gains[0],
        gains[1],
        d_params[0],
        d_params[1],
        d_params[2],
        state_grad,
        ends.T[None, None],
    )


def solution(mesh):
    return jax.shard_map(
        on_device,
        mesh=mesh,
        in_specs=(
            P("dp", "seq", None),
            P("seq", None),
            P("seq", None),
            P("seq", None),
            P("seq", None),
            P("seq"),
            P("seq"),
            P("seq", None),
            P("seq", None),
            P("seq", None),
            P("dp", None, None),
            P("dp", "seq", None),
            P("dp", "seq", None, None),
        ),
        out_specs=(
            P("dp", "seq", None),
            P("dp", "seq", None),
            P("seq", None),
            P("seq", None),
            P("seq", None),
            P("seq", None),
            P("seq"),
            P("seq"),
            P("seq", None),
            P("seq", None),
            P("seq", None),
            P("dp", "seq", None),
            P("dp", "seq", None, None),
        ),
        check_vma=False,
    )
```

```python
import functools
import math

import jax
import jax.numpy as jnp
from jax import lax
from jax.experimental import pallas as pl
from jax.experimental.pallas import tpu as pltpu
from jax.sharding import PartitionSpec as P

HEADS = 8
HD = 128
CTX = 128
NST = 16
LANES = 128
GROUP = 4
TEAM = 4

epsilon = 1e-05
far_below = -1e30
bf16 = jnp.bfloat16
f32 = jnp.float32


def swap(a, axis, bit):
    return lax.ppermute(a, axis, [(k, k ^ bit) for k in range(lax.axis_size(axis))])


def swap_team(a, r):
    if r == 1:
        return swap(a, "dp", 1)
    if r == 2:
        return swap(a, "seq", 1)
    nd, ns = lax.axis_size("dp"), lax.axis_size("seq")
    pairs = [(d * ns + k, (d ^ 1) * ns + (k ^ 1)) for d in range(nd) for k in range(ns)]
    return lax.ppermute(a, ("dp", "seq"), pairs)


def gather_team(a):
    far = swap_team(a, 2)
    return [a, swap_team(a, 1), far, swap_team(far, 1)]


def far_kernel(mine, came, out):
    out[...] = (mine[...] + came[...].astype(f32)).astype(bf16)


def sum_team(parts, middle=None, end=None):
    one, three = swap_team(parts[1], 1), swap_team(parts[3], 1)
    if middle is not None:
        three = after(three, middle)
    shape = jax.ShapeDtypeStruct(three.shape, bf16)
    near = call(far_kernel, "far_sum", shape, (parts[2], three), 0)
    far = swap_team(near, 2)
    if end is not None:
        one, far = after((one, far), end)
    return parts[0], one, far, near


def trade_team(parts):
    return [parts[0]] + [swap_team(parts[r], r) for r in (1, 2, 3)]


def high_bits(axis):
    size = lax.axis_size(axis)
    return [1 << k for k in reversed(range(1, size.bit_length() - 1))]


def pick(a, index, axis=0):
    return lax.dynamic_index_in_dim(a, index, axis, False)


def ordered(blocks, index):
    bit = len(blocks) // 2
    while bit:
        flip = (index & bit) != 0
        blocks = [jnp.where(flip, blocks[r ^ bit], blocks[r]) for r in range(len(blocks))]
        bit //= 2
    return blocks


def after(x, *others):
    return lax.optimization_barrier((x, others))[0]


def whole_spec():
    return pl.BlockSpec(memory_space=pltpu.VMEM)


def scalar_spec():
    return pl.BlockSpec(memory_space=pltpu.SMEM)


def any_spec():
    return pl.BlockSpec(memory_space=pl.ANY)


BIG = pltpu.CompilerParams(vmem_limit_bytes=32 * 2**20)
MIDDLE = pltpu.CompilerParams(vmem_limit_bytes=24 * 2**20)
SMALL = pltpu.CompilerParams(vmem_limit_bytes=20 * 2**20)


def block_of(shape):
    return pl.BlockSpec(shape, lambda *k: (0,) * len(shape), pipeline_mode=pl.Buffered(1))


def call(kernel, name, out_shape, args, scalars=1, **more):
    specs = [scalar_spec()] * scalars + [block_of(a.shape) for a in args[scalars:]]
    return pl.pallas_call(
        kernel,
        grid=(1,),
        out_shape=out_shape,
        in_specs=specs,
        out_specs=jax.tree.map(lambda o: block_of(o.shape), out_shape),
        compiler_params=MIDDLE,
        name=name,
        **more,
    )(*args)


def share_kernel(spots, copies, idx, *refs):
    ins, outs, sem = refs[:spots], refs[spots:-1], refs[-1]
    flying = []
    for n, (src, dst, rows_at, cols_at, size, to) in enumerate(copies):
        row = pl.multiple_of(rows_at(idx), 16)
        col = pl.multiple_of(cols_at(idx), LANES)
        flying.append(
            pltpu.make_async_copy(
                ins[src].at[pl.ds(row, size[0]), pl.ds(col, size[1])],
                outs[dst].at[:, pl.ds(to, size[1])],
                sem.at[n],
            )
        )
    for one in flying:
        one.start()
    for one in flying:
        one.wait()


def shares(idx, w_qkv, w_out, w_up, w_down, ny, ns):
    shard, dim = w_out.shape
    quarter = dim // TEAM
    rows, fb = shard // ny, w_down.shape[0] // TEAM
    low = fb // ny
    copies = []
    for away in (0, 1):
        def who(i, away=away):
            return i[0] ^ (2 * away)

        for part in range(3):
            copies.append((0, away, lambda i: i[1] * rows,
                           lambda i, w=who, p=part: p * dim + w(i) * quarter, (rows, quarter), part * quarter))
        copies.append((1, away, lambda i: i[1] * rows,
                       lambda i, w=who: w(i) * quarter, (rows, quarter), 3 * quarter))
        if fb % LANES == 0:
            for k in range(ns):
                copies.append((2, 2 + away, lambda i: i[1] * rows,
                               lambda i, w=who, k=k: (k * TEAM + w(i)) * fb, (rows, fb), k * fb))
        copies.append((3, 4 + away, lambda i, w=who: w(i) * fb + i[1] * low, lambda i: 0, (low, dim), 0))
    sizes = [(rows, dim)] * 2 + [(rows, ns * fb)] * 2 + [(low, dim)] * 2
    out = pl.pallas_call(
        functools.partial(share_kernel, 4, copies),
        out_shape=[jax.ShapeDtypeStruct(s, bf16) for s in sizes],
        in_specs=[scalar_spec()] + [any_spec()] * 4,
        out_specs=[whole_spec()] * 6,
        scratch_shapes=[pltpu.SemaphoreType.DMA((len(copies),))],
        name="shares",
    )(idx, w_qkv, w_out, w_up, w_down)
    out = [list(out[k : k + 2]) for k in (0, 2, 4)]
    if fb % LANES:
        mine = lax.dynamic_slice_in_dim(w_up, idx[1] * rows, rows, 0).reshape(rows, ns, TEAM, fb)
        out[1] = [pick(mine, idx[0] ^ r, 2).reshape(rows, ns * fb) for r in (0, 2)]
    return out


def place_kernel(maps, cuts, idx, places, *refs):
    ins, outs = refs[: len(maps)], refs[len(maps) :]
    for ref, (which, order, step, offset) in zip(ins, maps):
        rows = ref.shape[1]
        for k, r in enumerate(order):
            at = pl.multiple_of(((places[which] ^ r) * step + offset) * rows, 16)
            if cuts:
                width = outs[0].shape[1]
                outs[0][pl.ds(at, rows), :] = ref[k, :, :width]
                outs[-1][pl.ds(at, rows), :] = ref[k, :, width:]
            else:
                outs[0][pl.ds(at, rows), :] = ref[k]
    for r in range(cuts):
        rows = outs[1].shape[0]
        at = pl.multiple_of((idx[0] ^ r) * rows, 16)
        outs[1 + r][...] = outs[-1][pl.ds(at, rows), :]


def append_kernel(a_ref, b_ref, out):
    count = a_ref.shape[0]
    out[:count] = a_ref[...]
    out[count:] = b_ref[...]


def append(a, b):
    shape = jax.ShapeDtypeStruct((a.shape[0] + b.shape[0],) + a.shape[1:], bf16)
    return call(append_kernel, "append", shape, (a, b), 0)


class Gathering:
    def __init__(self, own, away, parted):
        ny = lax.axis_size("dp") // 2 if parted else 1
        self.seq_steps = [(1, ny)] + [(bit, bit * ny) for bit in high_bits("seq")]
        self.a, self.away, self.order, self.n = own[None], away[None], [0], 0

    def step(self, wait=None):
        bit, weight = self.seq_steps[self.n]
        if self.n:
            self.a = append(self.a, self.came)
            self.order = self.order + [r | self.seq_steps[self.n - 1][1] for r in self.order]
        sent = self.a if self.n else self.away
        self.came = swap(sent if wait is None else after(sent, wait), "seq", bit)
        self.n += 1
        if self.n == len(self.seq_steps):
            last = [r | weight for r in self.order]
            self.pieces = [(self.a, self.order), (self.came, last)]
        return self.came

    def rest(self, wait=None):
        while self.n < len(self.seq_steps) - 1:
            self.step(wait)
            wait = None
        return self.came

    def across(self, k, wait=None):
        new = [self.pieces[k]]
        for bit in high_bits("dp"):
            for a, order in list(new):
                a = a if wait is None else after(a, wait)
                new.append((swap(a, "dp", bit), [r | (bit // 2) for r in order]))
        self.pieces += new[1:]
        return new[1][0]


def place_weight(idx, places, groups, width=None):
    arrays = [a for pieces, *_ in groups for a, _ in pieces]
    maps = [(which, order, step, at) for pieces, which, step, at in groups for _, order in pieces]
    rows, cols = sum(a.shape[0] * a.shape[1] for a in arrays), arrays[0].shape[2]
    shapes = [(rows, cols)]
    scratch = []
    if width:
        shapes = [(rows, width)] + [(rows // TEAM, cols - width)] * TEAM
        scratch = [pltpu.VMEM((rows, cols - width), bf16)]
    return call(
        functools.partial(place_kernel, maps, TEAM if width else 0),
        "place_weight",
        [jax.ShapeDtypeStruct(s, bf16) for s in shapes],
        (idx, places, *arrays),
        2,
        scratch_shapes=scratch,
    )


def attn_grad_kernel(idx, x_ref, dq_ref, ctx_ref, dctx_ref, *refs):
    parts, out = refs[:TEAM], refs[TEAM]
    k = pl.program_id(0)
    width = dq_ref.shape[1] // 3
    grad = dot_tn(x_ref[...], dq_ref[...])
    far = dot_tn(ctx_ref[...], dctx_ref[...])
    out[:, :width] = grad[:, :width].astype(bf16)
    out[:, width : 3 * width] = (grad[:, width:] + far).astype(bf16)
    per = parts[0].shape[0] // out.shape[0]
    member = (k // per) ^ idx[0]
    at = pl.multiple_of((k % per) * out.shape[0], 16)
    for r in range(TEAM):
        @pl.when(member == r)
        def _(r=r):
            out[:, 3 * width :] = parts[r][pl.ds(at, out.shape[0]), :]


def attn_grad(idx, inputs, d_qkv, context, d_ctx_kv, parts):
    dim, step = inputs.shape[1], LANES
    return pl.pallas_call(
        attn_grad_kernel,
        grid=(dim // step,),
        out_shape=jax.ShapeDtypeStruct((dim, d_qkv.shape[1] + parts[0].shape[1]), bf16),
        in_specs=[
            scalar_spec(),
            pl.BlockSpec((inputs.shape[0], step), lambda k: (0, k)),
            block_of(d_qkv.shape),
            pl.BlockSpec((context.shape[0], step), lambda k: (0, k)),
            block_of(d_ctx_kv.shape),
        ]
        + [block_of(p.shape) for p in parts],
        out_specs=pl.BlockSpec((step, d_qkv.shape[1] + parts[0].shape[1]), lambda k: (k, 0)),
        compiler_params=SMALL,
        name="attn_grad",
    )(idx, inputs, d_qkv, context, d_ctx_kv, *parts)


def insert_bit(k, at, bit):
    return ((k >> at) << (at + 1)) | (bit << at) | (k & ((1 << at) - 1))


def split_kernel(before, side, at, place, x_ref, *refs):
    here = (place[0] >> side) & 1
    if before is None:
        (away_ref,) = refs
        for k in range(away_ref.shape[0]):
            away_ref[k] = x_ref[insert_bit(k, at, 1 - here)]
        return
    recv_ref, keep_ref, away_ref = refs

    def total(k):
        j = k if before is True else insert_bit(k, before[1], (place[0] >> before[0]) & 1)
        return (x_ref[j].astype(f32) + recv_ref[k].astype(f32)).astype(bf16)

    for k in range(away_ref.shape[0]):
        away_ref[k] = total(insert_bit(k, at, 1 - here))
        keep_ref[k] = total(insert_bit(k, at, here))


class Reduction:
    def __init__(self, x, place):
        ny = lax.axis_size("dp") // 2
        ns = lax.axis_size("seq")
        y_bits = ny.bit_length() - 1
        steps = [("dp", bit, (bit // 2).bit_length() - 1, 0) for bit in reversed(high_bits("dp"))]
        steps += [("seq", b, (b * ny).bit_length() - 1, 1) for b in reversed(high_bits("seq"))]
        self.steps = steps + [("seq", 1, y_bits, 0)]
        self.place, self.n, self.came = place, 0, None
        self.kept = x.reshape(ns * ny, -1, x.shape[1])

    def step(self, wait=None):
        n, x, recv = self.n, self.kept, self.came
        axis, bit, side, at = self.steps[n]
        if n == 0 and wait is not None:
            x = after(x, wait)
        elif wait is not None:
            recv = after(recv, wait)
        before = None if n == 0 else (self.steps[0][2:] if n == 1 else True)
        count = x.shape[0] // 2 if n == 0 else recv.shape[0] // 2
        half = jax.ShapeDtypeStruct((count,) + x.shape[1:], bf16)
        out = call(
            functools.partial(split_kernel, before, side, at),
            "split_sum",
            [half] if n == 0 else [half, half],
            (self.place, x) if n == 0 else (self.place, x, recv),
        )
        if n:
            self.kept = out[0]
        self.sent = out[-1]
        self.came = swap(self.sent, axis, bit)
        self.n += 1
        return self.sent

    def last(self, wait=None):
        while self.n < len(self.steps):
            self.step(wait)
            wait = None
        return self.kept, self.came


def halves_kernel(place, x_ref, out_ref, in_ref):
    y, z = place[0] & 1, (place[0] >> 2) & 1
    for k in range(out_ref.shape[0]):
        low = ((k >> 1) << 3) | ((k & 1) << 1) | (1 - y)
        out_ref[k] = x_ref[low | ((1 - z) << 2)]
        in_ref[k] = x_ref[low | (z << 2)]


def leave_kernel(place, x_ref, came_ref, out_ref):
    y, z = place[0] & 1, (place[0] >> 2) & 1
    for k in range(out_ref.shape[0]):
        mine = x_ref[((k >> 1) << 3) | ((1 - z) << 2) | ((k & 1) << 1) | y]
        out_ref[k] = (mine.astype(f32) + came_ref[k].astype(f32)).astype(bf16)


def stay_kernel(place, x_ref, came_ref, near_ref, keep_ref, out_ref):
    y, z, far = place[0] & 1, (place[0] >> 2) & 1, (place[0] >> 3) & 1

    def total(k):
        mine = x_ref[((k >> 1) << 3) | (z << 2) | ((k & 1) << 1) | y]
        return (mine.astype(f32) + came_ref[k].astype(f32) + near_ref[k].astype(f32)).astype(bf16)

    for k in (0, 1):
        keep_ref[k] = total((far << 1) | k)
        out_ref[k] = total(((1 - far) << 1) | k)


class HalvedReduction(Reduction):
    def step(self, wait=None):
        n = self.n
        if n > 2:
            self.steps = [None, None, None, ("seq", 1, 1, 0)]
            return super().step(wait)
        x = self.kept
        four = jax.ShapeDtypeStruct((x.shape[0] // 4,) + x.shape[1:], bf16)
        two = jax.ShapeDtypeStruct((2,) + x.shape[1:], bf16)
        if n == 0:
            x = x if wait is None else after(x, wait)
            out, stay = call(halves_kernel, "halves", (four, four), (self.place, x))
            self.sent = out
            self.out, self.stay = swap(out, "dp", 2), swap(stay, "dp", 2)
        elif n == 1:
            came = self.out if wait is None else after(self.out, wait)
            self.sent = call(leave_kernel, "leave_sum", four, (self.place, x, came))
            self.near = swap(self.sent, "seq", 2)
        else:
            came = self.near if wait is None else after(self.near, wait)
            args = (self.place, x, self.stay, came)
            self.kept, self.sent = call(stay_kernel, "stay_sum", (two, two), args)
            self.came = swap(self.sent, "seq", 4)
        self.n += 1
        return self.sent


def final_kernel(kind, fb, idx, mine_ref, other_ref, *outs):
    count, rows, width = mine_ref.shape
    for k in range(count):
        row = pl.multiple_of((idx[1] ^ (k // 2)) * rows, 16)
        for core, ref in enumerate((mine_ref, other_ref)):
            member = idx[0] ^ (2 * (k % 2) + core)
            if kind == "down":
                at = pl.multiple_of(member * (rows * count // 2) + row, 16)
                outs[0][pl.ds(at, rows), :] = ref[k].astype(f32)
            elif kind == "up":
                for n in range(width // fb):
                    col = pl.multiple_of((n * TEAM + member) * fb, LANES)
                    block = ref[k, :, n * fb : (n + 1) * fb]
                    outs[0][pl.ds(row, rows), pl.ds(col, fb)] = block.astype(f32)
            else:
                dim = outs[1].shape[1]
                quarter = dim // TEAM
                for part in range(4):
                    to = outs[0] if part < 3 else outs[1]
                    col = pl.multiple_of((part % 3) * dim * (part < 3) + member * quarter, LANES)
                    block = ref[k, :, part * quarter : (part + 1) * quarter]
                    to[pl.ds(row, rows), pl.ds(col, quarter)] = block.astype(f32)


def spread_places(pair):
    blocks = {0: append(*pair)}
    for bit in high_bits("dp"):
        for m in list(blocks):
            blocks[m | (bit // 2)] = swap(blocks[m], "dp", bit)
    return [blocks[m] for m in range(len(blocks))]


def spread_cores(blocks):
    while len(blocks) > 1:
        blocks = [append(a, b) for a, b in zip(blocks[0::2], blocks[1::2])]
    return blocks[0], swap(blocks[0], "dp", 1)


def spread_weight(kind, blocks, idx, shapes, fb=LANES):
    return call(
        functools.partial(final_kernel, kind, fb),
        "final_" + kind,
        [jax.ShapeDtypeStruct(s, f32) for s in shapes],
        (idx, *spread_cores(blocks)),
    )


def spread_narrow(blocks, idx, shape, fb):
    mine, other = spread_cores(blocks)
    teams = [mine[0::2], other[0::2], mine[1::2], other[1::2]]
    teams = jnp.stack(ordered(teams, idx[0]))
    rows = jnp.stack(ordered([teams[:, m] for m in range(teams.shape[1])], idx[1]), axis=1)
    rows = rows.reshape(TEAM, shape[0], shape[1] // (TEAM * fb), fb).transpose(1, 2, 0, 3)
    return rows.reshape(shape).astype(f32)


def ends_kernel(mid, u_ref, a_ref, mid_ref, end_ref):
    rows = u_ref.shape[0]
    a = [a_ref[n] for n in range(NST)]

    def eight(k, s):
        for t in range(8):
            u = u_ref[k * 8 + t]
            s = tuple(a[n] * s[n] + u for n in range(NST))
        return s

    zero = tuple(jnp.zeros_like(a[0]) for _ in range(NST))
    s = lax.fori_loop(0, mid // 8, eight, zero)
    for n in range(NST):
        mid_ref[n] = s[n]
    s = lax.fori_loop(mid // 8, rows // 8, eight, s)
    for n in range(NST):
        end_ref[n] = s[n]


def local_ends(u, a):
    shape = jax.ShapeDtypeStruct(a.shape, f32)
    kernel = functools.partial(ends_kernel, u.shape[0] - CTX)
    return call(kernel, "ssm_ends", (shape, shape), (u, a), 0)


def context_kernel(mid, late, u_ref, a_ref, gin_ref, gout_ref, h_ref, first_ref, second_ref, y_ref):
    half = NST // 2
    for base in (0, half):
        ns = range(base, base + half)
        a = [a_ref[n] for n in ns]
        gin = [gin_ref[n] for n in ns]
        gout = [gout_ref[n] for n in ns]

        def step(k, h):
            for t in range(4):
                p = k * 4 + t
                u = u_ref[mid + p]
                h = tuple(a[n] * h[n] + gin[n] * u for n in range(half))
                y = functools.reduce(jnp.add, [gout[n] * h[n] for n in range(half)])
                y_ref[p] = y if base == 0 else y_ref[p] + y
            return h

        lax.fori_loop(0, CTX // 4, step, tuple(h_ref[n] for n in ns))
    per = y_ref.shape[1] // TEAM
    for w in range(2):
        for c in range(per):
            own, other = y_ref[:, w * per + c, :], y_ref[:, (2 + w) * per + c, :]
            at = (slice(w * CTX, (w + 1) * CTX), slice(c * LANES, (c + 1) * LANES))
            first_ref[at] = jnp.where(late[0] == 1, other, own).astype(bf16)
            second_ref[at] = jnp.where(late[0] == 1, own, other).astype(bf16)


def contexts(half, u, a, gin, gout, h_mid):
    shape = jax.ShapeDtypeStruct((2 * CTX, u.shape[1] * LANES // TEAM), bf16)
    return call(
        functools.partial(context_kernel, u.shape[0] - CTX),
        "ssm_context",
        (shape, shape),
        (half, u, a, gin, gout, h_mid),
        scratch_shapes=[pltpu.VMEM((CTX,) + u.shape[1:], f32)],
    )


def tail_kernel(dy_ref, a_ref, gout_ref, lam_ref):
    half = dy_ref.shape[1]
    a = [a_ref[n, :half] for n in range(NST)]
    gout = [gout_ref[n, :half] for n in range(NST)]

    def eight(k, lam):
        for t in range(8):
            dy = dy_ref[CTX - 1 - (k * 8 + t)]
            lam = tuple(a[n] * lam[n] + gout[n] * dy for n in range(NST))
        return lam

    lam = lax.fori_loop(0, CTX // 8, eight, tuple(jnp.zeros_like(a[0]) for _ in range(NST)))
    for n in range(NST):
        lam_ref[n] = lam[n]


def tail_adjoint(dy, a, gout):
    shape = jax.ShapeDtypeStruct((NST,) + dy.shape[1:], f32)
    return call(tail_kernel, "ssm_tail", shape, (dy, a, gout), 0)


def first_context_kernel(dy0_ref, a_ref, gout_ref, init_ref, da_ref, dgout_ref, g0_ref, hs):
    half = a_ref.shape[1] // 2
    ns = range(a_ref.shape[0] // 2)

    def paired(ref):
        return [jnp.concatenate([ref[2 * n, :half], ref[2 * n + 1, :half]], axis=0) for n in ns]

    a, gout, init = paired(a_ref), paired(gout_ref), paired(init_ref)
    zero = tuple(jnp.zeros_like(a[0]) for _ in ns)

    def ahead(k, h):
        for t in range(8):
            h = tuple(a[n] * h[n] for n in ns)
            for n in ns:
                hs[k * 8 + t + 1, n] = h[n]
        return h

    h = tuple(init)
    for n in ns:
        hs[0, n] = h[n]
    lax.fori_loop(0, CTX // 8, ahead, h)

    def back(k, carry):
        mu, da, dgout = carry
        for t in range(4):
            q = CTX - 1 - (k * 4 + t)
            dy = dy0_ref[q]
            mu = tuple(mu[n] + gout[n] * dy for n in ns)
            dgout = tuple(dgout[n] + dy * hs[q + 1, n] for n in ns)
            da = tuple(da[n] + mu[n] * hs[q, n] for n in ns)
            mu = tuple(a[n] * mu[n] for n in ns)
        return mu, da, dgout

    results = lax.fori_loop(0, CTX // 4, back, (zero, zero, zero))
    rest = jnp.zeros_like(a[0][:half])
    for ref, values in zip((g0_ref, da_ref, dgout_ref), results):
        for n in ns:
            ref[2 * n] = jnp.concatenate([values[n][:half], rest], axis=0)
            ref[2 * n + 1] = jnp.concatenate([values[n][half:], rest], axis=0)


def first_context_back(dy0, a, gout, h_init):
    tile = dy0.shape[1:]
    states = pl.BlockSpec((2 * GROUP,) + tile, lambda g: (g, 0, 0))
    return pl.pallas_call(
        first_context_kernel,
        grid=(NST // (2 * GROUP),),
        out_shape=(jax.ShapeDtypeStruct(a.shape, f32),) * 3,
        in_specs=[pl.BlockSpec(dy0.shape, lambda g: (0, 0, 0))] + [states] * 3,
        out_specs=(states,) * 3,
        scratch_shapes=[pltpu.VMEM((CTX + 1, GROUP) + tile, f32)],
        name="first_context",
    )(dy0, a, gout, h_init)


def back_kernel(
    u_ref, dy_ref, a_ref, gin_ref, gout_ref, h_ref, lam_ref, da0_ref, dgout0_ref,
    du_ref, dgin_ref, da_ref, dgout_ref, g_ref, hs,
):
    first = pl.program_id(0) == 0
    rows = u_ref.shape[0]
    mid = rows - CTX
    ns = range(GROUP)
    a = [a_ref[n] for n in ns]
    gin = [gin_ref[n] for n in ns]
    gout = [gout_ref[n] for n in ns]
    zero = tuple(jnp.zeros_like(a[0]) for _ in ns)

    def ahead(k, h):
        for t in range(8):
            p = k * 8 + t
            u = u_ref[p]
            h = tuple(a[n] * h[n] + gin[n] * u for n in ns)
            for n in ns:
                hs[p + 1, n] = h[n]
        return h

    h = tuple(h_ref[n] for n in ns)
    for n in ns:
        hs[0, n] = h[n]
    lax.fori_loop(0, rows // 8, ahead, h)

    def tail(k, carry):
        lam, dgin, da, dgout = carry
        for t in range(4):
            q = CTX - 1 - (k * 4 + t)
            p = mid + q
            dy, u = dy_ref[q], u_ref[p]
            lam = tuple(lam[n] + gout[n] * dy for n in ns)
            dgout = tuple(dgout[n] + dy * hs[p + 1, n] for n in ns)
            dgin = tuple(dgin[n] + lam[n] * u for n in ns)
            da = tuple(da[n] + lam[n] * hs[p, n] for n in ns)
            du = functools.reduce(jnp.add, [gin[n] * lam[n] for n in ns])
            du_ref[p] = jnp.where(first, du, du_ref[p] + du)
            lam = tuple(a[n] * lam[n] for n in ns)
        return lam, dgin, da, dgout

    def head(k, carry):
        lam, dgin, da = carry
        for t in range(4):
            p = mid - 1 - (k * 4 + t)
            u = u_ref[p]
            dgin = tuple(dgin[n] + lam[n] * u for n in ns)
            da = tuple(da[n] + lam[n] * hs[p, n] for n in ns)
            du = functools.reduce(jnp.add, [gin[n] * lam[n] for n in ns])
            du_ref[p] = jnp.where(first, du, du_ref[p] + du)
            lam = tuple(a[n] * lam[n] for n in ns)
        return lam, dgin, da

    lam = tuple(lam_ref[n] for n in ns)
    da0, dgout0 = tuple(da0_ref[n] for n in ns), tuple(dgout0_ref[n] for n in ns)
    lam, dgin, da, dgout = lax.fori_loop(0, CTX // 4, tail, (lam, zero, da0, dgout0))
    lam, dgin, da = lax.fori_loop(0, mid // 4, head, (lam, dgin, da))
    for n in ns:
        g_ref[n] = lam[n]
        dgin_ref[n] = dgin[n]
        da_ref[n] = da[n]
        dgout_ref[n] = dgout[n]


def ssm_back(u, dy, a, gin, gout, state_in, lam_end, da0, dgout0):
    tile = u.shape[1:]
    states = pl.BlockSpec((GROUP,) + tile, lambda g: (g, 0, 0))
    rows = pl.BlockSpec(u.shape, lambda g: (0, 0, 0))
    tail = pl.BlockSpec(dy.shape, lambda g: (0, 0, 0))
    out = jax.ShapeDtypeStruct(a.shape, f32)
    return pl.pallas_call(
        back_kernel,
        grid=(NST // GROUP,),
        out_shape=(jax.ShapeDtypeStruct(u.shape, f32),) + (out,) * 4,
        in_specs=[rows, tail] + [states] * 7,
        out_specs=(rows,) + (states,) * 4,
        scratch_shapes=[pltpu.VMEM((u.shape[0] + 1, GROUP) + tile, f32)],
        compiler_params=SMALL,
        name="ssm_back",
    )(u, dy, a, gin, gout, state_in, lam_end, da0, dgout0)


def dot_nt(x, y):
    return lax.dot_general(x, y, (((1,), (1,)), ((), ())), preferred_element_type=f32)


def dot_nn(x, y):
    return jnp.dot(x, y, preferred_element_type=f32)


def dot_tn(x, y):
    return lax.dot_general(x, y, (((0,), (0,)), ((), ())), preferred_element_type=f32)


def softmax_parts(q, keys):
    rows = q.shape[0]
    scores = [dot_nt(q, k) * (1.0 / math.sqrt(HD)) for k in keys]
    at = lax.broadcasted_iota(jnp.int32, (rows, rows), 0)
    to = lax.broadcasted_iota(jnp.int32, (rows, rows), 1)
    scores[-1] = jnp.where(to <= at, scores[-1], far_below)
    top = functools.reduce(jnp.maximum, [jnp.max(s, axis=-1, keepdims=True) for s in scores])
    es = [jnp.exp(s - top) for s in scores]
    total = functools.reduce(jnp.add, [jnp.sum(e, axis=-1, keepdims=True) for e in es])
    return [e / total for e in es]


def attend_kernel(half_ref, q0, q1, k0, k1, v0, v1, kc, vc, out_ref):
    w, h = pl.program_id(0), pl.program_id(1)
    rows = q0.shape[0]
    for half, q, keys, values in ((0, q0, (kc, k0), (vc, v0)), (1, q1, (kc, k0, k1), (vc, v0, v1))):
        probs = softmax_parts(q[...], [k[...] for k in keys])
        out = [dot_nn(p.astype(bf16), v[...]) for p, v in zip(probs, values)]
        at = pl.multiple_of(((half ^ half_ref[0]) * 2 + w) * rows, 16)
        col = pl.multiple_of(h * HD, LANES)
        out_ref[pl.ds(at, rows), pl.ds(col, HD)] = functools.reduce(jnp.add, out).astype(bf16)


def attend_back_kernel(
    half_ref, q0, q1, k0, k1, v0, v1, kc, vc, do0, do1, dqkv_ref, dctx_ref
):
    w, h = pl.program_id(0), pl.program_id(1)
    rows, heads = q0.shape[0], pl.num_programs(1)
    scale = 1.0 / math.sqrt(HD)
    dk, dv = [0.0, 0.0, 0.0], [0.0, 0.0, 0.0]

    def row_of(half):
        return pl.multiple_of(((half ^ half_ref[0]) * 2 + w) * rows, 16)

    def col_of(part):
        return pl.multiple_of((part * heads + h) * HD, LANES)

    cases = ((0, q0, do0, (kc, k0), (vc, v0)), (1, q1, do1, (kc, k0, k1), (vc, v0, v1)))
    for half, q, do, keys, values in cases:
        query, d_out = q[...], do[...]
        probs = softmax_parts(query, [k[...] for k in keys])
        d_probs = [dot_nt(d_out, v[...]) for v in values]
        sums = [jnp.sum(p * d, axis=-1, keepdims=True) for p, d in zip(probs, d_probs)]
        delta = functools.reduce(jnp.add, sums)
        d_scores = [(p * (d - delta)).astype(bf16) for p, d in zip(probs, d_probs)]
        dq = functools.reduce(jnp.add, [dot_nn(d, k[...]) for d, k in zip(d_scores, keys)])
        dqkv_ref[pl.ds(row_of(half), rows), pl.ds(col_of(0), HD)] = (dq * scale).astype(bf16)
        for n, (d, p) in enumerate(zip(d_scores, probs)):
            dk[n] = dk[n] + dot_tn(d, query)
            dv[n] = dv[n] + dot_tn(p.astype(bf16), d_out)
    ctx_row = pl.multiple_of(w * CTX, 16)
    dctx_ref[pl.ds(ctx_row, CTX), pl.ds(col_of(0), HD)] = (dk[0] * scale).astype(bf16)
    dctx_ref[pl.ds(ctx_row, CTX), pl.ds(col_of(1), HD)] = dv[0].astype(bf16)
    for half in (0, 1):
        dqkv_ref[pl.ds(row_of(half), rows), pl.ds(col_of(1), HD)] = (dk[1 + half] * scale).astype(bf16)
        dqkv_ref[pl.ds(row_of(half), rows), pl.ds(col_of(2), HD)] = dv[1 + half].astype(bf16)


def attention_specs(rows, heads):
    def at(half, part):
        return pl.BlockSpec((rows, HD), lambda w, h, s: ((half ^ s[0]) * 2 + w, part * heads + h))

    def ctx(part):
        return pl.BlockSpec((CTX, HD), lambda w, h, s: (w, part * heads + h))

    return [at(half, part) for part in range(3) for half in (0, 1)] + [ctx(0), ctx(1)]


def whole_block(shape):
    return pl.BlockSpec(shape, lambda w, h, s: (0, 0))


def attend(half, qkv, ctx_kv):
    rows, heads = qkv.shape[0] // TEAM, qkv.shape[1] // (3 * HD)
    out = (qkv.shape[0], heads * HD)
    return pl.pallas_call(
        attend_kernel,
        grid_spec=pltpu.PrefetchScalarGridSpec(
            num_scalar_prefetch=1,
            grid=(2, heads),
            in_specs=attention_specs(rows, heads),
            out_specs=whole_block(out),
        ),
        out_shape=jax.ShapeDtypeStruct(out, bf16),
        compiler_params=SMALL,
        name="attend",
    )(half, *[qkv] * 6, ctx_kv, ctx_kv)


def attend_back(half, qkv, ctx_kv, d_attended):
    rows, heads = qkv.shape[0] // TEAM, qkv.shape[1] // (3 * HD)

    def at(side):
        return pl.BlockSpec((rows, HD), lambda w, h, s: ((side ^ s[0]) * 2 + w, h))

    return pl.pallas_call(
        attend_back_kernel,
        grid_spec=pltpu.PrefetchScalarGridSpec(
            num_scalar_prefetch=1,
            grid=(2, heads),
            in_specs=attention_specs(rows, heads) + [at(0), at(1)],
            out_specs=[whole_block(qkv.shape), whole_block(ctx_kv.shape)],
        ),
        out_shape=[jax.ShapeDtypeStruct(qkv.shape, bf16), jax.ShapeDtypeStruct(ctx_kv.shape, bf16)],
        compiler_params=SMALL,
        name="attend_back",
    )(half, *[qkv] * 6, ctx_kv, ctx_kv, d_attended, d_attended)


def pack_kernel(rate, gin, gout, g_one, g_two, out):
    for k, ref in enumerate((rate, gin, gout)):
        out[0, k * NST : (k + 1) * NST, :] = ref[...]
    out[0, 3 * NST : 3 * NST + 1, :] = g_one[...]
    out[0, 3 * NST + 1 : 3 * NST + 2, :] = g_two[...]


def norm_kernel(idx, gain, x0, x1, x2, x3, low_ref, inv_ref, u_ref):
    rows, dim = x0.shape
    cols = dim // TEAM
    for r, ref in enumerate((x0, x1, x2, x3)):
        x = ref[...].astype(f32)
        inv = lax.rsqrt(jnp.mean(x * x, axis=-1, keepdims=True) + epsilon)
        inv_ref[r * rows : (r + 1) * rows, :] = inv
        low_ref[r * rows : (r + 1) * rows, :] = (x * inv * gain[...]).astype(bf16)
        for c in range(cols // LANES):
            at = pl.multiple_of(idx[0] * cols + c * LANES, LANES)
            u = low_ref[r * rows : (r + 1) * rows, pl.ds(at, LANES)].astype(f32)
            u_ref[:, r * (cols // LANES) + c, :] = u


def first_norm(idx, gain, blocks):
    rows, dim = blocks[0].shape
    shapes = (
        jax.ShapeDtypeStruct((TEAM * rows, dim), bf16),
        jax.ShapeDtypeStruct((TEAM * rows, 1), f32),
        jax.ShapeDtypeStruct((rows, dim // LANES, LANES), f32),
    )
    return call(norm_kernel, "first_norm", shapes, (idx, gain[None], *blocks))


def part_types(rows, dim):
    return tuple(jax.ShapeDtypeStruct((rows, dim), (f32, bf16)[r % 2]) for r in range(TEAM))


def dot_kernel(x_ref, w_ref, *parts):
    rows = parts[0].shape[0]
    for r in (3, 1, 2, 0):
        part = dot_nn(x_ref[r * rows : (r + 1) * rows, :], w_ref[...])
        parts[r][...] = part.astype(parts[r].dtype)


def dot_parts(name, x, w):
    return call(dot_kernel, name, part_types(x.shape[0] // TEAM, w.shape[1]), (x, w), 0)


def out_kernel(idx, x_ref, w0, w1, w2, w3, *parts):
    rows, cols = parts[0].shape[0], w0.shape[1]
    for r in (3, 1, 2, 0):
        for q, w in enumerate((w0, w1, w2, w3)):
            at = pl.multiple_of((idx[0] ^ q) * cols, LANES)
            part = dot_nn(x_ref[r * rows : (r + 1) * rows, :], w[...])
            parts[r][:, pl.ds(at, cols)] = part.astype(parts[r].dtype)


def context_kv_kernel(idx, w_ref, c0, c1, c2, c3, kv_ref, context_ref):
    cols = c0.shape[1]
    width = w_ref.shape[1] // 3
    for r, part in enumerate((c0, c1, c2, c3)):
        at = pl.multiple_of((idx[0] ^ r) * cols, LANES)
        for w in (0, 1):
            v = w ^ (r & 1)
            context_ref[w * CTX : (w + 1) * CTX, pl.ds(at, cols)] = part[v * CTX : (v + 1) * CTX, :]
    kv_ref[...] = dot_nn(context_ref[...], w_ref[:, width:]).astype(bf16)


def mlp_kernel(m0, m1, m2, m3, g0, g1, g2, g3, up, down, act_ref, dpre_ref, *parts_and_sum):
    parts, total = parts_and_sum[:-1], parts_and_sum[-1]
    k = pl.program_id(0)
    rows = m0.shape[0]
    c = math.sqrt(2.0 / math.pi)
    for r, (m, g) in enumerate(((m0, g0), (m1, g1), (m2, g2), (m3, g3))):
        at = slice(r * rows, (r + 1) * rows)
        x = dot_nn(m[...], up[...])
        t = jnp.tanh(c * (x + 0.044715 * (x * x * x)))
        cdf = 0.5 * (1.0 + t)
        act_ref[at, :] = (x * cdf).astype(bf16)
        slope = cdf + (0.5 * c) * x * (1.0 - t * t) * (1.0 + (3 * 0.044715) * (x * x))
        d_pre = (dot_nt(g[...], down[...]) * slope).astype(bf16)
        dpre_ref[at, :] = d_pre
        new = dot_nt(d_pre, up[...])
        total[at, :] = jnp.where(k == 0, new, total[at, :] + new)

    @pl.when(k == pl.num_programs(0) - 1)
    def _():
        for r, part in enumerate(parts):
            part[...] = total[r * rows : (r + 1) * rows, :].astype(part.dtype)


def feed_forward(mlp_blocks, grad_blocks, up, down):
    rows, dim = mlp_blocks[0].shape
    units = up.shape[1]
    step = 256

    unit_out = jax.ShapeDtypeStruct((TEAM * rows, units), bf16)
    return pl.pallas_call(
        mlp_kernel,
        grid=(units // step,),
        out_shape=(unit_out, unit_out) + part_types(rows, dim),
        in_specs=[block_of((rows, dim))] * 8
        + [pl.BlockSpec((dim, step), lambda k: (0, k)), pl.BlockSpec((step, dim), lambda k: (k, 0))],
        out_specs=(pl.BlockSpec((TEAM * rows, step), lambda k: (0, k)),) * 2
        + (block_of((rows, dim)),) * TEAM,
        scratch_shapes=[pltpu.VMEM((TEAM * rows, dim), f32)],
        compiler_params=MIDDLE,
        name="feed_forward",
    )(*mlp_blocks, *grad_blocks, up, down)


def mlp_grad_kernel(x_ref, y0, y1, y2, y3, out):
    rows = y0.shape[0]
    grads = [dot_tn(x_ref[r * rows : (r + 1) * rows, :], y[...]) for r, y in enumerate((y0, y1, y2, y3))]
    out[...] = functools.reduce(jnp.add, grads).astype(bf16)


def down_grad(act, grad_blocks):
    rows, dim = grad_blocks[0].shape
    step = 256
    return pl.pallas_call(
        mlp_grad_kernel,
        grid=(act.shape[1] // step,),
        out_shape=jax.ShapeDtypeStruct((act.shape[1], dim), bf16),
        in_specs=[pl.BlockSpec((act.shape[0], step), lambda k: (0, k))]
        + [block_of((rows, dim))] * TEAM,
        out_specs=pl.BlockSpec((step, dim), lambda k: (k, 0)),
        compiler_params=SMALL,
        name="down_grad",
    )(act, *grad_blocks)


def up_grad_kernel(x0, x1, x2, x3, y_ref, out):
    rows = x0.shape[0]
    grads = [dot_tn(x[...], y_ref[r * rows : (r + 1) * rows, :]) for r, x in enumerate((x0, x1, x2, x3))]
    out[...] = functools.reduce(jnp.add, grads).astype(bf16)


def up_grad(mlp_blocks, d_pre):
    rows, dim = mlp_blocks[0].shape
    step = 256
    return pl.pallas_call(
        up_grad_kernel,
        grid=(dim // step,),
        out_shape=jax.ShapeDtypeStruct((dim, d_pre.shape[1]), bf16),
        in_specs=[pl.BlockSpec((rows, step), lambda k: (0, k))] * TEAM
        + [block_of(d_pre.shape)],
        out_specs=pl.BlockSpec((step, d_pre.shape[1]), lambda k: (k, 0)),
        compiler_params=SMALL,
        name="up_grad",
    )(*mlp_blocks, d_pre)


def attended_grad_kernel(idx, w0, w1, w2, w3, h0, h1, h2, h3, out):
    rows, cols = h0.shape[0], w0.shape[1]
    for r, h in enumerate((h0, h1, h2, h3)):
        grad = 0.0
        for q, w in enumerate((w0, w1, w2, w3)):
            at = pl.multiple_of((idx[0] ^ q) * cols, LANES)
            grad = grad + dot_nt(h[:, pl.ds(at, cols)], w[...])
        out[r * rows : (r + 1) * rows, :] = grad.astype(bf16)


def out_grad_kernel(idx, att_ref, h0, h1, h2, h3, *parts):
    rows, cols = h0.shape[0], parts[0].shape[1]
    for q, part in enumerate(parts):
        at = pl.multiple_of((idx[0] ^ q) * cols, LANES)
        grads = [
            dot_tn(att_ref[r * rows : (r + 1) * rows, :], h[:, pl.ds(at, cols)])
            for r, h in enumerate((h0, h1, h2, h3))
        ]
        part[...] = functools.reduce(jnp.add, grads).astype(bf16)


def context_grad_kernel(idx, d_ref, w_ref, *parts):
    cols = parts[0].shape[1]
    width = w_ref.shape[1] // 3
    for r, part in enumerate(parts):
        at = pl.multiple_of((idx[0] ^ r) * cols, 16)
        for w in (0, 1):
            v = w ^ (r & 1)
            grad = dot_nt(d_ref[w * CTX : (w + 1) * CTX, :], w_ref[pl.ds(at, cols), width:])
            part[v * CTX : (v + 1) * CTX, :] = grad.astype(part.dtype)


def inputs_grad_kernel(idx, dq_ref, w_ref, du_ref, inv_ref, x0, x1, x2, x3, *outs):
    parts, gain_ref, work = outs[:TEAM], outs[TEAM], outs[TEAM + 1]
    rows, dim = x0.shape
    cols = dim // TEAM
    gain = 0.0
    for r, x in enumerate((x0, x1, x2, x3)):
        at = slice(r * rows, (r + 1) * rows)
        work[...] = dot_nt(dq_ref[at, :], w_ref[...])
        for c in range(cols // LANES):
            col = pl.ds(pl.multiple_of(idx[0] * cols + c * LANES, LANES), LANES)
            work[:, col] = work[:, col] + du_ref[:, r * (cols // LANES) + c, :]
        grad = work[...]
        parts[r][...] = grad.astype(parts[r].dtype)
        gain = gain + jnp.sum(grad * (x[...].astype(f32) * inv_ref[at, :]), axis=0, keepdims=True)
    gain_ref[...] = gain


def cut_states_kernel(idx, init_ref, ends_ref, i0, i1, e0, e1, e2, e3):
    cols = i0.shape[1]
    for r, out in enumerate((e0, e1, e2, e3)):
        at = pl.multiple_of((idx[0] ^ r) * cols, LANES)
        out[...] = ends_ref[:, pl.ds(at, cols)]
        if r < 2:
            (i0, i1)[r][...] = init_ref[:, pl.ds(at, cols)]


def join_states_kernel(late, i0, i1, e0, e1, e2, e3, init_ref, twice_ref, first_ref, second_ref):
    per = init_ref.shape[1] // 2
    for w in range(2):
        for c in range(per):
            at = slice(c * LANES, (c + 1) * LANES)
            init = (i0, i1)[w][:, at]
            init_ref[:, w * per + c, :] = init
            twice_ref[:, w * per + c, :] = init
            twice_ref[:, (2 + w) * per + c, :] = init
            own, other = (e0, e1)[w][:, at], (e2, e3)[w][:, at]
            first_ref[:, w * per + c, :] = jnp.where(late[0] == 1, other, own)
            second_ref[:, w * per + c, :] = jnp.where(late[0] == 1, own, other)


def cut_ends_kernel(late, first_ref, second_ref, e0, e1, e2, e3):
    per = first_ref.shape[1] // 2
    for w in range(2):
        for c in range(per):
            at = slice(c * LANES, (c + 1) * LANES)
            one, two = first_ref[:, w * per + c, :], second_ref[:, w * per + c, :]
            (e0, e1)[w][:, at] = jnp.where(late[0] == 1, two, one)
            (e2, e3)[w][:, at] = jnp.where(late[0] == 1, one, two)


def join_ends_kernel(idx, e0, e1, e2, e3, out):
    cols = e0.shape[1]
    for r, part in enumerate((e0, e1, e2, e3)):
        at = pl.multiple_of((idx[0] ^ r) * cols, LANES)
        out[:, pl.ds(at, cols)] = part[...]


def small_pack_kernel(flags, a, d_a, d_in, d_out, g_in, g_init, one, two, out):
    per = d_a.shape[1] // TEAM
    row = 0
    for k, ref in enumerate((d_a, d_in, d_out)):
        for c in range(per):
            total = 0.0
            for r in range(TEAM):
                part = ref[:, r * per + c, :]
                total = total + (-a[:, r * per + c, :] * part if k == 0 else part)
            out[row : row + NST, :] = total
            row += NST
    for ref in (one, two):
        for c in range(ref.shape[1] // LANES):
            out[row : row + 1, :] = ref[:, c * LANES : (c + 1) * LANES]
            row += 1
    for s in range(2 * per):
        first = jnp.where(flags[0] == 1, g_in[:, 2 * per + s, :], g_in[:, s, :])
        out[row : row + NST, :] = g_init[:, s, :] + jnp.where(flags[1] == 0, first, 0.0)
        row += NST


def small_kernel(spots, p0, p1, p2, p3, gains_ref, rate_ref, in_ref, out_ref, init_ref):
    packs = [p[...] for p in (p0, p1, p2, p3)]
    tiles = packs[0].shape[0] - 3 * NST * 2 - NST * 4
    one, two = 3 * NST * 2, 3 * NST * 2 + tiles
    gains = functools.reduce(jnp.add, [p[one:two] for p in packs])
    row = lax.broadcasted_iota(jnp.int32, gains.shape, 0)
    for k in (0, 1):
        mine = row == k * (tiles // 2) + spots[1]
        gains_ref[k : k + 1, :] = jnp.sum(jnp.where(mine, gains, 0.0), axis=0, keepdims=True)
    chosen = packs[0]
    for r in (1, 2, 3):
        chosen = jnp.where(spots[0] == r, packs[r], chosen)
    side = spots[1] % 2 == 1

    def of_side(at):
        return jnp.where(side, chosen[at + NST : at + 2 * NST], chosen[at : at + NST])

    for k, ref in enumerate((rate_ref, in_ref, out_ref)):
        ref[...] = of_side(2 * NST * k)
    window = [of_side(two + 2 * NST * w) for w in (0, 1)]
    init_ref[...] = jnp.where(spots[0] % 2 == 1, window[1], window[0])


def added(p0, one, far):
    return p0[...] + one[...].astype(f32) + far[...].astype(f32)


def second_norm_kernel(tok, p0, one, far, gain, hidden_ref, inv_ref, low_ref):
    hidden = tok[...].astype(f32) + added(p0, one, far)
    inv = lax.rsqrt(jnp.mean(hidden * hidden, axis=-1, keepdims=True) + epsilon)
    hidden_ref[...] = hidden
    inv_ref[...] = inv
    low_ref[...] = (hidden * inv * gain[...]).astype(bf16)


def result_kernel(hidden, p0, one, far, out):
    out[...] = (hidden[...] + added(p0, one, far)).astype(bf16)


def norm_back(grad, normed, inv, gain):
    scaled = grad * gain
    return inv * (scaled - normed * jnp.mean(scaled * normed, axis=-1, keepdims=True))


def hidden_grad_kernel(cot, hidden, inv, gain, p0, one, far, out_ref, low_ref, gain_ref):
    grad = added(p0, one, far)
    normed = hidden[...] * inv[...]
    gain_ref[...] = jnp.sum(grad * normed, axis=0, keepdims=True)
    out = cot[...].astype(f32) + norm_back(grad, normed, inv[...], gain[...])
    out_ref[...] = out
    low_ref[...] = out.astype(bf16)


def tokens_grad_kernel(d_hidden, tok, inv, gain, p0, one, far, out):
    grad = added(p0, one, far)
    normed = tok[...].astype(f32) * inv[...]
    out[...] = (d_hidden[...] + norm_back(grad, normed, inv[...], gain[...])).astype(bf16)


def context_sum_kernel(p0, one, far, out):
    out[...] = added(p0, one, far).astype(bf16)


def first_rows_kernel(flags, own, dy0_full):
    per = dy0_full.shape[1] // TEAM
    zero = jnp.zeros((CTX, LANES), f32)
    for w in range(2):
        for c in range(per):
            at = (slice(w * CTX, (w + 1) * CTX), slice(c * LANES, (c + 1) * LANES))
            dy0 = jnp.where(flags[1] == 0, own[at].astype(f32), zero)
            dy0_full[:, w * per + c, :] = dy0
            dy0_full[:, (2 + w) * per + c, :] = dy0


def context_rows_kernel(flags, came, dy_ref, dy_full):
    per = dy_ref.shape[1] // 2
    zero = jnp.zeros((CTX, LANES), f32)
    for w in range(2):
        for c in range(per):
            at = (slice(w * CTX, (w + 1) * CTX), slice(c * LANES, (c + 1) * LANES))
            dy = came[at].astype(f32)
            dy_ref[:, w * per + c, :] = dy
            dy_full[:, w * per + c, :] = jnp.where(flags[0] == 1, dy, zero)
            dy_full[:, (2 + w) * per + c, :] = jnp.where(flags[0] == 1, zero, dy)


def on_device(
    tokens,
    w_qkv,
    w_out,
    w_up,
    w_down,
    g_attn,
    g_mlp,
    ssm_rate,
    ssm_in,
    ssm_out,
    h_init,
    cotangent,
    d_h_ends,
):
    nd, ns = lax.axis_size("dp"), lax.axis_size("seq")
    ny = nd // 2
    dp, seq = lax.axis_index("dp"), lax.axis_index("seq")
    late = seq % 2 == 1
    block = seq // 2
    me = (seq % 2) * 2 + dp % 2
    idx = jnp.stack([me, dp // 2]).astype(jnp.int32)
    place = (seq * ny + dp // 2).astype(jnp.int32).reshape(1)
    half = (seq % 2).astype(jnp.int32).reshape(1)
    rows, dim = tokens.shape[1:]
    shard = w_qkv.shape[0]
    width = HEADS * HD // TEAM
    cols = dim // TEAM
    fb = w_down.shape[0] // TEAM
    tile = (dim // LANES, LANES)
    half_tile = (dim // LANES // 2, LANES)

    def like(shape, dtype):
        return jax.ShapeDtypeStruct(shape, dtype)


    share_attn, share_up, share_down = shares(idx, w_qkv, w_out, w_up, w_down, ny, ns)
    attn, up = Gathering(*share_attn, True), Gathering(*share_up, True)
    down = Gathering(*share_down, True)
    attn_pair = attn.step()
    x_blocks = gather_team(after(tokens[0], attn_pair))
    up_pair = up.step(attn_pair)
    attn_first = attn.rest()
    attn_own = attn.a
    down_pair = down.step(attn_first)
    attn_second = attn.step(up_pair)
    attn_third = attn.across(0)
    small = call(
        pack_kernel,
        "pack_small",
        jax.ShapeDtypeStruct((1, 3 * NST + 2, shard), bf16),
        after((ssm_rate.T, ssm_in.T, ssm_out.T, g_attn[None], g_mlp[None]), share_attn[1]),
        0,
    )
    for bit in [1] + high_bits("seq")[::-1]:
        got = swap(after(small, attn_own) if bit > 2 else small, "seq", bit)
        upper = (seq & bit) != 0
        small = jnp.concatenate([jnp.where(upper, got, small), jnp.where(upper, small, got)], axis=0)
    small = small.astype(f32)
    gain_one = small[:, 3 * NST].reshape(dim)
    gain_two = small[:, 3 * NST + 1].reshape(dim)
    params = small[:, : 3 * NST].transpose(1, 0, 2).reshape(3 * NST, dim)
    params = lax.dynamic_slice_in_dim(params, me * cols, cols, 1)
    params = jnp.broadcast_to(params[:, None], (3 * NST, TEAM, cols)).reshape((3, NST) + tile)
    rate, gin, gout = params[0], params[1], params[2]
    half_rate = rate[:, : tile[0] // 2]

    by_channel = like((NST, cols), f32)
    init, near_init, *end_cot = call(
        cut_states_kernel,
        "cut_states",
        (by_channel,) * 6,
        (idx, h_init[0].T, after(d_h_ends[0, 0].T, share_attn[1])),
    )
    init, init_twice, end_first, end_second = call(
        join_states_kernel,
        "join_states",
        tuple(like((NST,) + t, f32) for t in (half_tile, tile, half_tile, half_tile)),
        (half, init, swap_team(near_init, 1), *trade_team(end_cot)),
    )
    end_cot = [end_first, end_second]

    def by_half(a, axis=1):
        n = a.shape[axis] // 2
        own, other = lax.slice_in_dim(a, 0, n, axis=axis), lax.slice_in_dim(a, n, 2 * n, axis=axis)
        return ordered([own, other], seq % 2)

    def by_owner(first, second):
        return jnp.concatenate(ordered([first, second], seq % 2), axis=1)

    inputs_low, inv_one, u = first_norm(idx, after(gain_one, attn_first), x_blocks)

    a = jnp.exp(-rate)
    s_mid, s_end = local_ends(u, a)
    attn_last = attn.across(1, s_end)
    up_first = up.rest((attn_second, s_end))
    decay = jnp.exp(-half_rate * rows)
    first_end, second_end = by_half(gin * s_end)
    span = 2 * rows

    def chain(inclusive, back, wait):
        exclusive, step = jnp.zeros_like(inclusive), 1
        while step < ns // 2:
            pairs = [(k, k + 2 * step) for k in range(ns - 2 * step)]
            got = lax.ppermute(inclusive, "seq", [(t, f) for f, t in pairs] if back else pairs)
            if step == 1:
                got = after(got, wait)
            exclusive = exclusive + jnp.exp(-half_rate * (span * (step - 1))) * got
            inclusive = inclusive + jnp.exp(-half_rate * (span * step)) * got
            step *= 2
        return exclusive

    entering = chain(after(decay * first_end + second_end, attn_third), False, (up_first, attn_last))
    state_zero = jnp.exp(-half_rate * (span * block).astype(f32)) * init + entering
    state_one = decay * state_zero + first_end
    state_two = decay * state_one + second_end
    state_in = by_owner(state_zero, state_one)
    ends = call(cut_ends_kernel, "cut_ends", (by_channel,) * TEAM, (half, state_one, state_two))
    ends = call(join_ends_kernel, "join_ends", like((NST, dim), f32), (idx, *trade_team(ends)))
    on_second = by_owner(jnp.zeros_like(init), jnp.ones_like(init))
    h_mid = jnp.exp(-rate * (rows - CTX)) * state_in + gin * s_mid
    h_mid = jnp.where(on_second > 0, h_mid, init_twice)
    y_first, y_second = contexts(half, u, a, gin * on_second, gout, h_mid)
    passed = lax.ppermute(y_second, "seq", [(k, k + 2) for k in range(ns - 2)])
    up_second = up.step(entering)
    up_third = up.across(0)
    places = jnp.stack([place[0], seq]).astype(jnp.int32)
    full_qkv, *full_out = place_weight(idx, places, [(attn.pieces, 0, 1, 0)], 3 * width)
    full_out = trade_team(full_out)
    context = jnp.where(block == 0, y_first, after(passed, (up_second, full_qkv, down_pair)))
    down_first = down.rest(passed)

    full_qkv = after(full_qkv, up_third)
    qkv = dot_nn(inputs_low, full_qkv).astype(bf16)
    context = gather_team(context)
    g_blocks = gather_team(after(cotangent[0], context[2]))
    context = after(context, qkv)
    ctx_kv, context = call(
        context_kv_kernel,
        "context_kv",
        (like((2 * CTX, 2 * width), bf16), like((2 * CTX, dim), bf16)),
        (idx, full_qkv, *context),
    )
    attended = attend(half, qkv, ctx_kv)

    up_last = up.across(1, up_third)
    down.came = after(down.came, ctx_kv)
    attended = after(attended, (g_blocks[2], down.came, up_last))
    down_second = down.step()
    down_third = down.across(0, up_last)
    attended_parts = call(out_kernel, "out_dot", part_types(rows, dim), (idx, attended, *full_out))
    attended_parts = sum_team(attended_parts, None, (down_second, down_third))
    down.across(1, down_third)
    (full_up,) = place_weight(idx, places, [(up.pieces, 0, 1, 0)])
    (full_down,) = place_weight(idx, places, [(down.pieces, 0, 1, 0)])

    hidden, inv_two, mlp_in = call(
        second_norm_kernel,
        "second_norm",
        (like((rows, dim), f32), like((rows, 1), f32), like((rows, dim), bf16)),
        (tokens[0], *attended_parts[:3], gain_two[None]),
        0,
    )
    mlp_in = gather_team(mlp_in)
    mlp_in = after(mlp_in, full_up)
    act, d_pre, *d_mlp = feed_forward(mlp_in, g_blocks, full_up, full_down)
    d_down = down_grad(act, g_blocks)
    reduction = HalvedReduction if (nd, ns) == (4, 8) else Reduction
    sum_down = reduction(d_down, place)
    sum_down.step()
    d_up = up_grad(mlp_in, after(d_pre, sum_down.sent))
    sum_up = reduction(d_up, place)
    sum_up.step()
    result = dot_parts("down_dot", after(act, sum_up.sent), full_down)
    d_mlp = sum_team(d_mlp, d_down, result)
    sum_down.step(d_mlp[3])
    d_hidden, d_hidden_low, d_gain_two = call(
        hidden_grad_kernel,
        "hidden_grad",
        (like((rows, dim), f32), like((rows, dim), bf16), like((1, dim), f32)),
        (after(cotangent[0], sum_down.sent), hidden, inv_two, gain_two[None], *d_mlp[:3]),
        0,
    )
    hidden_blocks = gather_team(d_hidden_low)
    sum_down.step(d_hidden)

    d_attended = call(
        attended_grad_kernel,
        "attended_grad",
        jax.ShapeDtypeStruct(attended.shape, bf16),
        (idx, after(full_out[0], sum_down.sent), *full_out[1:], *hidden_blocks),
    )
    d_out = call(
        out_grad_kernel,
        "out_grad",
        (jax.ShapeDtypeStruct((width, cols), bf16),) * TEAM,
        (idx, after(attended, d_attended), *hidden_blocks),
    )
    d_qkv, d_ctx_kv = attend_back(half, qkv, ctx_kv, after(d_attended, d_out))
    d_out = trade_team(d_out)
    sum_up.step(d_ctx_kv)
    sum_down.step(sum_up.sent)
    d_context = call(
        context_grad_kernel,
        "context_grad",
        part_types(2 * CTX, cols),
        (idx, after(d_ctx_kv, (sum_up.sent, sum_down.sent, d_out)), full_qkv),
    )
    d_attn = attn_grad(idx, inputs_low, after(d_qkv, d_context), context, d_ctx_kv, d_out)
    sum_attn = reduction(d_attn, place)
    d_context = sum_team(d_context, None, d_attn)
    d_context = call(context_sum_kernel, "context_sum", like((2 * CTX, cols), bf16), d_context[:3], 0)
    came = lax.ppermute(d_context, "seq", [(k + 2, k) for k in range(ns - 2)])
    sum_attn.step(d_context)
    flags = jnp.stack([seq % 2, block]).astype(jnp.int32)
    dy0_full = call(first_rows_kernel, "first_rows", like((CTX,) + tile, f32), (flags, d_context))
    dy, dy_full = call(
        context_rows_kernel,
        "context_rows",
        (like((CTX,) + half_tile, f32), like((CTX,) + tile, f32)),
        (flags, after(came, (ends, dy0_full, sum_attn.sent))),
    )

    lam_mid = tail_adjoint(dy, a, gout)
    g_second = jnp.exp(-half_rate * (rows - CTX + 1)) * lam_mid + decay * end_cot[1]
    d_down_pair = sum_down.last()
    d_a, d_gout, g_init = first_context_back(after(dy0_full, lam_mid), a, gout, init_twice)
    leaving = chain(decay * (end_cot[0] + g_second), True, (g_init, d_down_pair[1], sum_attn.out if reduction is HalvedReduction else g_init))
    down_blocks = spread_places(d_down_pair)
    sum_up.step(leaving)
    sum_attn.step(sum_up.sent)
    result = sum_team(result, d_context)
    lam_end = by_owner(end_cot[0] + g_second + decay * leaving, end_cot[1] + leaving)
    du, d_gin, d_a, d_gout, g_in = ssm_back(
        u, dy_full, a, gin, gout, state_in, after(lam_end, sum_attn.sent), d_a, d_gout
    )

    *d_inputs, d_gain_one = call(
        inputs_grad_kernel,
        "inputs_grad",
        part_types(rows, dim) + (jax.ShapeDtypeStruct((1, dim), f32),),
        (idx, d_qkv, full_qkv, after(du, result[:3]), inv_one, *x_blocks),
        scratch_shapes=[pltpu.VMEM((rows, dim), f32)],
    )
    sum_up.step((d_gain_one, down_blocks))
    sum_attn.step(sum_up.sent)
    d_inputs = after(d_inputs, sum_attn.sent)
    small_rows = (3 * NST * cols + 2 * dim + 2 * NST * cols) // LANES
    pack = call(
        small_pack_kernel,
        "small_pack",
        like((small_rows, LANES), f32),
        (flags, a, d_a, d_gin, d_gout, g_in, g_init, d_gain_one, d_gain_two),
    )
    small, first, *others = pack, *high_bits("seq")
    pack = pack + swap(pack, "seq", first)
    *d_inputs, d_inputs_far = sum_team(d_inputs, small)
    d_tokens = call(
        tokens_grad_kernel,
        "tokens_grad",
        like((rows, dim), bf16),
        (d_hidden, tokens[0], inv_one[:rows], gain_one[None], *d_inputs),
        0,
    )

    up_blocks = spread_places(after(sum_up.last(), d_tokens))
    d_down = spread_weight("down", down_blocks, idx, [w_down.shape])[0]
    if fb % LANES:
        d_up = spread_narrow(up_blocks, idx, w_up.shape, fb)
    else:
        d_up = spread_weight("up", up_blocks, idx, [w_up.shape], fb)[0]
    result = after(result[:3], d_gain_one)
    result = call(result_kernel, "result_sum", like((rows, dim), bf16), (hidden, *result), 0)
    sum_attn.step((pack, d_tokens, result))
    for bit in others:
        pack = pack + swap(pack, "seq", bit)
    one, two = 3 * NST * cols // LANES, 3 * NST * cols // LANES + 2 * dim // LANES
    shared = pack[:two]
    for bit in high_bits("dp"):
        shared = shared + swap(shared, "dp", bit)
    packs = gather_team(after(jnp.concatenate([shared, pack[two:]], axis=0), (d_down, d_up)))
    if shard == LANES:
        spots = jnp.stack([me ^ (seq * shard // cols), seq]).astype(jnp.int32)
        gains, *d_params, state_grad = call(
            small_kernel,
            "small_grads",
            (like((2, shard), f32),) + (like((NST, shard), f32),) * 4,
            (spots, *packs),
        )
        d_params, state_grad = [p.T for p in d_params], state_grad.T[None]
    else:
        packs = jnp.stack(packs)
        gains = packs[:, one:two].sum(0).reshape(2, ns, shard)
        gains = pick(gains, seq, 1)
        member = me ^ (seq * shard // cols)
        inner = seq * shard % cols
        chosen = pick(packs, member)
        d_params = chosen[:one].reshape(3, cols // LANES, NST, LANES).transpose(0, 2, 1, 3)
        d_params = d_params.reshape(3 * NST, cols)
        d_params = lax.dynamic_slice_in_dim(d_params, inner, shard, 1).reshape(3, NST, shard)
        d_params = d_params.transpose(0, 2, 1)
        state_grad = chosen[two:].reshape(2, cols // LANES, NST, LANES).transpose(2, 0, 1, 3)
        state_grad = state_grad.reshape(NST, 2, cols)
        state_grad = pick(state_grad, member % 2, 1)
        state_grad = lax.dynamic_slice_in_dim(state_grad, inner, shard, 1).T[None]

    d_wqkv, d_out = spread_weight("attn", spread_places(after(sum_attn.last(), pack)), idx, [w_qkv.shape, w_out.shape])
    return (
        result[None],
        d_tokens[None],
        d_wqkv,
        d_out,
        d_up,
        d_down,
        gains[0],
        gains[1],
        d_params[0],
        d_params[1],
        d_params[2],
        state_grad,
        ends.T[None, None],
    )


def solution(mesh):
    return jax.shard_map(
        on_device,
        mesh=mesh,
        in_specs=(
            P("dp", "seq", None),
            P("seq", None),
            P("seq", None),
            P("seq", None),
            P("seq", None),
            P("seq"),
            P("seq"),
            P("seq", None),
            P("seq", None),
            P("seq", None),
            P("dp", None, None),
            P("dp", "seq", None),
            P("dp", "seq", None, None),
        ),
        out_specs=(
            P("dp", "seq", None),
            P("dp", "seq", None),
            P("seq", None),
            P("seq", None),
            P("seq", None),
            P("seq", None),
            P("seq"),
            P("seq"),
            P("seq", None),
            P("seq", None),
            P("seq", None),
            P("dp", "seq", None),
            P("dp", "seq", None, None),
        ),
        check_vma=False,
    )
```
